32 devices in a mesh: ctx: 4 (over y, core), seq: 2 (over x), fsdp: 4 (over z).
Axes of the slice: x: 2, y: 2, z: 4, core: 2. Of those that a mesh axis runs over, the one named last changes fastest.
Arguments:
- tokens: int32 [8, 1024], replicated, may hold values from 0 to 50303
- segments: int32 [8, 1024], replicated, may hold values from -1 to 129, as said below
- next_ids: int32 [8, 1024], replicated, may hold values from 0 to 50303
- second_ids: int32 [8, 1024], replicated, may hold values from 0 to 50303
- table: float32 [51328, 768], P(('seq', 'fsdp'))
- attn_in: float32 [2, 768, 2304], P(None, ('seq', 'fsdp')), may hold values from -0.21875 to 0.21875
- attn_out: float32 [3, 768, 768], P(None, ('seq', 'fsdp'))
- mlp_in: float32 [2, 768, 3072], P(None, ('seq', 'fsdp')), may hold values from -0.21875 to 0.21875
- mlp_out: float32 [2, 3072, 768], P(None, ('seq', 'fsdp')), may hold values from -0.109375 to 0.109375
- vectors: float32 [26, 768], replicated
- table_rows: float32 [51328], P(('seq', 'fsdp')), may hold values from 6.0666305e-10 to 9.706609e-09
- table_cols: float32 [768], replicated, may hold values from 6.0666305e-10 to 9.706609e-09
- attn_in_rows: float32 [2, 768], P(None, ('seq', 'fsdp')), may hold values from 3.1789145e-07 to 1.2715658e-06
- attn_in_cols: float32 [2, 2304], replicated, may hold values from 3.1789145e-07 to 1.2715658e-06
- attn_out_rows: float32 [3, 768], P(None, ('seq', 'fsdp')), may hold values from 3.1789145e-07 to 1.2715658e-06
- attn_out_cols: float32 [3, 768], replicated, may hold values from 3.1789145e-07 to 1.2715658e-06
- mlp_in_rows: float32 [2, 768], P(None, ('seq', 'fsdp')), may hold values from 3.1789145e-07 to 1.2715658e-06
- mlp_in_cols: float32 [2, 3072], replicated, may hold values from 3.1789145e-07 to 1.2715658e-06
- mlp_out_rows: float32 [2, 3072], P(None, ('seq', 'fsdp')), may hold values from 3.1789145e-07 to 1.2715658e-06
- mlp_out_cols: float32 [2, 768], replicated, may hold values from 3.1789145e-07 to 1.2715658e-06
- vector_state: float32 [26, 768], replicated, may hold values from 3.1789145e-07 to 1.2715658e-06
Outputs:
- loss_sum: float32 [], replicated
- norms: float32 [12], replicated
- table_grad: float32 [51328, 768], P(('seq', 'fsdp'))
- table_rows_new: float32 [51328], P(('seq', 'fsdp'))
- table_cols_new: float32 [768], replicated
- table_new: float32 [51328, 768], P(('seq', 'fsdp'))
- table_copy: bfloat16 [51328, 768], P(('seq', 'fsdp'))
- attn_in_grad: float32 [2, 768, 2304], P(None, ('seq', 'fsdp'))
- attn_in_rows_new: float32 [2, 768], P(None, ('seq', 'fsdp'))
- attn_in_cols_new: float32 [2, 2304], replicated
- attn_in_new: float32 [2, 768, 2304], P(None, ('seq', 'fsdp'))
- attn_in_copy: bfloat16 [2, 768, 2304], P(None, ('seq', 'fsdp'))
- attn_out_grad: float32 [3, 768, 768], P(None, ('seq', 'fsdp'))
- attn_out_rows_new: float32 [3, 768], P(None, ('seq', 'fsdp'))
- attn_out_cols_new: float32 [3, 768], replicated
- attn_out_new: float32 [3, 768, 768], P(None, ('seq', 'fsdp'))
- attn_out_copy: bfloat16 [3, 768, 768], P(None, ('seq', 'fsdp'))
- mlp_in_grad: float32 [2, 768, 3072], P(None, ('seq', 'fsdp'))
- mlp_in_rows_new: float32 [2, 768], P(None, ('seq', 'fsdp'))
- mlp_in_cols_new: float32 [2, 3072], replicated
- mlp_in_new: float32 [2, 768, 3072], P(None, ('seq', 'fsdp'))
- mlp_in_copy: bfloat16 [2, 768, 3072], P(None, ('seq', 'fsdp'))
- mlp_out_grad: float32 [2, 3072, 768], P(None, ('seq', 'fsdp'))
- mlp_out_rows_new: float32 [2, 3072], P(None, ('seq', 'fsdp'))
- mlp_out_cols_new: float32 [2, 768], replicated
- mlp_out_new: float32 [2, 3072, 768], P(None, ('seq', 'fsdp'))
- mlp_out_copy: bfloat16 [2, 3072, 768], P(None, ('seq', 'fsdp'))
- vector_grad: float32 [26, 768], replicated
- vector_state_new: float32 [26, 768], replicated
- vectors_new: float32 [26, 768], replicated
The draws below stay inside these ranges and needn't reach their ends.
Inputs may be any that keep to these rules, and one draw needn't show every extreme that they name: `segments`: segment numbers never fall along a sequence; -1 marks padding, which stands at the start of every sequence, before its first document; documents are contiguous; every sequence's last document number is the largest.
All inputs are finite; a program needn't handle non-finite values.
Results may differ from the reference program's by a relative error of at most 0.0035.
The reference program's roundings to bfloat16 on the way count: a program that leaves them out, or rounds other values in their place, can miss the bound.
Values may be sent and summed in bfloat16 or wider, within the bound.
No kernel may reach another device: no remote copies, remote signals or barrier semaphores. Data moves between devices by JAX's collectives and lax.ppermute only.
A program may use at most 320 MiB of HBM per device.

```python
import math
import jax
import jax.numpy as jnp
import numpy as np
from jax import lax

D = 768
HEADS = 12
HEAD = 64
FF = 3072
VOCAB = 50304
LAYERS = 2
LEN = 1024
SEQS = 8
TABLE = 51328
NVEC = 26
N_CTX = 4


def base_draw(key, shape):
    return jax.random.normal(key, shape, jnp.float32)


def draw_segments(key, part):
    key = jax.random.fold_in(key, 17)
    ctx_span = LEN // N_CTX
    keys = jax.random.split(key, 2)
    front_gap = jax.random.randint(keys[0], (SEQS, 1), ctx_span // 2, 3 * ctx_span // 4 + 1)
    long_begin = front_gap + 1 + jax.random.randint(keys[1], (SEQS, 1), 0, ctx_span - 3 * ctx_span // 4 - 1)
    long_finish = LEN - ctx_span // 2
    steps_at = jnp.arange(LEN, dtype=jnp.int32)[None, :]
    starts = (steps_at == front_gap) | (steps_at == long_begin) | (steps_at >= long_finish)
    counted = jnp.cumsum(starts.astype(jnp.int32), axis=1) - 1
    return jnp.where(steps_at < front_gap, -1, counted).astype(jnp.int32)


def draw_table(key, part):
    key = jax.random.fold_in(key, 5)
    row_ids = jnp.arange(TABLE, dtype=jnp.float32)[:, None]
    climb = 2.0
    rise = jnp.where(row_ids < VOCAB, 1.0 + climb * row_ids / VOCAB, 1.0)
    spread = jnp.where(row_ids < VOCAB, D ** (-0.5), 0.5)
    return base_draw(key, (TABLE, D)) * rise * spread


def draw_attn_out(key, part):
    key = jax.random.fold_in(key, 23)
    stack_ids = jnp.arange(LAYERS + 1)[:, None, None]
    spread = jnp.where(stack_ids < LAYERS, 8.0, 1.0) * D ** (-0.5)
    return base_draw(key, (LAYERS + 1, D, D)) * spread


def draw_vectors(key, part):
    key = jax.random.fold_in(key, 31)
    keys = jax.random.split(key, 2)
    row_ids = jnp.arange(NVEC)[:, None]
    column_ids = jnp.arange(D, dtype=jnp.float32)[None, :]
    kind = row_ids % 12
    is_gain = (row_ids < 12 * LAYERS) & ((kind == 0) | (kind == 5)) | (row_ids == 12 * LAYERS)
    gains = (0.5 + column_ids / D) * (1.0 + 0.1 * base_draw(keys[0], (NVEC, D)))
    biases = 0.1 * base_draw(keys[1], (NVEC, D))
    return jnp.where(is_gain, gains, biases)


def place_ends(drawn, key, least, largest):
    longest = drawn.shape.index(max(drawn.shape))
    spots = []
    for shift in (0, 1):
        where = [jax.random.randint(jax.random.fold_in(key, axis), (), 0, length) for axis, length in enumerate(drawn.shape)]
        where[longest] = (where[longest] + shift) % drawn.shape[longest]
        spots.append(tuple(where))
    return drawn.at[spots[0]].set(least).at[spots[1]].set(largest)


def levels(own_key, dims, cuts, low, high):
    factor_of = 1.0
    for axis_at, blocks in cuts:
        draws = jax.random.uniform(jax.random.fold_in(jax.random.fold_in(own_key, 6), axis_at), (blocks,), jnp.float32, low / len(cuts), high / len(cuts))
        factor_of = factor_of * jnp.repeat(jnp.exp(draws), dims[axis_at] // blocks).reshape((-1,) + (1,) * (len(dims) - 1 - axis_at))
    return factor_of


def rank_bounds(amount, lean):
    loads = [(1 << 20) // math.isqrt(grade ** lean) + 1 for grade in range(1, amount + 1)]
    scale = 1 + sum(loads) // (1 << 30)
    return np.cumsum(np.array([max(1, weight // scale) for weight in loads]))


def skewed_ids(own_key, shape, number_of, slope):
    grid = rank_bounds(number_of, slope)
    pick = jax.random.randint(jax.random.fold_in(own_key, 1), shape, 0, int(grid[number_of - 1]))
    rank = jnp.searchsorted(jnp.asarray(grid, jnp.int32), pick, side="right")
    return jax.random.permutation(jax.random.fold_in(own_key, 2), number_of)[rank].astype(jnp.int32)


def bell_draw(key, dims, scale, reach, cuts=(), kind=jnp.bfloat16):
    entries = scale * jax.random.normal(key, dims, jnp.float32)
    if cuts:
        entries = entries * levels(key, dims, cuts, -0.22, 0.18)
    return jnp.clip(entries, -reach, reach).astype(kind)


def setup_inputs(seed: int = 0) -> dict:
    arg_keys = jax.random.split(jax.random.key(seed), 22)
    return {
        "tokens": place_ends(skewed_ids(arg_keys[0], (SEQS, LEN), VOCAB, 2), jax.random.fold_in(arg_keys[0], 3), 0, VOCAB - 1).astype(jnp.int32),
        "segments": draw_segments(jax.random.fold_in(arg_keys[21], 71), 0),
        "next_ids": place_ends(skewed_ids(arg_keys[2], (SEQS, LEN), VOCAB, 2), jax.random.fold_in(arg_keys[2], 3), 0, VOCAB - 1).astype(jnp.int32),
        "second_ids": place_ends(skewed_ids(arg_keys[3], (SEQS, LEN), VOCAB, 2), jax.random.fold_in(arg_keys[3], 3), 0, VOCAB - 1).astype(jnp.int32),
        "table": draw_table(jax.random.fold_in(arg_keys[21], 71), 0),
        "attn_in": bell_draw(arg_keys[5], (LAYERS, D, 3 * D), D ** -0.5, 0.21875, ((1, 8),), jnp.float32),
        "attn_out": draw_attn_out(jax.random.fold_in(arg_keys[21], 71), 0),
        "mlp_in": bell_draw(arg_keys[7], (LAYERS, D, FF), D ** -0.5, 0.21875, ((1, 8),), jnp.float32),
        "mlp_out": bell_draw(arg_keys[8], (LAYERS, FF, D), FF ** -0.5, 0.109375, ((1, 8),), jnp.float32),
        "vectors": draw_vectors(jax.random.fold_in(arg_keys[21], 71), 0),
        "table_rows": jnp.clip(jnp.exp(math.log(9.706608850024168e-09) - 2.7725887 * jax.random.uniform(arg_keys[10], (TABLE,), jnp.float32) ** levels(arg_keys[10], (TABLE,), ((0, 8),), -0.2, 0.2)), 6.066630531265105e-10, 9.706608850024168e-09),
        "table_cols": jnp.clip(jnp.exp(jax.random.uniform(arg_keys[11], (D,), jnp.float32, math.log(6.066630531265105e-10), math.log(9.706608850024168e-09))), 6.066630531265105e-10, 9.706608850024168e-09),
        "attn_in_rows": jnp.clip(jnp.exp(math.log(1.271565793103946e-06) - 1.3862944 * jax.random.uniform(arg_keys[12], (LAYERS, D), jnp.float32) ** levels(arg_keys[12], (LAYERS, D), ((1, 8),), -0.2, 0.2)), 3.178914482759865e-07, 1.271565793103946e-06),
        "attn_in_cols": jnp.clip(jnp.exp(jax.random.uniform(arg_keys[13], (LAYERS, 3 * D), jnp.float32, math.log(3.178914482759865e-07), math.log(1.271565793103946e-06))), 3.178914482759865e-07, 1.271565793103946e-06),
        "attn_out_rows": jnp.clip(jnp.exp(math.log(1.271565793103946e-06) - 1.3862944 * jax.random.uniform(arg_keys[14], (LAYERS + 1, D), jnp.float32) ** levels(arg_keys[14], (LAYERS + 1, D), ((1, 8),), -0.2, 0.2)), 3.178914482759865e-07, 1.271565793103946e-06),
        "attn_out_cols": jnp.clip(jnp.exp(jax.random.uniform(arg_keys[15], (LAYERS + 1, D), jnp.float32, math.log(3.178914482759865e-07), math.log(1.271565793103946e-06))), 3.178914482759865e-07, 1.271565793103946e-06),
        "mlp_in_rows": jnp.clip(jnp.exp(math.log(1.271565793103946e-06) - 1.3862944 * jax.random.uniform(arg_keys[16], (LAYERS, D), jnp.float32) ** levels(arg_keys[16], (LAYERS, D), ((1, 8),), -0.2, 0.2)), 3.178914482759865e-07, 1.271565793103946e-06),
        "mlp_in_cols": jnp.clip(jnp.exp(jax.random.uniform(arg_keys[17], (LAYERS, FF), jnp.float32, math.log(3.178914482759865e-07), math.log(1.271565793103946e-06))), 3.178914482759865e-07, 1.271565793103946e-06),
        "mlp_out_rows": jnp.clip(jnp.exp(math.log(1.271565793103946e-06) - 1.3862944 * jax.random.uniform(arg_keys[18], (LAYERS, FF), jnp.float32) ** levels(arg_keys[18], (LAYERS, FF), ((1, 8),), -0.2, 0.2)), 3.178914482759865e-07, 1.271565793103946e-06),
        "mlp_out_cols": jnp.clip(jnp.exp(jax.random.uniform(arg_keys[19], (LAYERS, D), jnp.float32, math.log(3.178914482759865e-07), math.log(1.271565793103946e-06))), 3.178914482759865e-07, 1.271565793103946e-06),
        "vector_state": jnp.clip(jnp.exp(jax.random.uniform(arg_keys[20], (NVEC, D), jnp.float32, math.log(3.178914482759865e-07), math.log(1.271565793103946e-06))), 3.178914482759865e-07, 1.271565793103946e-06),
    }


EPS_NORM = 1e-05
EPS_SQUARE = 1e-30
EPS_SCALE = 0.001
DECAY = 0.5
CLIP = 0.4
RATE = 0.6
SECOND = 0.3
MASKED = -1e+30
HIGHEST = lax.Precision.HIGHEST

@jax.custom_vjp
def low(v):
    return lax.optimization_barrier(v.astype(jnp.bfloat16)).astype(jnp.float32)

@jax.custom_vjp
def low_back(v):
    return v

def low_keep(v):
    return (low(v), None)

def low_pass(kept, grad):
    return (grad,)

def back_keep(v):
    return (v, None)

def back_low(kept, grad):
    return (low(grad),)
low.defvjp(low_keep, low_pass)
low_back.defvjp(back_keep, back_low)

def matmul(left, right):
    return jnp.dot(left, right, precision=HIGHEST)

def layer_norm(stream, gain, offset):
    center = stream - lax.optimization_barrier(jnp.mean(stream, -1, keepdims=True))
    spread = lax.optimization_barrier(jnp.mean(center * center, -1, keepdims=True))
    return center * lax.rsqrt(spread + EPS_NORM) * gain + offset

def gelu_tanh(value):
    return jax.nn.gelu(value, approximate=True)

def positions_of(segments):
    steps_at = jnp.arange(segments.shape[-1], dtype=jnp.int32)
    before = jnp.concatenate([jnp.full(segments.shape[:-1] + (1,), -2, jnp.int32), segments[..., :-1]], -1)
    starts = jnp.where(segments != before, steps_at, 0).astype(jnp.int32)
    first = lax.cummax(starts, axis=segments.ndim - 1)
    return jnp.where(segments >= 0, steps_at - first, 0).astype(jnp.int32)

def layer(stream, weights, vec, allowed):
    w_in, w_out, w_fc, w_down = weights
    normed = low(layer_norm(stream, vec[0], vec[1]))
    bias_qkv = jnp.concatenate([vec[2], jnp.zeros_like(vec[2]), vec[3]])
    qkv = low(low_back(matmul(normed, w_in) + bias_qkv))
    shaped = qkv.reshape(LEN, 3, HEADS, HEAD)
    scores = low_back(jnp.einsum('qhd,khd->hqk', shaped[:, 0], shaped[:, 1], precision=HIGHEST) * HEAD ** (-0.5))
    scores = jnp.where(allowed[None], scores, MASKED)
    probs = low(jax.nn.softmax(scores, axis=-1))
    mixed = jnp.einsum('hqk,khd->qhd', probs, shaped[:, 2], precision=HIGHEST).reshape(LEN, D)
    mixed = low(low_back(mixed))
    branch = low_back(matmul(mixed, w_out) + vec[4])
    middle = stream + branch
    normed_two = low(layer_norm(middle, vec[5], vec[6]))
    hidden = low_back(matmul(normed_two, w_fc) + vec[8:12].reshape(-1))
    output = low_back(matmul(low(gelu_tanh(hidden)), w_down) + vec[7])
    sums = jnp.stack([jnp.sum(stream * stream), jnp.sum(branch * branch), jnp.sum(output * output)])
    return (middle + output, sums)

def head_loss(final_rows, second_rows, vocab, next_row, second_row, valid):
    stacked = jnp.concatenate([final_rows, second_rows], 0)
    targets = jnp.concatenate([next_row, second_row]).astype(jnp.int32)
    weight = jnp.concatenate([valid, SECOND * valid])
    size_block = min(256, stacked.shape[0])
    count = stacked.shape[0] // size_block

    def block_loss(args):
        rows_part, target_part, weight_part = args
        logits = low_back(matmul(rows_part, vocab.T))
        total = jax.nn.logsumexp(logits, axis=-1)
        picked = jnp.take_along_axis(logits, target_part[:, None], axis=-1)[:, 0]
        return jnp.sum(weight_part * (total - picked))
    parts = lax.map(jax.checkpoint(block_loss), (stacked.reshape(count, size_block, D), targets.reshape(count, size_block), weight.reshape(count, size_block)))
    return jnp.sum(parts)

def sequence(params_low, vec, ints):
    tab, w_in, w_out, w_fc, w_down = params_low
    tokens_row, segments_row, next_row, second_row = ints
    positions = positions_of(segments_row)
    valid = (segments_row >= 0).astype(jnp.float32)
    stream = low_back(tab[tokens_row] + tab[VOCAB + positions])
    steps_at = jnp.arange(LEN, dtype=jnp.int32)
    allowed = (steps_at[:, None] == steps_at[None]) | (steps_at[None] < steps_at[:, None]) & (segments_row[:, None] == segments_row[None]) & (segments_row[None] >= 0)
    sums = []
    for layer_at in range(LAYERS):
        stream, layer_sums = layer(stream, (w_in[layer_at], w_out[layer_at], w_fc[layer_at], w_down[layer_at]), vec[12 * layer_at:12 * layer_at + 12], allowed)
        sums.append(layer_sums)
    final = low(layer_norm(stream, vec[12 * LAYERS], vec[12 * LAYERS + 1]))
    second = low(low_back(matmul(final, w_out[LAYERS])))
    loss = head_loss(final, second, tab[:VOCAB], next_row, second_row, valid)
    return (loss, jnp.stack(sums))

def finish(weight, update):
    size = jnp.sqrt(jnp.mean(update * update))
    update = update / jnp.maximum(1.0, size / CLIP)
    scale = jnp.maximum(EPS_SCALE, jnp.sqrt(jnp.mean(weight * weight)))
    return (weight - RATE * scale * update, size)

def factored(weight, grad, rows_state, cols_state):
    square = grad * grad + EPS_SQUARE
    rows_new = DECAY * rows_state + (1.0 - DECAY) * lax.optimization_barrier(jnp.mean(square, -1))
    cols_new = DECAY * cols_state + (1.0 - DECAY) * lax.optimization_barrier(jnp.mean(square, -2))
    scale = rows_new[..., :, None] * cols_new[..., None, :] / lax.optimization_barrier(jnp.mean(rows_new, -1))[..., None, None]
    new, size = finish(weight, grad * lax.rsqrt(scale))
    return (new, size, rows_new, cols_new)

def reference(tokens, segments, next_ids, second_ids, table, attn_in, attn_out, mlp_in, mlp_out, vectors, table_rows, table_cols, attn_in_rows, attn_in_cols, attn_out_rows, attn_out_cols, mlp_in_rows, mlp_in_cols, mlp_out_rows, mlp_out_cols, vector_state):
    total_tokens = SEQS * LEN

    def objective(params):
        vec = params[5]
        params_low = tuple((low(piece) for piece in params[:5]))

        def one(carry, ints):
            loss, sums = sequence(params_low, vec, ints)
            return ((carry[0] + loss, carry[1] + sums), None)
        start = (jnp.zeros((), jnp.float32), jnp.zeros((LAYERS, 3), jnp.float32))
        (loss, sums), _ = lax.scan(jax.checkpoint(one), start, (tokens, segments, next_ids, second_ids))
        return (loss / total_tokens, (loss, sums))
    params = (table, attn_in, attn_out, mlp_in, mlp_out, vectors)
    _, back, aux = jax.vjp(objective, params, has_aux=True)
    grads = back(jnp.ones((), jnp.float32))[0]
    loss_sum, sums = aux
    table_new, table_size, table_rows_new, table_cols_new = factored(table, grads[0], table_rows, table_cols)
    in_new, in_size, in_rows_new, in_cols_new = factored(attn_in, grads[1], attn_in_rows, attn_in_cols)
    out_new, out_size, out_rows_new, out_cols_new = factored(attn_out, grads[2], attn_out_rows, attn_out_cols)
    fc_new, fc_size, fc_rows_new, fc_cols_new = factored(mlp_in, grads[3], mlp_in_rows, mlp_in_cols)
    down_new, down_size, down_rows_new, down_cols_new = factored(mlp_out, grads[4], mlp_out_rows, mlp_out_cols)
    vector_grad = grads[5]
    vector_state_new = DECAY * vector_state + (1.0 - DECAY) * (vector_grad * vector_grad + EPS_SQUARE)
    vectors_new, vector_size = finish(vectors, vector_grad * lax.rsqrt(vector_state_new))
    norms = jnp.concatenate([jnp.sqrt(sums.reshape(-1) / total_tokens), jnp.stack([table_size, in_size, out_size, fc_size, down_size, vector_size])])
    return (loss_sum, norms, grads[0], table_rows_new, table_cols_new, table_new, table_new.astype(jnp.bfloat16), grads[1], in_rows_new, in_cols_new, in_new, in_new.astype(jnp.bfloat16), grads[2], out_rows_new, out_cols_new, out_new, out_new.astype(jnp.bfloat16), grads[3], fc_rows_new, fc_cols_new, fc_new, fc_new.astype(jnp.bfloat16), grads[4], down_rows_new, down_cols_new, down_new, down_new.astype(jnp.bfloat16), vector_grad, vector_state_new, vectors_new)
```

```python
import jax
import jax.numpy as jnp
from jax import lax
from jax.sharding import PartitionSpec as P

HEADS = 12
VOCAB = 50304


EPS_NORM = 1e-05
EPS_SQUARE = 1e-30
EPS_SCALE = 0.001
DECAY = 0.5
CLIP = 0.4
RATE = 0.6
SECOND = 0.3
MASKED = -1e30


def layer_norm(stream, gain, offset):
    center = stream - jnp.mean(stream, -1, keepdims=True)
    spread = jnp.mean(center * center, -1, keepdims=True)
    return center * lax.rsqrt(spread + EPS_NORM) * gain + offset


def gelu_tanh(value):
    return jax.nn.gelu(value, approximate=True)


def positions_of(segments):
    steps_at = jnp.arange(segments.shape[-1], dtype=jnp.int32)
    before = jnp.concatenate(
        [jnp.full(segments.shape[:-1] + (1,), -2, jnp.int32), segments[..., :-1]], -1
    )
    starts = jnp.where(segments != before, steps_at, 0)
    first = lax.cummax(starts, axis=segments.ndim - 1)
    return jnp.where(segments >= 0, steps_at - first, 0)


def product(left, right):
    return jnp.dot(left, right, preferred_element_type=jnp.float32)


def inner(left, right):
    return lax.dot_general(
        left, right, (((1,), (1,)), ((), ())), preferred_element_type=jnp.float32
    )


def outer(left, right):
    return lax.dot_general(
        left, right, (((0,), (0,)), ((), ())), preferred_element_type=jnp.float32
    )


def shift(block, axis, step):
    count = lax.axis_size(axis)
    return lax.ppermute(block, axis, [(i, (i + step) % count) for i in range(count)])


def shift_y(block, step):
    count = lax.axis_size("ctx")
    return lax.ppermute(block, "ctx", [(i, (i + 2 * step) % count) for i in range(count)])


def swap_core(block):
    count = lax.axis_size("ctx")
    return lax.ppermute(block, "ctx", [(i, i ^ 1) for i in range(count)])


def shift_seq(block, step):
    return shift(block, "seq", step)


def shift_fsdp(block, step):
    return shift(block, "fsdp", step)


def pick(parts, at, axis):
    return lax.dynamic_index_in_dim(parts, at, axis, False)


def scatter_sum(parts, mover, at, axis=0, sent=None):
    count = parts.shape[axis]
    total = pick(parts, at, axis)
    for step in range(1, count):
        piece = pick(parts, lax.rem(at + step, count), axis)
        if sent is not None:
            piece = piece.astype(sent)
        total = total + mover(piece, step).astype(total.dtype)
    return total


def gather_ordered(block, mover, at, count):
    parts = jnp.stack([block] + [mover(block, step) for step in range(1, count)])
    order = lax.rem(at - jnp.arange(count, dtype=jnp.int32) + count, count)
    return jnp.take(parts, order, axis=0, mode="clip")


def gather_near(block):
    n_y = lax.axis_size("ctx") // 2
    column = jnp.concatenate([block] + [shift_y(block, step) for step in range(1, n_y)], 0)
    return jnp.concatenate([column, swap_core(column)], 0)


def scatter_near(parts):
    n_y = lax.axis_size("ctx") // 2
    parts = parts.reshape((2, n_y, -1) + parts.shape[1:])
    column = parts[0] + swap_core(parts[1])
    total = column[0]
    for step in range(1, n_y):
        total = total + shift_y(column[step], n_y - step)
    return total


def half_of(block, at):
    width = block.shape[-1] // 2
    return jnp.where(at == 0, block[..., :width], block[..., width:])


def qkv_bias(vec):
    return jnp.concatenate([vec[2], jnp.zeros_like(vec[2]), vec[3]])


def attention_scores(query_low, keys, allowed, head_count):
    row_count, feature_width = query_low.shape
    head_size = feature_width // head_count
    scores = jnp.einsum(
        "qhd,khd->hqk",
        query_low.reshape(row_count, head_count, head_size),
        keys.reshape(-1, head_count, head_size),
        preferred_element_type=jnp.float32,
    ) * head_size ** (-0.5)
    return jnp.where(allowed[None], scores, MASKED)


def mix_values(probs_low, values, head_count):
    head_size = values.shape[1] // head_count
    mixed = jnp.einsum(
        "hqk,khd->qhd",
        probs_low,
        values.reshape(-1, head_count, head_size),
        preferred_element_type=jnp.float32,
    )
    return mixed.reshape(mixed.shape[0], -1)


def layer_forward(stream, weights, vec, allowed, head_count):
    w_in, w_out, w_fc, w_down = weights
    feature_width = stream.shape[1]
    a_low = layer_norm(stream, vec[0], vec[1]).astype(jnp.bfloat16)
    qkv_low = (product(a_low, w_in) + qkv_bias(vec)).astype(jnp.bfloat16)
    pairs = gather_near(qkv_low[:, feature_width:])
    keys, values = pairs[:, :feature_width], pairs[:, feature_width:]
    scores = attention_scores(qkv_low[:, :feature_width], keys, allowed, head_count)
    row_max = jnp.max(scores, -1)
    log_total = row_max + jnp.log(jnp.sum(jnp.exp(scores - row_max[..., None]), -1))
    probs = jnp.exp(scores - log_total[..., None])
    mixed_low = mix_values(probs.astype(jnp.bfloat16), values, head_count).astype(jnp.bfloat16)
    branch = product(mixed_low, w_out) + vec[4]
    middle = stream + branch
    m_low = layer_norm(middle, vec[5], vec[6]).astype(jnp.bfloat16)
    hidden = product(m_low, w_fc) + vec[8:12].reshape(-1)
    output = product(gelu_tanh(hidden).astype(jnp.bfloat16), w_down) + vec[7]
    sums = jnp.stack([jnp.sum(stream * stream), jnp.sum(branch * branch), jnp.sum(output * output)])
    kept = (stream, a_low, qkv_low, keys, values, log_total, mixed_low, middle, m_low, hidden)
    return (middle + output, kept, sums)


def shared_outer(pairs, core_at):
    lefts = [left for left, _ in pairs]
    rights = [right for _, right in pairs]
    away = swap_core(jnp.concatenate(lefts + [half_of(right, 1 - core_at) for right in rights], 1))
    at = 0
    whole_left = []
    for left in lefts:
        whole_left.append(jnp.concatenate([left, away[:, at : at + left.shape[1]]], 0))
        at += left.shape[1]
    grads = []
    for left, right in zip(whole_left, rights):
        width = right.shape[1] // 2
        whole_right = jnp.concatenate([half_of(right, core_at), away[:, at : at + width]], 0)
        at += width
        grads.append(outer(left, whole_right))
    return grads


def layer_backward(d_stream, kept, weights, vec, allowed, head_count, core_at, extra):
    stream, a_low, qkv_low, keys, values, log_total, mixed_low, middle, m_low, hidden = kept
    w_in, w_out, w_fc, w_down = weights
    row_count, feature_width = stream.shape
    head_size = feature_width // head_count
    scale = head_size ** (-0.5)
    norm_back_one = jax.vjp(layer_norm, stream, vec[0], vec[1])[1]
    query_low = qkv_low[:, :feature_width]
    probs = jnp.exp(attention_scores(query_low, keys, allowed, head_count) - log_total[..., None])
    probs_low = probs.astype(jnp.bfloat16)
    norm_back_two = jax.vjp(layer_norm, middle, vec[5], vec[6])[1]
    gelu_out, gelu_back = jax.vjp(gelu_tanh, hidden)
    u_low = gelu_out.astype(jnp.bfloat16)
    d_out_low = d_stream.astype(jnp.bfloat16)
    d_hidden_low = gelu_back(inner(d_out_low, w_down))[0].astype(jnp.bfloat16)
    first_grads = shared_outer(
        extra + [(m_low, d_hidden_low), (u_low, d_out_low)], core_at
    )
    d_m = inner(d_hidden_low, w_fc)
    d_two, d_gain_two, d_bias_two = norm_back_two(d_m)
    d_middle = d_stream + d_two
    d_middle_low = d_middle.astype(jnp.bfloat16)
    d_heads = (
        inner(d_middle_low, w_out).astype(jnp.bfloat16).reshape(row_count, head_count, head_size)
    )
    value_heads = values.reshape(-1, head_count, head_size)
    d_probs = jnp.einsum("qhd,khd->hqk", d_heads, value_heads, preferred_element_type=jnp.float32)
    d_scores = (probs * (d_probs - jnp.sum(probs * d_probs, -1, keepdims=True))).astype(
        jnp.bfloat16
    )
    d_query = (
        jnp.einsum(
            "hqk,khd->qhd",
            d_scores,
            keys.reshape(-1, head_count, head_size),
            preferred_element_type=jnp.float32,
        ).reshape(row_count, feature_width)
        * scale
    )
    d_keys = (
        jnp.einsum(
            "hqk,qhd->khd",
            d_scores,
            query_low.reshape(row_count, head_count, head_size),
            preferred_element_type=jnp.float32,
        ).reshape(-1, feature_width)
        * scale
    )
    d_values = jnp.einsum(
        "hqk,qhd->khd", probs_low, d_heads, preferred_element_type=jnp.float32
    ).reshape(-1, feature_width)
    d_pairs = scatter_near(jnp.concatenate([d_keys, d_values], 1))
    d_qkv_low = jnp.concatenate([d_query, d_pairs], 1).astype(jnp.bfloat16)
    later_grads = shared_outer([(a_low, d_qkv_low), (mixed_low, d_middle_low)], core_at)
    d_one, d_gain_one, d_bias_one = norm_back_one(inner(d_qkv_low, w_in))
    d_qkv = d_qkv_low.astype(jnp.float32)
    rows_head = jnp.stack(
        [
            d_gain_one,
            d_bias_one,
            jnp.sum(d_qkv[:, :feature_width], 0),
            jnp.sum(d_qkv[:, 2 * feature_width :], 0),
            jnp.sum(d_middle_low.astype(jnp.float32), 0),
            d_gain_two,
            d_bias_two,
            jnp.sum(d_out_low.astype(jnp.float32), 0),
        ]
    )
    vec_grad = jnp.concatenate(
        [rows_head, jnp.sum(d_hidden_low.astype(jnp.float32), 0).reshape(4, feature_width)], 0
    )
    return (d_middle + d_one, first_grads, later_grads, vec_grad)


def merge_stats(stats):
    for mover, axis in ((shift_seq, "seq"), (shift_fsdp, "fsdp")):
        parts = [stats] + [mover(stats, step) for step in range(1, lax.axis_size(axis))]
        top = parts[0][0]
        for part in parts[1:]:
            top = jnp.maximum(top, part[0])
        total = jnp.exp(parts[0][0] - top)
        picked = parts[0][1]
        for part in parts[1:]:
            total = total + jnp.exp(part[0] - top)
            picked = picked + part[1]
        stats = jnp.stack([top + jnp.log(total), picked])
    return stats


def local_index(ids, row_low, row_count):
    shifted = ids - row_low
    inside = (shifted >= 0) & (shifted < row_count)
    return (inside, jnp.clip(shifted, 0, row_count - 1))


def body(
    tokens,
    segments,
    next_ids,
    second_ids,
    table,
    attn_in,
    attn_out,
    mlp_in,
    mlp_out,
    vectors,
    table_rows,
    table_cols,
    attn_in_rows,
    attn_in_cols,
    attn_out_rows,
    attn_out_cols,
    mlp_in_rows,
    mlp_in_cols,
    mlp_out_rows,
    mlp_out_cols,
    vector_state,
):
    n_ctx = lax.axis_size("ctx")
    n_seq = lax.axis_size("seq")
    n_fsdp = lax.axis_size("fsdp")
    n_y = n_ctx // 2
    n_group = n_seq * n_fsdp
    ctx_at = lax.axis_index("ctx")
    seq_at = lax.axis_index("seq")
    fsdp_at = lax.axis_index("fsdp")
    y_at = ctx_at // 2
    core_at = lax.rem(ctx_at, 2)
    group_at = seq_at * n_fsdp + fsdp_at
    all_seqs, length = segments.shape
    seqs_dev = all_seqs // n_group
    ctx_span = length // n_ctx
    feature_width = table.shape[1]
    layer_count = attn_in.shape[0]
    head_count = HEADS
    total_tokens = all_seqs * length
    own_rows = seqs_dev * ctx_span
    block_start = ctx_at * ctx_span
    positions = positions_of(segments)

    def block_of(grid):
        return lax.dynamic_slice_in_dim(grid, block_start, ctx_span, 1)

    tok_block = block_of(tokens).reshape(-1)
    valid_block = (block_of(segments) >= 0).astype(jnp.float32).reshape(-1)
    next_block = block_of(next_ids).reshape(-1)
    second_block = block_of(second_ids).reshape(-1)
    my_segments = lax.dynamic_slice_in_dim(segments, group_at * seqs_dev, seqs_dev, 0)
    my_positions = lax.dynamic_slice_in_dim(positions, group_at * seqs_dev, seqs_dev, 0)
    near = jnp.asarray(
        [(side, step) for side in range(2) for step in range(n_y)], jnp.int32
    )
    near_ctx = 2 * lax.rem(y_at - near[:, 1] + n_y, n_y) + lax.rem(core_at + near[:, 0], 2)

    def near_order(grid):
        cut = grid.reshape(seqs_dev, n_ctx, ctx_span).transpose(1, 0, 2)
        return jnp.take(cut, near_ctx, axis=0, mode="clip").reshape(-1)

    def own_order(grid):
        return block_of(grid).reshape(-1)

    time_grid = jnp.broadcast_to(jnp.arange(length, dtype=jnp.int32)[None], (seqs_dev, length))
    seq_grid = jnp.broadcast_to(jnp.arange(seqs_dev, dtype=jnp.int32)[:, None], (seqs_dev, length))
    q_seg, k_seg = (own_order(my_segments), near_order(my_segments))
    q_time, k_time = (own_order(time_grid), near_order(time_grid))
    q_seq, k_seq = (own_order(seq_grid), near_order(seq_grid))
    allowed = (q_seq[:, None] == k_seq[None]) & (
        (q_time[:, None] == k_time[None])
        | (k_time[None] < q_time[:, None]) & (q_seg[:, None] == k_seg[None]) & (k_seg[None] >= 0)
    )
    rows_dev = table.shape[0]
    row_low = group_at * rows_dev
    rows_group = attn_in.shape[1]
    rows_part = rows_group // n_ctx
    down_cut = mlp_out.shape[1] // rows_group

    def pack_of(layer_at):
        down = mlp_out[layer_at].reshape(down_cut, rows_group, feature_width)
        return jnp.concatenate(
            [attn_in[layer_at], attn_out[layer_at], mlp_in[layer_at]]
            + [down[cut] for cut in range(down_cut)],
            1,
        ).astype(jnp.bfloat16)

    def gather_pack(pack):
        part = lax.dynamic_slice_in_dim(pack, ctx_at * rows_part, rows_part, 0)
        return lax.all_gather(part, ("seq", "fsdp", "ctx"), axis=0, tiled=True)

    in_width, out_width, fc_width = attn_in.shape[2], attn_out.shape[2], mlp_in.shape[2]

    def down_of(block):
        cut = block.reshape(n_group, rows_group, down_cut, feature_width)
        return cut.transpose(0, 2, 1, 3).reshape(-1, feature_width)

    def cut_pack(rest):
        return (
            rest[:, :out_width],
            rest[:, out_width : out_width + fc_width],
            down_of(rest[:, out_width + fc_width :]),
        )

    first_pack = pack_of(0)
    stored = [(gather_pack(first_pack[:, :in_width]),)]
    stored[0] = stored[0] + cut_pack(gather_pack(first_pack[:, in_width:]))
    for layer_at in range(1, layer_count):
        pack = pack_of(layer_at)
        if layer_at == layer_count - 1:
            pack = jnp.concatenate([pack, attn_out[layer_count].astype(jnp.bfloat16)], 1)
        pack = gather_pack(pack)
        if layer_at == layer_count - 1:
            head_weight = pack[:, -out_width:]
            pack = pack[:, :-out_width]
        stored.append((pack[:, :in_width],) + cut_pack(pack[:, in_width:]))

    tok_inside, tok_safe = local_index(tok_block, row_low, rows_dev)
    embed_term = jnp.where(
        tok_inside[:, None], jnp.take(table, tok_safe, axis=0, mode="clip"), 0.0
    ).astype(jnp.bfloat16)
    embed_term = embed_term.reshape(n_seq, n_fsdp, own_rows, feature_width)
    embed_term = scatter_sum(embed_term, shift_seq, seq_at)
    embed_term = scatter_sum(embed_term, shift_fsdp, fsdp_at)
    place_part = length // n_ctx
    place_low = VOCAB - rows_dev * (n_group - 1)
    places = lax.dynamic_slice_in_dim(table, place_low + ctx_at * place_part, place_part, 0)
    places = jnp.where(group_at == n_group - 1, places, 0.0).astype(jnp.bfloat16)
    total = places
    for step in range(1, n_seq):
        total = total + lax.ppermute(places, "seq", [(n_seq - 1, n_seq - 1 - step)])
    places = total
    for step in range(1, n_fsdp):
        total = total + lax.ppermute(places, "fsdp", [(n_fsdp - 1, n_fsdp - 1 - step)])
    places = gather_near(total)
    own_places = own_order(my_positions)
    place_ctx = own_places // place_part
    place_near = lax.rem(core_at + place_ctx, 2) * n_y + lax.rem(y_at - place_ctx // 2 + n_y, n_y)
    place_rows = jnp.take(
        places, place_near * place_part + lax.rem(own_places, place_part), axis=0, mode="clip"
    )
    stream = embed_term.astype(jnp.float32) + place_rows.astype(jnp.float32)
    table_low = table.astype(jnp.bfloat16)
    kept = []
    squares = []
    for layer_at in range(layer_count):
        stream, layer_kept, layer_sums = layer_forward(
            stream,
            stored[layer_at],
            vectors[12 * layer_at : 12 * layer_at + 12],
            allowed,
            head_count,
        )
        kept.append(layer_kept)
        squares.append(layer_sums)
    final_gain = vectors[12 * layer_count]
    final_bias = vectors[12 * layer_count + 1]
    final_norm, final_back = jax.vjp(layer_norm, stream, final_gain, final_bias)
    final_low = final_norm.astype(jnp.bfloat16)
    second_low = product(final_low, head_weight).astype(jnp.bfloat16)
    block_rows = 512
    columns = row_low + jnp.arange(rows_dev, dtype=jnp.int32)
    usable = columns < VOCAB

    def logits_of(rows_part):
        return jnp.where(usable[None], inner(rows_part, table_low), MASKED)

    def stats_of(args):
        rows_part, target_part = args
        logits = logits_of(rows_part)
        row_max = jnp.max(logits, -1)
        total = jnp.sum(jnp.exp(logits - row_max[:, None]), -1)
        picked = jnp.sum(jnp.where(columns[None] == target_part[:, None], logits, 0.0), -1)
        return (row_max + jnp.log(total), picked)

    def back_block(carry, args):
        rows_part, target_part, total_part, factor_part = args
        probs = jnp.exp(logits_of(rows_part) - total_part[:, None])
        hits = (columns[None] == target_part[:, None]).astype(jnp.float32)
        d_logits = (factor_part[:, None] * (probs - hits)).astype(jnp.bfloat16)
        return (carry + outer(d_logits, rows_part), product(d_logits, table_low))

    def head_stats(rows, targets):
        block_count = rows.shape[0] // block_rows
        log_part, picked = lax.map(
            stats_of,
            (
                rows.reshape(block_count, block_rows, feature_width),
                targets.reshape(block_count, block_rows),
            ),
        )
        return jnp.stack([log_part.reshape(-1), picked.reshape(-1)])

    def head_back(grad_so_far, rows, targets, log_total, factor):
        block_count = rows.shape[0] // block_rows
        grad, d_rows = lax.scan(
            back_block,
            grad_so_far,
            (
                rows.reshape(block_count, block_rows, feature_width),
                targets.reshape(block_count, block_rows),
                log_total.reshape(block_count, block_rows),
                factor.reshape(block_count, block_rows),
            ),
        )
        return grad, d_rows.reshape(n_seq, n_fsdp, own_rows, feature_width)

    def scatter_rows(parts):
        return scatter_sum(scatter_sum(parts, shift_seq, seq_at), shift_fsdp, fsdp_at)

    final_all = lax.all_gather(final_low, ("seq", "fsdp"), axis=0, tiled=True)
    second_all = lax.all_gather(second_low, ("seq", "fsdp"), axis=0, tiled=True)
    second_factor = SECOND * valid_block
    final_stats = merge_stats(head_stats(final_all, next_block))
    second_stats = merge_stats(head_stats(second_all, second_block))
    table_grad = jnp.zeros((rows_dev, feature_width), jnp.float32)
    table_grad, d_second = head_back(
        table_grad, second_all, second_block, second_stats[0], second_factor / total_tokens
    )
    table_grad, d_final = head_back(
        table_grad, final_all, next_block, final_stats[0], valid_block / total_tokens
    )
    loss_rows = (final_stats[0] - final_stats[1]) * valid_block + (
        second_stats[0] - second_stats[1]
    ) * second_factor
    loss_part = jnp.sum(
        lax.dynamic_slice_in_dim(loss_rows, group_at * own_rows, own_rows, 0)
    )
    d_second_low = scatter_rows(d_second).astype(jnp.bfloat16)
    d_final = scatter_rows(d_final)

    part_rows = -(-rows_dev // (128 * n_ctx)) * 128
    spare = part_rows * n_ctx - rows_dev
    table_parts = jnp.pad(table_grad, ((0, spare), (0, 0))).reshape(
        n_y, 2, part_rows, feature_width
    )
    table_part = pick(table_parts, core_at, 1) + swap_core(pick(table_parts, 1 - core_at, 1))
    table_part = scatter_sum(table_part, shift_y, y_at, sent=jnp.bfloat16)

    d_stream, d_gain_final, d_bias_final = final_back(d_final + inner(d_second_low, head_weight))

    def scatter_bundle(grads):
        parts = []
        for grad in grads:
            cut = grad.reshape(n_seq, n_fsdp, -1, rows_group, grad.shape[1])
            parts += [cut[:, :, at] for at in range(cut.shape[2])]
        away = jnp.concatenate(parts, -1)
        mine = scatter_sum(away, shift_seq, seq_at, sent=jnp.bfloat16)
        mine = mine.reshape(n_fsdp, n_y, rows_group // n_y, -1)
        mine = scatter_sum(mine, shift_y, y_at, axis=1, sent=jnp.bfloat16)
        return scatter_sum(mine, shift_fsdp, fsdp_at)

    def gather_bundle(mine, matrices):
        column = gather_ordered(mine, shift_y, y_at, n_y).reshape(rows_group, -1)
        both = gather_ordered(column, lambda block, step: swap_core(block), core_at, 2)
        at = 0
        grads = []
        for matrix in matrices:
            width = matrix.shape[-1] // 2
            cuts = []
            for _ in range(matrix.shape[-2] // rows_group):
                cuts.append(jnp.concatenate([both[0, :, at : at + width], both[1, :, at : at + width]], 1))
                at += width
            grads.append(jnp.concatenate(cuts, 0))
        return grads

    in_list = [None] * layer_count
    out_list = [None] * layer_count
    fc_list = [None] * layer_count
    down_list = [None] * layer_count
    vec_list = [None] * layer_count
    for layer_at in reversed(range(layer_count)):
        extra = [(final_low, d_second_low)] if layer_at == layer_count - 1 else []
        d_stream, first_grads, later_grads, vec_list[layer_at] = layer_backward(
            d_stream,
            kept[layer_at],
            stored[layer_at],
            vectors[12 * layer_at : 12 * layer_at + 12],
            allowed,
            head_count,
            core_at,
            extra,
        )
        first = gather_bundle(
            scatter_bundle(first_grads),
            [attn_out[layer_count]] * len(extra) + [mlp_in[layer_at], mlp_out[layer_at]],
        )
        later = gather_bundle(scatter_bundle(later_grads), [attn_in[layer_at], attn_out[layer_at]])
        if extra:
            head_reduced = first[0]
        fc_list[layer_at], down_list[layer_at] = first[-2:]
        in_list[layer_at], out_list[layer_at] = later
    embed_back = lax.all_gather(
        d_stream.astype(jnp.bfloat16), ("seq", "fsdp", "ctx"), axis=0, tiled=True
    )

    def device_order(grid):
        cut = grid.reshape(n_group, seqs_dev, n_ctx, ctx_span)
        return cut.transpose(0, 2, 1, 3).reshape(-1)

    part_low = row_low + ctx_at * part_rows
    part_ids = jnp.arange(part_rows, dtype=jnp.int32)
    part_live = part_ids < rows_dev - ctx_at * part_rows
    part_ids = jnp.where(part_live, part_low + part_ids, -1)
    hits = (part_ids[:, None] == device_order(tokens)[None]) | (
        part_ids[:, None] == device_order(positions)[None] + VOCAB
    )
    table_part = table_part + product(hits.astype(jnp.bfloat16), embed_back)
    table_part_low = table_part.astype(jnp.bfloat16)
    table_sum = lax.all_gather(table_part_low, "ctx", axis=0, tiled=True)[:rows_dev]
    table_sum = table_sum.astype(jnp.float32)
    table_part = table_part_low.astype(jnp.float32)

    summed = (
        table_sum,
        jnp.stack(in_list),
        jnp.stack(out_list + [head_reduced]),
        jnp.stack(fc_list),
        jnp.stack(down_list),
    )
    vector_grad = jnp.concatenate(vec_list + [jnp.stack([d_gain_final, d_bias_final])], 0)
    matrices = (table[None], attn_in, attn_out, mlp_in, mlp_out)
    grad_sums = (summed[0][None], summed[1], summed[2], summed[3], summed[4])
    row_states = (attn_in_rows, attn_out_rows, mlp_in_rows, mlp_out_rows)
    col_states = (table_cols[None], attn_in_cols, attn_out_cols, mlp_in_cols, mlp_out_cols)

    state_part = lax.dynamic_slice_in_dim(
        jnp.pad(table_rows, (0, spare)), ctx_at * part_rows, part_rows, 0
    )
    part_square = table_part * table_part
    part_renewed = DECAY * state_part + (1.0 - DECAY) * jnp.mean(part_square + EPS_SQUARE, -1)
    part_renewed = jnp.where(part_live, part_renewed, 1.0)
    live_count = jnp.sum(part_live.astype(jnp.float32))
    column_rows = gather_ordered(part_renewed, shift_y, y_at, n_y)
    both_rows = gather_ordered(
        column_rows, lambda block, step: swap_core(block), core_at, 2
    )
    table_rows_new = both_rows.transpose(1, 0, 2).reshape(-1)[:rows_dev]
    rows_new = [table_rows_new[None]]
    col_parts = [(jnp.sum(part_square, 0) + EPS_SQUARE * live_count)[None]]
    weighted_parts = [jnp.sum(part_square / part_renewed[:, None], 0)[None]]
    row_parts = [jnp.sum(jnp.where(part_live, part_renewed, 0.0)).reshape(1)]
    share = 1.0 / n_ctx
    for grad_sum, row_state in zip(grad_sums[1:], row_states):
        square = grad_sum * grad_sum
        renewed = DECAY * row_state + (1.0 - DECAY) * jnp.mean(square + EPS_SQUARE, -1)
        rows_new.append(renewed)
        col_parts.append(share * jnp.sum(square + EPS_SQUARE, -2))
        weighted_parts.append(share * jnp.sum(square / renewed[..., None], -2))
        row_parts.append(share * jnp.sum(renewed, -1))
    square_parts = [share * jnp.sum(weight * weight).reshape(1) for weight in matrices]
    own_stats = jnp.concatenate([loss_part.reshape(1), jnp.stack(squares).reshape(-1)])
    vector_sum, col_total, weighted_total, shared_total, own_total = lax.psum(
        (
            vector_grad,
            jnp.concatenate([part.reshape(-1) for part in col_parts]),
            jnp.concatenate([part.reshape(-1) for part in weighted_parts]),
            jnp.concatenate(row_parts + square_parts),
            own_stats,
        ),
        ("ctx", "seq", "fsdp"),
    )
    cols_new = []
    new_weights = []
    sizes_rms = []
    col_at = 0
    row_at = 0
    size_at = sum(part.shape[0] for part in row_parts)
    for matrix_at in range(5):
        grad_sum, renewed, col_state = (
            grad_sums[matrix_at],
            rows_new[matrix_at],
            col_states[matrix_at],
        )
        stack_count, row_local, col_count = grad_sum.shape
        row_total = row_local * n_group
        col_here = slice(col_at, col_at + stack_count * col_count)
        col_mean = col_total[col_here].reshape(stack_count, col_count) / row_total
        weighted = weighted_total[col_here].reshape(stack_count, col_count)
        col_at += stack_count * col_count
        renewed_cols = DECAY * col_state + (1.0 - DECAY) * col_mean
        row_mean = shared_total[row_at : row_at + stack_count] / row_total
        row_at += stack_count
        clip_total = jnp.sum(row_mean * jnp.sum(weighted / renewed_cols, -1))
        entries = grad_sum.size * n_group
        update_rms = jnp.sqrt(clip_total / entries)
        weight_rms = jnp.sqrt(shared_total[size_at + matrix_at] / entries)
        step_scale = RATE * jnp.maximum(EPS_SCALE, weight_rms) / jnp.maximum(1.0, update_rms / CLIP)
        second_moment = renewed[:, :, None] * renewed_cols[:, None, :] / row_mean[:, None, None]
        update = grad_sum * lax.rsqrt(second_moment)
        new_weights.append(matrices[matrix_at] - step_scale * update)
        cols_new.append(renewed_cols)
        sizes_rms.append(update_rms)
    vector_state_new = DECAY * vector_state + (1.0 - DECAY) * (vector_sum * vector_sum + EPS_SQUARE)
    vector_update = vector_sum * lax.rsqrt(vector_state_new)
    vector_rms = jnp.sqrt(jnp.mean(vector_update * vector_update))
    vector_scale = (
        RATE
        * jnp.maximum(EPS_SCALE, jnp.sqrt(jnp.mean(vectors * vectors)))
        / jnp.maximum(1.0, vector_rms / CLIP)
    )
    vectors_new = vectors - vector_scale * vector_update
    sizes_rms.append(vector_rms)
    norms = jnp.concatenate([jnp.sqrt(own_total[1:] / total_tokens), jnp.stack(sizes_rms)])
    table_new = new_weights[0][0]
    return (
        own_total[0],
        norms,
        summed[0],
        rows_new[0][0],
        cols_new[0][0],
        table_new,
        table_new.astype(jnp.bfloat16),
        summed[1],
        rows_new[1],
        cols_new[1],
        new_weights[1],
        new_weights[1].astype(jnp.bfloat16),
        summed[2],
        rows_new[2],
        cols_new[2],
        new_weights[2],
        new_weights[2].astype(jnp.bfloat16),
        summed[3],
        rows_new[3],
        cols_new[3],
        new_weights[3],
        new_weights[3].astype(jnp.bfloat16),
        summed[4],
        rows_new[4],
        cols_new[4],
        new_weights[4],
        new_weights[4].astype(jnp.bfloat16),
        vector_sum,
        vector_state_new,
        vectors_new,
    )


def solution(mesh):
    return jax.shard_map(
        body,
        mesh=mesh,
        in_specs=(
            P(),
            P(),
            P(),
            P(),
            P(("seq", "fsdp"), None),
            P(None, ("seq", "fsdp"), None),
            P(None, ("seq", "fsdp"), None),
            P(None, ("seq", "fsdp"), None),
            P(None, ("seq", "fsdp"), None),
            P(),
            P(("seq", "fsdp")),
            P(),
            P(None, ("seq", "fsdp")),
            P(),
            P(None, ("seq", "fsdp")),
            P(),
            P(None, ("seq", "fsdp")),
            P(),
            P(None, ("seq", "fsdp")),
            P(),
            P(),
        ),
        out_specs=(
            P(),
            P(),
            P(("seq", "fsdp"), None),
            P(("seq", "fsdp")),
            P(),
            P(("seq", "fsdp"), None),
            P(("seq", "fsdp"), None),
            P(None, ("seq", "fsdp"), None),
            P(None, ("seq", "fsdp")),
            P(),
            P(None, ("seq", "fsdp"), None),
            P(None, ("seq", "fsdp"), None),
            P(None, ("seq", "fsdp"), None),
            P(None, ("seq", "fsdp")),
            P(),
            P(None, ("seq", "fsdp"), None),
            P(None, ("seq", "fsdp"), None),
            P(None, ("seq", "fsdp"), None),
            P(None, ("seq", "fsdp")),
            P(),
            P(None, ("seq", "fsdp"), None),
            P(None, ("seq", "fsdp"), None),
            P(None, ("seq", "fsdp"), None),
            P(None, ("seq", "fsdp")),
            P(),
            P(None, ("seq", "fsdp"), None),
            P(None, ("seq", "fsdp"), None),
            P(),
            P(),
            P(),
        ),
        check_vma=False,
    )
```

```python
import functools

import jax
import jax.numpy as jnp
from jax import lax
from jax.experimental import pallas as pl
from jax.experimental.pallas import tpu as pltpu
from jax.sharding import PartitionSpec as P

HEADS = 12
VOCAB = 50304


EPS_NORM = 1e-05
EPS_SQUARE = 1e-30
EPS_SCALE = 0.001
DECAY = 0.5
CLIP = 0.4
RATE = 0.6
SECOND = 0.3
MASKED = -1e30
VMEM_BYTES = 56 * 1024 * 1024


def layer_norm(stream, gain, offset):
    center = stream - jnp.mean(stream, -1, keepdims=True)
    spread = jnp.mean(center * center, -1, keepdims=True)
    return center * lax.rsqrt(spread + EPS_NORM) * gain + offset


def gelu_tanh(value):
    return jax.nn.gelu(value, approximate=True)


def positions_of(segments):
    steps_at = jnp.arange(segments.shape[-1], dtype=jnp.int32)
    before = jnp.concatenate(
        [jnp.full(segments.shape[:-1] + (1,), -2, jnp.int32), segments[..., :-1]], -1
    )
    starts = jnp.where(segments != before, steps_at, 0)
    first = lax.cummax(starts, axis=segments.ndim - 1)
    return jnp.where(segments >= 0, steps_at - first, 0)


def product(left, right):
    return jnp.dot(left, right, preferred_element_type=jnp.float32)


def inner(left, right):
    return lax.dot_general(
        left, right, (((1,), (1,)), ((), ())), preferred_element_type=jnp.float32
    )


def outer(left, right):
    return lax.dot_general(
        left, right, (((0,), (0,)), ((), ())), preferred_element_type=jnp.float32
    )


def shift(block, axis, step):
    count = lax.axis_size(axis)
    return lax.ppermute(block, axis, [(i, (i + step) % count) for i in range(count)])


def shift_y(block, step):
    count = lax.axis_size("ctx")
    return lax.ppermute(block, "ctx", [(i, (i + 2 * step) % count) for i in range(count)])


def swap_core(block):
    count = lax.axis_size("ctx")
    return lax.ppermute(block, "ctx", [(i, i ^ 1) for i in range(count)])


def shift_seq(block, step):
    return shift(block, "seq", step)


def shift_fsdp(block, step):
    return shift(block, "fsdp", step)


def pick(parts, at, axis):
    return lax.dynamic_index_in_dim(parts, at, axis, False)


def send_parts(parts, mover, at, axis=0, sent=None):
    count = parts.shape[axis]
    moving = []
    for step in range(1, count):
        piece = pick(parts, lax.rem(at + step, count), axis)
        moving.append(mover(piece if sent is None else piece.astype(sent), step))
    return moving


def add_parts(parts, moved, at, axis=0):
    total = pick(parts, at, axis)
    for piece in moved:
        total = total + piece.astype(total.dtype)
    return total


def scatter_sum(parts, mover, at, axis=0, sent=None):
    return add_parts(parts, send_parts(parts, mover, at, axis, sent), at, axis)


def sum_all(block):
    for axis in ("ctx", "seq", "fsdp"):
        count = lax.axis_size(axis)
        hop = 1
        while hop < count:
            block = block + lax.ppermute(block, axis, [(i, i ^ hop) for i in range(count)])
            hop *= 2
    return block


def order_parts(parts, at):
    count = len(parts)
    if count == 2:
        first, second = parts
        return jnp.stack([jnp.where(at == 0, first, second), jnp.where(at == 0, second, first)])
    order = lax.rem(at - jnp.arange(count, dtype=jnp.int32) + count, count)
    return jnp.take(jnp.stack(parts), order, axis=0, mode="clip")


def gather_ordered(block, mover, at, count):
    return order_parts([block] + [mover(block, step) for step in range(1, count)], at)


def gather_near(block):
    n_y = lax.axis_size("ctx") // 2
    column = jnp.concatenate([block] + [shift_y(block, step) for step in range(1, n_y)], 0)
    return jnp.concatenate([column, swap_core(column)], 0)


def scatter_near(parts):
    n_y = lax.axis_size("ctx") // 2
    parts = parts.reshape((2, n_y, -1) + parts.shape[1:])
    column = parts[0] + swap_core(parts[1])
    total = column[0]
    for step in range(1, n_y):
        total = total + shift_y(column[step], n_y - step)
    return total


def half_of(block, at):
    width = block.shape[-1] // 2
    return jnp.where(at == 0, block[..., :width], block[..., width:])


def qkv_bias(vec):
    return jnp.concatenate([vec[2], jnp.zeros_like(vec[2]), vec[3]])


def attention_scores(query_low, keys, allowed, head_count):
    row_count, feature_width = query_low.shape
    head_size = feature_width // head_count
    scores = jnp.einsum(
        "qhd,khd->hqk",
        query_low.reshape(row_count, head_count, head_size),
        keys.reshape(-1, head_count, head_size),
        preferred_element_type=jnp.float32,
    ) * head_size ** (-0.5)
    return jnp.where(allowed[None], scores, MASKED)


def mix_values(probs_low, values, head_count):
    head_size = values.shape[1] // head_count
    mixed = jnp.einsum(
        "hqk,khd->qhd",
        probs_low,
        values.reshape(-1, head_count, head_size),
        preferred_element_type=jnp.float32,
    )
    return mixed.reshape(mixed.shape[0], -1)


def layer_forward(stream, weights, vec, allowed, head_count):
    w_in, w_out, w_fc, w_down = weights
    feature_width = stream.shape[1]
    a_low = layer_norm(stream, vec[0], vec[1]).astype(jnp.bfloat16)
    qkv_low = (product(a_low, w_in) + qkv_bias(vec)).astype(jnp.bfloat16)
    pairs = gather_near(qkv_low[:, feature_width:])
    keys, values = pairs[:, :feature_width], pairs[:, feature_width:]
    scores = attention_scores(qkv_low[:, :feature_width], keys, allowed, head_count)
    row_max = jnp.max(scores, -1)
    log_total = row_max + jnp.log(jnp.sum(jnp.exp(scores - row_max[..., None]), -1))
    probs = jnp.exp(scores - log_total[..., None])
    mixed_low = mix_values(probs.astype(jnp.bfloat16), values, head_count).astype(jnp.bfloat16)
    branch = product(mixed_low, w_out) + vec[4]
    middle = stream + branch
    m_low = layer_norm(middle, vec[5], vec[6]).astype(jnp.bfloat16)
    hidden = product(m_low, w_fc) + vec[8:12].reshape(-1)
    output = product(gelu_tanh(hidden).astype(jnp.bfloat16), w_down) + vec[7]
    sums = jnp.stack([jnp.sum(stream * stream), jnp.sum(branch * branch), jnp.sum(output * output)])
    kept = (stream, a_low, qkv_low, keys, values, log_total, mixed_low, middle, m_low, hidden)
    return (middle + output, kept, sums)


def swap_pairs(pairs, core_at):
    lefts = [left for left, _ in pairs]
    return swap_core(
        jnp.concatenate(lefts + [half_of(right, 1 - core_at) for _, right in pairs], 1)
    )


def shared_outer(pairs, away, core_at):
    at = 0
    whole_left = []
    for left, _ in pairs:
        whole_left.append(jnp.concatenate([left, away[:, at : at + left.shape[1]]], 0))
        at += left.shape[1]
    grads = []
    for left, (_, right) in zip(whole_left, pairs):
        width = right.shape[1] // 2
        whole_right = jnp.concatenate([half_of(right, core_at), away[:, at : at + width]], 0)
        at += width
        grads.append(outer(left, whole_right))
    return grads


def layer_backward(d_stream, kept, weights, vec, allowed, head_count, pending, first_task, later_task):
    stream, a_low, qkv_low, keys, values, log_total, mixed_low, middle, m_low, hidden = kept
    w_in, w_out, w_fc, w_down = weights
    row_count, feature_width = stream.shape
    head_size = feature_width // head_count
    scale = head_size ** (-0.5)
    norm_back_one = jax.vjp(layer_norm, stream, vec[0], vec[1])[1]
    query_low = qkv_low[:, :feature_width]
    probs = jnp.exp(attention_scores(query_low, keys, allowed, head_count) - log_total[..., None])
    probs_low = probs.astype(jnp.bfloat16)
    norm_back_two = jax.vjp(layer_norm, middle, vec[5], vec[6])[1]
    gelu_out, gelu_back = jax.vjp(gelu_tanh, hidden)
    u_low = gelu_out.astype(jnp.bfloat16)
    d_out_low = d_stream.astype(jnp.bfloat16)
    d_hidden_low = gelu_back(inner(d_out_low, w_down))[0].astype(jnp.bfloat16)
    d_hidden_low = pending.point(d_hidden_low)
    pending.add(first_task([(m_low, d_hidden_low), (u_low, d_out_low)]))
    d_m = inner(d_hidden_low, w_fc)
    d_two, d_gain_two, d_bias_two = norm_back_two(d_m)
    d_middle = d_stream + d_two
    d_middle = pending.point(d_middle)
    d_middle_low = d_middle.astype(jnp.bfloat16)
    d_heads = (
        inner(d_middle_low, w_out).astype(jnp.bfloat16).reshape(row_count, head_count, head_size)
    )
    value_heads = values.reshape(-1, head_count, head_size)
    d_probs = jnp.einsum("qhd,khd->hqk", d_heads, value_heads, preferred_element_type=jnp.float32)
    d_scores = (probs * (d_probs - jnp.sum(probs * d_probs, -1, keepdims=True))).astype(
        jnp.bfloat16
    )
    d_scores = pending.point(d_scores)
    d_query = (
        jnp.einsum(
            "hqk,khd->qhd",
            d_scores,
            keys.reshape(-1, head_count, head_size),
            preferred_element_type=jnp.float32,
        ).reshape(row_count, feature_width)
        * scale
    )
    d_keys = (
        jnp.einsum(
            "hqk,qhd->khd",
            d_scores,
            query_low.reshape(row_count, head_count, head_size),
            preferred_element_type=jnp.float32,
        ).reshape(-1, feature_width)
        * scale
    )
    d_values = jnp.einsum(
        "hqk,qhd->khd", probs_low, d_heads, preferred_element_type=jnp.float32
    ).reshape(-1, feature_width)
    d_pairs = scatter_near(jnp.concatenate([d_keys, d_values], 1))
    d_qkv_low = jnp.concatenate([d_query, d_pairs], 1).astype(jnp.bfloat16)
    d_qkv_low = pending.point(d_qkv_low)
    pending.add(later_task([(a_low, d_qkv_low), (mixed_low, d_middle_low)]))
    d_one, d_gain_one, d_bias_one = norm_back_one(inner(d_qkv_low, w_in))
    d_qkv = d_qkv_low.astype(jnp.float32)
    rows_head = jnp.stack(
        [
            d_gain_one,
            d_bias_one,
            jnp.sum(d_qkv[:, :feature_width], 0),
            jnp.sum(d_qkv[:, 2 * feature_width :], 0),
            jnp.sum(d_middle_low.astype(jnp.float32), 0),
            d_gain_two,
            d_bias_two,
            jnp.sum(d_out_low.astype(jnp.float32), 0),
        ]
    )
    vec_grad = jnp.concatenate(
        [rows_head, jnp.sum(d_hidden_low.astype(jnp.float32), 0).reshape(4, feature_width)], 0
    )
    return (pending.point(d_middle + d_one), vec_grad)


def merge_stats(stats):
    for mover, axis in ((shift_seq, "seq"), (shift_fsdp, "fsdp")):
        parts = [stats] + [mover(stats, step) for step in range(1, lax.axis_size(axis))]
        top = parts[0][0]
        for part in parts[1:]:
            top = jnp.maximum(top, part[0])
        total = jnp.exp(parts[0][0] - top)
        picked = parts[0][1]
        for part in parts[1:]:
            total = total + jnp.exp(part[0] - top)
            picked = picked + part[1]
        stats = jnp.stack([top + jnp.log(total), picked])
    return stats


def masked_logits(logits, live, first):
    column = lax.broadcasted_iota(jnp.int32, logits.shape, 0) + first
    return jnp.where(column < live, logits, MASKED)


def stats_kernel(row_block, live_ref, table_ref, rows_ref, target_ref, out_ref, top_ref, sum_ref, pick_ref):
    at = pl.program_id(0)
    tile = table_ref.shape[0]
    first = at * tile
    live = live_ref[0]

    @pl.when(at == 0)
    def _():
        top_ref[...] = jnp.full_like(top_ref, MASKED)
        sum_ref[...] = jnp.zeros_like(sum_ref)
        pick_ref[...] = jnp.zeros_like(pick_ref)

    def step(masked):
        for low in range(0, rows_ref.shape[1], row_block):
            here = slice(low, low + row_block)
            logits = jnp.dot(
                table_ref[...], rows_ref[:, here], preferred_element_type=jnp.float32
            )
            if masked:
                logits = masked_logits(logits, live, first)
            column = lax.broadcasted_iota(jnp.int32, logits.shape, 0)
            hit = column == target_ref[:, here] - first
            cut = logits.reshape(tile // 8, 8, row_block)
            top = top_ref[:, here]
            joint = jnp.maximum(top, jnp.max(cut, 0))
            total = jnp.sum(jnp.exp(cut - joint[None]), 0)
            sum_ref[:, here] = sum_ref[:, here] * jnp.exp(top - joint) + total
            top_ref[:, here] = joint
            pick_ref[:, here] += jnp.sum(
                jnp.where(hit, logits, 0.0).reshape(tile // 8, 8, row_block), 0
            )

    @pl.when(first + tile <= live)
    def _():
        step(False)

    @pl.when((first + tile > live) & (first < live))
    def _():
        step(True)

    @pl.when(at == pl.num_programs(0) - 1)
    def _():
        top = top_ref[...]
        joint = jnp.max(top, 0, keepdims=True)
        total = jnp.sum(sum_ref[...] * jnp.exp(top - joint), 0, keepdims=True)
        out_ref[0:1, :] = joint + jnp.log(total)
        out_ref[1:2, :] = jnp.sum(pick_ref[...], 0, keepdims=True)


def head_stats(live, table_low, rows_t, target, tile=512, row_block=512):
    depth, count = rows_t.shape
    height = table_low.shape[0]
    return pl.pallas_call(
        functools.partial(stats_kernel, row_block),
        out_shape=jax.ShapeDtypeStruct((2, count), jnp.float32),
        grid=(height // tile,),
        in_specs=[
            pl.BlockSpec(memory_space=pltpu.SMEM),
            pl.BlockSpec((tile, depth), lambda i: (i, 0)),
            pl.BlockSpec((depth, count), lambda i: (0, 0)),
            pl.BlockSpec((1, count), lambda i: (0, 0)),
        ],
        out_specs=pl.BlockSpec((2, count), lambda i: (0, 0)),
        scratch_shapes=[pltpu.VMEM((8, count), jnp.float32)] * 3,
        compiler_params=pltpu.CompilerParams(vmem_limit_bytes=VMEM_BYTES),
        cost_estimate=pl.CostEstimate(
            flops=2 * height * depth * count,
            bytes_accessed=2 * height * depth + 2 * depth * count,
            transcendentals=height * count,
        ),
    )(live, table_low, rows_t, target)


def back_kernel(row_block, added, live_ref, table_ref, table_t_ref, rows_ref, rows_t_ref, line_ref, *refs):
    if added:
        prior_ref, grad_ref, d_rows_ref = refs
    else:
        grad_ref, d_rows_ref = refs
    at = pl.program_id(0)
    tile = table_ref.shape[0]
    first = at * tile
    live = live_ref[0]
    width = d_rows_ref.shape[2]

    @pl.when(at == 0)
    def _():
        d_rows_ref[...] = jnp.zeros_like(d_rows_ref)

    def step(masked):
        grad = prior_ref[...] if added else None
        for low in range(0, rows_t_ref.shape[1], row_block):
            here = slice(low, low + row_block)
            logits = jnp.dot(
                table_ref[...], rows_t_ref[:, here], preferred_element_type=jnp.float32
            )
            if masked:
                logits = masked_logits(logits, live, first)
            column = lax.broadcasted_iota(jnp.int32, logits.shape, 0).astype(jnp.float32)
            probs = jnp.exp(logits - line_ref[0:1, here])
            hit = column == line_ref[2:3, here] - first.astype(jnp.float32)
            d_low = (line_ref[1:2, here] * jnp.where(hit, probs - 1.0, probs)).astype(jnp.bfloat16)
            part = jnp.dot(d_low, rows_ref[here, :], preferred_element_type=jnp.float32)
            grad = part if grad is None else grad + part
            d_part = jnp.dot(table_t_ref[...], d_low, preferred_element_type=jnp.float32)
            for inner_low in range(0, row_block, width):
                d_rows_ref[(low + inner_low) // width] += d_part[
                    :, inner_low : inner_low + width
                ]
        grad_ref[...] = grad

    @pl.when(first + tile <= live)
    def _():
        step(False)

    @pl.when((first + tile > live) & (first < live))
    def _():
        step(True)

    @pl.when(first >= live)
    def _():
        grad_ref[...] = prior_ref[...] if added else jnp.zeros_like(grad_ref)


def head_back(live, table_low, table_t, rows, rows_t, line, groups, prior=None, tile=512):
    depth, count = rows_t.shape
    height = table_low.shape[0]
    once = dict(pipeline_mode=pl.Buffered(1))
    row_block = min(1024, count)
    grad_spec = pl.BlockSpec((tile, depth), lambda i: (i, 0))
    added = prior is not None
    return pl.pallas_call(
        functools.partial(back_kernel, row_block, added),
        out_shape=(
            jax.ShapeDtypeStruct((height, depth), jnp.float32),
            jax.ShapeDtypeStruct((groups, depth, count // groups), jnp.float32),
        ),
        grid=(height // tile,),
        in_specs=[
            pl.BlockSpec(memory_space=pltpu.SMEM),
            pl.BlockSpec((tile, depth), lambda i: (i, 0)),
            pl.BlockSpec((depth, tile), lambda i: (0, i)),
            pl.BlockSpec((count, depth), lambda i: (0, 0), **once),
            pl.BlockSpec((depth, count), lambda i: (0, 0), **once),
            pl.BlockSpec((3, count), lambda i: (0, 0), **once),
        ]
        + ([grad_spec] if added else []),
        out_specs=(
            grad_spec,
            pl.BlockSpec((groups, depth, count // groups), lambda i: (0, 0, 0), **once),
        ),
        input_output_aliases={6: 0} if added else {},
        compiler_params=pltpu.CompilerParams(vmem_limit_bytes=VMEM_BYTES),
        cost_estimate=pl.CostEstimate(
            flops=6 * height * depth * count,
            bytes_accessed=4 * height * depth + 12 * depth * count + 8 * height * depth,
            transcendentals=height * count,
        ),
    )(live, table_low, table_t, rows, rows_t, line, *((prior,) if added else ()))


class Pending:
    def __init__(self):
        self.active = []

    def add(self, task):
        held, moving = next(task)
        self.active.append([task, held, moving])

    def point(self, main):
        ready = [entry for entry in self.active if entry[1] == 0]
        main, moved = lax.optimization_barrier((main, [entry[2] for entry in ready]))
        for entry in self.active:
            entry[1] -= 1
        for entry, arrived in zip(ready, moved):
            self.advance(entry, arrived)
        return main

    def advance(self, entry, arrived):
        try:
            entry[1:] = entry[0].send(arrived)
        except StopIteration:
            self.active.remove(entry)

    def finish(self):
        while self.active:
            entry = self.active[0]
            self.advance(entry, entry[2])


def local_index(ids, row_low, row_count):
    shifted = ids - row_low
    inside = (shifted >= 0) & (shifted < row_count)
    return (inside, jnp.clip(shifted, 0, row_count - 1))


def body(
    tokens,
    segments,
    next_ids,
    second_ids,
    table,
    attn_in,
    attn_out,
    mlp_in,
    mlp_out,
    vectors,
    table_rows,
    table_cols,
    attn_in_rows,
    attn_in_cols,
    attn_out_rows,
    attn_out_cols,
    mlp_in_rows,
    mlp_in_cols,
    mlp_out_rows,
    mlp_out_cols,
    vector_state,
):
    n_ctx = lax.axis_size("ctx")
    n_seq = lax.axis_size("seq")
    n_fsdp = lax.axis_size("fsdp")
    n_y = n_ctx // 2
    n_group = n_seq * n_fsdp
    ctx_at = lax.axis_index("ctx")
    seq_at = lax.axis_index("seq")
    fsdp_at = lax.axis_index("fsdp")
    y_at = ctx_at // 2
    core_at = lax.rem(ctx_at, 2)
    group_at = seq_at * n_fsdp + fsdp_at
    all_seqs, length = segments.shape
    seqs_dev = all_seqs // n_group
    ctx_span = length // n_ctx
    feature_width = table.shape[1]
    layer_count = attn_in.shape[0]
    head_count = HEADS
    total_tokens = all_seqs * length
    own_rows = seqs_dev * ctx_span
    block_start = ctx_at * ctx_span
    positions = positions_of(segments)

    def block_of(grid):
        return lax.dynamic_slice_in_dim(grid, block_start, ctx_span, 1)

    tok_block = block_of(tokens).reshape(-1)
    valid_block = (block_of(segments) >= 0).astype(jnp.float32).reshape(-1)
    next_block = block_of(next_ids).reshape(-1)
    second_block = block_of(second_ids).reshape(-1)
    my_segments = lax.dynamic_slice_in_dim(segments, group_at * seqs_dev, seqs_dev, 0)
    my_positions = lax.dynamic_slice_in_dim(positions, group_at * seqs_dev, seqs_dev, 0)
    near = jnp.asarray(
        [(side, step) for side in range(2) for step in range(n_y)], jnp.int32
    )
    near_ctx = 2 * lax.rem(y_at - near[:, 1] + n_y, n_y) + lax.rem(core_at + near[:, 0], 2)

    def near_order(grid):
        cut = grid.reshape(seqs_dev, n_ctx, ctx_span).transpose(1, 0, 2)
        return jnp.take(cut, near_ctx, axis=0, mode="clip").reshape(-1)

    def own_order(grid):
        return block_of(grid).reshape(-1)

    time_grid = jnp.broadcast_to(jnp.arange(length, dtype=jnp.int32)[None], (seqs_dev, length))
    seq_grid = jnp.broadcast_to(jnp.arange(seqs_dev, dtype=jnp.int32)[:, None], (seqs_dev, length))
    q_seg, k_seg = (own_order(my_segments), near_order(my_segments))
    q_time, k_time = (own_order(time_grid), near_order(time_grid))
    q_seq, k_seq = (own_order(seq_grid), near_order(seq_grid))
    allowed = (q_seq[:, None] == k_seq[None]) & (
        (q_time[:, None] == k_time[None])
        | (k_time[None] < q_time[:, None]) & (q_seg[:, None] == k_seg[None]) & (k_seg[None] >= 0)
    )
    rows_dev = table.shape[0]
    row_low = group_at * rows_dev
    rows_group = attn_in.shape[1]
    rows_part = rows_group // n_ctx
    down_cut = mlp_out.shape[1] // rows_group

    in_width, out_width, fc_width = attn_in.shape[2], attn_out.shape[2], mlp_in.shape[2]
    pack_width = in_width + out_width + fc_width + down_cut * feature_width
    part_width = pack_width // n_ctx
    model_rows = n_group * rows_group

    def gather_pack(layer_at):
        down = mlp_out[layer_at].reshape(down_cut, rows_group, feature_width)
        pack = jnp.concatenate(
            [attn_in[layer_at], mlp_in[layer_at], attn_out[layer_at]]
            + [down[cut] for cut in range(down_cut)],
            1,
        ).astype(jnp.bfloat16)
        part = lax.dynamic_slice_in_dim(pack, ctx_at * part_width, part_width, 1)
        if layer_at == layer_count - 1:
            head = lax.dynamic_slice_in_dim(
                attn_out[layer_count].astype(jnp.bfloat16), ctx_at * rows_part, rows_part, 0
            )
            head = jnp.pad(head.reshape(-1), (0, -head.size % part_width)).reshape(-1, part_width)
            part = jnp.concatenate([part, head], 0)
        whole = lax.all_gather(part, ("ctx", "seq", "fsdp"), axis=0)
        whole = whole.reshape(n_ctx, n_group, -1, part_width)
        body_rows = whole[:, :, :rows_group].reshape(n_ctx, model_rows, part_width)

        def columns_of(low, high):
            pieces = []
            for at in range(n_ctx):
                start, stop = max(low, at * part_width), min(high, (at + 1) * part_width)
                if start < stop:
                    pieces.append(body_rows[at, :, start - at * part_width : stop - at * part_width])
            return pieces[0] if len(pieces) == 1 else jnp.concatenate(pieces, 1)

        at = in_width + fc_width
        down = jnp.stack(
            [
                columns_of(low, low + feature_width).reshape(n_group, rows_group, feature_width)
                for low in range(at + out_width, pack_width, feature_width)
            ],
            1,
        )
        weights = (
            columns_of(0, in_width),
            columns_of(at, at + out_width),
            columns_of(in_width, at),
            down.reshape(-1, feature_width),
        )
        head = None
        if layer_at == layer_count - 1:
            head = whole[:, :, rows_group:].reshape(n_ctx, n_group, -1)
            head = head[:, :, : rows_part * out_width].reshape(n_ctx, n_group, rows_part, out_width)
            head = head.transpose(1, 0, 2, 3).reshape(model_rows, out_width)
        return weights, head

    stored = []
    for layer_at in range(layer_count):
        weights, head_weight = gather_pack(layer_at)
        stored.append(weights)

    tok_inside, tok_safe = local_index(tok_block, row_low, rows_dev)
    embed_term = jnp.where(
        tok_inside[:, None], jnp.take(table, tok_safe, axis=0, mode="clip"), 0.0
    ).astype(jnp.bfloat16)
    embed_term = embed_term.reshape(n_seq, n_fsdp, own_rows, feature_width)
    embed_term = scatter_sum(embed_term, shift_seq, seq_at)
    embed_term = scatter_sum(embed_term, shift_fsdp, fsdp_at)
    place_part = length // n_ctx
    place_low = VOCAB - rows_dev * (n_group - 1)
    places = lax.dynamic_slice_in_dim(table, place_low + ctx_at * place_part, place_part, 0)
    places = jnp.where(group_at == n_group - 1, places, 0.0).astype(jnp.bfloat16)
    total = places
    for step in range(1, n_seq):
        total = total + lax.ppermute(places, "seq", [(n_seq - 1, n_seq - 1 - step)])
    places = total
    for step in range(1, n_fsdp):
        total = total + lax.ppermute(places, "fsdp", [(n_fsdp - 1, n_fsdp - 1 - step)])
    places = gather_near(total)
    own_places = own_order(my_positions)
    place_ctx = own_places // place_part
    place_near = lax.rem(core_at + place_ctx, 2) * n_y + lax.rem(y_at - place_ctx // 2 + n_y, n_y)
    place_rows = jnp.take(
        places, place_near * place_part + lax.rem(own_places, place_part), axis=0, mode="clip"
    )
    stream = embed_term.astype(jnp.float32) + place_rows.astype(jnp.float32)
    part_rows = -(-rows_dev // (128 * n_ctx)) * 128
    spare = part_rows * n_ctx - rows_dev
    table_low = jnp.pad(table.astype(jnp.bfloat16), ((0, spare), (0, 0)))
    table_t = table_low.T
    kept = []
    squares = []
    for layer_at in range(layer_count):
        stream, layer_kept, layer_sums = layer_forward(
            stream,
            stored[layer_at],
            vectors[12 * layer_at : 12 * layer_at + 12],
            allowed,
            head_count,
        )
        kept.append(layer_kept)
        squares.append(layer_sums)
    final_gain = vectors[12 * layer_count]
    final_bias = vectors[12 * layer_count + 1]
    final_norm, final_back = jax.vjp(layer_norm, stream, final_gain, final_bias)
    final_low = final_norm.astype(jnp.bfloat16)
    second_low = product(final_low, head_weight).astype(jnp.bfloat16)
    live = jnp.clip(VOCAB - row_low, 0, rows_dev).astype(jnp.int32).reshape(1)

    def local_targets(ids):
        inside, safe = local_index(ids, row_low, rows_dev)
        return jnp.where(inside, safe, -1)

    def gather_group(rows):
        return lax.all_gather(rows, ("seq", "fsdp"), axis=0, tiled=True)

    final_all = gather_group(final_low)
    second_all = gather_group(second_low)
    second_factor = SECOND * valid_block
    final_local, second_local = local_targets(next_block), local_targets(second_block)
    final_t = final_all.T
    final_stats = head_stats(live, table_low, final_t, final_local[None])
    second_t = second_all.T
    second_stats = head_stats(live, table_low, second_t, second_local[None])
    final_stats, second_stats = merge_stats(final_stats), merge_stats(second_stats)

    def scatter_rows(parts):
        parts = parts.reshape((n_seq, n_fsdp) + parts.shape[1:])
        return scatter_sum(scatter_sum(parts, shift_seq, seq_at), shift_fsdp, fsdp_at)

    def line_of(stats, factor, local):
        return jnp.stack([stats[0], factor / total_tokens, local.astype(jnp.float32)])

    table_grad, d_final = head_back(
        live,
        table_low,
        table_t,
        final_all,
        final_t,
        line_of(final_stats, valid_block, final_local),
        n_group,
    )
    second_line = line_of(second_stats, second_factor, second_local)
    cuts = 2 if own_rows % 256 == 0 else 1
    chunk = own_rows // cuts
    d_seconds = []
    for cut in range(cuts):
        rows = second_all.reshape(n_group, cuts, chunk, feature_width)[:, cut].reshape(
            -1, feature_width
        )
        line = second_line.reshape(3, n_group, cuts, chunk)[:, :, cut].reshape(3, -1)
        table_grad, d_rows = head_back(
            live, table_low, table_t, rows, rows.T, line, n_group, table_grad
        )
        d_seconds.append(scatter_rows(d_rows))
    d_final = scatter_rows(d_final).T
    loss_rows = (final_stats[0] - final_stats[1]) * valid_block + (
        second_stats[0] - second_stats[1]
    ) * second_factor
    loss_part = jnp.sum(
        lax.dynamic_slice_in_dim(loss_rows, group_at * own_rows, own_rows, 0)
    )

    pending = Pending()
    results = {}

    def table_task():
        parts = table_grad.reshape(n_y, 2, part_rows, feature_width)
        (away,) = yield 0, [swap_core(pick(parts, 1 - core_at, 1))]
        column = pick(parts, core_at, 1) + away
        moved = yield 2, send_parts(column, shift_y, y_at, sent=jnp.bfloat16)
        results["table"] = add_parts(column, moved, y_at)

    def bundle_task(pairs, matrices, names):
        (away,) = yield 0, [swap_pairs(pairs, core_at)]
        grads = shared_outer(pairs, away, core_at)
        parts = []
        for grad in grads:
            cut = grad.reshape(n_seq, n_fsdp, -1, rows_group, grad.shape[1])
            parts += [cut[:, :, at] for at in range(cut.shape[2])]
        stacked = jnp.concatenate(parts, -1)
        moved = yield 1, send_parts(stacked, shift_seq, seq_at, sent=jnp.bfloat16)
        mine = add_parts(stacked, moved, seq_at)
        mine = mine.reshape(n_fsdp, n_y, rows_group // n_y, -1)
        moved = yield 0, send_parts(mine, shift_y, y_at, 1, jnp.bfloat16)
        mine = add_parts(mine, moved, y_at, 1)
        moved = yield 1, send_parts(mine, shift_fsdp, fsdp_at)
        mine = add_parts(mine, moved, fsdp_at)
        moved = yield 0, [shift_y(mine, step) for step in range(1, n_y)]
        column = order_parts([mine] + moved, y_at).reshape(rows_group, -1)
        (away,) = yield 0, [swap_core(column)]
        both = order_parts([column, away], core_at)
        at = 0
        for matrix, name in zip(matrices, names):
            width = matrix.shape[-1] // 2
            cuts = []
            for _ in range(matrix.shape[-2] // rows_group):
                cuts.append(
                    jnp.concatenate([both[0, :, at : at + width], both[1, :, at : at + width]], 1)
                )
                at += width
            results[name] = jnp.concatenate(cuts, 0)

    pending.add(table_task())
    d_seconds = jnp.concatenate(d_seconds, 1).T
    d_seconds = pending.point(d_seconds)
    d_second_low = d_seconds.astype(jnp.bfloat16)
    d_stream, d_gain_final, d_bias_final = final_back(d_final + inner(d_second_low, head_weight))

    vec_list = [None] * layer_count
    for layer_at in reversed(range(layer_count)):

        def first_task(pairs, at=layer_at):
            matrices, names = [mlp_in[at], mlp_out[at]], [("fc", at), ("down", at)]
            if at == layer_count - 1:
                pairs = [(final_low, d_second_low)] + pairs
                matrices = [attn_out[layer_count]] + matrices
                names = [("out", layer_count)] + names
            return bundle_task(pairs, matrices, names)

        def later_task(pairs, at=layer_at):
            return bundle_task(pairs, [attn_in[at], attn_out[at]], [("in", at), ("out", at)])

        d_stream, vec_list[layer_at] = layer_backward(
            d_stream,
            kept[layer_at],
            stored[layer_at],
            vectors[12 * layer_at : 12 * layer_at + 12],
            allowed,
            head_count,
            pending,
            first_task,
            later_task,
        )
    embed_back = lax.all_gather(
        d_stream.astype(jnp.bfloat16), ("seq", "fsdp", "ctx"), axis=0, tiled=True
    )

    def device_order(grid):
        cut = grid.reshape(n_group, seqs_dev, n_ctx, ctx_span)
        return cut.transpose(0, 2, 1, 3).reshape(-1)

    pending.finish()
    table_part = results["table"]
    part_low = row_low + ctx_at * part_rows
    part_ids = jnp.arange(part_rows, dtype=jnp.int32)
    part_live = part_ids < rows_dev - ctx_at * part_rows
    part_ids = jnp.where(part_live, part_low + part_ids, -1)
    hits = (part_ids[:, None] == device_order(tokens)[None]) | (
        part_ids[:, None] == device_order(positions)[None] + VOCAB
    )
    table_part = table_part + product(hits.astype(jnp.bfloat16), embed_back)
    table_part_low = table_part.astype(jnp.bfloat16)
    table_column = gather_ordered(table_part_low, shift_y, y_at, n_y)
    table_both = order_parts([table_column, swap_core(table_column)], core_at)
    table_sum = table_both.transpose(1, 0, 2, 3).reshape(-1, feature_width)[:rows_dev]
    table_sum = table_sum.astype(jnp.float32)
    table_part = table_part_low.astype(jnp.float32)

    summed = (
        table_sum,
        jnp.stack([results["in", at] for at in range(layer_count)]),
        jnp.stack([results["out", at] for at in range(layer_count + 1)]),
        jnp.stack([results["fc", at] for at in range(layer_count)]),
        jnp.stack([results["down", at] for at in range(layer_count)]),
    )
    vector_grad = jnp.concatenate(vec_list + [jnp.stack([d_gain_final, d_bias_final])], 0)
    matrices = (table[None], attn_in, attn_out, mlp_in, mlp_out)
    grad_sums = (summed[0][None], summed[1], summed[2], summed[3], summed[4])
    row_states = (attn_in_rows, attn_out_rows, mlp_in_rows, mlp_out_rows)
    col_states = (table_cols[None], attn_in_cols, attn_out_cols, mlp_in_cols, mlp_out_cols)

    state_part = lax.dynamic_slice_in_dim(
        jnp.pad(table_rows, (0, spare)), ctx_at * part_rows, part_rows, 0
    )
    part_square = table_part * table_part
    part_renewed = DECAY * state_part + (1.0 - DECAY) * jnp.mean(part_square + EPS_SQUARE, -1)
    part_renewed = jnp.where(part_live, part_renewed, 1.0)
    live_count = jnp.sum(part_live.astype(jnp.float32))
    column_rows = gather_ordered(part_renewed, shift_y, y_at, n_y)
    both_rows = order_parts([column_rows, swap_core(column_rows)], core_at)
    table_rows_new = both_rows.transpose(1, 0, 2).reshape(-1)[:rows_dev]
    rows_new = [table_rows_new[None]]
    late = jnp.concatenate(
        [
            jnp.sum(part_square, 0) + EPS_SQUARE * live_count,
            jnp.sum(part_square / part_renewed[:, None], 0),
            jnp.sum(jnp.where(part_live, part_renewed, 0.0)).reshape(1),
            jnp.zeros(-(2 * feature_width + 1) % 1024, jnp.float32),
        ]
    )
    late = sum_all(late.reshape(8, -1)).reshape(-1)
    share = 1.0 / n_ctx
    col_parts = []
    weighted_parts = []
    row_parts = []
    for grad_sum, row_state in zip(grad_sums[1:], row_states):
        square = grad_sum * grad_sum
        renewed = DECAY * row_state + (1.0 - DECAY) * jnp.mean(square + EPS_SQUARE, -1)
        rows_new.append(renewed)
        col_parts.append(share * jnp.sum(square + EPS_SQUARE, -2))
        weighted_parts.append(share * jnp.sum(square / renewed[..., None], -2))
        row_parts.append(share * jnp.sum(renewed, -1))
    square_parts = [share * jnp.sum(weight * weight).reshape(1) for weight in matrices]
    early_parts = (
        [vector_grad]
        + col_parts
        + weighted_parts
        + row_parts
        + square_parts
        + [loss_part.reshape(1), jnp.stack(squares)]
    )
    early = jnp.concatenate([part.reshape(-1) for part in early_parts])
    early_count = early.shape[0]
    early = jnp.pad(early, (0, -early_count % 1024)).reshape(-1, 128)
    early = lax.psum(early, ("ctx", "seq", "fsdp")).reshape(-1)
    early_at = 0
    early_sums = []
    for part in early_parts:
        early_sums.append(early[early_at : early_at + part.size].reshape(part.shape))
        early_at += part.size
    vector_sum = early_sums[0]
    col_sums = [late[None, :feature_width]] + early_sums[1:5]
    weighted_sums = [late[None, feature_width : 2 * feature_width]] + early_sums[5:9]
    row_sums = [late[2 * feature_width : 2 * feature_width + 1]] + early_sums[9:13]
    square_sums = early_sums[13:18]
    loss_sum = early_sums[18][0]
    square_total = early_sums[19].reshape(-1)
    cols_new = []
    new_weights = []
    sizes_rms = []
    for matrix_at in range(5):
        grad_sum, renewed, col_state = (
            grad_sums[matrix_at],
            rows_new[matrix_at],
            col_states[matrix_at],
        )
        stack_count, row_local, col_count = grad_sum.shape
        row_total = row_local * n_group
        weighted = weighted_sums[matrix_at]
        renewed_cols = DECAY * col_state + (1.0 - DECAY) * col_sums[matrix_at] / row_total
        row_mean = row_sums[matrix_at] / row_total
        clip_total = jnp.sum(row_mean * jnp.sum(weighted / renewed_cols, -1))
        entries = grad_sum.size * n_group
        update_rms = jnp.sqrt(clip_total / entries)
        weight_rms = jnp.sqrt(square_sums[matrix_at][0] / entries)
        step_scale = RATE * jnp.maximum(EPS_SCALE, weight_rms) / jnp.maximum(1.0, update_rms / CLIP)
        second_moment = renewed[:, :, None] * renewed_cols[:, None, :] / row_mean[:, None, None]
        update = grad_sum * lax.rsqrt(second_moment)
        new_weights.append(matrices[matrix_at] - step_scale * update)
        cols_new.append(renewed_cols)
        sizes_rms.append(update_rms)
    vector_state_new = DECAY * vector_state + (1.0 - DECAY) * (vector_sum * vector_sum + EPS_SQUARE)
    vector_update = vector_sum * lax.rsqrt(vector_state_new)
    vector_rms = jnp.sqrt(jnp.mean(vector_update * vector_update))
    vector_scale = (
        RATE
        * jnp.maximum(EPS_SCALE, jnp.sqrt(jnp.mean(vectors * vectors)))
        / jnp.maximum(1.0, vector_rms / CLIP)
    )
    vectors_new = vectors - vector_scale * vector_update
    sizes_rms.append(vector_rms)
    norms = jnp.concatenate([jnp.sqrt(square_total / total_tokens), jnp.stack(sizes_rms)])
    table_new = new_weights[0][0]
    return (
        loss_sum,
        norms,
        summed[0],
        rows_new[0][0],
        cols_new[0][0],
        table_new,
        table_new.astype(jnp.bfloat16),
        summed[1],
        rows_new[1],
        cols_new[1],
        new_weights[1],
        new_weights[1].astype(jnp.bfloat16),
        summed[2],
        rows_new[2],
        cols_new[2],
        new_weights[2],
        new_weights[2].astype(jnp.bfloat16),
        summed[3],
        rows_new[3],
        cols_new[3],
        new_weights[3],
        new_weights[3].astype(jnp.bfloat16),
        summed[4],
        rows_new[4],
        cols_new[4],
        new_weights[4],
        new_weights[4].astype(jnp.bfloat16),
        vector_sum,
        vector_state_new,
        vectors_new,
    )


def solution(mesh):
    return jax.shard_map(
        body,
        mesh=mesh,
        in_specs=(
            P(),
            P(),
            P(),
            P(),
            P(("seq", "fsdp"), None),
            P(None, ("seq", "fsdp"), None),
            P(None, ("seq", "fsdp"), None),
            P(None, ("seq", "fsdp"), None),
            P(None, ("seq", "fsdp"), None),
            P(),
            P(("seq", "fsdp")),
            P(),
            P(None, ("seq", "fsdp")),
            P(),
            P(None, ("seq", "fsdp")),
            P(),
            P(None, ("seq", "fsdp")),
            P(),
            P(None, ("seq", "fsdp")),
            P(),
            P(),
        ),
        out_specs=(
            P(),
            P(),
            P(("seq", "fsdp"), None),
            P(("seq", "fsdp")),
            P(),
            P(("seq", "fsdp"), None),
            P(("seq", "fsdp"), None),
            P(None, ("seq", "fsdp"), None),
            P(None, ("seq", "fsdp")),
            P(),
            P(None, ("seq", "fsdp"), None),
            P(None, ("seq", "fsdp"), None),
            P(None, ("seq", "fsdp"), None),
            P(None, ("seq", "fsdp")),
            P(),
            P(None, ("seq", "fsdp"), None),
            P(None, ("seq", "fsdp"), None),
            P(None, ("seq", "fsdp"), None),
            P(None, ("seq", "fsdp")),
            P(),
            P(None, ("seq", "fsdp"), None),
            P(None, ("seq", "fsdp"), None),
            P(None, ("seq", "fsdp"), None),
            P(None, ("seq", "fsdp")),
            P(),
            P(None, ("seq", "fsdp"), None),
            P(None, ("seq", "fsdp"), None),
            P(),
            P(),
            P(),
        ),
        check_vma=False,
    )
```

```python
import functools

import jax
import jax.numpy as jnp
from jax import lax
from jax.experimental import pallas as pl
from jax.experimental.pallas import tpu as pltpu
from jax.sharding import PartitionSpec as P

HEADS = 12
VOCAB = 50304


EPS_NORM = 1e-05
EPS_SQUARE = 1e-30
EPS_SCALE = 0.001
DECAY = 0.5
CLIP = 0.4
RATE = 0.6
SECOND = 0.3
MASKED = -1e30
VMEM_BYTES = 56 * 1024 * 1024


def layer_norm(stream, gain, offset):
    center = stream - jnp.mean(stream, -1, keepdims=True)
    spread = jnp.mean(center * center, -1, keepdims=True)
    return center * lax.rsqrt(spread + EPS_NORM) * gain + offset


def gelu_tanh(value):
    return jax.nn.gelu(value, approximate=True)


def positions_of(segments):
    steps_at = jnp.arange(segments.shape[-1], dtype=jnp.int32)
    before = jnp.concatenate(
        [jnp.full(segments.shape[:-1] + (1,), -2, jnp.int32), segments[..., :-1]], -1
    )
    starts = jnp.where(segments != before, steps_at, 0)
    first = lax.cummax(starts, axis=segments.ndim - 1)
    return jnp.where(segments >= 0, steps_at - first, 0)


def product(left, right):
    return jnp.dot(left, right, preferred_element_type=jnp.float32)


def inner(left, right):
    return lax.dot_general(
        left, right, (((1,), (1,)), ((), ())), preferred_element_type=jnp.float32
    )


def outer(left, right):
    return lax.dot_general(
        left, right, (((0,), (0,)), ((), ())), preferred_element_type=jnp.float32
    )


def shift(block, axis, step):
    count = lax.axis_size(axis)
    return lax.ppermute(block, axis, [(i, (i + step) % count) for i in range(count)])


def shift_y(block, step):
    count = lax.axis_size("ctx")
    return lax.ppermute(block, "ctx", [(i, (i + 2 * step) % count) for i in range(count)])


def swap_core(block):
    count = lax.axis_size("ctx")
    return lax.ppermute(block, "ctx", [(i, i ^ 1) for i in range(count)])


def shift_seq(block, step):
    return shift(block, "seq", step)


def shift_fsdp(block, step):
    return shift(block, "fsdp", step)


def pick(parts, at, axis):
    return lax.dynamic_index_in_dim(parts, at, axis, False)


def send_parts(parts, mover, at, axis=0, sent=None):
    count = parts.shape[axis]
    moving = []
    for step in range(1, count):
        piece = pick(parts, lax.rem(at + step, count), axis)
        moving.append(mover(piece if sent is None else piece.astype(sent), step))
    return moving


def add_parts(parts, moved, at, axis=0):
    total = pick(parts, at, axis)
    for piece in moved:
        total = total + piece.astype(total.dtype)
    return total


def scatter_sum(parts, mover, at, axis=0, sent=None):
    return add_parts(parts, send_parts(parts, mover, at, axis, sent), at, axis)


def scatter_fsdp(parts, at):
    count = parts.shape[0]
    if count != 4:
        moved = yield 0, send_parts(parts, shift_fsdp, at)
        return add_parts(parts, moved, at)
    outside = (at == 0) | (at == 3)
    mine = [jnp.where(outside, 0, 1), jnp.where(outside, 3, 2)]
    other = [jnp.where(outside, 1, 0), jnp.where(outside, 2, 3)]
    away = jnp.stack([pick(parts, slot, 0) for slot in other])
    (away,) = yield 0, [lax.ppermute(away, "fsdp", [(0, 1), (1, 0), (2, 3), (3, 2)])]
    first, second = (pick(parts, slot, 0) + away[k] for k, slot in enumerate(mine))
    away = jnp.where(at < 2, second, first)
    (away,) = yield 0, [lax.ppermute(away, "fsdp", [(0, 3), (3, 0), (1, 2), (2, 1)])]
    return jnp.where(at < 2, first, second) + away


def run(task):
    moving = next(task)[1]
    while True:
        try:
            moving = task.send(moving)[1]
        except StopIteration as stop:
            return stop.value


def sum_all(block, skip_y=False):
    for axis in ("ctx", "seq", "fsdp"):
        count = 2 if skip_y and axis == "ctx" else lax.axis_size(axis)
        whole = lax.axis_size(axis)
        hop = 1
        while hop < count:
            block = block + lax.ppermute(block, axis, [(i, i ^ hop) for i in range(whole)])
            hop *= 2
    return block


def order_parts(parts, at):
    count = len(parts)
    if count == 2:
        first, second = parts
        return jnp.stack([jnp.where(at == 0, first, second), jnp.where(at == 0, second, first)])
    order = lax.rem(at - jnp.arange(count, dtype=jnp.int32) + count, count)
    return jnp.take(jnp.stack(parts), order, axis=0, mode="clip")


def gather_near(block):
    n_y = lax.axis_size("ctx") // 2
    column = jnp.concatenate([block] + [shift_y(block, step) for step in range(1, n_y)], 0)
    return jnp.concatenate([column, swap_core(column)], 0)


def scatter_near(parts):
    n_y = lax.axis_size("ctx") // 2
    parts = parts.reshape((2, n_y, -1) + parts.shape[1:])
    column = parts[0] + swap_core(parts[1])
    total = column[0]
    for step in range(1, n_y):
        away = shift_y(column[step].astype(jnp.bfloat16), n_y - step)
        total = total + away.astype(total.dtype)
    return total


def half_of(block, at):
    width = block.shape[-1] // 2
    return jnp.where(at == 0, block[..., :width], block[..., width:])


def qkv_bias(vec):
    return jnp.concatenate([vec[2], jnp.zeros_like(vec[2]), vec[3]])


def attention_scores(query_low, keys, allowed, head_count):
    row_count, feature_width = query_low.shape
    head_size = feature_width // head_count
    scores = jnp.einsum(
        "qhd,khd->hqk",
        query_low.reshape(row_count, head_count, head_size),
        keys.reshape(-1, head_count, head_size),
        preferred_element_type=jnp.float32,
    ) * head_size ** (-0.5)
    return jnp.where(allowed[None], scores, MASKED)


def mix_values(probs_low, values, head_count):
    head_size = values.shape[1] // head_count
    mixed = jnp.einsum(
        "hqk,khd->qhd",
        probs_low,
        values.reshape(-1, head_count, head_size),
        preferred_element_type=jnp.float32,
    )
    return mixed.reshape(mixed.shape[0], -1)


def layer_forward(stream, weights, vec, allowed, head_count):
    w_in, w_out, w_fc, w_down = weights
    feature_width = stream.shape[1]
    a_low = layer_norm(stream, vec[0], vec[1]).astype(jnp.bfloat16)
    qkv_low = (product(a_low, w_in) + qkv_bias(vec)).astype(jnp.bfloat16)
    pairs = gather_near(qkv_low[:, feature_width:])
    keys, values = pairs[:, :feature_width], pairs[:, feature_width:]
    scores = attention_scores(qkv_low[:, :feature_width], keys, allowed, head_count)
    row_max = jnp.max(scores, -1)
    log_total = row_max + jnp.log(jnp.sum(jnp.exp(scores - row_max[..., None]), -1))
    probs = jnp.exp(scores - log_total[..., None])
    mixed_low = mix_values(probs.astype(jnp.bfloat16), values, head_count).astype(jnp.bfloat16)
    branch = product(mixed_low, w_out) + vec[4]
    middle = stream + branch
    m_low = layer_norm(middle, vec[5], vec[6]).astype(jnp.bfloat16)
    hidden = product(m_low, w_fc) + vec[8:12].reshape(-1)
    output = product(gelu_tanh(hidden).astype(jnp.bfloat16), w_down) + vec[7]
    sums = jnp.stack([jnp.sum(stream * stream), jnp.sum(branch * branch), jnp.sum(output * output)])
    kept = (stream, a_low, qkv_low, keys, values, log_total, mixed_low, middle, m_low, hidden)
    return (middle + output, kept, sums)


def swap_pairs(pairs, core_at):
    lefts = [left for left, _ in pairs]
    return swap_core(
        jnp.concatenate(lefts + [half_of(right, 1 - core_at) for _, right in pairs], 1)
    )


def shared_outer(pairs, away, core_at):
    at = 0
    whole_left = []
    for left, _ in pairs:
        whole_left.append(jnp.concatenate([left, away[:, at : at + left.shape[1]]], 0))
        at += left.shape[1]
    grads = []
    for left, (_, right) in zip(whole_left, pairs):
        width = right.shape[1] // 2
        whole_right = jnp.concatenate([half_of(right, core_at), away[:, at : at + width]], 0)
        at += width
        grads.append(outer(left, whole_right))
    return grads


def layer_backward(d_stream, kept, weights, vec, allowed, head_count, pending, first_task, later_task):
    stream, a_low, qkv_low, keys, values, log_total, mixed_low, middle, m_low, hidden = kept
    w_in, w_out, w_fc, w_down = weights
    row_count, feature_width = stream.shape
    head_size = feature_width // head_count
    scale = head_size ** (-0.5)
    norm_back_one = jax.vjp(layer_norm, stream, vec[0], vec[1])[1]
    query_low = qkv_low[:, :feature_width]
    probs = jnp.exp(attention_scores(query_low, keys, allowed, head_count) - log_total[..., None])
    probs_low = probs.astype(jnp.bfloat16)
    norm_back_two = jax.vjp(layer_norm, middle, vec[5], vec[6])[1]
    gelu_out, gelu_back = jax.vjp(gelu_tanh, hidden)
    u_low = gelu_out.astype(jnp.bfloat16)
    d_out_low = d_stream.astype(jnp.bfloat16)
    d_hidden_low = gelu_back(inner(d_out_low, w_down))[0].astype(jnp.bfloat16)
    d_hidden_low = pending.point(d_hidden_low)
    pending.add(first_task([(m_low, d_hidden_low), (u_low, d_out_low)]))
    d_m = inner(d_hidden_low, w_fc)
    d_two, d_gain_two, d_bias_two = norm_back_two(d_m)
    d_middle = d_stream + d_two
    d_middle = pending.point(d_middle)
    d_middle_low = d_middle.astype(jnp.bfloat16)
    d_heads = (
        inner(d_middle_low, w_out).astype(jnp.bfloat16).reshape(row_count, head_count, head_size)
    )
    value_heads = values.reshape(-1, head_count, head_size)
    d_probs = jnp.einsum("qhd,khd->hqk", d_heads, value_heads, preferred_element_type=jnp.float32)
    d_scores = (probs * (d_probs - jnp.sum(probs * d_probs, -1, keepdims=True))).astype(
        jnp.bfloat16
    )
    d_scores = pending.point(d_scores)
    d_query = (
        jnp.einsum(
            "hqk,khd->qhd",
            d_scores,
            keys.reshape(-1, head_count, head_size),
            preferred_element_type=jnp.float32,
        ).reshape(row_count, feature_width)
        * scale
    )
    d_keys = (
        jnp.einsum(
            "hqk,qhd->khd",
            d_scores,
            query_low.reshape(row_count, head_count, head_size),
            preferred_element_type=jnp.float32,
        ).reshape(-1, feature_width)
        * scale
    )
    d_values = jnp.einsum(
        "hqk,qhd->khd", probs_low, d_heads, preferred_element_type=jnp.float32
    ).reshape(-1, feature_width)
    d_pairs = scatter_near(jnp.concatenate([d_keys, d_values], 1))
    d_qkv_low = jnp.concatenate([d_query, d_pairs], 1).astype(jnp.bfloat16)
    d_qkv_low = pending.point(d_qkv_low)
    pending.add(later_task([(a_low, d_qkv_low), (mixed_low, d_middle_low)]))
    d_one, d_gain_one, d_bias_one = norm_back_one(inner(d_qkv_low, w_in))
    d_qkv = d_qkv_low.astype(jnp.float32)
    rows_head = jnp.stack(
        [
            d_gain_one,
            d_bias_one,
            jnp.sum(d_qkv[:, :feature_width], 0),
            jnp.sum(d_qkv[:, 2 * feature_width :], 0),
            jnp.sum(d_middle_low.astype(jnp.float32), 0),
            d_gain_two,
            d_bias_two,
            jnp.sum(d_out_low.astype(jnp.float32), 0),
        ]
    )
    vec_grad = jnp.concatenate(
        [rows_head, jnp.sum(d_hidden_low.astype(jnp.float32), 0).reshape(4, feature_width)], 0
    )
    return (pending.point(d_middle + d_one), vec_grad)


def merge_stats(stats):
    for mover, axis in ((shift_seq, "seq"), (shift_fsdp, "fsdp")):
        parts = [stats] + [mover(stats, step) for step in range(1, lax.axis_size(axis))]
        top = parts[0][0]
        for part in parts[1:]:
            top = jnp.maximum(top, part[0])
        total = jnp.exp(parts[0][0] - top)
        picked = parts[0][1]
        for part in parts[1:]:
            total = total + jnp.exp(part[0] - top)
            picked = picked + part[1]
        stats = jnp.stack([top + jnp.log(total), picked])
    return stats


def blocks_of(groups, width, row_block):
    step = max(1, row_block // width)
    return [
        (range(low, low + step), slice(low * width, (low + step) * width))
        for low in range(0, groups, step)
    ]


def side_by_side(ref, at_block):
    return jnp.concatenate([ref[at] for at in at_block], 1)


def masked_logits(logits, live, first):
    column = lax.broadcasted_iota(jnp.int32, logits.shape, 0) + first
    return jnp.where(column < live, logits, MASKED)


def stats_kernel(row_block, live_ref, table_ref, rows_ref, target_ref, out_ref, top_ref, sum_ref, pick_ref):
    at = pl.program_id(0)
    tile = table_ref.shape[0]
    first = at * tile
    live = live_ref[0]

    @pl.when(at == 0)
    def _():
        top_ref[...] = jnp.full_like(top_ref, MASKED)
        sum_ref[...] = jnp.zeros_like(sum_ref)
        pick_ref[...] = jnp.zeros_like(pick_ref)

    def step(masked):
        for at_block, here in blocks_of(rows_ref.shape[0], rows_ref.shape[2], row_block):
            logits = jnp.dot(
                table_ref[...], side_by_side(rows_ref, at_block), preferred_element_type=jnp.float32
            )
            if masked:
                logits = masked_logits(logits, live, first)
            column = lax.broadcasted_iota(jnp.int32, logits.shape, 0)
            hit = column == target_ref[:, here] - first
            cut = logits.reshape(tile // 8, 8, logits.shape[1])
            top = top_ref[:, here]
            joint = jnp.maximum(top, jnp.max(cut, 0))
            total = jnp.sum(jnp.exp(cut - joint[None]), 0)
            sum_ref[:, here] = sum_ref[:, here] * jnp.exp(top - joint) + total
            top_ref[:, here] = joint
            pick_ref[:, here] += jnp.sum(
                jnp.where(hit, logits, 0.0).reshape(cut.shape), 0
            )

    @pl.when(first + tile <= live)
    def _():
        step(False)

    @pl.when((first + tile > live) & (first < live))
    def _():
        step(True)

    @pl.when(at == pl.num_programs(0) - 1)
    def _():
        top = top_ref[...]
        joint = jnp.max(top, 0, keepdims=True)
        total = jnp.sum(sum_ref[...] * jnp.exp(top - joint), 0, keepdims=True)
        out_ref[0:1, :] = joint + jnp.log(total)
        out_ref[1:2, :] = jnp.sum(pick_ref[...], 0, keepdims=True)


def head_stats(live, table_low, rows_t, target, tile=512, row_block=512):
    groups, depth, width = rows_t.shape
    count = groups * width
    height = table_low.shape[0]
    return pl.pallas_call(
        functools.partial(stats_kernel, row_block),
        out_shape=jax.ShapeDtypeStruct((2, count), jnp.float32),
        grid=(height // tile,),
        in_specs=[
            pl.BlockSpec(memory_space=pltpu.SMEM),
            pl.BlockSpec((tile, depth), lambda i: (i, 0)),
            pl.BlockSpec((groups, depth, width), lambda i: (0, 0, 0)),
            pl.BlockSpec((1, count), lambda i: (0, 0)),
        ],
        out_specs=pl.BlockSpec((2, count), lambda i: (0, 0)),
        scratch_shapes=[pltpu.VMEM((8, count), jnp.float32)] * 3,
        compiler_params=pltpu.CompilerParams(vmem_limit_bytes=VMEM_BYTES),
        cost_estimate=pl.CostEstimate(
            flops=2 * height * depth * count,
            bytes_accessed=2 * height * depth + 2 * depth * count,
            transcendentals=height * count,
        ),
    )(live, table_low, rows_t, target)


def back_kernel(row_block, added, live_ref, table_ref, table_t_ref, rows_ref, rows_t_ref, line_ref, *refs):
    if added:
        prior_ref, grad_ref, d_rows_ref = refs
    else:
        grad_ref, d_rows_ref = refs
    at = pl.program_id(0)
    tile = table_ref.shape[0]
    first = at * tile
    live = live_ref[0]
    width = d_rows_ref.shape[2]

    @pl.when(at == 0)
    def _():
        d_rows_ref[...] = jnp.zeros_like(d_rows_ref)

    def step(masked):
        grad = prior_ref[...] if added else None
        for at_block, here in blocks_of(rows_t_ref.shape[0], width, row_block):
            logits = jnp.dot(
                table_ref[...],
                side_by_side(rows_t_ref, at_block),
                preferred_element_type=jnp.float32,
            )
            if masked:
                logits = masked_logits(logits, live, first)
            column = lax.broadcasted_iota(jnp.int32, logits.shape, 0).astype(jnp.float32)
            probs = jnp.exp(logits - line_ref[0:1, here])
            hit = column == line_ref[2:3, here] - first.astype(jnp.float32)
            d_low = (line_ref[1:2, here] * jnp.where(hit, probs - 1.0, probs)).astype(jnp.bfloat16)
            rows = rows_ref[at_block.start : at_block.stop].reshape(-1, rows_ref.shape[2])
            part = jnp.dot(d_low, rows, preferred_element_type=jnp.float32)
            grad = part if grad is None else grad + part
            d_part = jnp.dot(table_t_ref[...], d_low, preferred_element_type=jnp.float32)
            for at_width, at_group in enumerate(at_block):
                d_rows_ref[at_group] += d_part[:, at_width * width : (at_width + 1) * width]
        grad_ref[...] = grad

    @pl.when(first + tile <= live)
    def _():
        step(False)

    @pl.when((first + tile > live) & (first < live))
    def _():
        step(True)

    @pl.when(first >= live)
    def _():
        grad_ref[...] = prior_ref[...] if added else jnp.zeros_like(grad_ref)


def head_back(live, table_low, table_t, rows, rows_t, line, cut=0, prior=None, tile=512):
    groups, _, depth = rows.shape
    height = table_low.shape[0]
    count = line.shape[1]
    width = count // groups
    once = dict(pipeline_mode=pl.Buffered(1))
    grad_spec = pl.BlockSpec((tile, depth), lambda i: (i, 0))
    added = prior is not None
    return pl.pallas_call(
        functools.partial(back_kernel, 1024, added),
        out_shape=(
            jax.ShapeDtypeStruct((height, depth), jnp.float32),
            jax.ShapeDtypeStruct((groups, depth, width), jnp.float32),
        ),
        grid=(height // tile,),
        in_specs=[
            pl.BlockSpec(memory_space=pltpu.SMEM),
            pl.BlockSpec((tile, depth), lambda i: (i, 0)),
            pl.BlockSpec((depth, tile), lambda i: (0, i)),
            pl.BlockSpec((groups, width, depth), lambda i: (0, cut, 0), **once),
            pl.BlockSpec((groups, depth, width), lambda i: (0, 0, cut), **once),
            pl.BlockSpec((3, count), lambda i: (0, 0), **once),
        ]
        + ([grad_spec] if added else []),
        out_specs=(
            grad_spec,
            pl.BlockSpec((groups, depth, width), lambda i: (0, 0, 0), **once),
        ),
        input_output_aliases={6: 0} if added else {},
        compiler_params=pltpu.CompilerParams(vmem_limit_bytes=VMEM_BYTES),
        cost_estimate=pl.CostEstimate(
            flops=6 * height * depth * count,
            bytes_accessed=4 * height * depth + 12 * depth * count + 8 * height * depth,
            transcendentals=height * count,
        ),
    )(live, table_low, table_t, rows, rows_t, line, *((prior,) if added else ()))


class Pending:
    def __init__(self):
        self.active = []

    def add(self, task):
        held, moving = next(task)
        self.active.append([task, held, moving])

    def point(self, main):
        ready = [entry for entry in self.active if entry[1] == 0]
        main, moved = lax.optimization_barrier((main, [entry[2] for entry in ready]))
        for entry in self.active:
            entry[1] -= 1
        for entry, arrived in zip(ready, moved):
            self.advance(entry, arrived)
        return main

    def advance(self, entry, arrived):
        try:
            entry[1:] = entry[0].send(arrived)
        except StopIteration:
            self.active.remove(entry)

    def finish(self):
        while self.active:
            entry = self.active[0]
            self.advance(entry, entry[2])


def local_index(ids, row_low, row_count):
    shifted = ids - row_low
    inside = (shifted >= 0) & (shifted < row_count)
    return (inside, jnp.clip(shifted, 0, row_count - 1))


def body(
    tokens,
    segments,
    next_ids,
    second_ids,
    table,
    attn_in,
    attn_out,
    mlp_in,
    mlp_out,
    vectors,
    table_rows,
    table_cols,
    attn_in_rows,
    attn_in_cols,
    attn_out_rows,
    attn_out_cols,
    mlp_in_rows,
    mlp_in_cols,
    mlp_out_rows,
    mlp_out_cols,
    vector_state,
):
    n_ctx = lax.axis_size("ctx")
    n_seq = lax.axis_size("seq")
    n_fsdp = lax.axis_size("fsdp")
    n_y = n_ctx // 2
    n_group = n_seq * n_fsdp
    ctx_at = lax.axis_index("ctx")
    seq_at = lax.axis_index("seq")
    fsdp_at = lax.axis_index("fsdp")
    y_at = ctx_at // 2
    core_at = lax.rem(ctx_at, 2)
    group_at = seq_at * n_fsdp + fsdp_at
    all_seqs, length = segments.shape
    seqs_dev = all_seqs // n_group
    ctx_span = length // n_ctx
    feature_width = table.shape[1]
    layer_count = attn_in.shape[0]
    head_count = HEADS
    total_tokens = all_seqs * length
    own_rows = seqs_dev * ctx_span
    block_start = ctx_at * ctx_span
    positions = positions_of(segments)

    def block_of(grid):
        return lax.dynamic_slice_in_dim(grid, block_start, ctx_span, 1)

    tok_block = block_of(tokens).reshape(-1)
    valid_block = (block_of(segments) >= 0).astype(jnp.float32).reshape(-1)
    next_block = block_of(next_ids).reshape(-1)
    second_block = block_of(second_ids).reshape(-1)
    my_segments = lax.dynamic_slice_in_dim(segments, group_at * seqs_dev, seqs_dev, 0)
    my_positions = lax.dynamic_slice_in_dim(positions, group_at * seqs_dev, seqs_dev, 0)
    near = jnp.asarray(
        [(side, step) for side in range(2) for step in range(n_y)], jnp.int32
    )
    near_ctx = 2 * lax.rem(y_at - near[:, 1] + n_y, n_y) + lax.rem(core_at + near[:, 0], 2)

    def near_order(grid):
        cut = grid.reshape(seqs_dev, n_ctx, ctx_span).transpose(1, 0, 2)
        return jnp.take(cut, near_ctx, axis=0, mode="clip").reshape(-1)

    def own_order(grid):
        return block_of(grid).reshape(-1)

    time_grid = jnp.broadcast_to(jnp.arange(length, dtype=jnp.int32)[None], (seqs_dev, length))
    seq_grid = jnp.broadcast_to(jnp.arange(seqs_dev, dtype=jnp.int32)[:, None], (seqs_dev, length))
    q_seg, k_seg = (own_order(my_segments), near_order(my_segments))
    q_time, k_time = (own_order(time_grid), near_order(time_grid))
    q_seq, k_seq = (own_order(seq_grid), near_order(seq_grid))
    allowed = (q_seq[:, None] == k_seq[None]) & (
        (q_time[:, None] == k_time[None])
        | (k_time[None] < q_time[:, None]) & (q_seg[:, None] == k_seg[None]) & (k_seg[None] >= 0)
    )
    rows_dev = table.shape[0]
    row_low = group_at * rows_dev
    rows_group = attn_in.shape[1]
    rows_part = rows_group // n_ctx
    down_cut = mlp_out.shape[1] // rows_group

    in_width, out_width, fc_width = attn_in.shape[2], attn_out.shape[2], mlp_in.shape[2]
    pack_width = in_width + out_width + fc_width + down_cut * feature_width
    part_width = pack_width // n_ctx
    model_rows = n_group * rows_group

    def gather_pack(layer_at, after):
        down = mlp_out[layer_at].reshape(down_cut, rows_group, feature_width)
        pack = jnp.concatenate(
            [attn_in[layer_at], mlp_in[layer_at], attn_out[layer_at]]
            + [down[cut] for cut in range(down_cut)],
            1,
        ).astype(jnp.bfloat16)
        part = lax.dynamic_slice_in_dim(pack, ctx_at * part_width, part_width, 1)
        if layer_at == layer_count - 1:
            head = lax.dynamic_slice_in_dim(
                attn_out[layer_count].astype(jnp.bfloat16), ctx_at * rows_part, rows_part, 0
            )
            head = jnp.pad(head.reshape(-1), (0, -head.size % part_width)).reshape(-1, part_width)
            part = jnp.concatenate([part, head], 0)
        if after is not None:
            part, _ = lax.optimization_barrier((part, after))
        whole = lax.all_gather(part, ("ctx", "seq", "fsdp"), axis=0)
        after = whole[0, 0, :128]
        whole = whole.reshape(n_ctx, n_group, -1, part_width)
        body_rows = whole[:, :, :rows_group].reshape(n_ctx, model_rows, part_width)

        def columns_of(low, high):
            pieces = []
            for at in range(n_ctx):
                start, stop = max(low, at * part_width), min(high, (at + 1) * part_width)
                if start < stop:
                    pieces.append(body_rows[at, :, start - at * part_width : stop - at * part_width])
            return pieces[0] if len(pieces) == 1 else jnp.concatenate(pieces, 1)

        at = in_width + fc_width
        down = jnp.stack(
            [
                columns_of(low, low + feature_width).reshape(n_group, rows_group, feature_width)
                for low in range(at + out_width, pack_width, feature_width)
            ],
            1,
        )
        weights = (
            columns_of(0, in_width),
            columns_of(at, at + out_width),
            columns_of(in_width, at),
            down.reshape(-1, feature_width),
        )
        head = None
        if layer_at == layer_count - 1:
            head = whole[:, :, rows_group:].reshape(n_ctx, n_group, -1)
            head = head[:, :, : rows_part * out_width].reshape(n_ctx, n_group, rows_part, out_width)
            head = head.transpose(1, 0, 2, 3).reshape(model_rows, out_width)
        return weights, head, after

    stored = []
    after = None
    for layer_at in range(layer_count):
        weights, head_weight, after = gather_pack(layer_at, after)
        stored.append(weights)

    tok_inside, tok_safe = local_index(tok_block, row_low, rows_dev)
    embed_term = jnp.where(
        tok_inside[:, None], jnp.take(table, tok_safe, axis=0, mode="clip"), 0.0
    ).astype(jnp.bfloat16)
    embed_term = embed_term.reshape(n_seq, n_fsdp, own_rows, feature_width)
    embed_term = scatter_sum(embed_term, shift_seq, seq_at)
    embed_term = run(scatter_fsdp(embed_term, fsdp_at))
    place_part = length // n_ctx
    place_low = VOCAB - rows_dev * (n_group - 1)
    places = lax.dynamic_slice_in_dim(table, place_low + ctx_at * place_part, place_part, 0)
    places = jnp.where(group_at == n_group - 1, places, 0.0).astype(jnp.bfloat16)
    total = places
    for step in range(1, n_seq):
        total = total + lax.ppermute(places, "seq", [(n_seq - 1, n_seq - 1 - step)])
    places = total
    for step in range(1, n_fsdp):
        total = total + lax.ppermute(places, "fsdp", [(n_fsdp - 1, n_fsdp - 1 - step)])
    places = gather_near(total)
    own_places = own_order(my_positions)
    place_ctx = own_places // place_part
    place_near = lax.rem(core_at + place_ctx, 2) * n_y + lax.rem(y_at - place_ctx // 2 + n_y, n_y)
    place_rows = jnp.take(
        places, place_near * place_part + lax.rem(own_places, place_part), axis=0, mode="clip"
    )
    stream = embed_term.astype(jnp.float32) + place_rows.astype(jnp.float32)
    part_rows = -(-rows_dev // 512) * 256
    spare = part_rows * 2 - rows_dev
    table_low = jnp.pad(table.astype(jnp.bfloat16), ((0, spare), (0, 0)))
    share = 1.0 / n_ctx
    square_parts = [
        share * jnp.sum(weight * weight).reshape(1)
        for weight in (table, attn_in, attn_out, mlp_in, mlp_out)
    ]
    stream, table_low, table_t, square_parts = lax.optimization_barrier(
        (stream, table_low, table_low.T, square_parts)
    )
    kept = []
    squares = []
    for layer_at in range(layer_count):
        stream, layer_kept, layer_sums = layer_forward(
            stream,
            stored[layer_at],
            vectors[12 * layer_at : 12 * layer_at + 12],
            allowed,
            head_count,
        )
        kept.append(layer_kept)
        squares.append(layer_sums)
    final_gain = vectors[12 * layer_count]
    final_bias = vectors[12 * layer_count + 1]
    final_norm, final_back = jax.vjp(layer_norm, stream, final_gain, final_bias)
    final_low = final_norm.astype(jnp.bfloat16)
    second_low = product(final_low, head_weight).astype(jnp.bfloat16)
    live = jnp.clip(VOCAB - row_low, 0, rows_dev).astype(jnp.int32).reshape(1)

    def local_targets(ids):
        inside, safe = local_index(ids, row_low, rows_dev)
        return jnp.where(inside, safe, -1)

    final_all = lax.all_gather(final_low, ("seq", "fsdp"), axis=0)
    second_all = lax.all_gather(second_low, ("seq", "fsdp"), axis=0)
    second_factor = SECOND * valid_block
    final_local, second_local = local_targets(next_block), local_targets(second_block)
    final_t = final_all.swapaxes(1, 2)
    final_stats = head_stats(live, table_low, final_t, final_local[None])
    second_t = second_all.swapaxes(1, 2)
    second_stats = head_stats(live, table_low, second_t, second_local[None])
    stats = merge_stats(jnp.concatenate([final_stats, second_stats], 1))
    half_rows = final_stats.shape[1]
    final_stats, second_stats = stats[:, :half_rows], stats[:, half_rows:]

    pending = Pending()
    results = {}

    def rows_task(name, d_rows):
        parts = d_rows.reshape((n_seq, n_fsdp) + d_rows.shape[1:])
        moved = yield 0, send_parts(parts, shift_seq, seq_at, sent=jnp.bfloat16)
        mine = add_parts(parts, moved, seq_at)
        results[name] = yield from scatter_fsdp(mine, fsdp_at)

    def line_of(stats, factor, local):
        return jnp.stack([stats[0], factor / total_tokens, local.astype(jnp.float32)])

    final_line = line_of(final_stats, valid_block, final_local)
    table_grad, d_rows = head_back(live, table_low, table_t, final_all, final_t, final_line)
    pending.add(rows_task("final", d_rows))
    second_line = line_of(second_stats, second_factor, second_local)
    cuts = 2 if own_rows % 256 == 0 else 1
    for cut in range(cuts):
        line = second_line.reshape(3, n_group, cuts, -1)[:, :, cut].reshape(3, -1)
        table_grad, d_rows = head_back(
            live, table_low, table_t, second_all, second_t, line, cut, table_grad
        )
        table_grad = pending.point(table_grad)
        pending.add(rows_task(("second", cut), d_rows))
    pending.finish()
    d_final = results["final"].T
    d_second = jnp.concatenate([results["second", cut] for cut in range(cuts)], 1).T
    loss_rows = (final_stats[0] - final_stats[1]) * valid_block + (
        second_stats[0] - second_stats[1]
    ) * second_factor
    loss_part = jnp.sum(
        lax.dynamic_slice_in_dim(loss_rows, group_at * own_rows, own_rows, 0)
    )

    def table_task():
        parts = table_grad.reshape(2, part_rows, feature_width)
        (away,) = yield 0, [swap_core(pick(parts, 1 - core_at, 0))]
        mine = (pick(parts, core_at, 0) + away).astype(jnp.bfloat16)
        totals = []
        for low in range(0, part_rows, part_rows // 4):
            piece = mine[low : low + part_rows // 4]
            moved = yield 0, [shift_y(piece, step) for step in range(1, n_y)]
            ordered = order_parts([piece] + moved, y_at).astype(jnp.float32)
            total = ordered[0]
            for step in range(1, n_y):
                total = total + ordered[step]
            totals.append(total)
        results["table"] = jnp.concatenate(totals, 0)

    def bundle_task(pairs, matrices, names):
        (away,) = yield 0, [swap_pairs(pairs, core_at)]
        grads = shared_outer(pairs, away, core_at)
        parts = []
        for grad in grads:
            cut = grad.reshape(n_seq, n_fsdp, -1, rows_group, grad.shape[1])
            parts += [cut[:, :, at] for at in range(cut.shape[2])]
        stacked = jnp.concatenate(parts, -1)
        moved = yield 0, send_parts(stacked, shift_seq, seq_at, sent=jnp.bfloat16)
        mine = add_parts(stacked, moved, seq_at)
        mine = mine.reshape(n_fsdp, n_y, rows_group // n_y, -1)
        moved = yield 0, send_parts(mine, shift_y, y_at, 1, jnp.bfloat16)
        mine = add_parts(mine, moved, y_at, 1)
        mine = yield from scatter_fsdp(mine, fsdp_at)
        moved = yield 0, [shift_y(mine, step) for step in range(1, n_y)]
        column = order_parts([mine] + moved, y_at).reshape(rows_group, -1)
        (away,) = yield 0, [swap_core(column)]
        both = order_parts([column, away], core_at)
        at = 0
        for matrix, name in zip(matrices, names):
            width = matrix.shape[-1] // 2
            cuts = []
            for _ in range(matrix.shape[-2] // rows_group):
                cuts.append(
                    jnp.concatenate([both[0, :, at : at + width], both[1, :, at : at + width]], 1)
                )
                at += width
            results[name] = jnp.concatenate(cuts, 0)

    pending.add(table_task())
    d_second = pending.point(d_second)
    d_second_low = d_second.astype(jnp.bfloat16)
    d_stream, d_gain_final, d_bias_final = final_back(d_final + inner(d_second_low, head_weight))

    vec_list = [None] * layer_count
    for layer_at in reversed(range(layer_count)):

        def first_task(pairs, at=layer_at):
            matrices, names = [mlp_in[at], mlp_out[at]], [("fc", at), ("down", at)]
            if at == layer_count - 1:
                pairs = [(final_low, d_second_low)] + pairs
                matrices = [attn_out[layer_count]] + matrices
                names = [("out", layer_count)] + names
            return bundle_task(pairs, matrices, names)

        def later_task(pairs, at=layer_at):
            return bundle_task(pairs, [attn_in[at], attn_out[at]], [("in", at), ("out", at)])

        d_stream, vec_list[layer_at] = layer_backward(
            d_stream,
            kept[layer_at],
            stored[layer_at],
            vectors[12 * layer_at : 12 * layer_at + 12],
            allowed,
            head_count,
            pending,
            first_task,
            later_task,
        )
    embed_back = lax.all_gather(
        d_stream.astype(jnp.bfloat16), ("seq", "fsdp", "ctx"), axis=0, tiled=True
    )

    def device_order(grid):
        cut = grid.reshape(n_group, seqs_dev, n_ctx, ctx_span)
        return cut.transpose(0, 2, 1, 3).reshape(-1)

    pending.finish()
    table_part = results["table"]
    part_ids = jnp.arange(part_rows, dtype=jnp.int32)
    part_live = part_ids < rows_dev - core_at * part_rows
    part_ids = jnp.where(part_live, row_low + core_at * part_rows + part_ids, -1)
    hits = (part_ids[:, None] == device_order(tokens)[None]) | (
        part_ids[:, None] == device_order(positions)[None] + VOCAB
    )
    table_part = table_part + product(hits.astype(jnp.bfloat16), embed_back)
    table_away = swap_core(table_part)

    def join_core(mine, away):
        first = jnp.where(core_at == 0, mine, away)
        second = jnp.where(core_at == 0, away, mine)
        return jnp.concatenate([first, second[: rows_dev - part_rows]], 0)

    table_sum = join_core(table_part, table_away)

    summed = (
        table_sum,
        jnp.stack([results["in", at] for at in range(layer_count)]),
        jnp.stack([results["out", at] for at in range(layer_count + 1)]),
        jnp.stack([results["fc", at] for at in range(layer_count)]),
        jnp.stack([results["down", at] for at in range(layer_count)]),
    )
    vector_grad = jnp.concatenate(vec_list + [jnp.stack([d_gain_final, d_bias_final])], 0)
    matrices = (table[None], attn_in, attn_out, mlp_in, mlp_out)
    grad_sums = (summed[0][None], summed[1], summed[2], summed[3], summed[4])
    row_states = (attn_in_rows, attn_out_rows, mlp_in_rows, mlp_out_rows)
    col_states = (table_cols[None], attn_in_cols, attn_out_cols, mlp_in_cols, mlp_out_cols)

    state_part = lax.dynamic_slice_in_dim(
        jnp.pad(table_rows, (0, spare)), core_at * part_rows, part_rows, 0
    )
    part_square = table_part * table_part
    part_renewed = DECAY * state_part + (1.0 - DECAY) * jnp.mean(part_square + EPS_SQUARE, -1)
    part_renewed = jnp.where(part_live, part_renewed, 1.0)
    live_count = jnp.sum(part_live.astype(jnp.float32))
    table_rows_new = join_core(part_renewed, swap_core(part_renewed))
    rows_new = [table_rows_new[None]]
    late = jnp.concatenate(
        [
            jnp.sum(part_square, 0) + EPS_SQUARE * live_count,
            jnp.sum(part_square / part_renewed[:, None], 0),
            jnp.sum(jnp.where(part_live, part_renewed, 0.0)).reshape(1),
            jnp.zeros(-(2 * feature_width + 1) % 1024, jnp.float32),
        ]
    )
    late = sum_all(late.reshape(8, -1), skip_y=True).reshape(-1)
    col_parts = []
    weighted_parts = []
    row_parts = []
    for grad_sum, row_state in zip(grad_sums[1:], row_states):
        square = grad_sum * grad_sum
        renewed = DECAY * row_state + (1.0 - DECAY) * jnp.mean(square + EPS_SQUARE, -1)
        rows_new.append(renewed)
        col_parts.append(share * jnp.sum(square + EPS_SQUARE, -2))
        weighted_parts.append(share * jnp.sum(square / renewed[..., None], -2))
        row_parts.append(share * jnp.sum(renewed, -1))
    early_parts = (
        [vector_grad]
        + col_parts
        + weighted_parts
        + row_parts
        + square_parts
        + [loss_part.reshape(1), jnp.stack(squares)]
    )
    early = jnp.concatenate([part.reshape(-1) for part in early_parts])
    early_count = early.shape[0]
    early = jnp.pad(early, (0, -early_count % 1024)).reshape(-1, 128)
    early = sum_all(early).reshape(-1)
    early_at = 0
    early_sums = []
    for part in early_parts:
        early_sums.append(early[early_at : early_at + part.size].reshape(part.shape))
        early_at += part.size
    vector_sum = early_sums[0]
    col_sums = [late[None, :feature_width]] + early_sums[1:5]
    weighted_sums = [late[None, feature_width : 2 * feature_width]] + early_sums[5:9]
    row_sums = [late[2 * feature_width : 2 * feature_width + 1]] + early_sums[9:13]
    square_sums = early_sums[13:18]
    loss_sum = early_sums[18][0]
    square_total = early_sums[19].reshape(-1)
    cols_new = []
    new_weights = []
    sizes_rms = []
    for matrix_at in range(5):
        grad_sum, renewed, col_state = (
            grad_sums[matrix_at],
            rows_new[matrix_at],
            col_states[matrix_at],
        )
        stack_count, row_local, col_count = grad_sum.shape
        row_total = row_local * n_group
        weighted = weighted_sums[matrix_at]
        renewed_cols = DECAY * col_state + (1.0 - DECAY) * col_sums[matrix_at] / row_total
        row_mean = row_sums[matrix_at] / row_total
        clip_total = jnp.sum(row_mean * jnp.sum(weighted / renewed_cols, -1))
        entries = grad_sum.size * n_group
        update_rms = jnp.sqrt(clip_total / entries)
        weight_rms = jnp.sqrt(square_sums[matrix_at][0] / entries)
        step_scale = RATE * jnp.maximum(EPS_SCALE, weight_rms) / jnp.maximum(1.0, update_rms / CLIP)
        second_moment = renewed[:, :, None] * renewed_cols[:, None, :] / row_mean[:, None, None]
        update = grad_sum * lax.rsqrt(second_moment)
        new_weights.append(matrices[matrix_at] - step_scale * update)
        cols_new.append(renewed_cols)
        sizes_rms.append(update_rms)
    vector_state_new = DECAY * vector_state + (1.0 - DECAY) * (vector_sum * vector_sum + EPS_SQUARE)
    vector_update = vector_sum * lax.rsqrt(vector_state_new)
    vector_rms = jnp.sqrt(jnp.mean(vector_update * vector_update))
    vector_scale = (
        RATE
        * jnp.maximum(EPS_SCALE, jnp.sqrt(jnp.mean(vectors * vectors)))
        / jnp.maximum(1.0, vector_rms / CLIP)
    )
    vectors_new = vectors - vector_scale * vector_update
    sizes_rms.append(vector_rms)
    norms = jnp.concatenate([jnp.sqrt(square_total / total_tokens), jnp.stack(sizes_rms)])
    table_new = new_weights[0][0]
    return (
        loss_sum,
        norms,
        summed[0],
        rows_new[0][0],
        cols_new[0][0],
        table_new,
        table_new.astype(jnp.bfloat16),
        summed[1],
        rows_new[1],
        cols_new[1],
        new_weights[1],
        new_weights[1].astype(jnp.bfloat16),
        summed[2],
        rows_new[2],
        cols_new[2],
        new_weights[2],
        new_weights[2].astype(jnp.bfloat16),
        summed[3],
        rows_new[3],
        cols_new[3],
        new_weights[3],
        new_weights[3].astype(jnp.bfloat16),
        summed[4],
        rows_new[4],
        cols_new[4],
        new_weights[4],
        new_weights[4].astype(jnp.bfloat16),
        vector_sum,
        vector_state_new,
        vectors_new,
    )


def solution(mesh):
    return jax.shard_map(
        body,
        mesh=mesh,
        in_specs=(
            P(),
            P(),
            P(),
            P(),
            P(("seq", "fsdp"), None),
            P(None, ("seq", "fsdp"), None),
            P(None, ("seq", "fsdp"), None),
            P(None, ("seq", "fsdp"), None),
            P(None, ("seq", "fsdp"), None),
            P(),
            P(("seq", "fsdp")),
            P(),
            P(None, ("seq", "fsdp")),
            P(),
            P(None, ("seq", "fsdp")),
            P(),
            P(None, ("seq", "fsdp")),
            P(),
            P(None, ("seq", "fsdp")),
            P(),
            P(),
        ),
        out_specs=(
            P(),
            P(),
            P(("seq", "fsdp"), None),
            P(("seq", "fsdp")),
            P(),
            P(("seq", "fsdp"), None),
            P(("seq", "fsdp"), None),
            P(None, ("seq", "fsdp"), None),
            P(None, ("seq", "fsdp")),
            P(),
            P(None, ("seq", "fsdp"), None),
            P(None, ("seq", "fsdp"), None),
            P(None, ("seq", "fsdp"), None),
            P(None, ("seq", "fsdp")),
            P(),
            P(None, ("seq", "fsdp"), None),
            P(None, ("seq", "fsdp"), None),
            P(None, ("seq", "fsdp"), None),
            P(None, ("seq", "fsdp")),
            P(),
            P(None, ("seq", "fsdp"), None),
            P(None, ("seq", "fsdp"), None),
            P(None, ("seq", "fsdp"), None),
            P(None, ("seq", "fsdp")),
            P(),
            P(None, ("seq", "fsdp"), None),
            P(None, ("seq", "fsdp"), None),
            P(),
            P(),
            P(),
        ),
        check_vma=False,
    )
```

```python
import functools

import jax
import jax.numpy as jnp
from jax import lax
from jax.experimental import pallas as pl
from jax.experimental.pallas import tpu as pltpu
from jax.sharding import PartitionSpec as P

HEADS = 12
VOCAB = 50304


EPS_NORM = 1e-05
EPS_SQUARE = 1e-30
EPS_SCALE = 0.001
DECAY = 0.5
CLIP = 0.4
RATE = 0.6
SECOND = 0.3
MASKED = -1e30
VMEM_BYTES = 56 * 1024 * 1024
NEAR_FIRST = [(0, 1), (1, 0), (2, 3), (3, 2)]
NEAR_SECOND = [(0, 3), (3, 0), (1, 2), (2, 1)]


def layer_norm(stream, gain, offset):
    center = stream - jnp.mean(stream, -1, keepdims=True)
    spread = jnp.mean(center * center, -1, keepdims=True)
    return center * lax.rsqrt(spread + EPS_NORM) * gain + offset


def gelu_tanh(value):
    return jax.nn.gelu(value, approximate=True)


def positions_of(segments):
    steps_at = jnp.arange(segments.shape[-1], dtype=jnp.int32)
    before = jnp.concatenate(
        [jnp.full(segments.shape[:-1] + (1,), -2, jnp.int32), segments[..., :-1]], -1
    )
    starts = jnp.where(segments != before, steps_at, 0)
    first = lax.cummax(starts, axis=segments.ndim - 1)
    return jnp.where(segments >= 0, steps_at - first, 0)


def product(left, right):
    return jnp.dot(left, right, preferred_element_type=jnp.float32)


def inner(left, right):
    return lax.dot_general(
        left, right, (((1,), (1,)), ((), ())), preferred_element_type=jnp.float32
    )


def outer(left, right):
    return lax.dot_general(
        left, right, (((0,), (0,)), ((), ())), preferred_element_type=jnp.float32
    )


def shift(block, axis, step):
    count = lax.axis_size(axis)
    return lax.ppermute(block, axis, [(i, (i + step) % count) for i in range(count)])


def shift_y(block, step):
    count = lax.axis_size("ctx")
    return lax.ppermute(block, "ctx", [(i, (i + 2 * step) % count) for i in range(count)])


def swap_core(block):
    count = lax.axis_size("ctx")
    return lax.ppermute(block, "ctx", [(i, i ^ 1) for i in range(count)])


def shift_seq(block, step):
    return shift(block, "seq", step)


def shift_fsdp(block, step):
    return shift(block, "fsdp", step)


def pick(parts, at, axis):
    return lax.dynamic_index_in_dim(parts, at, axis, False)


def send_parts(parts, mover, at, axis=0, sent=None):
    count = parts.shape[axis]
    moving = []
    for step in range(1, count):
        piece = pick(parts, lax.rem(at + step, count), axis)
        moving.append(mover(piece if sent is None else piece.astype(sent), step))
    return moving


def add_parts(parts, moved, at, axis=0):
    total = pick(parts, at, axis)
    for piece in moved:
        total = total + piece.astype(total.dtype)
    return total


def scatter_sum(parts, mover, at, axis=0, sent=None):
    return add_parts(parts, send_parts(parts, mover, at, axis, sent), at, axis)


def scatter_fsdp(parts, at):
    count = parts.shape[0]
    if count != 4:
        moved = yield 0, send_parts(parts, shift_fsdp, at, sent=jnp.bfloat16)
        return add_parts(parts, moved, at)
    outside = (at == 0) | (at == 3)
    mine = [jnp.where(outside, 0, 1), jnp.where(outside, 3, 2)]
    other = [jnp.where(outside, 1, 0), jnp.where(outside, 2, 3)]
    away = jnp.stack([pick(parts, slot, 0) for slot in other]).astype(jnp.bfloat16)
    (away,) = yield 0, [lax.ppermute(away, "fsdp", NEAR_FIRST)]
    first, second = (
        pick(parts, slot, 0) + away[k].astype(parts.dtype) for k, slot in enumerate(mine)
    )
    away = jnp.where(at < 2, second, first).astype(jnp.bfloat16)
    (away,) = yield 0, [lax.ppermute(away, "fsdp", NEAR_SECOND)]
    return jnp.where(at < 2, first, second) + away.astype(parts.dtype)


def run(task):
    moving = next(task)[1]
    while True:
        try:
            moving = task.send(moving)[1]
        except StopIteration as stop:
            return stop.value


def sum_all(block, skip_y=False):
    for axis in ("ctx", "seq", "fsdp"):
        count = 2 if skip_y and axis == "ctx" else lax.axis_size(axis)
        whole = lax.axis_size(axis)
        hop = 1
        while hop < count:
            block = block + lax.ppermute(block, axis, [(i, i ^ hop) for i in range(whole)])
            hop *= 2
    return block


def order_parts(parts, at):
    count = len(parts)
    if count == 2:
        first, second = parts
        return jnp.stack([jnp.where(at == 0, first, second), jnp.where(at == 0, second, first)])
    order = lax.rem(at - jnp.arange(count, dtype=jnp.int32) + count, count)
    return jnp.take(jnp.stack(parts), order, axis=0, mode="clip")


def gather_near(block):
    n_y = lax.axis_size("ctx") // 2
    column = jnp.concatenate([block] + [shift_y(block, step) for step in range(1, n_y)], 0)
    return jnp.concatenate([column, swap_core(column)], 0)


def scatter_near(parts):
    n_y = lax.axis_size("ctx") // 2
    parts = parts.reshape((2, n_y, -1) + parts.shape[1:])
    column = parts[0] + swap_core(parts[1])
    total = column[0]
    for step in range(1, n_y):
        away = shift_y(column[step].astype(jnp.bfloat16), n_y - step)
        total = total + away.astype(total.dtype)
    return total


def half_of(block, at):
    width = block.shape[-1] // 2
    return jnp.where(at == 0, block[..., :width], block[..., width:])


def qkv_bias(vec):
    return jnp.concatenate([vec[2], jnp.zeros_like(vec[2]), vec[3]])


def attention_scores(query_low, keys, allowed, head_count):
    row_count, feature_width = query_low.shape
    head_size = feature_width // head_count
    scores = jnp.einsum(
        "qhd,khd->hqk",
        query_low.reshape(row_count, head_count, head_size),
        keys.reshape(-1, head_count, head_size),
        preferred_element_type=jnp.float32,
    ) * head_size ** (-0.5)
    return jnp.where(allowed[None], scores, MASKED)


def mix_values(probs_low, values, head_count):
    head_size = values.shape[1] // head_count
    mixed = jnp.einsum(
        "hqk,khd->qhd",
        probs_low,
        values.reshape(-1, head_count, head_size),
        preferred_element_type=jnp.float32,
    )
    return mixed.reshape(mixed.shape[0], -1)


def layer_forward(stream, weights, vec, allowed, head_count):
    w_in, w_out, w_fc, w_down = weights
    feature_width = stream.shape[1]
    a_low = layer_norm(stream, vec[0], vec[1]).astype(jnp.bfloat16)
    qkv_low = (product(a_low, w_in) + qkv_bias(vec)).astype(jnp.bfloat16)
    pairs = gather_near(qkv_low[:, feature_width:])
    keys, values = pairs[:, :feature_width], pairs[:, feature_width:]
    scores = attention_scores(qkv_low[:, :feature_width], keys, allowed, head_count)
    row_max = jnp.max(scores, -1)
    log_total = row_max + jnp.log(jnp.sum(jnp.exp(scores - row_max[..., None]), -1))
    probs = jnp.exp(scores - log_total[..., None])
    mixed_low = mix_values(probs.astype(jnp.bfloat16), values, head_count).astype(jnp.bfloat16)
    branch = product(mixed_low, w_out) + vec[4]
    middle = stream + branch
    m_low = layer_norm(middle, vec[5], vec[6]).astype(jnp.bfloat16)
    hidden = product(m_low, w_fc) + vec[8:12].reshape(-1)
    output = product(gelu_tanh(hidden).astype(jnp.bfloat16), w_down) + vec[7]
    sums = jnp.stack([jnp.sum(stream * stream), jnp.sum(branch * branch), jnp.sum(output * output)])
    kept = (stream, a_low, qkv_low, keys, values, log_total, mixed_low, middle, m_low, hidden)
    return (middle + output, kept, sums)


def swap_pairs(pairs, core_at):
    lefts = [left for left, _ in pairs]
    return swap_core(
        jnp.concatenate(lefts + [half_of(right, 1 - core_at) for _, right in pairs], 1)
    )


def shared_outer(pairs, away, core_at):
    at = 0
    whole_left = []
    for left, _ in pairs:
        whole_left.append(jnp.concatenate([left, away[:, at : at + left.shape[1]]], 0))
        at += left.shape[1]
    grads = []
    for left, (_, right) in zip(whole_left, pairs):
        width = right.shape[1] // 2
        whole_right = jnp.concatenate([half_of(right, core_at), away[:, at : at + width]], 0)
        at += width
        grads.append(outer(left, whole_right))
    return grads


def layer_backward(d_stream, kept, weights, vec, allowed, head_count, pending, first_task, later_task):
    stream, a_low, qkv_low, keys, values, log_total, mixed_low, middle, m_low, hidden = kept
    w_in, w_out, w_fc, w_down = weights
    row_count, feature_width = stream.shape
    head_size = feature_width // head_count
    scale = head_size ** (-0.5)
    norm_back_one = jax.vjp(layer_norm, stream, vec[0], vec[1])[1]
    query_low = qkv_low[:, :feature_width]
    probs = jnp.exp(attention_scores(query_low, keys, allowed, head_count) - log_total[..., None])
    probs_low = probs.astype(jnp.bfloat16)
    norm_back_two = jax.vjp(layer_norm, middle, vec[5], vec[6])[1]
    gelu_out, gelu_back = jax.vjp(gelu_tanh, hidden)
    u_low = gelu_out.astype(jnp.bfloat16)
    d_out_low = d_stream.astype(jnp.bfloat16)
    d_hidden_low = gelu_back(inner(d_out_low, w_down))[0].astype(jnp.bfloat16)
    d_hidden_low = pending.point(d_hidden_low)
    pending.add(first_task([(m_low, d_hidden_low), (u_low, d_out_low)]))
    d_m = inner(d_hidden_low, w_fc)
    d_two, d_gain_two, d_bias_two = norm_back_two(d_m)
    d_middle = d_stream + d_two
    d_middle = pending.point(d_middle)
    d_middle_low = d_middle.astype(jnp.bfloat16)
    d_heads = (
        inner(d_middle_low, w_out).astype(jnp.bfloat16).reshape(row_count, head_count, head_size)
    )
    value_heads = values.reshape(-1, head_count, head_size)
    d_probs = jnp.einsum("qhd,khd->hqk", d_heads, value_heads, preferred_element_type=jnp.float32)
    d_scores = (probs * (d_probs - jnp.sum(probs * d_probs, -1, keepdims=True))).astype(
        jnp.bfloat16
    )
    d_scores = pending.point(d_scores)
    d_query = (
        jnp.einsum(
            "hqk,khd->qhd",
            d_scores,
            keys.reshape(-1, head_count, head_size),
            preferred_element_type=jnp.float32,
        ).reshape(row_count, feature_width)
        * scale
    )
    d_keys = (
        jnp.einsum(
            "hqk,qhd->khd",
            d_scores,
            query_low.reshape(row_count, head_count, head_size),
            preferred_element_type=jnp.float32,
        ).reshape(-1, feature_width)
        * scale
    )
    d_values = jnp.einsum(
        "hqk,qhd->khd", probs_low, d_heads, preferred_element_type=jnp.float32
    ).reshape(-1, feature_width)
    d_pairs = scatter_near(jnp.concatenate([d_keys, d_values], 1))
    d_qkv_low = jnp.concatenate([d_query, d_pairs], 1).astype(jnp.bfloat16)
    d_qkv_low = pending.point(d_qkv_low)
    pending.add(later_task([(a_low, d_qkv_low), (mixed_low, d_middle_low)]))
    d_one, d_gain_one, d_bias_one = norm_back_one(inner(d_qkv_low, w_in))
    d_qkv = d_qkv_low.astype(jnp.float32)
    rows_head = jnp.stack(
        [
            d_gain_one,
            d_bias_one,
            jnp.sum(d_qkv[:, :feature_width], 0),
            jnp.sum(d_qkv[:, 2 * feature_width :], 0),
            jnp.sum(d_middle_low.astype(jnp.float32), 0),
            d_gain_two,
            d_bias_two,
            jnp.sum(d_out_low.astype(jnp.float32), 0),
        ]
    )
    vec_grad = jnp.concatenate(
        [rows_head, jnp.sum(d_hidden_low.astype(jnp.float32), 0).reshape(4, feature_width)], 0
    )
    return (pending.point(d_middle + d_one), vec_grad)


def merge_stats(stats):
    for mover, axis in ((shift_seq, "seq"), (shift_fsdp, "fsdp")):
        parts = [stats] + [mover(stats, step) for step in range(1, lax.axis_size(axis))]
        top = parts[0][0]
        for part in parts[1:]:
            top = jnp.maximum(top, part[0])
        total = jnp.exp(parts[0][0] - top)
        picked = parts[0][1]
        for part in parts[1:]:
            total = total + jnp.exp(part[0] - top)
            picked = picked + part[1]
        stats = jnp.stack([top + jnp.log(total), picked])
    return stats


def blocks_of(groups, width, row_block):
    step = max(1, row_block // width)
    return [
        (range(low, low + step), slice(low * width, (low + step) * width))
        for low in range(0, groups, step)
    ]


def side_by_side(ref, at_block):
    return jnp.concatenate([ref[at] for at in at_block], 1)


def masked_logits(logits, live, first):
    column = lax.broadcasted_iota(jnp.int32, logits.shape, 0) + first
    return jnp.where(column < live, logits, MASKED)


def stats_kernel(row_block, live_ref, table_ref, rows_ref, target_ref, out_ref, top_ref, sum_ref, pick_ref):
    at = pl.program_id(0)
    tile = table_ref.shape[0]
    first = at * tile
    live = live_ref[0]

    @pl.when(at == 0)
    def _():
        top_ref[...] = jnp.full_like(top_ref, MASKED)
        sum_ref[...] = jnp.zeros_like(sum_ref)
        pick_ref[...] = jnp.zeros_like(pick_ref)

    def step(masked):
        for at_block, here in blocks_of(rows_ref.shape[0], rows_ref.shape[2], row_block):
            logits = jnp.dot(
                table_ref[...], side_by_side(rows_ref, at_block), preferred_element_type=jnp.float32
            )
            if masked:
                logits = masked_logits(logits, live, first)
            column = lax.broadcasted_iota(jnp.int32, logits.shape, 0)
            hit = column == target_ref[:, here] - first
            cut = logits.reshape(tile // 8, 8, logits.shape[1])
            top = top_ref[:, here]
            joint = jnp.maximum(top, jnp.max(cut, 0))
            total = jnp.sum(jnp.exp(cut - joint[None]), 0)
            sum_ref[:, here] = sum_ref[:, here] * jnp.exp(top - joint) + total
            top_ref[:, here] = joint
            pick_ref[:, here] += jnp.sum(
                jnp.where(hit, logits, 0.0).reshape(cut.shape), 0
            )

    @pl.when(first + tile <= live)
    def _():
        step(False)

    @pl.when((first + tile > live) & (first < live))
    def _():
        step(True)

    @pl.when(at == pl.num_programs(0) - 1)
    def _():
        top = top_ref[...]
        joint = jnp.max(top, 0, keepdims=True)
        total = jnp.sum(sum_ref[...] * jnp.exp(top - joint), 0, keepdims=True)
        out_ref[0:1, :] = joint + jnp.log(total)
        out_ref[1:2, :] = jnp.sum(pick_ref[...], 0, keepdims=True)


def head_stats(live, table_low, rows_t, target, tile=512, row_block=512):
    groups, depth, width = rows_t.shape
    count = groups * width
    height = table_low.shape[0]
    return pl.pallas_call(
        functools.partial(stats_kernel, row_block),
        out_shape=jax.ShapeDtypeStruct((2, count), jnp.float32),
        grid=(height // tile,),
        in_specs=[
            pl.BlockSpec(memory_space=pltpu.SMEM),
            pl.BlockSpec((tile, depth), lambda i: (i, 0)),
            pl.BlockSpec((groups, depth, width), lambda i: (0, 0, 0)),
            pl.BlockSpec((1, count), lambda i: (0, 0)),
        ],
        out_specs=pl.BlockSpec((2, count), lambda i: (0, 0)),
        scratch_shapes=[pltpu.VMEM((8, count), jnp.float32)] * 3,
        compiler_params=pltpu.CompilerParams(vmem_limit_bytes=VMEM_BYTES),
        cost_estimate=pl.CostEstimate(
            flops=2 * height * depth * count,
            bytes_accessed=2 * height * depth + 2 * depth * count,
            transcendentals=height * count,
        ),
    )(live, table_low, rows_t, target)


def back_kernel(row_block, added, live_ref, table_ref, table_t_ref, rows_ref, rows_t_ref, line_ref, *refs):
    if added:
        prior_ref, grad_ref, d_rows_ref = refs
    else:
        grad_ref, d_rows_ref = refs
    at = pl.program_id(0)
    tile = table_ref.shape[0]
    first = at * tile
    live = live_ref[0]
    width = d_rows_ref.shape[2]

    @pl.when(at == 0)
    def _():
        d_rows_ref[...] = jnp.zeros_like(d_rows_ref)

    def step(masked):
        grad = prior_ref[...] if added else None
        for at_block, here in blocks_of(rows_t_ref.shape[0], width, row_block):
            logits = jnp.dot(
                table_ref[...],
                side_by_side(rows_t_ref, at_block),
                preferred_element_type=jnp.float32,
            )
            if masked:
                logits = masked_logits(logits, live, first)
            column = lax.broadcasted_iota(jnp.int32, logits.shape, 0).astype(jnp.float32)
            probs = jnp.exp(logits - line_ref[0:1, here])
            hit = column == line_ref[2:3, here] - first.astype(jnp.float32)
            d_low = (line_ref[1:2, here] * jnp.where(hit, probs - 1.0, probs)).astype(jnp.bfloat16)
            rows = rows_ref[at_block.start : at_block.stop].reshape(-1, rows_ref.shape[2])
            part = jnp.dot(d_low, rows, preferred_element_type=jnp.float32)
            grad = part if grad is None else grad + part
            d_part = jnp.dot(table_t_ref[...], d_low, preferred_element_type=jnp.float32)
            for at_width, at_group in enumerate(at_block):
                d_rows_ref[at_group] += d_part[:, at_width * width : (at_width + 1) * width]
        grad_ref[...] = grad

    @pl.when(first + tile <= live)
    def _():
        step(False)

    @pl.when((first + tile > live) & (first < live))
    def _():
        step(True)

    @pl.when(first >= live)
    def _():
        grad_ref[...] = prior_ref[...] if added else jnp.zeros_like(grad_ref)


def head_back(live, table_low, table_t, rows, rows_t, line, cut=0, prior=None, tile=512):
    groups, _, depth = rows.shape
    height = table_low.shape[0]
    count = line.shape[1]
    width = count // groups
    once = dict(pipeline_mode=pl.Buffered(1))
    grad_spec = pl.BlockSpec((tile, depth), lambda i: (i, 0))
    added = prior is not None
    return pl.pallas_call(
        functools.partial(back_kernel, 1024, added),
        out_shape=(
            jax.ShapeDtypeStruct((height, depth), jnp.float32),
            jax.ShapeDtypeStruct((groups, depth, width), jnp.float32),
        ),
        grid=(height // tile,),
        in_specs=[
            pl.BlockSpec(memory_space=pltpu.SMEM),
            pl.BlockSpec((tile, depth), lambda i: (i, 0)),
            pl.BlockSpec((depth, tile), lambda i: (0, i)),
            pl.BlockSpec((groups, width, depth), lambda i: (0, cut, 0), **once),
            pl.BlockSpec((groups, depth, width), lambda i: (0, 0, cut), **once),
            pl.BlockSpec((3, count), lambda i: (0, 0), **once),
        ]
        + ([grad_spec] if added else []),
        out_specs=(
            grad_spec,
            pl.BlockSpec((groups, depth, width), lambda i: (0, 0, 0), **once),
        ),
        input_output_aliases={6: 0} if added else {},
        compiler_params=pltpu.CompilerParams(vmem_limit_bytes=VMEM_BYTES),
        cost_estimate=pl.CostEstimate(
            flops=6 * height * depth * count,
            bytes_accessed=4 * height * depth + 12 * depth * count + 8 * height * depth,
            transcendentals=height * count,
        ),
    )(live, table_low, table_t, rows, rows_t, line, *((prior,) if added else ()))


class Pending:
    def __init__(self):
        self.active = []

    def add(self, task):
        held, moving = next(task)
        self.active.append([task, held, moving])

    def point(self, main):
        ready = [entry for entry in self.active if entry[1] == 0]
        main, moved = lax.optimization_barrier((main, [entry[2] for entry in ready]))
        for entry in self.active:
            entry[1] -= 1
        for entry, arrived in zip(ready, moved):
            self.advance(entry, arrived)
        return main

    def advance(self, entry, arrived):
        try:
            entry[1:] = entry[0].send(arrived)
        except StopIteration:
            self.active.remove(entry)

    def finish(self):
        while self.active:
            entry = self.active[0]
            self.advance(entry, entry[2])


def local_index(ids, row_low, row_count):
    shifted = ids - row_low
    inside = (shifted >= 0) & (shifted < row_count)
    return (inside, jnp.clip(shifted, 0, row_count - 1))


def body(
    tokens,
    segments,
    next_ids,
    second_ids,
    table,
    attn_in,
    attn_out,
    mlp_in,
    mlp_out,
    vectors,
    table_rows,
    table_cols,
    attn_in_rows,
    attn_in_cols,
    attn_out_rows,
    attn_out_cols,
    mlp_in_rows,
    mlp_in_cols,
    mlp_out_rows,
    mlp_out_cols,
    vector_state,
):
    n_ctx = lax.axis_size("ctx")
    n_seq = lax.axis_size("seq")
    n_fsdp = lax.axis_size("fsdp")
    n_y = n_ctx // 2
    n_group = n_seq * n_fsdp
    ctx_at = lax.axis_index("ctx")
    seq_at = lax.axis_index("seq")
    fsdp_at = lax.axis_index("fsdp")
    y_at = ctx_at // 2
    core_at = lax.rem(ctx_at, 2)
    group_at = seq_at * n_fsdp + fsdp_at
    all_seqs, length = segments.shape
    seqs_dev = all_seqs // n_group
    ctx_span = length // n_ctx
    feature_width = table.shape[1]
    layer_count = attn_in.shape[0]
    head_count = HEADS
    total_tokens = all_seqs * length
    own_rows = seqs_dev * ctx_span
    block_start = ctx_at * ctx_span
    positions = positions_of(segments)

    def block_of(grid):
        return lax.dynamic_slice_in_dim(grid, block_start, ctx_span, 1)

    tok_block = block_of(tokens).reshape(-1)
    valid_block = (block_of(segments) >= 0).astype(jnp.float32).reshape(-1)
    next_block = block_of(next_ids).reshape(-1)
    second_block = block_of(second_ids).reshape(-1)
    my_segments = lax.dynamic_slice_in_dim(segments, group_at * seqs_dev, seqs_dev, 0)
    my_positions = lax.dynamic_slice_in_dim(positions, group_at * seqs_dev, seqs_dev, 0)
    near = jnp.asarray(
        [(side, step) for side in range(2) for step in range(n_y)], jnp.int32
    )
    near_ctx = 2 * lax.rem(y_at - near[:, 1] + n_y, n_y) + lax.rem(core_at + near[:, 0], 2)

    def near_order(grid):
        cut = grid.reshape(seqs_dev, n_ctx, ctx_span).transpose(1, 0, 2)
        return jnp.take(cut, near_ctx, axis=0, mode="clip").reshape(-1)

    def own_order(grid):
        return block_of(grid).reshape(-1)

    time_grid = jnp.broadcast_to(jnp.arange(length, dtype=jnp.int32)[None], (seqs_dev, length))
    seq_grid = jnp.broadcast_to(jnp.arange(seqs_dev, dtype=jnp.int32)[:, None], (seqs_dev, length))
    q_seg, k_seg = (own_order(my_segments), near_order(my_segments))
    q_time, k_time = (own_order(time_grid), near_order(time_grid))
    q_seq, k_seq = (own_order(seq_grid), near_order(seq_grid))
    allowed = (q_seq[:, None] == k_seq[None]) & (
        (q_time[:, None] == k_time[None])
        | (k_time[None] < q_time[:, None]) & (q_seg[:, None] == k_seg[None]) & (k_seg[None] >= 0)
    )
    rows_dev = table.shape[0]
    row_low = group_at * rows_dev
    rows_group = attn_in.shape[1]
    rows_part = rows_group // n_ctx
    down_cut = mlp_out.shape[1] // rows_group

    in_width, out_width, fc_width = attn_in.shape[2], attn_out.shape[2], mlp_in.shape[2]
    pack_width = in_width + out_width + fc_width + down_cut * feature_width
    part_width = pack_width // n_ctx
    model_rows = n_group * rows_group

    def gather_pack(layer_at, after):
        down = mlp_out[layer_at].reshape(down_cut, rows_group, feature_width)
        pack = jnp.concatenate(
            [attn_in[layer_at], mlp_in[layer_at], attn_out[layer_at]]
            + [down[cut] for cut in range(down_cut)],
            1,
        ).astype(jnp.bfloat16)
        part = lax.dynamic_slice_in_dim(pack, ctx_at * part_width, part_width, 1)
        if layer_at == layer_count - 1:
            head = lax.dynamic_slice_in_dim(
                attn_out[layer_count].astype(jnp.bfloat16), ctx_at * rows_part, rows_part, 0
            )
            head = jnp.pad(head.reshape(-1), (0, -head.size % part_width)).reshape(-1, part_width)
            part = jnp.concatenate([part, head], 0)
        if after is not None:
            part, _ = lax.optimization_barrier((part, after))
        whole = lax.all_gather(part, ("ctx", "seq", "fsdp"), axis=0)
        return whole, whole[0, 0, :128]

    def cut_pack(layer_at, whole):
        whole = whole.reshape(n_ctx, n_group, -1, part_width)
        body_rows = whole[:, :, :rows_group].reshape(n_ctx, model_rows, part_width)

        def columns_of(low, high):
            pieces = []
            for at in range(n_ctx):
                start, stop = max(low, at * part_width), min(high, (at + 1) * part_width)
                if start < stop:
                    pieces.append(body_rows[at, :, start - at * part_width : stop - at * part_width])
            return pieces[0] if len(pieces) == 1 else jnp.concatenate(pieces, 1)

        at = in_width + fc_width
        down = jnp.stack(
            [
                columns_of(low, low + feature_width).reshape(n_group, rows_group, feature_width)
                for low in range(at + out_width, pack_width, feature_width)
            ],
            1,
        )
        weights = (
            columns_of(0, in_width),
            columns_of(at, at + out_width),
            columns_of(in_width, at),
            down.reshape(-1, feature_width),
        )
        head = None
        if layer_at == layer_count - 1:
            head = whole[:, :, rows_group:].reshape(n_ctx, n_group, -1)
            head = head[:, :, : rows_part * out_width].reshape(n_ctx, n_group, rows_part, out_width)
            head = head.transpose(1, 0, 2, 3).reshape(model_rows, out_width)
        return weights, head

    stored = []
    after = None
    for layer_at in range(layer_count):
        whole, after = gather_pack(layer_at, after)
        stored.append(whole)

    tok_inside, tok_safe = local_index(tok_block, row_low, rows_dev)
    embed_term = jnp.where(
        tok_inside[:, None], jnp.take(table, tok_safe, axis=0, mode="clip"), 0.0
    ).astype(jnp.bfloat16)
    embed_term = embed_term.reshape(n_seq, n_fsdp, own_rows, feature_width)
    place_part = length // n_ctx
    place_low = VOCAB - rows_dev * (n_group - 1)
    places = lax.dynamic_slice_in_dim(table, place_low + ctx_at * place_part, place_part, 0)
    places = jnp.where(group_at == n_group - 1, places, 0.0).astype(jnp.bfloat16)
    table_later = table
    if (n_seq, n_fsdp) == (2, 4):
        flat = (-1, feature_width)
        sent = pick(embed_term, 1 - seq_at, 0).reshape(flat)
        away = shift_seq(jnp.concatenate([sent, places], 0), 1)
        away, table_later = lax.optimization_barrier((away, table))
        mine = pick(embed_term, seq_at, 0) + away[:-place_part].reshape(embed_term.shape[1:])
        places = places + away[-place_part:]
        outside = (fsdp_at == 0) | (fsdp_at == 3)
        pair = jnp.where(outside, mine[1:3], jnp.stack([mine[0], mine[3]]))
        sent = jnp.concatenate([pair.reshape(flat), places], 0)
        away = lax.ppermute(sent, "fsdp", NEAR_FIRST)
        kept_pair = jnp.where(outside, jnp.stack([mine[0], mine[3]]), mine[1:3])
        kept_pair = kept_pair + away[:-place_part].reshape(kept_pair.shape)
        places = places + away[-place_part:]
        sent = jnp.concatenate([jnp.where(fsdp_at < 2, kept_pair[1], kept_pair[0]), places], 0)
        away = lax.ppermute(sent, "fsdp", NEAR_SECOND)
        embed_term = jnp.where(fsdp_at < 2, kept_pair[0], kept_pair[1]) + away[:-place_part]
        total = places + away[-place_part:]
    else:
        embed_term = scatter_sum(embed_term, shift_seq, seq_at)
        embed_term = run(scatter_fsdp(embed_term, fsdp_at))
        total = places
        for step in range(1, n_seq):
            total = total + lax.ppermute(places, "seq", [(n_seq - 1, n_seq - 1 - step)])
        places = total
        for step in range(1, n_fsdp):
            total = total + lax.ppermute(places, "fsdp", [(n_fsdp - 1, n_fsdp - 1 - step)])
    places = gather_near(total)
    own_places = own_order(my_positions)
    place_ctx = own_places // place_part
    place_near = lax.rem(core_at + place_ctx, 2) * n_y + lax.rem(y_at - place_ctx // 2 + n_y, n_y)
    place_rows = jnp.take(
        places, place_near * place_part + lax.rem(own_places, place_part), axis=0, mode="clip"
    )
    stream = embed_term.astype(jnp.float32) + place_rows.astype(jnp.float32)
    part_rows = -(-rows_dev // 512) * 256
    spare = part_rows * 2 - rows_dev
    table_low = jnp.pad(table_later.astype(jnp.bfloat16), ((0, spare), (0, 0)))
    share = 1.0 / n_ctx
    square_parts = [
        share * jnp.sum(weight * weight).reshape(1)
        for weight in (table_later, attn_in, attn_out, mlp_in, mlp_out)
    ]
    table_low = lax.optimization_barrier(table_low)
    stream, table_low, table_t, square_parts = lax.optimization_barrier(
        (stream, table_low, table_low.T, square_parts)
    )
    kept = []
    squares = []
    for layer_at in range(layer_count):
        if layer_at:
            stream, stored[layer_at] = lax.optimization_barrier((stream, stored[layer_at]))
        stored[layer_at], head_weight = cut_pack(layer_at, stored[layer_at])
        stream, layer_kept, layer_sums = layer_forward(
            stream,
            stored[layer_at],
            vectors[12 * layer_at : 12 * layer_at + 12],
            allowed,
            head_count,
        )
        kept.append(layer_kept)
        squares.append(layer_sums)
    final_gain = vectors[12 * layer_count]
    final_bias = vectors[12 * layer_count + 1]
    final_norm, final_back = jax.vjp(layer_norm, stream, final_gain, final_bias)
    final_low = final_norm.astype(jnp.bfloat16)
    second_low = product(final_low, head_weight).astype(jnp.bfloat16)
    live = jnp.clip(VOCAB - row_low, 0, rows_dev).astype(jnp.int32).reshape(1)

    def local_targets(ids):
        inside, safe = local_index(ids, row_low, rows_dev)
        return jnp.where(inside, safe, -1)

    final_all = lax.all_gather(final_low, ("seq", "fsdp"), axis=0)
    second_all = lax.all_gather(second_low, ("seq", "fsdp"), axis=0)
    second_factor = SECOND * valid_block
    final_local, second_local = local_targets(next_block), local_targets(second_block)
    final_t = final_all.swapaxes(1, 2)
    final_stats = head_stats(live, table_low, final_t, final_local[None])
    final_stats, second_all = lax.optimization_barrier((final_stats, second_all))
    second_t = second_all.swapaxes(1, 2)
    second_stats = head_stats(live, table_low, second_t, second_local[None])
    stats = merge_stats(jnp.concatenate([final_stats, second_stats], 1))
    half_rows = final_stats.shape[1]
    final_stats, second_stats = stats[:, :half_rows], stats[:, half_rows:]

    pending = Pending()
    results = {}

    def rows_task(name, d_rows):
        parts = d_rows.reshape((n_seq, n_fsdp) + d_rows.shape[1:])
        moved = yield 0, send_parts(parts, shift_seq, seq_at, sent=jnp.bfloat16)
        mine = add_parts(parts, moved, seq_at)
        results[name] = yield from scatter_fsdp(mine, fsdp_at)

    def line_of(stats, factor, local):
        return jnp.stack([stats[0], factor / total_tokens, local.astype(jnp.float32)])

    final_line = line_of(final_stats, valid_block, final_local)
    table_grad, d_rows = head_back(live, table_low, table_t, final_all, final_t, final_line)
    pending.add(rows_task("final", d_rows))
    second_line = line_of(second_stats, second_factor, second_local)
    cuts = 2 if own_rows % 256 == 0 else 1
    for cut in range(cuts):
        line = second_line.reshape(3, n_group, cuts, -1)[:, :, cut].reshape(3, -1)
        table_grad, d_rows = head_back(
            live, table_low, table_t, second_all, second_t, line, cut, table_grad
        )
        table_grad = pending.point(table_grad)
        pending.add(rows_task(("second", cut), d_rows))
    pending.finish()
    d_final = results["final"].T
    d_second = jnp.concatenate([results["second", cut] for cut in range(cuts)], 1).T
    loss_rows = (final_stats[0] - final_stats[1]) * valid_block + (
        second_stats[0] - second_stats[1]
    ) * second_factor
    loss_part = jnp.sum(
        lax.dynamic_slice_in_dim(loss_rows, group_at * own_rows, own_rows, 0)
    )

    def table_task():
        parts = table_grad.reshape(2, part_rows, feature_width)
        (away,) = yield 0, [swap_core(pick(parts, 1 - core_at, 0))]
        mine = (pick(parts, core_at, 0) + away).astype(jnp.bfloat16)
        totals = []
        quarter = part_rows // 4
        for low, wait in ((0, 2), (2 * quarter, 3)):
            pieces = [mine[low : low + quarter], mine[low + quarter : low + 2 * quarter]]
            moved = yield wait, [
                [shift_y(piece, step) for step in range(1, n_y)] for piece in pieces
            ]
            for piece, away in zip(pieces, moved):
                ordered = order_parts([piece] + away, y_at).astype(jnp.float32)
                total = ordered[0]
                for step in range(1, n_y):
                    total = total + ordered[step]
                totals.append(total)
            if not low:
                yield 0, []
        results["table"] = jnp.concatenate(totals, 0)

    def bundle_task(pairs, matrices, names, waits):
        (away,) = yield 0, [swap_pairs(pairs, core_at)]
        grads = shared_outer(pairs, away, core_at)
        parts = []
        for grad in grads:
            cut = grad.reshape(n_seq, n_fsdp, -1, rows_group, grad.shape[1])
            parts += [cut[:, :, at] for at in range(cut.shape[2])]
        stacked = jnp.concatenate(parts, -1)
        moved = yield waits[0], send_parts(stacked, shift_seq, seq_at, sent=jnp.bfloat16)
        mine = add_parts(stacked, moved, seq_at)
        mine = mine.reshape(n_fsdp, n_y, rows_group // n_y, -1)
        moved = yield waits[1], send_parts(mine, shift_y, y_at, 1, jnp.bfloat16)
        mine = add_parts(mine, moved, y_at, 1)
        mine = yield from scatter_fsdp(mine, fsdp_at)
        moved = yield 0, [shift_y(mine, step) for step in range(1, n_y)]
        column = order_parts([mine] + moved, y_at).reshape(rows_group, -1)
        (away,) = yield 0, [swap_core(column)]
        both = order_parts([column, away], core_at)
        at = 0
        for matrix, name in zip(matrices, names):
            width = matrix.shape[-1] // 2
            cuts = []
            for _ in range(matrix.shape[-2] // rows_group):
                cuts.append(
                    jnp.concatenate([both[0, :, at : at + width], both[1, :, at : at + width]], 1)
                )
                at += width
            results[name] = jnp.concatenate(cuts, 0)

    pending.add(table_task())
    d_second = pending.point(d_second)
    d_second_low = d_second.astype(jnp.bfloat16)
    d_stream, d_gain_final, d_bias_final = final_back(d_final + inner(d_second_low, head_weight))

    vec_list = [None] * layer_count
    for layer_at in reversed(range(layer_count)):

        def first_task(pairs, at=layer_at):
            matrices, names = [mlp_in[at], mlp_out[at]], [("fc", at), ("down", at)]
            if at == layer_count - 1:
                pairs = [(final_low, d_second_low)] + pairs
                matrices = [attn_out[layer_count]] + matrices
                names = [("out", layer_count)] + names
            return bundle_task(pairs, matrices, names, (1, 3) if at else (2, 0))

        def later_task(pairs, at=layer_at):
            names = [("in", at), ("out", at)]
            return bundle_task(pairs, [attn_in[at], attn_out[at]], names, (1, 1))

        d_stream, vec_list[layer_at] = layer_backward(
            d_stream,
            kept[layer_at],
            stored[layer_at],
            vectors[12 * layer_at : 12 * layer_at + 12],
            allowed,
            head_count,
            pending,
            first_task,
            later_task,
        )
    embed_back = lax.all_gather(
        d_stream.astype(jnp.bfloat16), ("seq", "fsdp", "ctx"), axis=0, tiled=True
    )

    def device_order(grid):
        cut = grid.reshape(n_group, seqs_dev, n_ctx, ctx_span)
        return cut.transpose(0, 2, 1, 3).reshape(-1)

    pending.finish()
    table_part = results["table"]
    summed = (
        None,
        jnp.stack([results["in", at] for at in range(layer_count)]),
        jnp.stack([results["out", at] for at in range(layer_count + 1)]),
        jnp.stack([results["fc", at] for at in range(layer_count)]),
        jnp.stack([results["down", at] for at in range(layer_count)]),
    )
    vector_grad = jnp.concatenate(vec_list + [jnp.stack([d_gain_final, d_bias_final])], 0)
    matrices = (table[None], attn_in, attn_out, mlp_in, mlp_out)
    row_states = (attn_in_rows, attn_out_rows, mlp_in_rows, mlp_out_rows)
    col_states = (table_cols[None], attn_in_cols, attn_out_cols, mlp_in_cols, mlp_out_cols)

    col_parts = []
    weighted_parts = []
    row_parts = []
    rows_new = []
    for grad_sum, row_state in zip(summed[1:], row_states):
        square = grad_sum * grad_sum
        renewed = DECAY * row_state + (1.0 - DECAY) * jnp.mean(square + EPS_SQUARE, -1)
        rows_new.append(renewed)
        col_parts.append(share * jnp.sum(square + EPS_SQUARE, -2))
        weighted_parts.append(share * jnp.sum(square / renewed[..., None], -2))
        row_parts.append(share * jnp.sum(renewed, -1))
    early_parts = (
        [vector_grad]
        + col_parts
        + weighted_parts
        + row_parts
        + square_parts
        + [loss_part.reshape(1), jnp.stack(squares)]
    )
    early = jnp.concatenate([part.reshape(-1) for part in early_parts])
    early_count = early.shape[0]
    early = jnp.pad(early, (0, -early_count % 1024)).reshape(-1, 128)
    early = sum_all(early).reshape(-1)
    embed_back, early = lax.optimization_barrier((embed_back, early))
    part_ids = jnp.arange(part_rows, dtype=jnp.int32)
    part_live = part_ids < rows_dev - core_at * part_rows
    part_ids = jnp.where(part_live, row_low + core_at * part_rows + part_ids, -1)
    hits = (part_ids[:, None] == device_order(tokens)[None]) | (
        part_ids[:, None] == device_order(positions)[None] + VOCAB
    )
    table_part = table_part + product(hits.astype(jnp.bfloat16), embed_back)
    table_away = swap_core(table_part)

    def join_core(mine, away):
        first = jnp.where(core_at == 0, mine, away)
        second = jnp.where(core_at == 0, away, mine)
        return jnp.concatenate([first, second[: rows_dev - part_rows]], 0)

    table_sum = join_core(table_part, table_away)

    state_part = lax.dynamic_slice_in_dim(
        jnp.pad(table_rows, (0, spare)), core_at * part_rows, part_rows, 0
    )
    part_square = table_part * table_part
    part_renewed = DECAY * state_part + (1.0 - DECAY) * jnp.mean(part_square + EPS_SQUARE, -1)
    part_renewed = jnp.where(part_live, part_renewed, 1.0)
    live_count = jnp.sum(part_live.astype(jnp.float32))
    table_rows_new = join_core(part_renewed, swap_core(part_renewed))
    rows_new = [table_rows_new[None]] + rows_new
    grad_sums = (table_sum[None],) + summed[1:]
    late = jnp.concatenate(
        [
            jnp.sum(part_square, 0) + EPS_SQUARE * live_count,
            jnp.sum(part_square / part_renewed[:, None], 0),
            jnp.sum(jnp.where(part_live, part_renewed, 0.0)).reshape(1),
            jnp.zeros(-(2 * feature_width + 1) % 1024, jnp.float32),
        ]
    )
    late, early = lax.optimization_barrier((late, early))
    late = sum_all(late.reshape(8, -1), skip_y=True).reshape(-1)
    early_at = 0
    early_sums = []
    for part in early_parts:
        early_sums.append(early[early_at : early_at + part.size].reshape(part.shape))
        early_at += part.size
    vector_sum = early_sums[0]
    col_sums = [late[None, :feature_width]] + early_sums[1:5]
    weighted_sums = [late[None, feature_width : 2 * feature_width]] + early_sums[5:9]
    row_sums = [late[2 * feature_width : 2 * feature_width + 1]] + early_sums[9:13]
    square_sums = early_sums[13:18]
    loss_sum = early_sums[18][0]
    square_total = early_sums[19].reshape(-1)
    cols_new = []
    new_weights = []
    sizes_rms = []
    for matrix_at in range(5):
        grad_sum, renewed, col_state = (
            grad_sums[matrix_at],
            rows_new[matrix_at],
            col_states[matrix_at],
        )
        stack_count, row_local, col_count = grad_sum.shape
        row_total = row_local * n_group
        weighted = weighted_sums[matrix_at]
        renewed_cols = DECAY * col_state + (1.0 - DECAY) * col_sums[matrix_at] / row_total
        row_mean = row_sums[matrix_at] / row_total
        clip_total = jnp.sum(row_mean * jnp.sum(weighted / renewed_cols, -1))
        entries = grad_sum.size * n_group
        update_rms = jnp.sqrt(clip_total / entries)
        weight_rms = jnp.sqrt(square_sums[matrix_at][0] / entries)
        step_scale = RATE * jnp.maximum(EPS_SCALE, weight_rms) / jnp.maximum(1.0, update_rms / CLIP)
        second_moment = renewed[:, :, None] * renewed_cols[:, None, :] / row_mean[:, None, None]
        update = grad_sum * lax.rsqrt(second_moment)
        new_weights.append(matrices[matrix_at] - step_scale * update)
        cols_new.append(renewed_cols)
        sizes_rms.append(update_rms)
    vector_state_new = DECAY * vector_state + (1.0 - DECAY) * (vector_sum * vector_sum + EPS_SQUARE)
    vector_update = vector_sum * lax.rsqrt(vector_state_new)
    vector_rms = jnp.sqrt(jnp.mean(vector_update * vector_update))
    vector_scale = (
        RATE
        * jnp.maximum(EPS_SCALE, jnp.sqrt(jnp.mean(vectors * vectors)))
        / jnp.maximum(1.0, vector_rms / CLIP)
    )
    vectors_new = vectors - vector_scale * vector_update
    sizes_rms.append(vector_rms)
    norms = jnp.concatenate([jnp.sqrt(square_total / total_tokens), jnp.stack(sizes_rms)])
    table_new = new_weights[0][0]
    return (
        loss_sum,
        norms,
        table_sum,
        rows_new[0][0],
        cols_new[0][0],
        table_new,
        table_new.astype(jnp.bfloat16),
        summed[1],
        rows_new[1],
        cols_new[1],
        new_weights[1],
        new_weights[1].astype(jnp.bfloat16),
        summed[2],
        rows_new[2],
        cols_new[2],
        new_weights[2],
        new_weights[2].astype(jnp.bfloat16),
        summed[3],
        rows_new[3],
        cols_new[3],
        new_weights[3],
        new_weights[3].astype(jnp.bfloat16),
        summed[4],
        rows_new[4],
        cols_new[4],
        new_weights[4],
        new_weights[4].astype(jnp.bfloat16),
        vector_sum,
        vector_state_new,
        vectors_new,
    )


def solution(mesh):
    return jax.shard_map(
        body,
        mesh=mesh,
        in_specs=(
            P(),
            P(),
            P(),
            P(),
            P(("seq", "fsdp"), None),
            P(None, ("seq", "fsdp"), None),
            P(None, ("seq", "fsdp"), None),
            P(None, ("seq", "fsdp"), None),
            P(None, ("seq", "fsdp"), None),
            P(),
            P(("seq", "fsdp")),
            P(),
            P(None, ("seq", "fsdp")),
            P(),
            P(None, ("seq", "fsdp")),
            P(),
            P(None, ("seq", "fsdp")),
            P(),
            P(None, ("seq", "fsdp")),
            P(),
            P(),
        ),
        out_specs=(
            P(),
            P(),
            P(("seq", "fsdp"), None),
            P(("seq", "fsdp")),
            P(),
            P(("seq", "fsdp"), None),
            P(("seq", "fsdp"), None),
            P(None, ("seq", "fsdp"), None),
            P(None, ("seq", "fsdp")),
            P(),
            P(None, ("seq", "fsdp"), None),
            P(None, ("seq", "fsdp"), None),
            P(None, ("seq", "fsdp"), None),
            P(None, ("seq", "fsdp")),
            P(),
            P(None, ("seq", "fsdp"), None),
            P(None, ("seq", "fsdp"), None),
            P(None, ("seq", "fsdp"), None),
            P(None, ("seq", "fsdp")),
            P(),
            P(None, ("seq", "fsdp"), None),
            P(None, ("seq", "fsdp"), None),
            P(None, ("seq", "fsdp"), None),
            P(None, ("seq", "fsdp")),
            P(),
            P(None, ("seq", "fsdp"), None),
            P(None, ("seq", "fsdp"), None),
            P(),
            P(),
            P(),
        ),
        check_vma=False,
    )
```

```python
import functools

import jax
import jax.numpy as jnp
from jax import lax
from jax.experimental import pallas as pl
from jax.experimental.pallas import tpu as pltpu
from jax.sharding import PartitionSpec as P

HEADS = 12
VOCAB = 50304


EPS_NORM = 1e-05
EPS_SQUARE = 1e-30
EPS_SCALE = 0.001
DECAY = 0.5
CLIP = 0.4
RATE = 0.6
SECOND = 0.3
MASKED = -1e30
VMEM_BYTES = 56 * 1024 * 1024
NEAR_FIRST = [(0, 1), (1, 0), (2, 3), (3, 2)]
NEAR_SECOND = [(0, 3), (3, 0), (1, 2), (2, 1)]


def layer_norm(stream, gain, offset):
    center = stream - jnp.mean(stream, -1, keepdims=True)
    spread = jnp.mean(center * center, -1, keepdims=True)
    return center * lax.rsqrt(spread + EPS_NORM) * gain + offset


def gelu_tanh(value):
    return jax.nn.gelu(value, approximate=True)


def positions_of(segments):
    steps_at = jnp.arange(segments.shape[-1], dtype=jnp.int32)
    before = jnp.concatenate(
        [jnp.full(segments.shape[:-1] + (1,), -2, jnp.int32), segments[..., :-1]], -1
    )
    starts = jnp.where(segments != before, steps_at, 0)
    first = lax.cummax(starts, axis=segments.ndim - 1)
    return jnp.where(segments >= 0, steps_at - first, 0)


def product(left, right):
    return jnp.dot(left, right, preferred_element_type=jnp.float32)


def inner(left, right):
    return lax.dot_general(
        left, right, (((1,), (1,)), ((), ())), preferred_element_type=jnp.float32
    )


def outer(left, right):
    return lax.dot_general(
        left, right, (((0,), (0,)), ((), ())), preferred_element_type=jnp.float32
    )


def shift(block, axis, step):
    count = lax.axis_size(axis)
    return lax.ppermute(block, axis, [(i, (i + step) % count) for i in range(count)])


def shift_y(block, step):
    count = lax.axis_size("ctx")
    return lax.ppermute(block, "ctx", [(i, (i + 2 * step) % count) for i in range(count)])


def swap_core(block):
    count = lax.axis_size("ctx")
    return lax.ppermute(block, "ctx", [(i, i ^ 1) for i in range(count)])


def shift_seq(block, step):
    return shift(block, "seq", step)


def shift_fsdp(block, step):
    return shift(block, "fsdp", step)


def pick(parts, at, axis):
    return lax.dynamic_index_in_dim(parts, at, axis, False)


def send_parts(parts, mover, at, axis=0, sent=None):
    count = parts.shape[axis]
    moving = []
    for step in range(1, count):
        piece = pick(parts, lax.rem(at + step, count), axis)
        moving.append(mover(piece if sent is None else piece.astype(sent), step))
    return moving


def add_parts(parts, moved, at, axis=0):
    total = pick(parts, at, axis)
    for piece in moved:
        total = total + piece.astype(total.dtype)
    return total


def scatter_sum(parts, mover, at, axis=0, sent=None):
    return add_parts(parts, send_parts(parts, mover, at, axis, sent), at, axis)


def scatter_fsdp(parts, at):
    count = parts.shape[0]
    if count != 4:
        moved = yield 0, send_parts(parts, shift_fsdp, at, sent=jnp.bfloat16)
        return add_parts(parts, moved, at)
    outside = (at == 0) | (at == 3)
    mine = [jnp.where(outside, 0, 1), jnp.where(outside, 3, 2)]
    other = [jnp.where(outside, 1, 0), jnp.where(outside, 2, 3)]
    away = jnp.stack([pick(parts, slot, 0) for slot in other]).astype(jnp.bfloat16)
    (away,) = yield 0, [lax.ppermute(away, "fsdp", NEAR_FIRST)]
    first, second = (
        pick(parts, slot, 0) + away[k].astype(parts.dtype) for k, slot in enumerate(mine)
    )
    away = jnp.where(at < 2, second, first).astype(jnp.bfloat16)
    (away,) = yield 0, [lax.ppermute(away, "fsdp", NEAR_SECOND)]
    return jnp.where(at < 2, first, second) + away.astype(parts.dtype)


def run(task):
    moving = next(task)[1]
    while True:
        try:
            moving = task.send(moving)[1]
        except StopIteration as stop:
            return stop.value


def sum_all(block, skip_y=False):
    for axis in ("ctx", "seq", "fsdp"):
        count = 2 if skip_y and axis == "ctx" else lax.axis_size(axis)
        whole = lax.axis_size(axis)
        hop = 1
        while hop < count:
            block = block + lax.ppermute(block, axis, [(i, i ^ hop) for i in range(whole)])
            hop *= 2
    return block


def order_parts(parts, at):
    count = len(parts)
    if count == 2:
        first, second = parts
        return jnp.stack([jnp.where(at == 0, first, second), jnp.where(at == 0, second, first)])
    order = lax.rem(at - jnp.arange(count, dtype=jnp.int32) + count, count)
    return jnp.take(jnp.stack(parts), order, axis=0, mode="clip")


def gather_near(block):
    n_y = lax.axis_size("ctx") // 2
    column = jnp.concatenate([block] + [shift_y(block, step) for step in range(1, n_y)], 0)
    return jnp.concatenate([column, swap_core(column)], 0)


def scatter_near(parts):
    n_y = lax.axis_size("ctx") // 2
    parts = parts.reshape((2, n_y, -1) + parts.shape[1:])
    column = parts[0] + swap_core(parts[1])
    total = column[0]
    for step in range(1, n_y):
        away = shift_y(column[step].astype(jnp.bfloat16), n_y - step)
        total = total + away.astype(total.dtype)
    return total


def half_of(block, at):
    width = block.shape[-1] // 2
    return jnp.where(at == 0, block[..., :width], block[..., width:])


def qkv_bias(vec):
    return jnp.concatenate([vec[2], jnp.zeros_like(vec[2]), vec[3]])


def attention_scores(query_low, keys, allowed, head_count):
    row_count, feature_width = query_low.shape
    head_size = feature_width // head_count
    scores = jnp.einsum(
        "qhd,khd->hqk",
        query_low.reshape(row_count, head_count, head_size),
        keys.reshape(-1, head_count, head_size),
        preferred_element_type=jnp.float32,
    ) * head_size ** (-0.5)
    return jnp.where(allowed[None], scores, MASKED)


def mix_values(probs_low, values, head_count):
    head_size = values.shape[1] // head_count
    mixed = jnp.einsum(
        "hqk,khd->qhd",
        probs_low,
        values.reshape(-1, head_count, head_size),
        preferred_element_type=jnp.float32,
    )
    return mixed.reshape(mixed.shape[0], -1)


def layer_forward(stream, weights, vec, allowed, head_count):
    w_in, w_out, w_fc, w_down = weights
    feature_width = stream.shape[1]
    a_low = layer_norm(stream, vec[0], vec[1]).astype(jnp.bfloat16)
    qkv_low = (product(a_low, w_in) + qkv_bias(vec)).astype(jnp.bfloat16)
    pairs = gather_near(qkv_low[:, feature_width:])
    keys, values = pairs[:, :feature_width], pairs[:, feature_width:]
    scores = attention_scores(qkv_low[:, :feature_width], keys, allowed, head_count)
    row_max = jnp.max(scores, -1)
    log_total = row_max + jnp.log(jnp.sum(jnp.exp(scores - row_max[..., None]), -1))
    probs = jnp.exp(scores - log_total[..., None])
    mixed_low = mix_values(probs.astype(jnp.bfloat16), values, head_count).astype(jnp.bfloat16)
    branch = product(mixed_low, w_out) + vec[4]
    middle = stream + branch
    m_low = layer_norm(middle, vec[5], vec[6]).astype(jnp.bfloat16)
    hidden = product(m_low, w_fc) + vec[8:12].reshape(-1)
    output = product(gelu_tanh(hidden).astype(jnp.bfloat16), w_down) + vec[7]
    sums = jnp.stack([jnp.sum(stream * stream), jnp.sum(branch * branch), jnp.sum(output * output)])
    kept = (stream, a_low, qkv_low, keys, values, log_total, mixed_low, middle, m_low, hidden)
    return (middle + output, kept, sums)


def swap_pairs(pairs, core_at):
    lefts = [left for left, _ in pairs]
    return swap_core(
        jnp.concatenate(lefts + [half_of(right, 1 - core_at) for _, right in pairs], 1)
    )


def shared_outer(pairs, away, core_at):
    at = 0
    whole_left = []
    for left, _ in pairs:
        whole_left.append(jnp.concatenate([left, away[:, at : at + left.shape[1]]], 0))
        at += left.shape[1]
    grads = []
    for left, (_, right) in zip(whole_left, pairs):
        width = right.shape[1] // 2
        whole_right = jnp.concatenate([half_of(right, core_at), away[:, at : at + width]], 0)
        at += width
        grads.append(outer(left, whole_right))
    return grads


def layer_backward(d_stream, kept, weights, vec, allowed, head_count, pending, first_task, later_task):
    stream, a_low, qkv_low, keys, values, log_total, mixed_low, middle, m_low, hidden = kept
    w_in, w_out, w_fc, w_down = weights
    row_count, feature_width = stream.shape
    head_size = feature_width // head_count
    scale = head_size ** (-0.5)
    norm_back_one = jax.vjp(layer_norm, stream, vec[0], vec[1])[1]
    query_low = qkv_low[:, :feature_width]
    probs = jnp.exp(attention_scores(query_low, keys, allowed, head_count) - log_total[..., None])
    probs_low = probs.astype(jnp.bfloat16)
    norm_back_two = jax.vjp(layer_norm, middle, vec[5], vec[6])[1]
    gelu_out, gelu_back = jax.vjp(gelu_tanh, hidden)
    u_low = gelu_out.astype(jnp.bfloat16)
    d_out_low = d_stream.astype(jnp.bfloat16)
    d_hidden_low = gelu_back(inner(d_out_low, w_down))[0].astype(jnp.bfloat16)
    d_hidden_low = pending.point(d_hidden_low)
    pending.add(first_task([(m_low, d_hidden_low), (u_low, d_out_low)]))
    d_m = inner(d_hidden_low, w_fc)
    d_two, d_gain_two, d_bias_two = norm_back_two(d_m)
    d_middle = d_stream + d_two
    d_middle = pending.point(d_middle)
    d_middle_low = d_middle.astype(jnp.bfloat16)
    d_heads = (
        inner(d_middle_low, w_out).astype(jnp.bfloat16).reshape(row_count, head_count, head_size)
    )
    value_heads = values.reshape(-1, head_count, head_size)
    d_probs = jnp.einsum("qhd,khd->hqk", d_heads, value_heads, preferred_element_type=jnp.float32)
    d_scores = (probs * (d_probs - jnp.sum(probs * d_probs, -1, keepdims=True))).astype(
        jnp.bfloat16
    )
    d_scores = pending.point(d_scores)
    d_query = (
        jnp.einsum(
            "hqk,khd->qhd",
            d_scores,
            keys.reshape(-1, head_count, head_size),
            preferred_element_type=jnp.float32,
        ).reshape(row_count, feature_width)
        * scale
    )
    d_keys = (
        jnp.einsum(
            "hqk,qhd->khd",
            d_scores,
            query_low.reshape(row_count, head_count, head_size),
            preferred_element_type=jnp.float32,
        ).reshape(-1, feature_width)
        * scale
    )
    d_values = jnp.einsum(
        "hqk,qhd->khd", probs_low, d_heads, preferred_element_type=jnp.float32
    ).reshape(-1, feature_width)
    d_pairs = scatter_near(jnp.concatenate([d_keys, d_values], 1))
    d_qkv_low = jnp.concatenate([d_query, d_pairs], 1).astype(jnp.bfloat16)
    d_qkv_low = pending.point(d_qkv_low)
    pending.add(later_task([(a_low, d_qkv_low), (mixed_low, d_middle_low)]))
    d_one, d_gain_one, d_bias_one = norm_back_one(inner(d_qkv_low, w_in))
    d_qkv = d_qkv_low.astype(jnp.float32)
    rows_head = jnp.stack(
        [
            d_gain_one,
            d_bias_one,
            jnp.sum(d_qkv[:, :feature_width], 0),
            jnp.sum(d_qkv[:, 2 * feature_width :], 0),
            jnp.sum(d_middle_low.astype(jnp.float32), 0),
            d_gain_two,
            d_bias_two,
            jnp.sum(d_out_low.astype(jnp.float32), 0),
        ]
    )
    vec_grad = jnp.concatenate(
        [rows_head, jnp.sum(d_hidden_low.astype(jnp.float32), 0).reshape(4, feature_width)], 0
    )
    return (pending.point(d_middle + d_one), vec_grad)


def merge_stats(stats):
    for mover, axis in ((shift_seq, "seq"), (shift_fsdp, "fsdp")):
        parts = [stats] + [mover(stats, step) for step in range(1, lax.axis_size(axis))]
        top = parts[0][0]
        for part in parts[1:]:
            top = jnp.maximum(top, part[0])
        total = jnp.exp(parts[0][0] - top)
        picked = parts[0][1]
        for part in parts[1:]:
            total = total + jnp.exp(part[0] - top)
            picked = picked + part[1]
        stats = jnp.stack([top + jnp.log(total), picked])
    return stats


def blocks_of(groups, width, row_block):
    step = max(1, row_block // width)
    return [
        (range(low, low + step), slice(low * width, (low + step) * width))
        for low in range(0, groups, step)
    ]


def side_by_side(ref, at_block):
    return jnp.concatenate([ref[at] for at in at_block], 1)


def masked_logits(logits, live, first):
    column = lax.broadcasted_iota(jnp.int32, logits.shape, 0) + first
    return jnp.where(column < live, logits, MASKED)


def stats_kernel(row_block, live_ref, table_ref, rows_ref, target_ref, out_ref, top_ref, sum_ref, pick_ref):
    at = pl.program_id(0)
    tile = table_ref.shape[0]
    first = at * tile
    live = live_ref[0]

    @pl.when(at == 0)
    def _():
        top_ref[...] = jnp.full_like(top_ref, MASKED)
        sum_ref[...] = jnp.zeros_like(sum_ref)
        pick_ref[...] = jnp.zeros_like(pick_ref)

    def step(masked):
        for at_block, here in blocks_of(rows_ref.shape[0], rows_ref.shape[2], row_block):
            logits = jnp.dot(
                table_ref[...], side_by_side(rows_ref, at_block), preferred_element_type=jnp.float32
            )
            if masked:
                logits = masked_logits(logits, live, first)
            column = lax.broadcasted_iota(jnp.int32, logits.shape, 0)
            hit = column == target_ref[:, here] - first
            cut = logits.reshape(tile // 8, 8, logits.shape[1])
            top = top_ref[:, here]
            joint = jnp.maximum(top, jnp.max(cut, 0))
            total = jnp.sum(jnp.exp(cut - joint[None]), 0)
            sum_ref[:, here] = sum_ref[:, here] * jnp.exp(top - joint) + total
            top_ref[:, here] = joint
            pick_ref[:, here] += jnp.sum(
                jnp.where(hit, logits, 0.0).reshape(cut.shape), 0
            )

    @pl.when(first + tile <= live)
    def _():
        step(False)

    @pl.when((first + tile > live) & (first < live))
    def _():
        step(True)

    @pl.when(at == pl.num_programs(0) - 1)
    def _():
        top = top_ref[...]
        joint = jnp.max(top, 0, keepdims=True)
        total = jnp.sum(sum_ref[...] * jnp.exp(top - joint), 0, keepdims=True)
        out_ref[0:1, :] = joint + jnp.log(total)
        out_ref[1:2, :] = jnp.sum(pick_ref[...], 0, keepdims=True)


def head_stats(live, table_low, rows_t, target, tile=512, row_block=512):
    groups, depth, width = rows_t.shape
    count = groups * width
    height = table_low.shape[0]
    return pl.pallas_call(
        functools.partial(stats_kernel, row_block),
        out_shape=jax.ShapeDtypeStruct((2, count), jnp.float32),
        grid=(height // tile,),
        in_specs=[
            pl.BlockSpec(memory_space=pltpu.SMEM),
            pl.BlockSpec((tile, depth), lambda i: (i, 0)),
            pl.BlockSpec((groups, depth, width), lambda i: (0, 0, 0)),
            pl.BlockSpec((1, count), lambda i: (0, 0)),
        ],
        out_specs=pl.BlockSpec((2, count), lambda i: (0, 0)),
        scratch_shapes=[pltpu.VMEM((8, count), jnp.float32)] * 3,
        compiler_params=pltpu.CompilerParams(vmem_limit_bytes=VMEM_BYTES),
        cost_estimate=pl.CostEstimate(
            flops=2 * height * depth * count,
            bytes_accessed=2 * height * depth + 2 * depth * count,
            transcendentals=height * count,
        ),
    )(live, table_low, rows_t, target)


def back_kernel(row_block, added, live_ref, table_ref, table_t_ref, rows_ref, rows_t_ref, line_ref, *refs):
    if added:
        prior_ref, grad_ref, d_rows_ref = refs
    else:
        grad_ref, d_rows_ref = refs
    at = pl.program_id(0)
    tile = table_ref.shape[0]
    first = at * tile
    live = live_ref[0]
    width = d_rows_ref.shape[2]

    @pl.when(at == 0)
    def _():
        d_rows_ref[...] = jnp.zeros_like(d_rows_ref)

    def step(masked):
        grad = prior_ref[...] if added else None
        for at_block, here in blocks_of(rows_t_ref.shape[0], width, row_block):
            logits = jnp.dot(
                table_ref[...],
                side_by_side(rows_t_ref, at_block),
                preferred_element_type=jnp.float32,
            )
            if masked:
                logits = masked_logits(logits, live, first)
            column = lax.broadcasted_iota(jnp.int32, logits.shape, 0).astype(jnp.float32)
            probs = jnp.exp(logits - line_ref[0:1, here])
            hit = column == line_ref[2:3, here] - first.astype(jnp.float32)
            d_low = (line_ref[1:2, here] * jnp.where(hit, probs - 1.0, probs)).astype(jnp.bfloat16)
            rows = rows_ref[at_block.start : at_block.stop].reshape(-1, rows_ref.shape[2])
            part = jnp.dot(d_low, rows, preferred_element_type=jnp.float32)
            grad = part if grad is None else grad + part
            d_part = jnp.dot(table_t_ref[...], d_low, preferred_element_type=jnp.float32)
            for at_width, at_group in enumerate(at_block):
                d_rows_ref[at_group] += d_part[:, at_width * width : (at_width + 1) * width]
        grad_ref[...] = grad

    @pl.when(first + tile <= live)
    def _():
        step(False)

    @pl.when((first + tile > live) & (first < live))
    def _():
        step(True)

    @pl.when(first >= live)
    def _():
        grad_ref[...] = prior_ref[...] if added else jnp.zeros_like(grad_ref)


def head_back(live, table_low, table_t, rows, rows_t, line, cut=0, prior=None, tile=512):
    groups, _, depth = rows.shape
    height = table_low.shape[0]
    count = line.shape[1]
    width = count // groups
    once = dict(pipeline_mode=pl.Buffered(1))
    grad_spec = pl.BlockSpec((tile, depth), lambda i: (i, 0))
    added = prior is not None
    return pl.pallas_call(
        functools.partial(back_kernel, 1024, added),
        out_shape=(
            jax.ShapeDtypeStruct((height, depth), jnp.float32),
            jax.ShapeDtypeStruct((groups, depth, width), jnp.float32),
        ),
        grid=(height // tile,),
        in_specs=[
            pl.BlockSpec(memory_space=pltpu.SMEM),
            pl.BlockSpec((tile, depth), lambda i: (i, 0)),
            pl.BlockSpec((depth, tile), lambda i: (0, i)),
            pl.BlockSpec((groups, width, depth), lambda i: (0, cut, 0), **once),
            pl.BlockSpec((groups, depth, width), lambda i: (0, 0, cut), **once),
            pl.BlockSpec((3, count), lambda i: (0, 0), **once),
        ]
        + ([grad_spec] if added else []),
        out_specs=(
            grad_spec,
            pl.BlockSpec((groups, depth, width), lambda i: (0, 0, 0), **once),
        ),
        input_output_aliases={6: 0} if added else {},
        compiler_params=pltpu.CompilerParams(vmem_limit_bytes=VMEM_BYTES),
        cost_estimate=pl.CostEstimate(
            flops=6 * height * depth * count,
            bytes_accessed=4 * height * depth + 12 * depth * count + 8 * height * depth,
            transcendentals=height * count,
        ),
    )(live, table_low, table_t, rows, rows_t, line, *((prior,) if added else ()))


def prepare_kernel(row_count, table_ref, low_ref, turned_ref, square_ref):
    at = pl.program_id(0)
    tile = table_ref.shape[0]
    row = lax.broadcasted_iota(jnp.int32, table_ref.shape, 0) + at * tile
    block = jnp.where(row < row_count, table_ref[...], 0.0)
    low_ref[...] = block.astype(jnp.bfloat16)
    turned_ref[...] = block.T.astype(jnp.bfloat16)
    part = jnp.sum((block * block).reshape(tile // 8, 8, block.shape[1]), 0)

    @pl.when(at == 0)
    def _():
        square_ref[...] = part

    @pl.when(at > 0)
    def _():
        square_ref[...] += part


def prepare_table(table, height, tile=512):
    row_count, depth = table.shape
    return pl.pallas_call(
        functools.partial(prepare_kernel, row_count),
        out_shape=(
            jax.ShapeDtypeStruct((height, depth), jnp.bfloat16),
            jax.ShapeDtypeStruct((depth, height), jnp.bfloat16),
            jax.ShapeDtypeStruct((8, depth), jnp.float32),
        ),
        grid=(height // tile,),
        in_specs=[pl.BlockSpec((tile, depth), lambda i: (i, 0))],
        out_specs=(
            pl.BlockSpec((tile, depth), lambda i: (i, 0)),
            pl.BlockSpec((depth, tile), lambda i: (0, i)),
            pl.BlockSpec((8, depth), lambda i: (0, 0)),
        ),
        compiler_params=pltpu.CompilerParams(vmem_limit_bytes=VMEM_BYTES),
        cost_estimate=pl.CostEstimate(
            flops=2 * row_count * depth,
            bytes_accessed=4 * row_count * depth + 4 * height * depth,
            transcendentals=0,
        ),
    )(table)


class Pending:
    def __init__(self):
        self.active = []

    def add(self, task):
        held, moving = next(task)
        self.active.append([task, held, moving])

    def point(self, main):
        ready = [entry for entry in self.active if entry[1] == 0]
        main, moved = lax.optimization_barrier((main, [entry[2] for entry in ready]))
        for entry in self.active:
            entry[1] -= 1
        for entry, arrived in zip(ready, moved):
            self.advance(entry, arrived)
        return main

    def advance(self, entry, arrived):
        try:
            entry[1:] = entry[0].send(arrived)
        except StopIteration:
            self.active.remove(entry)

    def finish(self):
        while self.active:
            entry = self.active[0]
            self.advance(entry, entry[2])


def local_index(ids, row_low, row_count):
    shifted = ids - row_low
    inside = (shifted >= 0) & (shifted < row_count)
    return (inside, jnp.clip(shifted, 0, row_count - 1))


def body(
    tokens,
    segments,
    next_ids,
    second_ids,
    table,
    attn_in,
    attn_out,
    mlp_in,
    mlp_out,
    vectors,
    table_rows,
    table_cols,
    attn_in_rows,
    attn_in_cols,
    attn_out_rows,
    attn_out_cols,
    mlp_in_rows,
    mlp_in_cols,
    mlp_out_rows,
    mlp_out_cols,
    vector_state,
):
    n_ctx = lax.axis_size("ctx")
    n_seq = lax.axis_size("seq")
    n_fsdp = lax.axis_size("fsdp")
    n_y = n_ctx // 2
    n_group = n_seq * n_fsdp
    ctx_at = lax.axis_index("ctx")
    seq_at = lax.axis_index("seq")
    fsdp_at = lax.axis_index("fsdp")
    y_at = ctx_at // 2
    core_at = lax.rem(ctx_at, 2)
    group_at = seq_at * n_fsdp + fsdp_at
    all_seqs, length = segments.shape
    seqs_dev = all_seqs // n_group
    ctx_span = length // n_ctx
    feature_width = table.shape[1]
    layer_count = attn_in.shape[0]
    head_count = HEADS
    total_tokens = all_seqs * length
    own_rows = seqs_dev * ctx_span
    block_start = ctx_at * ctx_span
    positions = positions_of(segments)

    def block_of(grid):
        return lax.dynamic_slice_in_dim(grid, block_start, ctx_span, 1)

    tok_block = block_of(tokens).reshape(-1)
    valid_block = (block_of(segments) >= 0).astype(jnp.float32).reshape(-1)
    next_block = block_of(next_ids).reshape(-1)
    second_block = block_of(second_ids).reshape(-1)
    my_segments = lax.dynamic_slice_in_dim(segments, group_at * seqs_dev, seqs_dev, 0)
    my_positions = lax.dynamic_slice_in_dim(positions, group_at * seqs_dev, seqs_dev, 0)
    near = jnp.asarray(
        [(side, step) for side in range(2) for step in range(n_y)], jnp.int32
    )
    near_ctx = 2 * lax.rem(y_at - near[:, 1] + n_y, n_y) + lax.rem(core_at + near[:, 0], 2)

    def near_order(grid):
        cut = grid.reshape(seqs_dev, n_ctx, ctx_span).transpose(1, 0, 2)
        return jnp.take(cut, near_ctx, axis=0, mode="clip").reshape(-1)

    def own_order(grid):
        return block_of(grid).reshape(-1)

    time_grid = jnp.broadcast_to(jnp.arange(length, dtype=jnp.int32)[None], (seqs_dev, length))
    seq_grid = jnp.broadcast_to(jnp.arange(seqs_dev, dtype=jnp.int32)[:, None], (seqs_dev, length))
    q_seg, k_seg = (own_order(my_segments), near_order(my_segments))
    q_time, k_time = (own_order(time_grid), near_order(time_grid))
    q_seq, k_seq = (own_order(seq_grid), near_order(seq_grid))
    allowed = (q_seq[:, None] == k_seq[None]) & (
        (q_time[:, None] == k_time[None])
        | (k_time[None] < q_time[:, None]) & (q_seg[:, None] == k_seg[None]) & (k_seg[None] >= 0)
    )
    rows_dev = table.shape[0]
    row_low = group_at * rows_dev
    rows_group = attn_in.shape[1]
    rows_part = rows_group // n_ctx
    down_cut = mlp_out.shape[1] // rows_group

    in_width, out_width, fc_width = attn_in.shape[2], attn_out.shape[2], mlp_in.shape[2]
    pack_width = in_width + out_width + fc_width + down_cut * feature_width
    part_width = pack_width // n_ctx
    model_rows = n_group * rows_group

    def gather_pack(layer_at, after):
        down = mlp_out[layer_at].reshape(down_cut, rows_group, feature_width)
        pack = jnp.concatenate(
            [attn_in[layer_at], mlp_in[layer_at], attn_out[layer_at]]
            + [down[cut] for cut in range(down_cut)],
            1,
        ).astype(jnp.bfloat16)
        part = lax.dynamic_slice_in_dim(pack, ctx_at * part_width, part_width, 1)
        if layer_at == layer_count - 1:
            head = lax.dynamic_slice_in_dim(
                attn_out[layer_count].astype(jnp.bfloat16), ctx_at * rows_part, rows_part, 0
            )
            head = jnp.pad(head.reshape(-1), (0, -head.size % part_width)).reshape(-1, part_width)
            part = jnp.concatenate([part, head], 0)
        if after is not None:
            part, after = lax.optimization_barrier((part, after))
        whole = lax.all_gather(part, ("ctx", "seq", "fsdp"), axis=0)
        return whole, whole[0, 0, :128]

    def cut_pack(layer_at, whole):
        whole = whole.reshape(n_ctx, n_group, -1, part_width)
        body_rows = whole[:, :, :rows_group].reshape(n_ctx, model_rows, part_width)

        def columns_of(low, high):
            pieces = []
            for at in range(n_ctx):
                start, stop = max(low, at * part_width), min(high, (at + 1) * part_width)
                if start < stop:
                    pieces.append(body_rows[at, :, start - at * part_width : stop - at * part_width])
            return pieces[0] if len(pieces) == 1 else jnp.concatenate(pieces, 1)

        at = in_width + fc_width
        down = jnp.stack(
            [
                columns_of(low, low + feature_width).reshape(n_group, rows_group, feature_width)
                for low in range(at + out_width, pack_width, feature_width)
            ],
            1,
        )
        weights = (
            columns_of(0, in_width),
            columns_of(at, at + out_width),
            columns_of(in_width, at),
            down.reshape(-1, feature_width),
        )
        head = None
        if layer_at == layer_count - 1:
            head = whole[:, :, rows_group:].reshape(n_ctx, n_group, -1)
            head = head[:, :, : rows_part * out_width].reshape(n_ctx, n_group, rows_part, out_width)
            head = head.transpose(1, 0, 2, 3).reshape(model_rows, out_width)
        return weights, head

    whole, after = gather_pack(0, None)
    stored = [whole]

    tok_inside, tok_safe = local_index(tok_block, row_low, rows_dev)
    embed_term = jnp.where(
        tok_inside[:, None], jnp.take(table, tok_safe, axis=0, mode="clip"), 0.0
    ).astype(jnp.bfloat16)
    embed_term = embed_term.reshape(n_seq, n_fsdp, own_rows, feature_width)
    place_part = length // n_ctx
    place_low = VOCAB - rows_dev * (n_group - 1)
    places = lax.dynamic_slice_in_dim(table, place_low + ctx_at * place_part, place_part, 0)
    places = jnp.where(group_at == n_group - 1, places, 0.0).astype(jnp.bfloat16)
    part_rows = -(-rows_dev // 512) * 256
    spare = part_rows * 2 - rows_dev
    table_low, table_t, table_square = prepare_table(table, 2 * part_rows)
    if (n_seq, n_fsdp) == (2, 4):
        flat = (-1, feature_width)
        sent = pick(embed_term, 1 - seq_at, 0).reshape(flat)
        away = shift_seq(jnp.concatenate([sent, places], 0), 1)
        away, table_low, table_t, table_square = lax.optimization_barrier(
            (away, table_low, table_t, table_square)
        )
        mine = pick(embed_term, seq_at, 0) + away[:-place_part].reshape(embed_term.shape[1:])
        places = places + away[-place_part:]
        outside = (fsdp_at == 0) | (fsdp_at == 3)
        pair = jnp.where(outside, mine[1:3], jnp.stack([mine[0], mine[3]]))
        sent = jnp.concatenate([pair.reshape(flat), places], 0)
        away = lax.ppermute(sent, "fsdp", NEAR_FIRST)
        kept_pair = jnp.where(outside, jnp.stack([mine[0], mine[3]]), mine[1:3])
        kept_pair = kept_pair + away[:-place_part].reshape(kept_pair.shape)
        places = places + away[-place_part:]
        sent = jnp.concatenate([jnp.where(fsdp_at < 2, kept_pair[1], kept_pair[0]), places], 0)
        away = lax.ppermute(sent, "fsdp", NEAR_SECOND)
        embed_term = jnp.where(fsdp_at < 2, kept_pair[0], kept_pair[1]) + away[:-place_part]
        total = places + away[-place_part:]
    else:
        embed_term = scatter_sum(embed_term, shift_seq, seq_at)
        embed_term = run(scatter_fsdp(embed_term, fsdp_at))
        total = places
        for step in range(1, n_seq):
            total = total + lax.ppermute(places, "seq", [(n_seq - 1, n_seq - 1 - step)])
        places = total
        for step in range(1, n_fsdp):
            total = total + lax.ppermute(places, "fsdp", [(n_fsdp - 1, n_fsdp - 1 - step)])
    places = gather_near(total)
    own_places = own_order(my_positions)
    place_ctx = own_places // place_part
    place_near = lax.rem(core_at + place_ctx, 2) * n_y + lax.rem(y_at - place_ctx // 2 + n_y, n_y)
    place_rows = jnp.take(
        places, place_near * place_part + lax.rem(own_places, place_part), axis=0, mode="clip"
    )
    stream = embed_term.astype(jnp.float32) + place_rows.astype(jnp.float32)
    share = 1.0 / n_ctx
    square_parts = [share * jnp.sum(table_square).reshape(1)] + [
        share * jnp.sum(weight * weight).reshape(1)
        for weight in (attn_in, attn_out, mlp_in, mlp_out)
    ]
    for layer_at in range(1, layer_count):
        whole, after = gather_pack(layer_at, (after, stream[0, :128]))
        stored.append(whole)
    kept = []
    squares = []
    for layer_at in range(layer_count):
        if layer_at:
            stream, stored[layer_at] = lax.optimization_barrier((stream, stored[layer_at]))
        stored[layer_at], head_weight = cut_pack(layer_at, stored[layer_at])
        stream, layer_kept, layer_sums = layer_forward(
            stream,
            stored[layer_at],
            vectors[12 * layer_at : 12 * layer_at + 12],
            allowed,
            head_count,
        )
        kept.append(layer_kept)
        squares.append(layer_sums)
    final_gain = vectors[12 * layer_count]
    final_bias = vectors[12 * layer_count + 1]
    final_norm, final_back = jax.vjp(layer_norm, stream, final_gain, final_bias)
    final_low = final_norm.astype(jnp.bfloat16)
    second_low = product(final_low, head_weight).astype(jnp.bfloat16)
    live = jnp.clip(VOCAB - row_low, 0, rows_dev).astype(jnp.int32).reshape(1)

    def local_targets(ids):
        inside, safe = local_index(ids, row_low, rows_dev)
        return jnp.where(inside, safe, -1)

    final_all = lax.all_gather(final_low, ("seq", "fsdp"), axis=0)
    second_all = lax.all_gather(second_low, ("seq", "fsdp"), axis=0)
    second_factor = SECOND * valid_block
    final_local, second_local = local_targets(next_block), local_targets(second_block)
    final_t = final_all.swapaxes(1, 2)
    final_stats = head_stats(live, table_low, final_t, final_local[None])
    final_stats, second_all = lax.optimization_barrier((final_stats, second_all))
    second_t = second_all.swapaxes(1, 2)
    second_stats = head_stats(live, table_low, second_t, second_local[None])
    stats = merge_stats(jnp.concatenate([final_stats, second_stats], 1))
    half_rows = final_stats.shape[1]
    final_stats, second_stats = stats[:, :half_rows], stats[:, half_rows:]

    pending = Pending()
    results = {}

    def rows_task(name, d_rows):
        parts = d_rows.reshape((n_seq, n_fsdp) + d_rows.shape[1:])
        moved = yield 0, send_parts(parts, shift_seq, seq_at, sent=jnp.bfloat16)
        mine = add_parts(parts, moved, seq_at)
        results[name] = yield from scatter_fsdp(mine, fsdp_at)

    def line_of(stats, factor, local):
        return jnp.stack([stats[0], factor / total_tokens, local.astype(jnp.float32)])

    final_line = line_of(final_stats, valid_block, final_local)
    table_grad, d_rows = head_back(live, table_low, table_t, final_all, final_t, final_line)
    pending.add(rows_task("final", d_rows))
    second_line = line_of(second_stats, second_factor, second_local)
    cuts = 2 if own_rows % 256 == 0 else 1
    for cut in range(cuts):
        line = second_line.reshape(3, n_group, cuts, -1)[:, :, cut].reshape(3, -1)
        table_grad, d_rows = head_back(
            live, table_low, table_t, second_all, second_t, line, cut, table_grad
        )
        table_grad = pending.point(table_grad)
        pending.add(rows_task(("second", cut), d_rows))
    pending.finish()
    d_final = results["final"].T
    d_second = jnp.concatenate([results["second", cut] for cut in range(cuts)], 1).T
    loss_rows = (final_stats[0] - final_stats[1]) * valid_block + (
        second_stats[0] - second_stats[1]
    ) * second_factor
    loss_part = jnp.sum(
        lax.dynamic_slice_in_dim(loss_rows, group_at * own_rows, own_rows, 0)
    )

    def table_task():
        parts = table_grad.reshape(2, part_rows, feature_width)
        (away,) = yield 0, [swap_core(pick(parts, 1 - core_at, 0))]
        mine = (pick(parts, core_at, 0) + away).astype(jnp.bfloat16)
        totals = []
        quarter = part_rows // 4
        for low, wait in ((0, 2), (2 * quarter, 3)):
            pieces = [mine[low : low + quarter], mine[low + quarter : low + 2 * quarter]]
            moved = yield wait, [
                [shift_y(piece, step) for step in range(1, n_y)] for piece in pieces
            ]
            for piece, away in zip(pieces, moved):
                ordered = order_parts([piece] + away, y_at).astype(jnp.float32)
                total = ordered[0]
                for step in range(1, n_y):
                    total = total + ordered[step]
                totals.append(total)
            if not low:
                yield 0, []
        results["table"] = jnp.concatenate(totals, 0)

    def bundle_task(pairs, matrices, names, waits):
        (away,) = yield 0, [swap_pairs(pairs, core_at)]
        grads = shared_outer(pairs, away, core_at)
        parts = []
        for grad in grads:
            cut = grad.reshape(n_seq, n_fsdp, -1, rows_group, grad.shape[1])
            parts += [cut[:, :, at] for at in range(cut.shape[2])]
        stacked = jnp.concatenate(parts, -1)
        moved = yield waits[0], send_parts(stacked, shift_seq, seq_at, sent=jnp.bfloat16)
        mine = add_parts(stacked, moved, seq_at)
        mine = mine.reshape(n_fsdp, n_y, rows_group // n_y, -1)
        moved = yield waits[1], send_parts(mine, shift_y, y_at, 1, jnp.bfloat16)
        mine = add_parts(mine, moved, y_at, 1)
        mine = yield from scatter_fsdp(mine, fsdp_at)
        moved = yield 0, [shift_y(mine, step) for step in range(1, n_y)]
        column = order_parts([mine] + moved, y_at).reshape(rows_group, -1)
        (away,) = yield 0, [swap_core(column)]
        both = order_parts([column, away], core_at)
        at = 0
        for matrix, name in zip(matrices, names):
            width = matrix.shape[-1] // 2
            cuts = []
            for _ in range(matrix.shape[-2] // rows_group):
                cuts.append(
                    jnp.concatenate([both[0, :, at : at + width], both[1, :, at : at + width]], 1)
                )
                at += width
            results[name] = jnp.concatenate(cuts, 0)

    pending.add(table_task())
    d_second = pending.point(d_second)
    d_second_low = d_second.astype(jnp.bfloat16)
    d_stream, d_gain_final, d_bias_final = final_back(d_final + inner(d_second_low, head_weight))

    vec_list = [None] * layer_count
    for layer_at in reversed(range(layer_count)):

        def first_task(pairs, at=layer_at):
            matrices, names = [mlp_in[at], mlp_out[at]], [("fc", at), ("down", at)]
            if at == layer_count - 1:
                pairs = [(final_low, d_second_low)] + pairs
                matrices = [attn_out[layer_count]] + matrices
                names = [("out", layer_count)] + names
            return bundle_task(pairs, matrices, names, (1, 3) if at else (2, 0))

        def later_task(pairs, at=layer_at):
            names = [("in", at), ("out", at)]
            return bundle_task(
                pairs, [attn_in[at], attn_out[at]], names, (1, 1) if at else (1, 0)
            )

        d_stream, vec_list[layer_at] = layer_backward(
            d_stream,
            kept[layer_at],
            stored[layer_at],
            vectors[12 * layer_at : 12 * layer_at + 12],
            allowed,
            head_count,
            pending,
            first_task,
            later_task,
        )
    def device_order(grid):
        cut = grid.reshape(n_group, seqs_dev, n_ctx, ctx_span)
        return cut.transpose(0, 2, 1, 3).reshape(n_group, n_ctx, own_rows)

    part_ids = jnp.arange(part_rows, dtype=jnp.int32)
    part_live = part_ids < rows_dev - core_at * part_rows
    part_ids = jnp.where(part_live, row_low + core_at * part_rows + part_ids, -1)[:, None]
    token_ids, place_ids = device_order(tokens), device_order(positions) + VOCAB

    def spread(token_part, place_part, rows):
        hits = (part_ids == token_part.reshape(1, -1)) | (part_ids == place_part.reshape(1, -1))
        return product(hits.astype(jnp.bfloat16), rows.reshape(-1, feature_width))

    mine = d_stream.astype(jnp.bfloat16)
    if (n_seq, n_fsdp, n_y) == (2, 4, 2):
        half = own_rows // 2
        near_fsdp = jnp.stack([fsdp_at, 3 - fsdp_at, fsdp_at ^ 1, 3 - (fsdp_at ^ 1)])

        def ids_of(ids, seq_from, y_from, core_from):
            cut = pick(ids.reshape(n_seq, n_fsdp, n_y, 2, 2, half), seq_from, 0)
            cut = pick(pick(cut, y_from, 1), core_from, 1)
            return jnp.take(cut, near_fsdp, axis=0, mode="clip")

        def ids_near(pieces):
            def joined(ids):
                return jnp.concatenate(
                    [
                        ids_of(ids, seq_from, y_from, core_from)[:, which].reshape(-1)
                        for core_from in (core_at, 1 - core_at)
                        for seq_from, y_from, which in pieces
                    ]
                )

            return joined(token_ids), joined(place_ids)

        def flat(block):
            return block.reshape(-1, feature_width)

        away = pending.point(lax.ppermute(mine, "fsdp", NEAR_SECOND))
        mine = jnp.concatenate([mine, away], 0)
        away = pending.point(lax.ppermute(mine, "fsdp", NEAR_FIRST))
        mine = jnp.concatenate([mine, away], 0).reshape(4, 2, half, feature_width)
        front, back = flat(mine[:, 0]), flat(mine[:, 1])
        front_x, back_y = shift_seq(front, 1), shift_y(back, 1)
        here = jnp.concatenate([front, back], 0)
        here = jnp.concatenate([here, swap_core(here)], 0)
        table_part = results["table"] + spread(
            *ids_near([(seq_at, y_at, 0), (seq_at, y_at, 1)]), here
        )
        table_part, front_x, back_y = pending.point((table_part, front_x, back_y))
        front_y = shift_y(jnp.concatenate([front, front_x], 0), 1)
        back_x = shift_seq(jnp.concatenate([back, back_y], 0), 1)
        here = jnp.concatenate([front_x, back_y], 0)
        here = jnp.concatenate([here, swap_core(here)], 0)
        table_part = table_part + spread(
            *ids_near([(1 - seq_at, y_at, 0), (seq_at, 1 - y_at, 1)]), here
        )
        table_part, front_y, back_x = pending.point((table_part, front_y, back_x))
        here = jnp.concatenate([front_y, back_x], 0)
        here = jnp.concatenate([here, swap_core(here)], 0)
        table_part = table_part + spread(
            *ids_near(
                [
                    (seq_at, 1 - y_at, 0),
                    (1 - seq_at, 1 - y_at, 0),
                    (1 - seq_at, y_at, 1),
                    (1 - seq_at, 1 - y_at, 1),
                ]
            ),
            here,
        )
        pending.finish()
    else:
        pending.finish()
        embed_back = lax.all_gather(mine, ("seq", "fsdp", "ctx"), axis=0, tiled=True)
        table_part = results["table"] + spread(token_ids, place_ids, embed_back)
    summed = (
        None,
        jnp.stack([results["in", at] for at in range(layer_count)]),
        jnp.stack([results["out", at] for at in range(layer_count + 1)]),
        jnp.stack([results["fc", at] for at in range(layer_count)]),
        jnp.stack([results["down", at] for at in range(layer_count)]),
    )
    vector_grad = jnp.concatenate(vec_list + [jnp.stack([d_gain_final, d_bias_final])], 0)
    matrices = (table[None], attn_in, attn_out, mlp_in, mlp_out)
    row_states = (attn_in_rows, attn_out_rows, mlp_in_rows, mlp_out_rows)
    col_states = (table_cols[None], attn_in_cols, attn_out_cols, mlp_in_cols, mlp_out_cols)

    col_parts = []
    weighted_parts = []
    row_parts = []
    rows_new = []
    for grad_sum, row_state in zip(summed[1:], row_states):
        square = grad_sum * grad_sum
        renewed = DECAY * row_state + (1.0 - DECAY) * jnp.mean(square + EPS_SQUARE, -1)
        rows_new.append(renewed)
        col_parts.append(share * jnp.sum(square + EPS_SQUARE, -2))
        weighted_parts.append(share * jnp.sum(square / renewed[..., None], -2))
        row_parts.append(share * jnp.sum(renewed, -1))
    early_parts = (
        [vector_grad]
        + col_parts
        + weighted_parts
        + row_parts
        + square_parts
        + [loss_part.reshape(1), jnp.stack(squares)]
    )
    early = jnp.concatenate([part.reshape(-1) for part in early_parts])
    early_count = early.shape[0]
    early = jnp.pad(early, (0, -early_count % 1024)).reshape(-1, 128)
    early = sum_all(early).reshape(-1)
    table_away = swap_core(table_part)

    def join_core(mine, away):
        first = jnp.where(core_at == 0, mine, away)
        second = jnp.where(core_at == 0, away, mine)
        return jnp.concatenate([first, second[: rows_dev - part_rows]], 0)

    table_sum = join_core(table_part, table_away)

    state_part = lax.dynamic_slice_in_dim(
        jnp.pad(table_rows, (0, spare)), core_at * part_rows, part_rows, 0
    )
    part_square = table_part * table_part
    part_renewed = DECAY * state_part + (1.0 - DECAY) * jnp.mean(part_square + EPS_SQUARE, -1)
    part_renewed = jnp.where(part_live, part_renewed, 1.0)
    live_count = jnp.sum(part_live.astype(jnp.float32))
    table_rows_new = join_core(part_renewed, swap_core(part_renewed))
    rows_new = [table_rows_new[None]] + rows_new
    grad_sums = (table_sum[None],) + summed[1:]
    late = jnp.concatenate(
        [
            jnp.sum(part_square, 0) + EPS_SQUARE * live_count,
            jnp.sum(part_square / part_renewed[:, None], 0),
            jnp.sum(jnp.where(part_live, part_renewed, 0.0)).reshape(1),
            jnp.zeros(-(2 * feature_width + 1) % 1024, jnp.float32),
        ]
    )
    late, early = lax.optimization_barrier((late, early))
    late = sum_all(late.reshape(8, -1), skip_y=True).reshape(-1)
    early_at = 0
    early_sums = []
    for part in early_parts:
        early_sums.append(early[early_at : early_at + part.size].reshape(part.shape))
        early_at += part.size
    vector_sum = early_sums[0]
    col_sums = [late[None, :feature_width]] + early_sums[1:5]
    weighted_sums = [late[None, feature_width : 2 * feature_width]] + early_sums[5:9]
    row_sums = [late[2 * feature_width : 2 * feature_width + 1]] + early_sums[9:13]
    square_sums = early_sums[13:18]
    loss_sum = early_sums[18][0]
    square_total = early_sums[19].reshape(-1)
    cols_new = []
    new_weights = []
    sizes_rms = []
    for matrix_at in range(5):
        grad_sum, renewed, col_state = (
            grad_sums[matrix_at],
            rows_new[matrix_at],
            col_states[matrix_at],
        )
        stack_count, row_local, col_count = grad_sum.shape
        row_total = row_local * n_group
        weighted = weighted_sums[matrix_at]
        renewed_cols = DECAY * col_state + (1.0 - DECAY) * col_sums[matrix_at] / row_total
        row_mean = row_sums[matrix_at] / row_total
        clip_total = jnp.sum(row_mean * jnp.sum(weighted / renewed_cols, -1))
        entries = grad_sum.size * n_group
        update_rms = jnp.sqrt(clip_total / entries)
        weight_rms = jnp.sqrt(square_sums[matrix_at][0] / entries)
        step_scale = RATE * jnp.maximum(EPS_SCALE, weight_rms) / jnp.maximum(1.0, update_rms / CLIP)
        second_moment = renewed[:, :, None] * renewed_cols[:, None, :] / row_mean[:, None, None]
        update = grad_sum * lax.rsqrt(second_moment)
        new_weights.append(matrices[matrix_at] - step_scale * update)
        cols_new.append(renewed_cols)
        sizes_rms.append(update_rms)
    vector_state_new = DECAY * vector_state + (1.0 - DECAY) * (vector_sum * vector_sum + EPS_SQUARE)
    vector_update = vector_sum * lax.rsqrt(vector_state_new)
    vector_rms = jnp.sqrt(jnp.mean(vector_update * vector_update))
    vector_scale = (
        RATE
        * jnp.maximum(EPS_SCALE, jnp.sqrt(jnp.mean(vectors * vectors)))
        / jnp.maximum(1.0, vector_rms / CLIP)
    )
    vectors_new = vectors - vector_scale * vector_update
    sizes_rms.append(vector_rms)
    norms = jnp.concatenate([jnp.sqrt(square_total / total_tokens), jnp.stack(sizes_rms)])
    table_new = new_weights[0][0]
    return (
        loss_sum,
        norms,
        table_sum,
        rows_new[0][0],
        cols_new[0][0],
        table_new,
        table_new.astype(jnp.bfloat16),
        summed[1],
        rows_new[1],
        cols_new[1],
        new_weights[1],
        new_weights[1].astype(jnp.bfloat16),
        summed[2],
        rows_new[2],
        cols_new[2],
        new_weights[2],
        new_weights[2].astype(jnp.bfloat16),
        summed[3],
        rows_new[3],
        cols_new[3],
        new_weights[3],
        new_weights[3].astype(jnp.bfloat16),
        summed[4],
        rows_new[4],
        cols_new[4],
        new_weights[4],
        new_weights[4].astype(jnp.bfloat16),
        vector_sum,
        vector_state_new,
        vectors_new,
    )


def solution(mesh):
    return jax.shard_map(
        body,
        mesh=mesh,
        in_specs=(
            P(),
            P(),
            P(),
            P(),
            P(("seq", "fsdp"), None),
            P(None, ("seq", "fsdp"), None),
            P(None, ("seq", "fsdp"), None),
            P(None, ("seq", "fsdp"), None),
            P(None, ("seq", "fsdp"), None),
            P(),
            P(("seq", "fsdp")),
            P(),
            P(None, ("seq", "fsdp")),
            P(),
            P(None, ("seq", "fsdp")),
            P(),
            P(None, ("seq", "fsdp")),
            P(),
            P(None, ("seq", "fsdp")),
            P(),
            P(),
        ),
        out_specs=(
            P(),
            P(),
            P(("seq", "fsdp"), None),
            P(("seq", "fsdp")),
            P(),
            P(("seq", "fsdp"), None),
            P(("seq", "fsdp"), None),
            P(None, ("seq", "fsdp"), None),
            P(None, ("seq", "fsdp")),
            P(),
            P(None, ("seq", "fsdp"), None),
            P(None, ("seq", "fsdp"), None),
            P(None, ("seq", "fsdp"), None),
            P(None, ("seq", "fsdp")),
            P(),
            P(None, ("seq", "fsdp"), None),
            P(None, ("seq", "fsdp"), None),
            P(None, ("seq", "fsdp"), None),
            P(None, ("seq", "fsdp")),
            P(),
            P(None, ("seq", "fsdp"), None),
            P(None, ("seq", "fsdp"), None),
            P(None, ("seq", "fsdp"), None),
            P(None, ("seq", "fsdp")),
            P(),
            P(None, ("seq", "fsdp"), None),
            P(None, ("seq", "fsdp"), None),
            P(),
            P(),
            P(),
        ),
        check_vma=False,
    )
```

```python
import functools

import jax
import jax.numpy as jnp
from jax import lax
from jax.experimental import pallas as pl
from jax.experimental.pallas import tpu as pltpu
from jax.sharding import PartitionSpec as P

HEADS = 12
VOCAB = 50304


EPS_NORM = 1e-05
EPS_SQUARE = 1e-30
EPS_SCALE = 0.001
DECAY = 0.5
CLIP = 0.4
RATE = 0.6
SECOND = 0.3
MASKED = -1e30
VMEM_BYTES = 56 * 1024 * 1024
NEAR_FIRST = [(0, 1), (1, 0), (2, 3), (3, 2)]
NEAR_SECOND = [(0, 3), (3, 0), (1, 2), (2, 1)]


def layer_norm(stream, gain, offset):
    center = stream - jnp.mean(stream, -1, keepdims=True)
    spread = jnp.mean(center * center, -1, keepdims=True)
    return center * lax.rsqrt(spread + EPS_NORM) * gain + offset


def gelu_tanh(value):
    return jax.nn.gelu(value, approximate=True)


def positions_of(segments):
    steps_at = jnp.arange(segments.shape[-1], dtype=jnp.int32)
    before = jnp.concatenate(
        [jnp.full(segments.shape[:-1] + (1,), -2, jnp.int32), segments[..., :-1]], -1
    )
    starts = jnp.where(segments != before, steps_at, 0)
    first = lax.cummax(starts, axis=segments.ndim - 1)
    return jnp.where(segments >= 0, steps_at - first, 0)


def product(left, right):
    return jnp.dot(left, right, preferred_element_type=jnp.float32)


def inner(left, right):
    return lax.dot_general(
        left, right, (((1,), (1,)), ((), ())), preferred_element_type=jnp.float32
    )


def outer(left, right):
    return lax.dot_general(
        left, right, (((0,), (0,)), ((), ())), preferred_element_type=jnp.float32
    )


def shift(block, axis, step):
    count = lax.axis_size(axis)
    return lax.ppermute(block, axis, [(i, (i + step) % count) for i in range(count)])


def shift_y(block, step):
    count = lax.axis_size("ctx")
    return lax.ppermute(block, "ctx", [(i, (i + 2 * step) % count) for i in range(count)])


def swap_core(block):
    count = lax.axis_size("ctx")
    return lax.ppermute(block, "ctx", [(i, i ^ 1) for i in range(count)])


def shift_seq(block, step):
    return shift(block, "seq", step)


def shift_fsdp(block, step):
    return shift(block, "fsdp", step)


def pick(parts, at, axis):
    return lax.dynamic_index_in_dim(parts, at, axis, False)


def send_parts(parts, mover, at, axis=0, sent=None):
    count = parts.shape[axis]
    moving = []
    for step in range(1, count):
        piece = pick(parts, lax.rem(at + step, count), axis)
        moving.append(mover(piece if sent is None else piece.astype(sent), step))
    return moving


def add_parts(parts, moved, at, axis=0):
    total = pick(parts, at, axis)
    for piece in moved:
        total = total + piece.astype(total.dtype)
    return total


def scatter_sum(parts, mover, at, axis=0, sent=None):
    return add_parts(parts, send_parts(parts, mover, at, axis, sent), at, axis)


def scatter_fsdp(parts, at):
    count = parts.shape[0]
    if count != 4:
        moved = yield 0, send_parts(parts, shift_fsdp, at, sent=jnp.bfloat16)
        return add_parts(parts, moved, at)
    outside = (at == 0) | (at == 3)
    mine = [jnp.where(outside, 0, 1), jnp.where(outside, 3, 2)]
    other = [jnp.where(outside, 1, 0), jnp.where(outside, 2, 3)]
    away = jnp.stack([pick(parts, slot, 0) for slot in other]).astype(jnp.bfloat16)
    (away,) = yield 0, [lax.ppermute(away, "fsdp", NEAR_FIRST)]
    first, second = (
        pick(parts, slot, 0) + away[k].astype(parts.dtype) for k, slot in enumerate(mine)
    )
    away = jnp.where(at < 2, second, first).astype(jnp.bfloat16)
    (away,) = yield 0, [lax.ppermute(away, "fsdp", NEAR_SECOND)]
    return jnp.where(at < 2, first, second) + away.astype(parts.dtype)


def run(task):
    moving = next(task)[1]
    while True:
        try:
            moving = task.send(moving)[1]
        except StopIteration as stop:
            return stop.value


def sum_all(block, skip_y=False):
    for axis in ("ctx", "seq", "fsdp"):
        count = 2 if skip_y and axis == "ctx" else lax.axis_size(axis)
        whole = lax.axis_size(axis)
        hop = 1
        while hop < count:
            block = block + lax.ppermute(block, axis, [(i, i ^ hop) for i in range(whole)])
            hop *= 2
    return block


def order_parts(parts, at):
    count = len(parts)
    if count == 2:
        first, second = parts
        return jnp.stack([jnp.where(at == 0, first, second), jnp.where(at == 0, second, first)])
    order = lax.rem(at - jnp.arange(count, dtype=jnp.int32) + count, count)
    return jnp.take(jnp.stack(parts), order, axis=0, mode="clip")


def gather_near(block):
    n_y = lax.axis_size("ctx") // 2
    column = jnp.concatenate([block] + [shift_y(block, step) for step in range(1, n_y)], 0)
    return jnp.concatenate([column, swap_core(column)], 0)


def scatter_near(parts):
    n_y = lax.axis_size("ctx") // 2
    parts = parts.reshape((2, n_y, -1) + parts.shape[1:])
    column = parts[0] + swap_core(parts[1])
    total = column[0]
    for step in range(1, n_y):
        away = shift_y(column[step].astype(jnp.bfloat16), n_y - step)
        total = total + away.astype(total.dtype)
    return total


def half_of(block, at):
    width = block.shape[-1] // 2
    return jnp.where(at == 0, block[..., :width], block[..., width:])


def qkv_bias(vec):
    return jnp.concatenate([vec[2], jnp.zeros_like(vec[2]), vec[3]])


def attention_scores(query_low, keys, allowed, head_count):
    row_count, feature_width = query_low.shape
    head_size = feature_width // head_count
    scores = jnp.einsum(
        "qhd,khd->hqk",
        query_low.reshape(row_count, head_count, head_size),
        keys.reshape(-1, head_count, head_size),
        preferred_element_type=jnp.float32,
    ) * head_size ** (-0.5)
    return jnp.where(allowed[None], scores, MASKED)


def mix_values(probs_low, values, head_count):
    head_size = values.shape[1] // head_count
    mixed = jnp.einsum(
        "hqk,khd->qhd",
        probs_low,
        values.reshape(-1, head_count, head_size),
        preferred_element_type=jnp.float32,
    )
    return mixed.reshape(mixed.shape[0], -1)


def layer_forward(stream, weights, vec, allowed, head_count):
    w_in, w_out, w_fc, w_down = weights
    feature_width = stream.shape[1]
    a_low = layer_norm(stream, vec[0], vec[1]).astype(jnp.bfloat16)
    qkv_low = (product(a_low, w_in) + qkv_bias(vec)).astype(jnp.bfloat16)
    pairs = gather_near(qkv_low[:, feature_width:])
    keys, values = pairs[:, :feature_width], pairs[:, feature_width:]
    scores = attention_scores(qkv_low[:, :feature_width], keys, allowed, head_count)
    row_max = jnp.max(scores, -1)
    log_total = row_max + jnp.log(jnp.sum(jnp.exp(scores - row_max[..., None]), -1))
    probs = jnp.exp(scores - log_total[..., None])
    mixed_low = mix_values(probs.astype(jnp.bfloat16), values, head_count).astype(jnp.bfloat16)
    branch = product(mixed_low, w_out) + vec[4]
    middle = stream + branch
    m_low = layer_norm(middle, vec[5], vec[6]).astype(jnp.bfloat16)
    hidden = product(m_low, w_fc) + vec[8:12].reshape(-1)
    output = product(gelu_tanh(hidden).astype(jnp.bfloat16), w_down) + vec[7]
    sums = jnp.stack([jnp.sum(stream * stream), jnp.sum(branch * branch), jnp.sum(output * output)])
    kept = (stream, a_low, qkv_low, keys, values, log_total, mixed_low, middle, m_low, hidden)
    return (middle + output, kept, sums)


def swap_pairs(pairs, core_at):
    lefts = [left for left, _ in pairs]
    return swap_core(
        jnp.concatenate(lefts + [half_of(right, 1 - core_at) for _, right in pairs], 1)
    )


def shared_outer(pairs, away, core_at):
    at = 0
    whole_left = []
    for left, _ in pairs:
        whole_left.append(jnp.concatenate([left, away[:, at : at + left.shape[1]]], 0))
        at += left.shape[1]
    grads = []
    for left, (_, right) in zip(whole_left, pairs):
        width = right.shape[1] // 2
        whole_right = jnp.concatenate([half_of(right, core_at), away[:, at : at + width]], 0)
        at += width
        grads.append(outer(left, whole_right))
    return grads


def layer_backward(d_stream, kept, weights, vec, allowed, head_count, pending, first_task, later_task):
    stream, a_low, qkv_low, keys, values, log_total, mixed_low, middle, m_low, hidden = kept
    w_in, w_out, w_fc, w_down = weights
    row_count, feature_width = stream.shape
    head_size = feature_width // head_count
    scale = head_size ** (-0.5)
    norm_back_one = jax.vjp(layer_norm, stream, vec[0], vec[1])[1]
    query_low = qkv_low[:, :feature_width]
    probs = jnp.exp(attention_scores(query_low, keys, allowed, head_count) - log_total[..., None])
    probs_low = probs.astype(jnp.bfloat16)
    norm_back_two = jax.vjp(layer_norm, middle, vec[5], vec[6])[1]
    gelu_out, gelu_back = jax.vjp(gelu_tanh, hidden)
    u_low = gelu_out.astype(jnp.bfloat16)
    d_out_low = d_stream.astype(jnp.bfloat16)
    d_hidden_low = gelu_back(inner(d_out_low, w_down))[0].astype(jnp.bfloat16)
    d_hidden_low = pending.point(d_hidden_low)
    pending.add(first_task([(m_low, d_hidden_low), (u_low, d_out_low)]))
    d_m = inner(d_hidden_low, w_fc)
    d_two, d_gain_two, d_bias_two = norm_back_two(d_m)
    d_middle = d_stream + d_two
    d_middle = pending.point(d_middle)
    d_middle_low = d_middle.astype(jnp.bfloat16)
    d_heads = (
        inner(d_middle_low, w_out).astype(jnp.bfloat16).reshape(row_count, head_count, head_size)
    )
    value_heads = values.reshape(-1, head_count, head_size)
    d_probs = jnp.einsum("qhd,khd->hqk", d_heads, value_heads, preferred_element_type=jnp.float32)
    d_scores = (probs * (d_probs - jnp.sum(probs * d_probs, -1, keepdims=True))).astype(
        jnp.bfloat16
    )
    d_scores = pending.point(d_scores)
    d_query = (
        jnp.einsum(
            "hqk,khd->qhd",
            d_scores,
            keys.reshape(-1, head_count, head_size),
            preferred_element_type=jnp.float32,
        ).reshape(row_count, feature_width)
        * scale
    )
    d_keys = (
        jnp.einsum(
            "hqk,qhd->khd",
            d_scores,
            query_low.reshape(row_count, head_count, head_size),
            preferred_element_type=jnp.float32,
        ).reshape(-1, feature_width)
        * scale
    )
    d_values = jnp.einsum(
        "hqk,qhd->khd", probs_low, d_heads, preferred_element_type=jnp.float32
    ).reshape(-1, feature_width)
    d_pairs = scatter_near(jnp.concatenate([d_keys, d_values], 1))
    d_qkv_low = jnp.concatenate([d_query, d_pairs], 1).astype(jnp.bfloat16)
    d_qkv_low = pending.point(d_qkv_low)
    pending.add(later_task([(a_low, d_qkv_low), (mixed_low, d_middle_low)]))
    d_one, d_gain_one, d_bias_one = norm_back_one(inner(d_qkv_low, w_in))
    d_qkv = d_qkv_low.astype(jnp.float32)
    rows_head = jnp.stack(
        [
            d_gain_one,
            d_bias_one,
            jnp.sum(d_qkv[:, :feature_width], 0),
            jnp.sum(d_qkv[:, 2 * feature_width :], 0),
            jnp.sum(d_middle_low.astype(jnp.float32), 0),
            d_gain_two,
            d_bias_two,
            jnp.sum(d_out_low.astype(jnp.float32), 0),
        ]
    )
    vec_grad = jnp.concatenate(
        [rows_head, jnp.sum(d_hidden_low.astype(jnp.float32), 0).reshape(4, feature_width)], 0
    )
    return (pending.point(d_middle + d_one), vec_grad)


def merge_stats(stats):
    for mover, axis in ((shift_seq, "seq"), (shift_fsdp, "fsdp")):
        parts = [stats] + [mover(stats, step) for step in range(1, lax.axis_size(axis))]
        top = parts[0][0]
        for part in parts[1:]:
            top = jnp.maximum(top, part[0])
        total = jnp.exp(parts[0][0] - top)
        picked = parts[0][1]
        for part in parts[1:]:
            total = total + jnp.exp(part[0] - top)
            picked = picked + part[1]
        stats = jnp.stack([top + jnp.log(total), picked])
    return stats


def blocks_of(groups, width, row_block):
    step = max(1, row_block // width)
    return [
        (range(low, low + step), slice(low * width, (low + step) * width))
        for low in range(0, groups, step)
    ]


def side_by_side(ref, at_block):
    return jnp.concatenate([ref[at] for at in at_block], 1)


def masked_logits(logits, live, first):
    column = lax.broadcasted_iota(jnp.int32, logits.shape, 0) + first
    return jnp.where(column < live, logits, MASKED)


def stats_kernel(row_block, live_ref, table_ref, rows_ref, target_ref, out_ref, top_ref, sum_ref, pick_ref):
    at = pl.program_id(0)
    tile = table_ref.shape[0]
    first = at * tile
    live = live_ref[0]

    @pl.when(at == 0)
    def _():
        top_ref[...] = jnp.full_like(top_ref, MASKED)
        sum_ref[...] = jnp.zeros_like(sum_ref)
        pick_ref[...] = jnp.zeros_like(pick_ref)

    def step(masked):
        for at_block, here in blocks_of(rows_ref.shape[0], rows_ref.shape[2], row_block):
            logits = jnp.dot(
                table_ref[...], side_by_side(rows_ref, at_block), preferred_element_type=jnp.float32
            )
            if masked:
                logits = masked_logits(logits, live, first)
            column = lax.broadcasted_iota(jnp.int32, logits.shape, 0)
            hit = column == target_ref[:, here] - first
            cut = logits.reshape(tile // 8, 8, logits.shape[1])
            top = top_ref[:, here]
            joint = jnp.maximum(top, jnp.max(cut, 0))
            total = jnp.sum(jnp.exp(cut - joint[None]), 0)
            sum_ref[:, here] = sum_ref[:, here] * jnp.exp(top - joint) + total
            top_ref[:, here] = joint
            pick_ref[:, here] += jnp.sum(
                jnp.where(hit, logits, 0.0).reshape(cut.shape), 0
            )

    @pl.when(first + tile <= live)
    def _():
        step(False)

    @pl.when((first + tile > live) & (first < live))
    def _():
        step(True)

    @pl.when(at == pl.num_programs(0) - 1)
    def _():
        top = top_ref[...]
        joint = jnp.max(top, 0, keepdims=True)
        total = jnp.sum(sum_ref[...] * jnp.exp(top - joint), 0, keepdims=True)
        out_ref[0:1, :] = joint + jnp.log(total)
        out_ref[1:2, :] = jnp.sum(pick_ref[...], 0, keepdims=True)


def head_stats(live, table_low, rows_t, target, tile=512, row_block=512):
    groups, depth, width = rows_t.shape
    count = groups * width
    height = table_low.shape[0]
    return pl.pallas_call(
        functools.partial(stats_kernel, row_block),
        out_shape=jax.ShapeDtypeStruct((2, count), jnp.float32),
        grid=(height // tile,),
        in_specs=[
            pl.BlockSpec(memory_space=pltpu.SMEM),
            pl.BlockSpec((tile, depth), lambda i: (i, 0)),
            pl.BlockSpec((groups, depth, width), lambda i: (0, 0, 0)),
            pl.BlockSpec((1, count), lambda i: (0, 0)),
        ],
        out_specs=pl.BlockSpec((2, count), lambda i: (0, 0)),
        scratch_shapes=[pltpu.VMEM((8, count), jnp.float32)] * 3,
        compiler_params=pltpu.CompilerParams(vmem_limit_bytes=VMEM_BYTES),
        cost_estimate=pl.CostEstimate(
            flops=2 * height * depth * count,
            bytes_accessed=2 * height * depth + 2 * depth * count,
            transcendentals=height * count,
        ),
    )(live, table_low, rows_t, target)


def back_kernel(row_block, added, live_ref, table_ref, table_t_ref, rows_ref, rows_t_ref, line_ref, *refs):
    if added:
        prior_ref, grad_ref, d_rows_ref = refs
    else:
        grad_ref, d_rows_ref = refs
    at = pl.program_id(0)
    tile = table_ref.shape[0]
    first = at * tile
    live = live_ref[0]
    width = d_rows_ref.shape[2]

    @pl.when(at == 0)
    def _():
        d_rows_ref[...] = jnp.zeros_like(d_rows_ref)

    def step(masked):
        grad = prior_ref[...] if added else None
        for at_block, here in blocks_of(rows_t_ref.shape[0], width, row_block):
            logits = jnp.dot(
                table_ref[...],
                side_by_side(rows_t_ref, at_block),
                preferred_element_type=jnp.float32,
            )
            if masked:
                logits = masked_logits(logits, live, first)
            column = lax.broadcasted_iota(jnp.int32, logits.shape, 0).astype(jnp.float32)
            probs = jnp.exp(logits - line_ref[0:1, here])
            hit = column == line_ref[2:3, here] - first.astype(jnp.float32)
            d_low = (line_ref[1:2, here] * jnp.where(hit, probs - 1.0, probs)).astype(jnp.bfloat16)
            rows = rows_ref[at_block.start : at_block.stop].reshape(-1, rows_ref.shape[2])
            part = jnp.dot(d_low, rows, preferred_element_type=jnp.float32)
            grad = part if grad is None else grad + part
            d_part = jnp.dot(table_t_ref[...], d_low, preferred_element_type=jnp.float32)
            for at_width, at_group in enumerate(at_block):
                d_rows_ref[at_group] += d_part[:, at_width * width : (at_width + 1) * width]
        grad_ref[...] = grad

    @pl.when(first + tile <= live)
    def _():
        step(False)

    @pl.when((first + tile > live) & (first < live))
    def _():
        step(True)

    @pl.when(first >= live)
    def _():
        grad_ref[...] = prior_ref[...] if added else jnp.zeros_like(grad_ref)


def head_back(live, table_low, table_t, rows, rows_t, line, cut=0, prior=None, tile=512):
    groups, _, depth = rows.shape
    height = table_low.shape[0]
    count = line.shape[1]
    width = count // groups
    once = dict(pipeline_mode=pl.Buffered(1))
    grad_spec = pl.BlockSpec((tile, depth), lambda i: (i, 0))
    added = prior is not None
    return pl.pallas_call(
        functools.partial(back_kernel, 1024, added),
        out_shape=(
            jax.ShapeDtypeStruct((height, depth), jnp.float32),
            jax.ShapeDtypeStruct((groups, depth, width), jnp.float32),
        ),
        grid=(height // tile,),
        in_specs=[
            pl.BlockSpec(memory_space=pltpu.SMEM),
            pl.BlockSpec((tile, depth), lambda i: (i, 0)),
            pl.BlockSpec((depth, tile), lambda i: (0, i)),
            pl.BlockSpec((groups, width, depth), lambda i: (0, cut, 0), **once),
            pl.BlockSpec((groups, depth, width), lambda i: (0, 0, cut), **once),
            pl.BlockSpec((3, count), lambda i: (0, 0), **once),
        ]
        + ([grad_spec] if added else []),
        out_specs=(
            grad_spec,
            pl.BlockSpec((groups, depth, width), lambda i: (0, 0, 0), **once),
        ),
        input_output_aliases={6: 0} if added else {},
        compiler_params=pltpu.CompilerParams(vmem_limit_bytes=VMEM_BYTES),
        cost_estimate=pl.CostEstimate(
            flops=6 * height * depth * count,
            bytes_accessed=4 * height * depth + 12 * depth * count + 8 * height * depth,
            transcendentals=height * count,
        ),
    )(live, table_low, table_t, rows, rows_t, line, *((prior,) if added else ()))


def prepare_kernel(row_count, table_ref, low_ref, turned_ref, square_ref):
    at = pl.program_id(0)
    tile = table_ref.shape[0]
    row = lax.broadcasted_iota(jnp.int32, table_ref.shape, 0) + at * tile
    block = jnp.where(row < row_count, table_ref[...], 0.0)
    low_ref[...] = block.astype(jnp.bfloat16)
    turned_ref[...] = block.T.astype(jnp.bfloat16)
    part = jnp.sum((block * block).reshape(tile // 8, 8, block.shape[1]), 0)

    @pl.when(at == 0)
    def _():
        square_ref[...] = part

    @pl.when(at > 0)
    def _():
        square_ref[...] += part


def prepare_table(table, height, tile=512):
    row_count, depth = table.shape
    return pl.pallas_call(
        functools.partial(prepare_kernel, row_count),
        out_shape=(
            jax.ShapeDtypeStruct((height, depth), jnp.bfloat16),
            jax.ShapeDtypeStruct((depth, height), jnp.bfloat16),
            jax.ShapeDtypeStruct((8, depth), jnp.float32),
        ),
        grid=(height // tile,),
        in_specs=[pl.BlockSpec((tile, depth), lambda i: (i, 0))],
        out_specs=(
            pl.BlockSpec((tile, depth), lambda i: (i, 0)),
            pl.BlockSpec((depth, tile), lambda i: (0, i)),
            pl.BlockSpec((8, depth), lambda i: (0, 0)),
        ),
        compiler_params=pltpu.CompilerParams(vmem_limit_bytes=VMEM_BYTES),
        cost_estimate=pl.CostEstimate(
            flops=2 * row_count * depth,
            bytes_accessed=4 * row_count * depth + 4 * height * depth,
            transcendentals=0,
        ),
    )(table)


def update_kernel(used, core_ref, scale_ref, mine_ref, away_ref, mine_rows_ref, away_rows_ref, cols_ref, weight_ref, *outs):
    grad_ref, new_ref, copy_ref = outs
    half = pl.program_id(0) // (pl.num_programs(0) // 2)
    chosen = half == core_ref[0]
    grad = jnp.where(chosen, mine_ref[...], away_ref[...])
    rows = jnp.where(chosen, mine_rows_ref[...], away_rows_ref[...])
    update = grad * lax.rsqrt(rows * cols_ref[...])
    new = weight_ref[...] - scale_ref[0] * update

    @pl.when(pl.program_id(0) < used)
    def _():
        grad_ref[...] = grad
        new_ref[...] = new
        copy_ref[...] = new.astype(copy_ref.dtype)


def update_table(core, scale, mine, away, mine_rows, away_rows, cols, weight, tile=256):
    row_count, depth = weight.shape
    steps = mine.shape[0] // tile
    used = -(-row_count // tile)

    def mine_at(i, core_ref):
        return (jnp.clip(i - core_ref[0] * steps, 0, steps - 1), 0)

    def away_at(i, core_ref):
        return (jnp.clip(i - (1 - core_ref[0]) * steps, 0, steps - 1), 0)

    def whole_at(i, core_ref):
        return (jnp.minimum(i, used - 1), 0)

    whole = pl.BlockSpec((tile, depth), whole_at)
    return pl.pallas_call(
        functools.partial(update_kernel, used),
        out_shape=(
            jax.ShapeDtypeStruct(weight.shape, jnp.float32),
            jax.ShapeDtypeStruct(weight.shape, jnp.float32),
            jax.ShapeDtypeStruct(weight.shape, jnp.bfloat16),
        ),
        grid_spec=pltpu.PrefetchScalarGridSpec(
            num_scalar_prefetch=1,
            grid=(2 * steps,),
            in_specs=[
                pl.BlockSpec(memory_space=pltpu.SMEM),
                pl.BlockSpec((tile, depth), mine_at),
                pl.BlockSpec((tile, depth), away_at),
                pl.BlockSpec((tile, 1), mine_at),
                pl.BlockSpec((tile, 1), away_at),
                pl.BlockSpec((1, depth), lambda i, core_ref: (0, 0)),
                whole,
            ],
            out_specs=(whole, whole, whole),
        ),
        compiler_params=pltpu.CompilerParams(vmem_limit_bytes=VMEM_BYTES),
        cost_estimate=pl.CostEstimate(
            flops=6 * row_count * depth,
            bytes_accessed=18 * row_count * depth,
            transcendentals=row_count * depth,
        ),
    )(core, scale, mine, away, mine_rows, away_rows, cols, weight)


class Pending:
    def __init__(self):
        self.active = []

    def add(self, task):
        held, moving = next(task)
        self.active.append([task, held, moving])

    def point(self, main):
        ready = [entry for entry in self.active if entry[1] == 0]
        main, moved = lax.optimization_barrier((main, [entry[2] for entry in ready]))
        for entry in self.active:
            entry[1] -= 1
        for entry, arrived in zip(ready, moved):
            self.advance(entry, arrived)
        return main

    def advance(self, entry, arrived):
        try:
            entry[1:] = entry[0].send(arrived)
        except StopIteration:
            self.active.remove(entry)

    def finish(self):
        while self.active:
            entry = self.active[0]
            self.advance(entry, entry[2])


def local_index(ids, row_low, row_count):
    shifted = ids - row_low
    inside = (shifted >= 0) & (shifted < row_count)
    return (inside, jnp.clip(shifted, 0, row_count - 1))


def body(
    tokens,
    segments,
    next_ids,
    second_ids,
    table,
    attn_in,
    attn_out,
    mlp_in,
    mlp_out,
    vectors,
    table_rows,
    table_cols,
    attn_in_rows,
    attn_in_cols,
    attn_out_rows,
    attn_out_cols,
    mlp_in_rows,
    mlp_in_cols,
    mlp_out_rows,
    mlp_out_cols,
    vector_state,
):
    n_ctx = lax.axis_size("ctx")
    n_seq = lax.axis_size("seq")
    n_fsdp = lax.axis_size("fsdp")
    n_y = n_ctx // 2
    n_group = n_seq * n_fsdp
    ctx_at = lax.axis_index("ctx")
    seq_at = lax.axis_index("seq")
    fsdp_at = lax.axis_index("fsdp")
    y_at = ctx_at // 2
    core_at = lax.rem(ctx_at, 2)
    group_at = seq_at * n_fsdp + fsdp_at
    all_seqs, length = segments.shape
    seqs_dev = all_seqs // n_group
    ctx_span = length // n_ctx
    feature_width = table.shape[1]
    layer_count = attn_in.shape[0]
    head_count = HEADS
    total_tokens = all_seqs * length
    own_rows = seqs_dev * ctx_span
    block_start = ctx_at * ctx_span
    positions = positions_of(segments)

    def block_of(grid):
        return lax.dynamic_slice_in_dim(grid, block_start, ctx_span, 1)

    tok_block = block_of(tokens).reshape(-1)
    valid_block = (block_of(segments) >= 0).astype(jnp.float32).reshape(-1)
    next_block = block_of(next_ids).reshape(-1)
    second_block = block_of(second_ids).reshape(-1)
    my_segments = lax.dynamic_slice_in_dim(segments, group_at * seqs_dev, seqs_dev, 0)
    my_positions = lax.dynamic_slice_in_dim(positions, group_at * seqs_dev, seqs_dev, 0)
    hops = jnp.asarray([(side, step) for side in range(2) for step in range(n_y)], jnp.int32)
    near_ctx = 2 * lax.rem(y_at - hops[:, 1] + n_y, n_y) + lax.rem(core_at + hops[:, 0], 2)

    def near_order(grid):
        cut = grid.reshape(seqs_dev, n_ctx, ctx_span).transpose(1, 0, 2)
        return jnp.take(cut, near_ctx, axis=0, mode="clip").reshape(-1)

    def own_order(grid):
        return block_of(grid).reshape(-1)

    time_grid = jnp.broadcast_to(jnp.arange(length, dtype=jnp.int32)[None], (seqs_dev, length))
    seq_grid = jnp.broadcast_to(jnp.arange(seqs_dev, dtype=jnp.int32)[:, None], (seqs_dev, length))
    q_seg, k_seg = (own_order(my_segments), near_order(my_segments))
    q_time, k_time = (own_order(time_grid), near_order(time_grid))
    q_seq, k_seq = (own_order(seq_grid), near_order(seq_grid))
    allowed = (q_seq[:, None] == k_seq[None]) & (
        (q_time[:, None] == k_time[None])
        | (k_time[None] < q_time[:, None]) & (q_seg[:, None] == k_seg[None]) & (k_seg[None] >= 0)
    )
    rows_dev = table.shape[0]
    row_low = group_at * rows_dev
    rows_group = attn_in.shape[1]
    rows_part = rows_group // n_ctx
    down_cut = mlp_out.shape[1] // rows_group

    in_width, out_width, fc_width = attn_in.shape[2], attn_out.shape[2], mlp_in.shape[2]
    pack_width = in_width + out_width + fc_width + down_cut * feature_width
    part_width = pack_width // n_ctx
    model_rows = n_group * rows_group

    def gather_pack(layer_at):
        down = mlp_out[layer_at].reshape(down_cut, rows_group, feature_width)
        pack = jnp.concatenate(
            [attn_in[layer_at], mlp_in[layer_at], attn_out[layer_at]]
            + [down[cut] for cut in range(down_cut)],
            1,
        ).astype(jnp.bfloat16)
        part = lax.dynamic_slice_in_dim(pack, ctx_at * part_width, part_width, 1)
        if layer_at == layer_count - 1:
            head = lax.dynamic_slice_in_dim(
                attn_out[layer_count].astype(jnp.bfloat16), ctx_at * rows_part, rows_part, 0
            )
            head = jnp.pad(head.reshape(-1), (0, -head.size % part_width)).reshape(-1, part_width)
            part = jnp.concatenate([part, head], 0)
        return lax.all_gather(part, ("ctx", "seq", "fsdp"), axis=0)

    def cut_pack(layer_at, whole):
        whole = whole.reshape(n_ctx, n_group, -1, part_width)
        body_rows = whole[:, :, :rows_group].reshape(n_ctx, model_rows, part_width)

        def columns_of(low, high):
            pieces = []
            for at in range(n_ctx):
                start, stop = max(low, at * part_width), min(high, (at + 1) * part_width)
                if start < stop:
                    pieces.append(body_rows[at, :, start - at * part_width : stop - at * part_width])
            return pieces[0] if len(pieces) == 1 else jnp.concatenate(pieces, 1)

        at = in_width + fc_width
        down = jnp.stack(
            [
                columns_of(low, low + feature_width).reshape(n_group, rows_group, feature_width)
                for low in range(at + out_width, pack_width, feature_width)
            ],
            1,
        )
        weights = (
            columns_of(0, in_width),
            columns_of(at, at + out_width),
            columns_of(in_width, at),
            down.reshape(-1, feature_width),
        )
        head = None
        if layer_at == layer_count - 1:
            head = whole[:, :, rows_group:].reshape(n_ctx, n_group, -1)
            head = head[:, :, : rows_part * out_width].reshape(n_ctx, n_group, rows_part, out_width)
            head = head.transpose(1, 0, 2, 3).reshape(model_rows, out_width)
        return weights, head

    stored = [gather_pack(0)]

    tok_inside, tok_safe = local_index(tok_block, row_low, rows_dev)
    embed_term = jnp.where(
        tok_inside[:, None], jnp.take(table, tok_safe, axis=0, mode="clip"), 0.0
    ).astype(jnp.bfloat16)
    embed_term = embed_term.reshape(n_seq, n_fsdp, own_rows, feature_width)
    place_part = length // n_ctx
    place_low = VOCAB - rows_dev * (n_group - 1)
    places = lax.dynamic_slice_in_dim(table, place_low + ctx_at * place_part, place_part, 0)
    places = jnp.where(group_at == n_group - 1, places, 0.0).astype(jnp.bfloat16)
    def device_order(grid):
        cut = grid.reshape(n_group, seqs_dev, n_ctx, ctx_span)
        return cut.transpose(0, 2, 1, 3).reshape(n_group * n_ctx, own_rows)

    ids_grid = jnp.stack([device_order(tokens), device_order(positions) + VOCAB])
    near = (n_seq, n_fsdp, n_y) == (2, 4, 2)
    if near:
        across = [k << 2 for k in (0, 3, 1, 2)]
        stages = [
            [(0, 0), (0, 1)],
            [(16, 0), (2, 1)],
            [(2, 0), (18, 0), (16, 1), (18, 1)],
        ]
        order = [
            ((seat ^ step ^ side) << 1) | which
            for pieces in stages
            for side in (0, 1)
            for seat, which in pieces
            for step in across
        ]
        order = jnp.asarray(order, jnp.int32) ^ ((group_at * n_ctx + ctx_at) << 1)
        ids_grid = ids_grid.reshape(2, 2 * n_group * n_ctx, own_rows // 2)
        ids_grid = jnp.take(ids_grid, order, axis=1, mode="clip")
    ids_grid = ids_grid.reshape(2, -1)
    part_rows = -(-rows_dev // 512) * 256
    spare = part_rows * 2 - rows_dev
    table_low, table_t, table_square = prepare_table(table, 2 * part_rows)
    if near:
        flat = (-1, feature_width)
        sent = pick(embed_term, 1 - seq_at, 0).reshape(flat)
        away = shift_seq(jnp.concatenate([sent, places], 0), 1)
        away, table_low, table_t, table_square, ids_grid = lax.optimization_barrier(
            (away, table_low, table_t, table_square, ids_grid)
        )
        mine = pick(embed_term, seq_at, 0) + away[:-place_part].reshape(embed_term.shape[1:])
        places = places + away[-place_part:]
        outside = (fsdp_at == 0) | (fsdp_at == 3)
        pair = jnp.where(outside, mine[1:3], jnp.stack([mine[0], mine[3]]))
        sent = jnp.concatenate([pair.reshape(flat), places], 0)
        away = lax.ppermute(sent, "fsdp", NEAR_FIRST)
        kept_pair = jnp.where(outside, jnp.stack([mine[0], mine[3]]), mine[1:3])
        kept_pair = kept_pair + away[:-place_part].reshape(kept_pair.shape)
        places = places + away[-place_part:]
        sent = jnp.concatenate([jnp.where(fsdp_at < 2, kept_pair[1], kept_pair[0]), places], 0)
        away = lax.ppermute(sent, "fsdp", NEAR_SECOND)
        embed_term = jnp.where(fsdp_at < 2, kept_pair[0], kept_pair[1]) + away[:-place_part]
        total = places + away[-place_part:]
    else:
        embed_term = scatter_sum(embed_term, shift_seq, seq_at)
        embed_term = run(scatter_fsdp(embed_term, fsdp_at))
        total = places
        for step in range(1, n_seq):
            total = total + lax.ppermute(places, "seq", [(n_seq - 1, n_seq - 1 - step)])
        places = total
        for step in range(1, n_fsdp):
            total = total + lax.ppermute(places, "fsdp", [(n_fsdp - 1, n_fsdp - 1 - step)])
    places = gather_near(total)
    own_places = own_order(my_positions)
    place_ctx = own_places // place_part
    place_near = lax.rem(core_at + place_ctx, 2) * n_y + lax.rem(y_at - place_ctx // 2 + n_y, n_y)
    place_rows = jnp.take(
        places, place_near * place_part + lax.rem(own_places, place_part), axis=0, mode="clip"
    )
    stream = embed_term.astype(jnp.float32) + place_rows.astype(jnp.float32)
    share = 1.0 / n_ctx
    square_parts = [share * jnp.sum(table_square).reshape(1)] + [
        share * jnp.sum(weight * weight).reshape(1)
        for weight in (attn_in, attn_out, mlp_in, mlp_out)
    ]
    for layer_at in range(1, layer_count):
        stored.append(gather_pack(layer_at))
    kept = []
    squares = []
    for layer_at in range(layer_count):
        if layer_at:
            stream, stored[layer_at] = lax.optimization_barrier((stream, stored[layer_at]))
        stored[layer_at], head_weight = cut_pack(layer_at, stored[layer_at])
        stream, layer_kept, layer_sums = layer_forward(
            stream,
            stored[layer_at],
            vectors[12 * layer_at : 12 * layer_at + 12],
            allowed,
            head_count,
        )
        kept.append(layer_kept)
        squares.append(layer_sums)
    final_gain = vectors[12 * layer_count]
    final_bias = vectors[12 * layer_count + 1]
    final_norm, final_back = jax.vjp(layer_norm, stream, final_gain, final_bias)
    final_low = final_norm.astype(jnp.bfloat16)
    second_low = product(final_low, head_weight).astype(jnp.bfloat16)
    live = jnp.clip(VOCAB - row_low, 0, rows_dev).astype(jnp.int32).reshape(1)

    def local_targets(ids):
        inside, safe = local_index(ids, row_low, rows_dev)
        return jnp.where(inside, safe, -1)

    final_all = lax.all_gather(final_low, ("seq", "fsdp"), axis=0)
    second_all = lax.all_gather(second_low, ("seq", "fsdp"), axis=0)
    second_factor = SECOND * valid_block
    final_local, second_local = local_targets(next_block), local_targets(second_block)
    final_t = final_all.swapaxes(1, 2)
    final_stats = head_stats(live, table_low, final_t, final_local[None])
    final_stats, second_all = lax.optimization_barrier((final_stats, second_all))
    second_t = second_all.swapaxes(1, 2)
    second_stats = head_stats(live, table_low, second_t, second_local[None])
    stats = merge_stats(jnp.concatenate([final_stats, second_stats], 1))
    half_rows = final_stats.shape[1]
    final_stats, second_stats = stats[:, :half_rows], stats[:, half_rows:]

    pending = Pending()
    results = {}

    def rows_task(name, d_rows):
        parts = d_rows.reshape((n_seq, n_fsdp) + d_rows.shape[1:])
        moved = yield 0, send_parts(parts, shift_seq, seq_at, sent=jnp.bfloat16)
        mine = add_parts(parts, moved, seq_at)
        results[name] = yield from scatter_fsdp(mine, fsdp_at)

    def line_of(stats, factor, local):
        return jnp.stack([stats[0], factor / total_tokens, local.astype(jnp.float32)])

    final_line = line_of(final_stats, valid_block, final_local)
    table_grad, d_rows = head_back(live, table_low, table_t, final_all, final_t, final_line)
    pending.add(rows_task("final", d_rows))
    second_line = line_of(second_stats, second_factor, second_local)
    cuts = 2 if own_rows % 256 == 0 else 1
    for cut in range(cuts):
        line = second_line.reshape(3, n_group, cuts, -1)[:, :, cut].reshape(3, -1)
        table_grad, d_rows = head_back(
            live, table_low, table_t, second_all, second_t, line, cut, table_grad
        )
        table_grad = pending.point(table_grad)
        pending.add(rows_task(("second", cut), d_rows))
    pending.finish()
    d_final = results["final"].T
    d_second = jnp.concatenate([results["second", cut] for cut in range(cuts)], 1).T
    loss_rows = (final_stats[0] - final_stats[1]) * valid_block + (
        second_stats[0] - second_stats[1]
    ) * second_factor
    loss_part = jnp.sum(
        lax.dynamic_slice_in_dim(loss_rows, group_at * own_rows, own_rows, 0)
    )

    def table_task():
        parts = table_grad.reshape(2, part_rows, feature_width)
        (away,) = yield 0, [swap_core(pick(parts, 1 - core_at, 0))]
        mine = (pick(parts, core_at, 0) + away).astype(jnp.bfloat16)
        totals = []
        quarter = part_rows // 4
        for low, wait in ((0, 2), (2 * quarter, 3)):
            pieces = [mine[low : low + quarter], mine[low + quarter : low + 2 * quarter]]
            if low:
                pieces = yield 0, pieces
            moved = yield wait, [
                [shift_y(piece, step) for step in range(1, n_y)] for piece in pieces
            ]
            for piece, away in zip(pieces, moved):
                ordered = order_parts([piece] + away, y_at).astype(jnp.float32)
                total = ordered[0]
                for step in range(1, n_y):
                    total = total + ordered[step]
                totals.append(total)
        results["table"] = jnp.concatenate(totals, 0)

    def bundle_task(pairs, matrices, names, waits):
        (away,) = yield 0, [swap_pairs(pairs, core_at)]
        grads = shared_outer(pairs, away, core_at)
        parts = []
        for grad in grads:
            cut = grad.reshape(n_seq, n_fsdp, -1, rows_group, grad.shape[1])
            parts += [cut[:, :, at] for at in range(cut.shape[2])]
        stacked = jnp.concatenate(parts, -1)
        moved = yield waits[0], send_parts(stacked, shift_seq, seq_at, sent=jnp.bfloat16)
        mine = add_parts(stacked, moved, seq_at)
        mine = mine.reshape(n_fsdp, n_y, rows_group // n_y, -1)
        moved = yield waits[1], send_parts(mine, shift_y, y_at, 1, jnp.bfloat16)
        mine = add_parts(mine, moved, y_at, 1)
        mine = yield from scatter_fsdp(mine, fsdp_at)
        moved = yield 0, [shift_y(mine, step) for step in range(1, n_y)]
        column = order_parts([mine] + moved, y_at).reshape(rows_group, -1)
        (away,) = yield 0, [swap_core(column)]
        both = order_parts([column, away], core_at)
        at = 0
        for matrix, name in zip(matrices, names):
            width = matrix.shape[-1] // 2
            cuts = []
            for _ in range(matrix.shape[-2] // rows_group):
                cuts.append(
                    jnp.concatenate([both[0, :, at : at + width], both[1, :, at : at + width]], 1)
                )
                at += width
            results[name] = jnp.concatenate(cuts, 0)

    pending.add(table_task())
    d_second = pending.point(d_second)
    d_second_low = d_second.astype(jnp.bfloat16)
    d_stream, d_gain_final, d_bias_final = final_back(d_final + inner(d_second_low, head_weight))

    vec_list = [None] * layer_count
    for layer_at in reversed(range(layer_count)):

        def first_task(pairs, at=layer_at):
            matrices, names = [mlp_in[at], mlp_out[at]], [("fc", at), ("down", at)]
            if at == layer_count - 1:
                pairs = [(final_low, d_second_low)] + pairs
                matrices = [attn_out[layer_count]] + matrices
                names = [("out", layer_count)] + names
            return bundle_task(pairs, matrices, names, (1, 3) if at else (2, 0))

        def later_task(pairs, at=layer_at):
            names = [("in", at), ("out", at)]
            return bundle_task(
                pairs, [attn_in[at], attn_out[at]], names, (1, 1) if at else (1, 0)
            )

        d_stream, vec_list[layer_at] = layer_backward(
            d_stream,
            kept[layer_at],
            stored[layer_at],
            vectors[12 * layer_at : 12 * layer_at + 12],
            allowed,
            head_count,
            pending,
            first_task,
            later_task,
        )
    part_ids = jnp.arange(part_rows, dtype=jnp.int32)
    part_live = part_ids < rows_dev - core_at * part_rows
    part_ids = jnp.where(part_live, row_low + core_at * part_rows + part_ids, -1)[:, None]

    def spread(low, rows):
        ids = ids_grid[:, low : low + rows.shape[0]]
        hits = (part_ids == ids[0][None]) | (part_ids == ids[1][None])
        return product(hits.astype(jnp.bfloat16), rows)

    mine = d_stream.astype(jnp.bfloat16)
    if near:
        half = own_rows // 2
        def flat(block):
            return block.reshape(-1, feature_width)

        away = pending.point(lax.ppermute(mine, "fsdp", NEAR_SECOND))
        mine = jnp.concatenate([mine, away], 0)
        away = pending.point(lax.ppermute(mine, "fsdp", NEAR_FIRST))
        mine = jnp.concatenate([mine, away], 0).reshape(4, 2, half, feature_width)
        front, back = flat(mine[:, 0]), flat(mine[:, 1])
        front_x, back_y = shift_seq(front, 1), shift_y(back, 1)
        here = jnp.concatenate([front, back], 0)
        here = jnp.concatenate([here, swap_core(here)], 0)
        table_part = results["table"] + spread(0, here)
        done = here.shape[0]
        table_part, front_x, back_y = pending.point((table_part, front_x, back_y))
        front_y = shift_y(jnp.concatenate([front, front_x], 0), 1)
        back_x = shift_seq(jnp.concatenate([back, back_y], 0), 1)
        here = jnp.concatenate([front_x, back_y], 0)
        here = jnp.concatenate([here, swap_core(here)], 0)
        table_part = table_part + spread(done, here)
        done += here.shape[0]
        table_part, front_y, back_x = pending.point((table_part, front_y, back_x))
        here = jnp.concatenate([front_y, back_x], 0)
        here = jnp.concatenate([here, swap_core(here)], 0)
        table_part = table_part + spread(done, here)
        pending.finish()
    else:
        pending.finish()
        embed_back = lax.all_gather(mine, ("seq", "fsdp", "ctx"), axis=0, tiled=True)
        table_part = results["table"] + spread(0, embed_back)
    summed = (
        None,
        jnp.stack([results["in", at] for at in range(layer_count)]),
        jnp.stack([results["out", at] for at in range(layer_count + 1)]),
        jnp.stack([results["fc", at] for at in range(layer_count)]),
        jnp.stack([results["down", at] for at in range(layer_count)]),
    )
    vector_grad = jnp.concatenate(vec_list + [jnp.stack([d_gain_final, d_bias_final])], 0)
    row_states = (attn_in_rows, attn_out_rows, mlp_in_rows, mlp_out_rows)
    table_away = swap_core(table_part)
    state_part = lax.dynamic_slice_in_dim(
        jnp.pad(table_rows, (0, spare)), core_at * part_rows, part_rows, 0
    )
    live_rows = part_live[:, None]
    part_square = table_part * table_part
    part_renewed = DECAY * state_part[:, None] + (1.0 - DECAY) * jnp.mean(
        part_square + EPS_SQUARE, -1, keepdims=True
    )
    part_renewed = jnp.where(live_rows, part_renewed, 1.0)
    away_renewed = swap_core(part_renewed)
    live_count = jnp.sum(part_live.astype(jnp.float32))
    copies = 1.0 / n_y
    rows_new = [
        jnp.concatenate(
            [
                jnp.where(core_at == 0, part_renewed, away_renewed),
                jnp.where(core_at == 0, away_renewed, part_renewed),
            ],
            0,
        )[:rows_dev, 0][None]
    ]
    col_parts = [copies * (jnp.sum(part_square, 0) + EPS_SQUARE * live_count)]
    weighted_parts = [copies * jnp.sum(part_square / part_renewed, 0)]
    row_parts = [copies * jnp.sum(jnp.where(live_rows, part_renewed, 0.0)).reshape(1)]
    for grad_sum, row_state in zip(summed[1:], row_states):
        square = grad_sum * grad_sum
        renewed = DECAY * row_state + (1.0 - DECAY) * jnp.mean(square + EPS_SQUARE, -1)
        rows_new.append(renewed)
        col_parts.append(share * jnp.sum(square + EPS_SQUARE, -2))
        weighted_parts.append(share * jnp.sum(square / renewed[..., None], -2))
        row_parts.append(share * jnp.sum(renewed, -1))
    numbers = jnp.concatenate(
        row_parts + square_parts + [loss_part.reshape(1), jnp.stack(squares).reshape(-1)]
    )
    row_count = sum(part.shape[0] for part in row_parts)
    numbers = jnp.pad(numbers, (0, feature_width - numbers.shape[0]))
    col_rows = [part.reshape(-1, feature_width) for part in col_parts]
    weighted_rows = [part.reshape(-1, feature_width) for part in weighted_parts]
    col_count = sum(part.shape[0] for part in col_rows)
    everything = jnp.concatenate(col_rows + weighted_rows + [numbers[None], vector_grad], 0)
    everything = sum_all(jnp.pad(everything, ((0, -everything.shape[0] % 8), (0, 0))))
    numbers = everything[2 * col_count]
    vector_sum = everything[2 * col_count + 1 : 2 * col_count + 1 + vector_grad.shape[0]]
    loss_sum = numbers[row_count + 5]
    square_total = numbers[row_count + 6 : row_count + 6 + 3 * layer_count]
    matrices = (table[None], attn_in, attn_out, mlp_in, mlp_out)
    col_states = (table_cols[None], attn_in_cols, attn_out_cols, mlp_in_cols, mlp_out_cols)
    row_totals = [rows_dev * n_group] + [weight.shape[1] * n_group for weight in matrices[1:]]
    shares = jnp.concatenate(
        [
            jnp.full((rows.shape[0], 1), (1.0 - DECAY) / row_total, jnp.float32)
            for rows, row_total in zip(col_rows, row_totals)
        ],
        0,
    )
    old_cols = jnp.concatenate([state.reshape(-1, feature_width) for state in col_states], 0)
    new_cols = DECAY * old_cols + shares * everything[:col_count]
    ratios = jnp.sum(everything[col_count : 2 * col_count] / new_cols, -1)
    cols_new = []
    new_weights = []
    sizes_rms = []
    col_at = 0
    row_at = 0
    for matrix_at in range(5):
        weight, renewed, col_state = matrices[matrix_at], rows_new[matrix_at], col_states[matrix_at]
        stack_count = weight.shape[0]
        height = col_rows[matrix_at].shape[0]
        renewed_cols = new_cols[col_at : col_at + height].reshape(col_state.shape)
        row_mean = numbers[row_at : row_at + stack_count] / row_totals[matrix_at]
        row_at += stack_count
        ratio = jnp.sum(ratios[col_at : col_at + height].reshape(stack_count, -1), -1)
        col_at += height
        clip_total = jnp.sum(row_mean * ratio)
        entries = weight.size * n_group
        update_rms = jnp.sqrt(clip_total / entries)
        weight_rms = jnp.sqrt(numbers[row_count + matrix_at] / entries)
        step_scale = RATE * jnp.maximum(EPS_SCALE, weight_rms) / jnp.maximum(1.0, update_rms / CLIP)
        cols_new.append(renewed_cols)
        sizes_rms.append(update_rms)
        if matrix_at == 0:
            table_sum, table_new, table_copy = update_table(
                core_at.astype(jnp.int32).reshape(1),
                step_scale.reshape(1),
                table_part,
                table_away,
                part_renewed,
                away_renewed,
                renewed_cols / row_mean[0],
                table,
            )
            new_weights.append(table_new)
            continue
        second_moment = renewed[:, :, None] * renewed_cols[:, None, :] / row_mean[:, None, None]
        update = summed[matrix_at] * lax.rsqrt(second_moment)
        new_weights.append(weight - step_scale * update)
    vector_state_new = DECAY * vector_state + (1.0 - DECAY) * (vector_sum * vector_sum + EPS_SQUARE)
    vector_update = vector_sum * lax.rsqrt(vector_state_new)
    vector_rms = jnp.sqrt(jnp.mean(vector_update * vector_update))
    vector_scale = (
        RATE
        * jnp.maximum(EPS_SCALE, jnp.sqrt(jnp.mean(vectors * vectors)))
        / jnp.maximum(1.0, vector_rms / CLIP)
    )
    vectors_new = vectors - vector_scale * vector_update
    sizes_rms.append(vector_rms)
    norms = jnp.concatenate([jnp.sqrt(square_total / total_tokens), jnp.stack(sizes_rms)])
    return (
        loss_sum,
        norms,
        table_sum,
        rows_new[0][0],
        cols_new[0][0],
        table_new,
        table_copy,
        summed[1],
        rows_new[1],
        cols_new[1],
        new_weights[1],
        new_weights[1].astype(jnp.bfloat16),
        summed[2],
        rows_new[2],
        cols_new[2],
        new_weights[2],
        new_weights[2].astype(jnp.bfloat16),
        summed[3],
        rows_new[3],
        cols_new[3],
        new_weights[3],
        new_weights[3].astype(jnp.bfloat16),
        summed[4],
        rows_new[4],
        cols_new[4],
        new_weights[4],
        new_weights[4].astype(jnp.bfloat16),
        vector_sum,
        vector_state_new,
        vectors_new,
    )


def solution(mesh):
    return jax.shard_map(
        body,
        mesh=mesh,
        in_specs=(
            P(),
            P(),
            P(),
            P(),
            P(("seq", "fsdp"), None),
            P(None, ("seq", "fsdp"), None),
            P(None, ("seq", "fsdp"), None),
            P(None, ("seq", "fsdp"), None),
            P(None, ("seq", "fsdp"), None),
            P(),
            P(("seq", "fsdp")),
            P(),
            P(None, ("seq", "fsdp")),
            P(),
            P(None, ("seq", "fsdp")),
            P(),
            P(None, ("seq", "fsdp")),
            P(),
            P(None, ("seq", "fsdp")),
            P(),
            P(),
        ),
        out_specs=(
            P(),
            P(),
            P(("seq", "fsdp"), None),
            P(("seq", "fsdp")),
            P(),
            P(("seq", "fsdp"), None),
            P(("seq", "fsdp"), None),
            P(None, ("seq", "fsdp"), None),
            P(None, ("seq", "fsdp")),
            P(),
            P(None, ("seq", "fsdp"), None),
            P(None, ("seq", "fsdp"), None),
            P(None, ("seq", "fsdp"), None),
            P(None, ("seq", "fsdp")),
            P(),
            P(None, ("seq", "fsdp"), None),
            P(None, ("seq", "fsdp"), None),
            P(None, ("seq", "fsdp"), None),
            P(None, ("seq", "fsdp")),
            P(),
            P(None, ("seq", "fsdp"), None),
            P(None, ("seq", "fsdp"), None),
            P(None, ("seq", "fsdp"), None),
            P(None, ("seq", "fsdp")),
            P(),
            P(None, ("seq", "fsdp"), None),
            P(None, ("seq", "fsdp"), None),
            P(),
            P(),
            P(),
        ),
        check_vma=False,
    )
```

```python
import functools

import jax
import jax.numpy as jnp
from jax import lax
from jax.experimental import pallas as pl
from jax.experimental.pallas import tpu as pltpu
from jax.sharding import PartitionSpec as P

HEADS = 12
VOCAB = 50304


EPS_NORM = 1e-05
EPS_SQUARE = 1e-30
EPS_SCALE = 0.001
DECAY = 0.5
CLIP = 0.4
RATE = 0.6
SECOND = 0.3
MASKED = -1e30
VMEM_BYTES = 56 * 1024 * 1024
NEAR_FIRST = [(0, 1), (1, 0), (2, 3), (3, 2)]
NEAR_SECOND = [(0, 3), (3, 0), (1, 2), (2, 1)]


def layer_norm(stream, gain, offset):
    center = stream - jnp.mean(stream, -1, keepdims=True)
    spread = jnp.mean(center * center, -1, keepdims=True)
    return center * lax.rsqrt(spread + EPS_NORM) * gain + offset


def gelu_tanh(value):
    return jax.nn.gelu(value, approximate=True)


def positions_of(segments):
    steps_at = jnp.arange(segments.shape[-1], dtype=jnp.int32)
    before = jnp.concatenate(
        [jnp.full(segments.shape[:-1] + (1,), -2, jnp.int32), segments[..., :-1]], -1
    )
    starts = jnp.where(segments != before, steps_at, 0)
    first = lax.cummax(starts, axis=segments.ndim - 1)
    return jnp.where(segments >= 0, steps_at - first, 0)


def product(left, right):
    return jnp.dot(left, right, preferred_element_type=jnp.float32)


def inner(left, right):
    return lax.dot_general(
        left, right, (((1,), (1,)), ((), ())), preferred_element_type=jnp.float32
    )


def outer(left, right):
    return lax.dot_general(
        left, right, (((0,), (0,)), ((), ())), preferred_element_type=jnp.float32
    )


def shift(block, axis, step):
    count = lax.axis_size(axis)
    return lax.ppermute(block, axis, [(i, (i + step) % count) for i in range(count)])


def shift_y(block, step):
    count = lax.axis_size("ctx")
    return lax.ppermute(block, "ctx", [(i, (i + 2 * step) % count) for i in range(count)])


def swap_core(block):
    count = lax.axis_size("ctx")
    return lax.ppermute(block, "ctx", [(i, i ^ 1) for i in range(count)])


def shift_seq(block, step):
    return shift(block, "seq", step)


def shift_fsdp(block, step):
    return shift(block, "fsdp", step)


def pick(parts, at, axis):
    return lax.dynamic_index_in_dim(parts, at, axis, False)


def send_parts(parts, mover, at, axis=0, sent=None):
    count = parts.shape[axis]
    moving = []
    for step in range(1, count):
        piece = pick(parts, lax.rem(at + step, count), axis)
        moving.append(mover(piece if sent is None else piece.astype(sent), step))
    return moving


def add_parts(parts, moved, at, axis=0):
    total = pick(parts, at, axis)
    for piece in moved:
        total = total + piece.astype(total.dtype)
    return total


def scatter_sum(parts, mover, at, axis=0, sent=None):
    return add_parts(parts, send_parts(parts, mover, at, axis, sent), at, axis)


def scatter_fsdp(parts, at):
    count = parts.shape[0]
    if count != 4:
        moved = yield 0, send_parts(parts, shift_fsdp, at, sent=jnp.bfloat16)
        return add_parts(parts, moved, at)
    outside = (at == 0) | (at == 3)
    mine = [jnp.where(outside, 0, 1), jnp.where(outside, 3, 2)]
    other = [jnp.where(outside, 1, 0), jnp.where(outside, 2, 3)]
    away = jnp.stack([pick(parts, slot, 0) for slot in other]).astype(jnp.bfloat16)
    (away,) = yield 0, [lax.ppermute(away, "fsdp", NEAR_FIRST)]
    first, second = (
        pick(parts, slot, 0) + away[k].astype(parts.dtype) for k, slot in enumerate(mine)
    )
    away = jnp.where(at < 2, second, first).astype(jnp.bfloat16)
    (away,) = yield 0, [lax.ppermute(away, "fsdp", NEAR_SECOND)]
    return jnp.where(at < 2, first, second) + away.astype(parts.dtype)


def run(task):
    moving = next(task)[1]
    while True:
        try:
            moving = task.send(moving)[1]
        except StopIteration as stop:
            return stop.value


def sum_hops(block, skip_y=False):
    for axis in ("ctx", "seq", "fsdp"):
        whole = lax.axis_size(axis)
        count = 2 if skip_y and axis == "ctx" else whole
        hop = 1
        while hop < count:
            moved = yield lax.ppermute(block, axis, [(i, i ^ hop) for i in range(whole)])
            block = block + moved
            hop *= 2
    return block


def sum_all(block, skip_y=False):
    hops = sum_hops(block, skip_y)
    moved = next(hops)
    while True:
        try:
            moved = hops.send(moved)
        except StopIteration as stop:
            return stop.value


def order_parts(parts, at):
    count = len(parts)
    if count == 2:
        first, second = parts
        return jnp.stack([jnp.where(at == 0, first, second), jnp.where(at == 0, second, first)])
    order = lax.rem(at - jnp.arange(count, dtype=jnp.int32) + count, count)
    return jnp.take(jnp.stack(parts), order, axis=0, mode="clip")


def gather_near(block):
    n_y = lax.axis_size("ctx") // 2
    column = jnp.concatenate([block] + [shift_y(block, step) for step in range(1, n_y)], 0)
    return jnp.concatenate([column, swap_core(column)], 0)


def scatter_near(parts):
    n_y = lax.axis_size("ctx") // 2
    parts = parts.reshape((2, n_y, -1) + parts.shape[1:])
    column = parts[0] + swap_core(parts[1])
    total = column[0]
    for step in range(1, n_y):
        away = shift_y(column[step].astype(jnp.bfloat16), n_y - step)
        total = total + away.astype(total.dtype)
    return total


def half_of(block, at):
    width = block.shape[-1] // 2
    return jnp.where(at == 0, block[..., :width], block[..., width:])


def qkv_bias(vec):
    return jnp.concatenate([vec[2], jnp.zeros_like(vec[2]), vec[3]])


def attention_scores(query_low, keys, allowed, head_count):
    row_count, feature_width = query_low.shape
    head_size = feature_width // head_count
    scores = jnp.einsum(
        "qhd,khd->hqk",
        query_low.reshape(row_count, head_count, head_size),
        keys.reshape(-1, head_count, head_size),
        preferred_element_type=jnp.float32,
    ) * head_size ** (-0.5)
    return jnp.where(allowed[None], scores, MASKED)


def mix_values(probs_low, values, head_count):
    head_size = values.shape[1] // head_count
    mixed = jnp.einsum(
        "hqk,khd->qhd",
        probs_low,
        values.reshape(-1, head_count, head_size),
        preferred_element_type=jnp.float32,
    )
    return mixed.reshape(mixed.shape[0], -1)


def layer_forward(stream, weights, vec, allowed, head_count):
    w_in, w_out, w_fc, w_down = weights
    feature_width = stream.shape[1]
    a_low = layer_norm(stream, vec[0], vec[1]).astype(jnp.bfloat16)
    qkv_low = (product(a_low, w_in) + qkv_bias(vec)).astype(jnp.bfloat16)
    pairs = gather_near(qkv_low[:, feature_width:])
    keys, values = pairs[:, :feature_width], pairs[:, feature_width:]
    scores = attention_scores(qkv_low[:, :feature_width], keys, allowed, head_count)
    row_max = jnp.max(scores, -1)
    log_total = row_max + jnp.log(jnp.sum(jnp.exp(scores - row_max[..., None]), -1))
    probs = jnp.exp(scores - log_total[..., None])
    mixed_low = mix_values(probs.astype(jnp.bfloat16), values, head_count).astype(jnp.bfloat16)
    branch = product(mixed_low, w_out) + vec[4]
    middle = stream + branch
    m_low = layer_norm(middle, vec[5], vec[6]).astype(jnp.bfloat16)
    hidden = product(m_low, w_fc) + vec[8:12].reshape(-1)
    output = product(gelu_tanh(hidden).astype(jnp.bfloat16), w_down) + vec[7]
    sums = jnp.stack([jnp.sum(stream * stream), jnp.sum(branch * branch), jnp.sum(output * output)])
    kept = (stream, a_low, qkv_low, keys, values, log_total, mixed_low, middle, m_low, hidden)
    return (middle + output, kept, sums)


def swap_pairs(pairs, core_at):
    lefts = [left for left, _ in pairs]
    return swap_core(
        jnp.concatenate(lefts + [half_of(right, 1 - core_at) for _, right in pairs], 1)
    )


def shared_outer(pairs, away, core_at):
    at = 0
    whole_left = []
    for left, _ in pairs:
        whole_left.append(jnp.concatenate([left, away[:, at : at + left.shape[1]]], 0))
        at += left.shape[1]
    grads = []
    for left, (_, right) in zip(whole_left, pairs):
        width = right.shape[1] // 2
        whole_right = jnp.concatenate([half_of(right, core_at), away[:, at : at + width]], 0)
        at += width
        grads.append(outer(left, whole_right))
    return grads


def layer_backward(d_stream, kept, weights, vec, allowed, head_count, pending, first_task, later_task):
    stream, a_low, qkv_low, keys, values, log_total, mixed_low, middle, m_low, hidden = kept
    w_in, w_out, w_fc, w_down = weights
    row_count, feature_width = stream.shape
    head_size = feature_width // head_count
    scale = head_size ** (-0.5)
    norm_back_one = jax.vjp(layer_norm, stream, vec[0], vec[1])[1]
    query_low = qkv_low[:, :feature_width]
    probs = jnp.exp(attention_scores(query_low, keys, allowed, head_count) - log_total[..., None])
    probs_low = probs.astype(jnp.bfloat16)
    norm_back_two = jax.vjp(layer_norm, middle, vec[5], vec[6])[1]
    gelu_out, gelu_back = jax.vjp(gelu_tanh, hidden)
    u_low = gelu_out.astype(jnp.bfloat16)
    d_out_low = d_stream.astype(jnp.bfloat16)
    d_hidden_low = gelu_back(inner(d_out_low, w_down))[0].astype(jnp.bfloat16)
    d_hidden_low = pending.point(d_hidden_low)
    pending.add(first_task([(m_low, d_hidden_low), (u_low, d_out_low)]))
    d_m = inner(d_hidden_low, w_fc)
    d_two, d_gain_two, d_bias_two = norm_back_two(d_m)
    d_middle = d_stream + d_two
    d_middle = pending.point(d_middle)
    d_middle_low = d_middle.astype(jnp.bfloat16)
    d_heads = (
        inner(d_middle_low, w_out).astype(jnp.bfloat16).reshape(row_count, head_count, head_size)
    )
    value_heads = values.reshape(-1, head_count, head_size)
    d_probs = jnp.einsum("qhd,khd->hqk", d_heads, value_heads, preferred_element_type=jnp.float32)
    d_scores = (probs * (d_probs - jnp.sum(probs * d_probs, -1, keepdims=True))).astype(
        jnp.bfloat16
    )
    d_scores = pending.point(d_scores)
    d_query = (
        jnp.einsum(
            "hqk,khd->qhd",
            d_scores,
            keys.reshape(-1, head_count, head_size),
            preferred_element_type=jnp.float32,
        ).reshape(row_count, feature_width)
        * scale
    )
    d_keys = (
        jnp.einsum(
            "hqk,qhd->khd",
            d_scores,
            query_low.reshape(row_count, head_count, head_size),
            preferred_element_type=jnp.float32,
        ).reshape(-1, feature_width)
        * scale
    )
    d_values = jnp.einsum(
        "hqk,qhd->khd", probs_low, d_heads, preferred_element_type=jnp.float32
    ).reshape(-1, feature_width)
    d_pairs = scatter_near(jnp.concatenate([d_keys, d_values], 1))
    d_qkv_low = jnp.concatenate([d_query, d_pairs], 1).astype(jnp.bfloat16)
    d_qkv_low = pending.point(d_qkv_low)
    pending.add(later_task([(a_low, d_qkv_low), (mixed_low, d_middle_low)]))
    d_one, d_gain_one, d_bias_one = norm_back_one(inner(d_qkv_low, w_in))
    d_qkv = d_qkv_low.astype(jnp.float32)
    rows_head = jnp.stack(
        [
            d_gain_one,
            d_bias_one,
            jnp.sum(d_qkv[:, :feature_width], 0),
            jnp.sum(d_qkv[:, 2 * feature_width :], 0),
            jnp.sum(d_middle_low.astype(jnp.float32), 0),
            d_gain_two,
            d_bias_two,
            jnp.sum(d_out_low.astype(jnp.float32), 0),
        ]
    )
    vec_grad = jnp.concatenate(
        [rows_head, jnp.sum(d_hidden_low.astype(jnp.float32), 0).reshape(4, feature_width)], 0
    )
    return (pending.point(d_middle + d_one), vec_grad)


def merge_stats(stats):
    for mover, axis in ((shift_seq, "seq"), (shift_fsdp, "fsdp")):
        parts = [stats] + [mover(stats, step) for step in range(1, lax.axis_size(axis))]
        top = parts[0][0]
        for part in parts[1:]:
            top = jnp.maximum(top, part[0])
        total = jnp.exp(parts[0][0] - top)
        picked = parts[0][1]
        for part in parts[1:]:
            total = total + jnp.exp(part[0] - top)
            picked = picked + part[1]
        stats = jnp.stack([top + jnp.log(total), picked])
    return stats


def blocks_of(groups, width, row_block):
    step = max(1, row_block // width)
    return [
        (range(low, low + step), slice(low * width, (low + step) * width))
        for low in range(0, groups, step)
    ]


def side_by_side(ref, at_block):
    return jnp.concatenate([ref[at] for at in at_block], 1)


def masked_logits(logits, live, first):
    column = lax.broadcasted_iota(jnp.int32, logits.shape, 0) + first
    return jnp.where(column < live, logits, MASKED)


def stats_kernel(row_block, live_ref, table_ref, rows_ref, target_ref, out_ref, top_ref, sum_ref, pick_ref):
    at = pl.program_id(0)
    tile = table_ref.shape[0]
    first = at * tile
    live = live_ref[0]

    @pl.when(at == 0)
    def _():
        top_ref[...] = jnp.full_like(top_ref, MASKED)
        sum_ref[...] = jnp.zeros_like(sum_ref)
        pick_ref[...] = jnp.zeros_like(pick_ref)

    def step(masked):
        for at_block, here in blocks_of(rows_ref.shape[0], rows_ref.shape[2], row_block):
            logits = jnp.dot(
                table_ref[...], side_by_side(rows_ref, at_block), preferred_element_type=jnp.float32
            )
            if masked:
                logits = masked_logits(logits, live, first)
            column = lax.broadcasted_iota(jnp.int32, logits.shape, 0)
            hit = column == target_ref[:, here] - first
            cut = logits.reshape(tile // 8, 8, logits.shape[1])
            top = top_ref[:, here]
            joint = jnp.maximum(top, jnp.max(cut, 0))
            total = jnp.sum(jnp.exp(cut - joint[None]), 0)
            sum_ref[:, here] = sum_ref[:, here] * jnp.exp(top - joint) + total
            top_ref[:, here] = joint
            pick_ref[:, here] += jnp.sum(
                jnp.where(hit, logits, 0.0).reshape(cut.shape), 0
            )

    @pl.when(first + tile <= live)
    def _():
        step(False)

    @pl.when((first + tile > live) & (first < live))
    def _():
        step(True)

    @pl.when(at == pl.num_programs(0) - 1)
    def _():
        top = top_ref[...]
        joint = jnp.max(top, 0, keepdims=True)
        total = jnp.sum(sum_ref[...] * jnp.exp(top - joint), 0, keepdims=True)
        out_ref[0:1, :] = joint + jnp.log(total)
        out_ref[1:2, :] = jnp.sum(pick_ref[...], 0, keepdims=True)


def head_stats(live, table_low, rows_t, target, tile=512, row_block=512):
    groups, depth, width = rows_t.shape
    count = groups * width
    height = table_low.shape[0]
    return pl.pallas_call(
        functools.partial(stats_kernel, row_block),
        out_shape=jax.ShapeDtypeStruct((2, count), jnp.float32),
        grid=(height // tile,),
        in_specs=[
            pl.BlockSpec(memory_space=pltpu.SMEM),
            pl.BlockSpec((tile, depth), lambda i: (i, 0)),
            pl.BlockSpec((groups, depth, width), lambda i: (0, 0, 0)),
            pl.BlockSpec((1, count), lambda i: (0, 0)),
        ],
        out_specs=pl.BlockSpec((2, count), lambda i: (0, 0)),
        scratch_shapes=[pltpu.VMEM((8, count), jnp.float32)] * 3,
        compiler_params=pltpu.CompilerParams(vmem_limit_bytes=VMEM_BYTES),
        cost_estimate=pl.CostEstimate(
            flops=2 * height * depth * count,
            bytes_accessed=2 * height * depth + 2 * depth * count,
            transcendentals=height * count,
        ),
    )(live, table_low, rows_t, target)


def back_kernel(row_block, added, live_ref, table_ref, table_t_ref, rows_ref, rows_t_ref, line_ref, *refs):
    if added:
        prior_ref, grad_ref, d_rows_ref = refs
    else:
        grad_ref, d_rows_ref = refs
    at = pl.program_id(0)
    tile = table_ref.shape[0]
    first = at * tile
    live = live_ref[0]
    width = d_rows_ref.shape[2]

    @pl.when(at == 0)
    def _():
        d_rows_ref[...] = jnp.zeros_like(d_rows_ref)

    def step(masked):
        grad = prior_ref[...] if added else None
        for at_block, here in blocks_of(rows_t_ref.shape[0], width, row_block):
            logits = jnp.dot(
                table_ref[...],
                side_by_side(rows_t_ref, at_block),
                preferred_element_type=jnp.float32,
            )
            if masked:
                logits = masked_logits(logits, live, first)
            column = lax.broadcasted_iota(jnp.int32, logits.shape, 0).astype(jnp.float32)
            probs = jnp.exp(logits - line_ref[0:1, here])
            hit = column == line_ref[2:3, here] - first.astype(jnp.float32)
            d_low = (line_ref[1:2, here] * jnp.where(hit, probs - 1.0, probs)).astype(jnp.bfloat16)
            rows = rows_ref[at_block.start : at_block.stop].reshape(-1, rows_ref.shape[2])
            part = jnp.dot(d_low, rows, preferred_element_type=jnp.float32)
            grad = part if grad is None else grad + part
            d_part = jnp.dot(table_t_ref[...], d_low, preferred_element_type=jnp.float32)
            for at_width, at_group in enumerate(at_block):
                d_rows_ref[at_group] += d_part[:, at_width * width : (at_width + 1) * width]
        grad_ref[...] = grad

    @pl.when(first + tile <= live)
    def _():
        step(False)

    @pl.when((first + tile > live) & (first < live))
    def _():
        step(True)

    @pl.when(first >= live)
    def _():
        grad_ref[...] = prior_ref[...] if added else jnp.zeros_like(grad_ref)


def head_back(live, table_low, table_t, rows, rows_t, line, cut=0, prior=None, tile=512):
    groups, _, depth = rows.shape
    height = table_low.shape[0]
    count = line.shape[1]
    width = count // groups
    once = dict(pipeline_mode=pl.Buffered(1))
    grad_spec = pl.BlockSpec((tile, depth), lambda i: (i, 0))
    added = prior is not None
    return pl.pallas_call(
        functools.partial(back_kernel, 1024, added),
        out_shape=(
            jax.ShapeDtypeStruct((height, depth), jnp.float32),
            jax.ShapeDtypeStruct((groups, depth, width), jnp.float32),
        ),
        grid=(height // tile,),
        in_specs=[
            pl.BlockSpec(memory_space=pltpu.SMEM),
            pl.BlockSpec((tile, depth), lambda i: (i, 0)),
            pl.BlockSpec((depth, tile), lambda i: (0, i)),
            pl.BlockSpec((groups, width, depth), lambda i: (0, cut, 0), **once),
            pl.BlockSpec((groups, depth, width), lambda i: (0, 0, cut), **once),
            pl.BlockSpec((3, count), lambda i: (0, 0), **once),
        ]
        + ([grad_spec] if added else []),
        out_specs=(
            grad_spec,
            pl.BlockSpec((groups, depth, width), lambda i: (0, 0, 0), **once),
        ),
        input_output_aliases={6: 0} if added else {},
        compiler_params=pltpu.CompilerParams(vmem_limit_bytes=VMEM_BYTES),
        cost_estimate=pl.CostEstimate(
            flops=6 * height * depth * count,
            bytes_accessed=4 * height * depth + 12 * depth * count + 8 * height * depth,
            transcendentals=height * count,
        ),
    )(live, table_low, table_t, rows, rows_t, line, *((prior,) if added else ()))


def prepare_kernel(row_count, table_ref, low_ref, turned_ref, square_ref):
    at = pl.program_id(0)
    tile = table_ref.shape[0]
    row = lax.broadcasted_iota(jnp.int32, table_ref.shape, 0) + at * tile
    block = jnp.where(row < row_count, table_ref[...], 0.0)
    low_ref[...] = block.astype(jnp.bfloat16)
    turned_ref[...] = block.T.astype(jnp.bfloat16)
    part = jnp.sum((block * block).reshape(tile // 8, 8, block.shape[1]), 0)

    @pl.when(at == 0)
    def _():
        square_ref[...] = part

    @pl.when(at > 0)
    def _():
        square_ref[...] += part


def prepare_table(table, height, tile=512):
    row_count, depth = table.shape
    return pl.pallas_call(
        functools.partial(prepare_kernel, row_count),
        out_shape=(
            jax.ShapeDtypeStruct((height, depth), jnp.bfloat16),
            jax.ShapeDtypeStruct((depth, height), jnp.bfloat16),
            jax.ShapeDtypeStruct((8, depth), jnp.float32),
        ),
        grid=(height // tile,),
        in_specs=[pl.BlockSpec((tile, depth), lambda i: (i, 0))],
        out_specs=(
            pl.BlockSpec((tile, depth), lambda i: (i, 0)),
            pl.BlockSpec((depth, tile), lambda i: (0, i)),
            pl.BlockSpec((8, depth), lambda i: (0, 0)),
        ),
        compiler_params=pltpu.CompilerParams(vmem_limit_bytes=VMEM_BYTES),
        cost_estimate=pl.CostEstimate(
            flops=2 * row_count * depth,
            bytes_accessed=4 * row_count * depth + 4 * height * depth,
            transcendentals=0,
        ),
    )(table)


def update_kernel(used, core_ref, scale_ref, mine_ref, away_ref, mine_rows_ref, away_rows_ref, cols_ref, weight_ref, *outs):
    grad_ref, new_ref, copy_ref = outs
    half = pl.program_id(0) // (pl.num_programs(0) // 2)
    chosen = half == core_ref[0]
    grad = jnp.where(chosen, mine_ref[...], away_ref[...])
    rows = jnp.where(chosen, mine_rows_ref[...], away_rows_ref[...])
    update = grad * lax.rsqrt(rows * cols_ref[...])
    new = weight_ref[...] - scale_ref[0] * update

    @pl.when(pl.program_id(0) < used)
    def _():
        grad_ref[...] = grad
        new_ref[...] = new
        copy_ref[...] = new.astype(copy_ref.dtype)


def update_table(core, scale, mine, away, mine_rows, away_rows, cols, weight):
    row_count, depth = weight.shape
    tile = mine.shape[0] // 4
    steps = mine.shape[0] // tile
    used = -(-row_count // tile)

    def mine_at(i, core_ref):
        return (jnp.clip(i - core_ref[0] * steps, 0, steps - 1), 0)

    def away_at(i, core_ref):
        return (jnp.clip(i - (1 - core_ref[0]) * steps, 0, steps - 1), 0)

    def whole_at(i, core_ref):
        return (jnp.minimum(i, used - 1), 0)

    whole = pl.BlockSpec((tile, depth), whole_at)
    return pl.pallas_call(
        functools.partial(update_kernel, used),
        out_shape=(
            jax.ShapeDtypeStruct(weight.shape, jnp.float32),
            jax.ShapeDtypeStruct(weight.shape, jnp.float32),
            jax.ShapeDtypeStruct(weight.shape, jnp.bfloat16),
        ),
        grid_spec=pltpu.PrefetchScalarGridSpec(
            num_scalar_prefetch=1,
            grid=(2 * steps,),
            in_specs=[
                pl.BlockSpec(memory_space=pltpu.SMEM),
                pl.BlockSpec((tile, depth), mine_at),
                pl.BlockSpec((tile, depth), away_at),
                pl.BlockSpec((tile, 1), mine_at),
                pl.BlockSpec((tile, 1), away_at),
                pl.BlockSpec((1, depth), lambda i, core_ref: (0, 0)),
                whole,
            ],
            out_specs=(whole, whole, whole),
        ),
        compiler_params=pltpu.CompilerParams(vmem_limit_bytes=VMEM_BYTES),
        cost_estimate=pl.CostEstimate(
            flops=6 * row_count * depth,
            bytes_accessed=18 * row_count * depth,
            transcendentals=row_count * depth,
        ),
    )(core, scale, mine, away, mine_rows, away_rows, cols, weight)


class Pending:
    def __init__(self):
        self.active = []

    def add(self, task):
        held, moving = next(task)
        self.active.append([task, held, moving])

    def point(self, main):
        ready = [entry for entry in self.active if entry[1] == 0]
        main, moved = lax.optimization_barrier((main, [entry[2] for entry in ready]))
        for entry in self.active:
            entry[1] -= 1
        for entry, arrived in zip(ready, moved):
            self.advance(entry, arrived)
        return main

    def advance(self, entry, arrived):
        try:
            entry[1:] = entry[0].send(arrived)
        except StopIteration:
            self.active.remove(entry)

    def finish(self):
        while self.active:
            entry = self.active[0]
            self.advance(entry, entry[2])


def local_index(ids, row_low, row_count):
    shifted = ids - row_low
    inside = (shifted >= 0) & (shifted < row_count)
    return (inside, jnp.clip(shifted, 0, row_count - 1))


def body(
    tokens,
    segments,
    next_ids,
    second_ids,
    table,
    attn_in,
    attn_out,
    mlp_in,
    mlp_out,
    vectors,
    table_rows,
    table_cols,
    attn_in_rows,
    attn_in_cols,
    attn_out_rows,
    attn_out_cols,
    mlp_in_rows,
    mlp_in_cols,
    mlp_out_rows,
    mlp_out_cols,
    vector_state,
):
    n_ctx = lax.axis_size("ctx")
    n_seq = lax.axis_size("seq")
    n_fsdp = lax.axis_size("fsdp")
    n_y = n_ctx // 2
    n_group = n_seq * n_fsdp
    ctx_at = lax.axis_index("ctx")
    seq_at = lax.axis_index("seq")
    fsdp_at = lax.axis_index("fsdp")
    y_at = ctx_at // 2
    core_at = lax.rem(ctx_at, 2)
    group_at = seq_at * n_fsdp + fsdp_at
    all_seqs, length = segments.shape
    seqs_dev = all_seqs // n_group
    ctx_span = length // n_ctx
    feature_width = table.shape[1]
    layer_count = attn_in.shape[0]
    head_count = HEADS
    total_tokens = all_seqs * length
    own_rows = seqs_dev * ctx_span
    block_start = ctx_at * ctx_span
    positions = positions_of(segments)

    def block_of(grid):
        return lax.dynamic_slice_in_dim(grid, block_start, ctx_span, 1)

    tok_block = block_of(tokens).reshape(-1)
    valid_block = (block_of(segments) >= 0).astype(jnp.float32).reshape(-1)
    next_block = block_of(next_ids).reshape(-1)
    second_block = block_of(second_ids).reshape(-1)
    my_segments = lax.dynamic_slice_in_dim(segments, group_at * seqs_dev, seqs_dev, 0)
    my_positions = lax.dynamic_slice_in_dim(positions, group_at * seqs_dev, seqs_dev, 0)
    hops = jnp.asarray([(side, step) for side in range(2) for step in range(n_y)], jnp.int32)
    near_ctx = 2 * lax.rem(y_at - hops[:, 1] + n_y, n_y) + lax.rem(core_at + hops[:, 0], 2)

    def near_order(grid):
        cut = grid.reshape(seqs_dev, n_ctx, ctx_span).transpose(1, 0, 2)
        return jnp.take(cut, near_ctx, axis=0, mode="clip").reshape(-1)

    def own_order(grid):
        return block_of(grid).reshape(-1)

    time_grid = jnp.broadcast_to(jnp.arange(length, dtype=jnp.int32)[None], (seqs_dev, length))
    seq_grid = jnp.broadcast_to(jnp.arange(seqs_dev, dtype=jnp.int32)[:, None], (seqs_dev, length))
    q_seg, k_seg = (own_order(my_segments), near_order(my_segments))
    q_time, k_time = (own_order(time_grid), near_order(time_grid))
    q_seq, k_seq = (own_order(seq_grid), near_order(seq_grid))
    allowed = (q_seq[:, None] == k_seq[None]) & (
        (q_time[:, None] == k_time[None])
        | (k_time[None] < q_time[:, None]) & (q_seg[:, None] == k_seg[None]) & (k_seg[None] >= 0)
    )
    rows_dev = table.shape[0]
    row_low = group_at * rows_dev
    rows_group = attn_in.shape[1]
    rows_part = rows_group // n_ctx
    down_cut = mlp_out.shape[1] // rows_group

    in_width, out_width, fc_width = attn_in.shape[2], attn_out.shape[2], mlp_in.shape[2]
    pack_width = in_width + out_width + fc_width + down_cut * feature_width
    part_width = pack_width // n_ctx
    model_rows = n_group * rows_group

    def gather_pack(layer_at):
        down = mlp_out[layer_at].reshape(down_cut, rows_group, feature_width)
        pack = jnp.concatenate(
            [attn_in[layer_at], mlp_in[layer_at], attn_out[layer_at]]
            + [down[cut] for cut in range(down_cut)],
            1,
        ).astype(jnp.bfloat16)
        part = lax.dynamic_slice_in_dim(pack, ctx_at * part_width, part_width, 1)
        if layer_at == layer_count - 1:
            head = lax.dynamic_slice_in_dim(
                attn_out[layer_count].astype(jnp.bfloat16), ctx_at * rows_part, rows_part, 0
            )
            head = jnp.pad(head.reshape(-1), (0, -head.size % part_width)).reshape(-1, part_width)
            part = jnp.concatenate([part, head], 0)
        return lax.all_gather(part, ("ctx", "seq", "fsdp"), axis=0)

    def cut_pack(layer_at, whole):
        whole = whole.reshape(n_ctx, n_group, -1, part_width)
        body_rows = whole[:, :, :rows_group].reshape(n_ctx, model_rows, part_width)

        def columns_of(low, high):
            pieces = []
            for at in range(n_ctx):
                start, stop = max(low, at * part_width), min(high, (at + 1) * part_width)
                if start < stop:
                    pieces.append(body_rows[at, :, start - at * part_width : stop - at * part_width])
            return pieces[0] if len(pieces) == 1 else jnp.concatenate(pieces, 1)

        at = in_width + fc_width
        down = jnp.stack(
            [
                columns_of(low, low + feature_width).reshape(n_group, rows_group, feature_width)
                for low in range(at + out_width, pack_width, feature_width)
            ],
            1,
        )
        weights = (
            columns_of(0, in_width),
            columns_of(at, at + out_width),
            columns_of(in_width, at),
            down.reshape(-1, feature_width),
        )
        head = None
        if layer_at == layer_count - 1:
            head = whole[:, :, rows_group:].reshape(n_ctx, n_group, -1)
            head = head[:, :, : rows_part * out_width].reshape(n_ctx, n_group, rows_part, out_width)
            head = head.transpose(1, 0, 2, 3).reshape(model_rows, out_width)
        return weights, head

    stored = [gather_pack(0)]

    tok_inside, tok_safe = local_index(tok_block, row_low, rows_dev)
    embed_term = jnp.where(
        tok_inside[:, None], jnp.take(table, tok_safe, axis=0, mode="clip"), 0.0
    ).astype(jnp.bfloat16)
    embed_term = embed_term.reshape(n_seq, n_fsdp, own_rows, feature_width)
    place_part = length // n_ctx
    place_low = VOCAB - rows_dev * (n_group - 1)
    places = lax.dynamic_slice_in_dim(table, place_low + ctx_at * place_part, place_part, 0)
    places = jnp.where(group_at == n_group - 1, places, 0.0).astype(jnp.bfloat16)
    def device_order(grid):
        cut = grid.reshape(n_group, seqs_dev, n_ctx, ctx_span)
        return cut.transpose(0, 2, 1, 3).reshape(n_group * n_ctx, own_rows)

    ids_grid = jnp.stack([device_order(tokens), device_order(positions) + VOCAB])
    near = (n_seq, n_fsdp, n_y) == (2, 4, 2)
    if near:
        across = [k << 2 for k in (0, 3, 1, 2)]
        stages = [
            [(0, 0), (0, 1)],
            [(16, 0), (2, 1)],
            [(2, 0), (18, 0), (16, 1), (18, 1)],
        ]
        order = [
            ((seat ^ step ^ side) << 1) | which
            for pieces in stages
            for side in (0, 1)
            for seat, which in pieces
            for step in across
        ]
        order = jnp.asarray(order, jnp.int32) ^ ((group_at * n_ctx + ctx_at) << 1)
        ids_grid = ids_grid.reshape(2, 2 * n_group * n_ctx, own_rows // 2)
        ids_grid = jnp.take(ids_grid, order, axis=1, mode="clip")
    ids_grid = ids_grid.reshape(2, -1)
    part_rows = -(-rows_dev // 512) * 256
    spare = part_rows * 2 - rows_dev
    table_low, table_t, table_square = prepare_table(table, 2 * part_rows)
    if near:
        flat = (-1, feature_width)
        sent = pick(embed_term, 1 - seq_at, 0).reshape(flat)
        away = shift_seq(jnp.concatenate([sent, places], 0), 1)
        away, table_low, table_t, table_square, ids_grid = lax.optimization_barrier(
            (away, table_low, table_t, table_square, ids_grid)
        )
        mine = pick(embed_term, seq_at, 0) + away[:-place_part].reshape(embed_term.shape[1:])
        places = places + away[-place_part:]
        outside = (fsdp_at == 0) | (fsdp_at == 3)
        pair = jnp.where(outside, mine[1:3], jnp.stack([mine[0], mine[3]]))
        sent = jnp.concatenate([pair.reshape(flat), places], 0)
        away = lax.ppermute(sent, "fsdp", NEAR_FIRST)
        kept_pair = jnp.where(outside, jnp.stack([mine[0], mine[3]]), mine[1:3])
        kept_pair = kept_pair + away[:-place_part].reshape(kept_pair.shape)
        places = places + away[-place_part:]
        sent = jnp.concatenate([jnp.where(fsdp_at < 2, kept_pair[1], kept_pair[0]), places], 0)
        away = lax.ppermute(sent, "fsdp", NEAR_SECOND)
        embed_term = jnp.where(fsdp_at < 2, kept_pair[0], kept_pair[1]) + away[:-place_part]
        total = places + away[-place_part:]
    else:
        embed_term = scatter_sum(embed_term, shift_seq, seq_at)
        embed_term = run(scatter_fsdp(embed_term, fsdp_at))
        total = places
        for step in range(1, n_seq):
            total = total + lax.ppermute(places, "seq", [(n_seq - 1, n_seq - 1 - step)])
        places = total
        for step in range(1, n_fsdp):
            total = total + lax.ppermute(places, "fsdp", [(n_fsdp - 1, n_fsdp - 1 - step)])
    places = gather_near(total)
    own_places = own_order(my_positions)
    place_ctx = own_places // place_part
    place_near = lax.rem(core_at + place_ctx, 2) * n_y + lax.rem(y_at - place_ctx // 2 + n_y, n_y)
    place_rows = jnp.take(
        places, place_near * place_part + lax.rem(own_places, place_part), axis=0, mode="clip"
    )
    stream = embed_term.astype(jnp.float32) + place_rows.astype(jnp.float32)
    share = 1.0 / n_ctx
    square_parts = [share * jnp.sum(table_square).reshape(1)] + [
        share * jnp.sum(weight * weight).reshape(1)
        for weight in (attn_in, attn_out, mlp_in, mlp_out)
    ]
    for layer_at in range(1, layer_count):
        stored.append(gather_pack(layer_at))
    kept = []
    squares = []
    for layer_at in range(layer_count):
        if layer_at:
            stream, stored[layer_at] = lax.optimization_barrier((stream, stored[layer_at]))
        stored[layer_at], head_weight = cut_pack(layer_at, stored[layer_at])
        stream, layer_kept, layer_sums = layer_forward(
            stream,
            stored[layer_at],
            vectors[12 * layer_at : 12 * layer_at + 12],
            allowed,
            head_count,
        )
        kept.append(layer_kept)
        squares.append(layer_sums)
    final_gain = vectors[12 * layer_count]
    final_bias = vectors[12 * layer_count + 1]
    final_norm, final_back = jax.vjp(layer_norm, stream, final_gain, final_bias)
    final_low = final_norm.astype(jnp.bfloat16)
    second_low = product(final_low, head_weight).astype(jnp.bfloat16)
    live = jnp.clip(VOCAB - row_low, 0, rows_dev).astype(jnp.int32).reshape(1)

    def local_targets(ids):
        inside, safe = local_index(ids, row_low, rows_dev)
        return jnp.where(inside, safe, -1)

    final_all = lax.all_gather(final_low, ("seq", "fsdp"), axis=0)
    second_all = lax.all_gather(second_low, ("seq", "fsdp"), axis=0)
    second_factor = SECOND * valid_block
    final_local, second_local = local_targets(next_block), local_targets(second_block)
    final_t = final_all.swapaxes(1, 2)
    final_stats = head_stats(live, table_low, final_t, final_local[None])
    final_stats, second_all = lax.optimization_barrier((final_stats, second_all))
    second_t = second_all.swapaxes(1, 2)
    second_stats = head_stats(live, table_low, second_t, second_local[None])
    stats = merge_stats(jnp.concatenate([final_stats, second_stats], 1))
    half_rows = final_stats.shape[1]
    final_stats, second_stats = stats[:, :half_rows], stats[:, half_rows:]

    pending = Pending()
    results = {}

    def rows_task(name, d_rows):
        parts = d_rows.reshape((n_seq, n_fsdp) + d_rows.shape[1:])
        moved = yield 0, send_parts(parts, shift_seq, seq_at, sent=jnp.bfloat16)
        mine = add_parts(parts, moved, seq_at)
        results[name] = yield from scatter_fsdp(mine, fsdp_at)

    def line_of(stats, factor, local):
        return jnp.stack([stats[0], factor / total_tokens, local.astype(jnp.float32)])

    final_line = line_of(final_stats, valid_block, final_local)
    table_grad, d_rows = head_back(live, table_low, table_t, final_all, final_t, final_line)
    pending.add(rows_task("final", d_rows))
    second_line = line_of(second_stats, second_factor, second_local)
    cuts = 2 if own_rows % 256 == 0 else 1
    for cut in range(cuts):
        line = second_line.reshape(3, n_group, cuts, -1)[:, :, cut].reshape(3, -1)
        table_grad, d_rows = head_back(
            live, table_low, table_t, second_all, second_t, line, cut, table_grad
        )
        table_grad = pending.point(table_grad)
        pending.add(rows_task(("second", cut), d_rows))
    pending.finish()
    d_final = results["final"].T
    d_second = jnp.concatenate([results["second", cut] for cut in range(cuts)], 1).T
    loss_rows = (final_stats[0] - final_stats[1]) * valid_block + (
        second_stats[0] - second_stats[1]
    ) * second_factor
    loss_part = jnp.sum(
        lax.dynamic_slice_in_dim(loss_rows, group_at * own_rows, own_rows, 0)
    )

    def table_task():
        parts = table_grad.reshape(2, part_rows, feature_width)
        (away,) = yield 0, [swap_core(pick(parts, 1 - core_at, 0))]
        mine = (pick(parts, core_at, 0) + away).astype(jnp.bfloat16)
        totals = []
        quarter = part_rows // 4
        for low, wait in ((0, 2), (2 * quarter, 3)):
            pieces = [mine[low : low + quarter], mine[low + quarter : low + 2 * quarter]]
            if low:
                pieces = yield 0, pieces
            moved = yield wait, [
                [shift_y(piece, step) for step in range(1, n_y)] for piece in pieces
            ]
            for piece, away in zip(pieces, moved):
                ordered = order_parts([piece] + away, y_at).astype(jnp.float32)
                total = ordered[0]
                for step in range(1, n_y):
                    total = total + ordered[step]
                totals.append(total)
        results["table"] = totals

    def bundle_task(pairs, matrices, names, waits):
        (away,) = yield 0, [swap_pairs(pairs, core_at)]
        grads = shared_outer(pairs, away, core_at)
        parts = []
        for grad in grads:
            cut = grad.reshape(n_seq, n_fsdp, -1, rows_group, grad.shape[1])
            parts += [cut[:, :, at] for at in range(cut.shape[2])]
        stacked = jnp.concatenate(parts, -1)
        moved = yield waits[0], send_parts(stacked, shift_seq, seq_at, sent=jnp.bfloat16)
        mine = add_parts(stacked, moved, seq_at)
        mine = mine.reshape(n_fsdp, n_y, rows_group // n_y, -1)
        moved = yield waits[1], send_parts(mine, shift_y, y_at, 1, jnp.bfloat16)
        mine = add_parts(mine, moved, y_at, 1)
        mine = yield from scatter_fsdp(mine, fsdp_at)
        moved = yield 0, [shift_y(mine, step) for step in range(1, n_y)]
        column = order_parts([mine] + moved, y_at).reshape(rows_group, -1)
        (away,) = yield 0, [swap_core(column)]
        both = order_parts([column, away], core_at)
        at = 0
        for matrix, name in zip(matrices, names):
            width = matrix.shape[-1] // 2
            cuts = []
            for _ in range(matrix.shape[-2] // rows_group):
                cuts.append(
                    jnp.concatenate([both[0, :, at : at + width], both[1, :, at : at + width]], 1)
                )
                at += width
            results[name] = jnp.concatenate(cuts, 0)

    pending.add(table_task())
    d_second = pending.point(d_second)
    d_second_low = d_second.astype(jnp.bfloat16)
    d_stream, d_gain_final, d_bias_final = final_back(d_final + inner(d_second_low, head_weight))

    vec_list = [None] * layer_count
    for layer_at in reversed(range(layer_count)):

        def first_task(pairs, at=layer_at):
            matrices, names = [mlp_in[at], mlp_out[at]], [("fc", at), ("down", at)]
            if at == layer_count - 1:
                pairs = [(final_low, d_second_low)] + pairs
                matrices = [attn_out[layer_count]] + matrices
                names = [("out", layer_count)] + names
            return bundle_task(pairs, matrices, names, (1, 3) if at else (2, 0))

        def later_task(pairs, at=layer_at):
            names = [("in", at), ("out", at)]
            return bundle_task(
                pairs, [attn_in[at], attn_out[at]], names, (1, 1) if at else (1, 0)
            )

        d_stream, vec_list[layer_at] = layer_backward(
            d_stream,
            kept[layer_at],
            stored[layer_at],
            vectors[12 * layer_at : 12 * layer_at + 12],
            allowed,
            head_count,
            pending,
            first_task,
            later_task,
        )
    part_ids = jnp.arange(part_rows, dtype=jnp.int32)
    part_live = part_ids < rows_dev - core_at * part_rows
    part_ids = jnp.where(part_live, row_low + core_at * part_rows + part_ids, -1)[:, None]

    quarter = part_rows // 4

    def spread(pieces, low, rows, between):
        ids = ids_grid[:, low : low + rows.shape[0]]
        added = []
        for at, piece in enumerate(pieces):
            here = part_ids[at * quarter : (at + 1) * quarter]
            hits = (here == ids[0][None]) | (here == ids[1][None])
            added.append(between(piece + product(hits.astype(jnp.bfloat16), rows)))
        return added

    mine = d_stream.astype(jnp.bfloat16)
    if near:
        half = own_rows // 2
        def flat(block):
            return block.reshape(-1, feature_width)

        mine = jnp.concatenate([mine, lax.ppermute(mine, "fsdp", NEAR_SECOND)], 0)
        mine = jnp.concatenate([mine, lax.ppermute(mine, "fsdp", NEAR_FIRST)], 0)
        mine = mine.reshape(4, 2, half, feature_width)
        front, back = flat(mine[:, 0]), flat(mine[:, 1])
        front_x, back_y = shift_seq(front, 1), shift_y(back, 1)
        here = jnp.concatenate([front, back], 0)
        here = jnp.concatenate([here, swap_core(here)], 0)
        pieces = spread(results["table"], 0, here, pending.point)
        done = here.shape[0]
        pieces[-1], front_x, back_y = lax.optimization_barrier((pieces[-1], front_x, back_y))
        front_y = shift_y(jnp.concatenate([front, front_x], 0), 1)
        back_x = shift_seq(jnp.concatenate([back, back_y], 0), 1)
        here = jnp.concatenate([front_x, back_y], 0)
        here = jnp.concatenate([here, swap_core(here)], 0)
        pieces = spread(pieces, done, here, pending.point)
        done += here.shape[0]
        pending.finish()
        last = jnp.concatenate([front_y, back_x], 0)
        last = jnp.concatenate([last, swap_core(last)], 0)
    else:
        pending.finish()
        last = lax.all_gather(mine, ("seq", "fsdp", "ctx"), axis=0, tiled=True)
        pieces, done = results["table"], 0
    summed = (
        None,
        jnp.stack([results["in", at] for at in range(layer_count)]),
        jnp.stack([results["out", at] for at in range(layer_count + 1)]),
        jnp.stack([results["fc", at] for at in range(layer_count)]),
        jnp.stack([results["down", at] for at in range(layer_count)]),
    )
    vector_grad = jnp.concatenate(vec_list + [jnp.stack([d_gain_final, d_bias_final])], 0)
    row_states = (attn_in_rows, attn_out_rows, mlp_in_rows, mlp_out_rows)
    rows_new = [None]
    col_parts = []
    weighted_parts = []
    row_parts = []
    for grad_sum, row_state in zip(summed[1:], row_states):
        square = grad_sum * grad_sum
        renewed = DECAY * row_state + (1.0 - DECAY) * jnp.mean(square + EPS_SQUARE, -1)
        rows_new.append(renewed)
        col_parts.append(share * jnp.sum(square + EPS_SQUARE, -2))
        weighted_parts.append(share * jnp.sum(square / renewed[..., None], -2))
        row_parts.append(share * jnp.sum(renewed, -1))
    numbers = jnp.concatenate(
        row_parts + square_parts + [loss_part.reshape(1), jnp.stack(squares).reshape(-1)]
    )
    row_count = sum(part.shape[0] for part in row_parts)
    numbers = jnp.pad(numbers, (0, feature_width - numbers.shape[0]))
    col_rows = [part.reshape(-1, feature_width) for part in col_parts]
    weighted_rows = [part.reshape(-1, feature_width) for part in weighted_parts]
    col_count = sum(part.shape[0] for part in col_rows)
    early = jnp.concatenate(col_rows + weighted_rows + [numbers[None], vector_grad], 0)
    early = jnp.pad(early, ((0, -early.shape[0] % 8), (0, 0)))
    hops = sum_hops(early)
    state = [next(hops)]

    def advance(piece):
        piece, state[0] = lax.optimization_barrier((piece, state[0]))
        state[0] = hops.send(state[0])
        return piece

    pieces = spread(pieces, done, last, advance)
    while True:
        try:
            state[0] = hops.send(state[0])
        except StopIteration as stop:
            everything = stop.value
            break
    table_part = jnp.concatenate(pieces, 0)
    table_away = swap_core(table_part)
    state_part = lax.dynamic_slice_in_dim(
        jnp.pad(table_rows, (0, spare)), core_at * part_rows, part_rows, 0
    )
    live_rows = part_live[:, None]
    part_square = table_part * table_part
    part_renewed = DECAY * state_part[:, None] + (1.0 - DECAY) * jnp.mean(
        part_square + EPS_SQUARE, -1, keepdims=True
    )
    part_renewed = jnp.where(live_rows, part_renewed, 1.0)
    away_renewed = swap_core(part_renewed)
    live_count = jnp.sum(part_live.astype(jnp.float32))
    rows_new[0] = jnp.concatenate(
        [
            jnp.where(core_at == 0, part_renewed, away_renewed),
            jnp.where(core_at == 0, away_renewed, part_renewed),
        ],
        0,
    )[:rows_dev, 0][None]
    row_sum = jnp.sum(jnp.where(live_rows, part_renewed, 0.0))
    late = jnp.concatenate(
        [
            (jnp.sum(part_square, 0) + EPS_SQUARE * live_count)[None],
            jnp.sum(part_square / part_renewed, 0)[None],
            jnp.full((6, feature_width), row_sum),
        ],
        0,
    )
    late = sum_all(late, skip_y=True)
    numbers = everything[2 * col_count]
    vector_sum = everything[2 * col_count + 1 : 2 * col_count + 1 + vector_grad.shape[0]]
    loss_sum = numbers[row_count + 5]
    square_total = numbers[row_count + 6 : row_count + 6 + 3 * layer_count]
    matrices = (table[None], attn_in, attn_out, mlp_in, mlp_out)
    col_states = (table_cols[None], attn_in_cols, attn_out_cols, mlp_in_cols, mlp_out_cols)
    row_totals = [rows_dev * n_group] + [weight.shape[1] * n_group for weight in matrices[1:]]
    shares = jnp.concatenate(
        [
            jnp.full((rows.shape[0], 1), (1.0 - DECAY) / row_total, jnp.float32)
            for rows, row_total in zip(col_rows, row_totals[1:])
        ],
        0,
    )
    old_cols = jnp.concatenate([state.reshape(-1, feature_width) for state in col_states[1:]], 0)
    new_cols = DECAY * old_cols + shares * everything[:col_count]
    ratios = jnp.sum(everything[col_count : 2 * col_count] / new_cols, -1)
    cols_new = []
    new_weights = []
    sizes_rms = []
    col_at = 0
    row_at = 0
    for matrix_at in range(5):
        weight, renewed, col_state = matrices[matrix_at], rows_new[matrix_at], col_states[matrix_at]
        if matrix_at == 0:
            renewed_cols = DECAY * col_state + (1.0 - DECAY) / row_totals[0] * late[:1]
            row_mean = late[2, :1] / row_totals[0]
            clip_total = jnp.sum(row_mean * jnp.sum(late[1:2] / renewed_cols, -1))
        else:
            stack_count = weight.shape[0]
            height = col_rows[matrix_at - 1].shape[0]
            renewed_cols = new_cols[col_at : col_at + height].reshape(col_state.shape)
            row_mean = numbers[row_at : row_at + stack_count] / row_totals[matrix_at]
            row_at += stack_count
            ratio = jnp.sum(ratios[col_at : col_at + height].reshape(stack_count, -1), -1)
            col_at += height
            clip_total = jnp.sum(row_mean * ratio)
        entries = weight.size * n_group
        update_rms = jnp.sqrt(clip_total / entries)
        weight_rms = jnp.sqrt(numbers[row_count + matrix_at] / entries)
        step_scale = RATE * jnp.maximum(EPS_SCALE, weight_rms) / jnp.maximum(1.0, update_rms / CLIP)
        cols_new.append(renewed_cols)
        sizes_rms.append(update_rms)
        if matrix_at == 0:
            table_sum, table_new, table_copy = update_table(
                core_at.astype(jnp.int32).reshape(1),
                step_scale.reshape(1),
                table_part,
                table_away,
                part_renewed,
                away_renewed,
                renewed_cols / row_mean[0],
                table,
            )
            new_weights.append(table_new)
            continue
        second_moment = renewed[:, :, None] * renewed_cols[:, None, :] / row_mean[:, None, None]
        update = summed[matrix_at] * lax.rsqrt(second_moment)
        new_weights.append(weight - step_scale * update)
    vector_state_new = DECAY * vector_state + (1.0 - DECAY) * (vector_sum * vector_sum + EPS_SQUARE)
    vector_update = vector_sum * lax.rsqrt(vector_state_new)
    vector_rms = jnp.sqrt(jnp.mean(vector_update * vector_update))
    vector_scale = (
        RATE
        * jnp.maximum(EPS_SCALE, jnp.sqrt(jnp.mean(vectors * vectors)))
        / jnp.maximum(1.0, vector_rms / CLIP)
    )
    vectors_new = vectors - vector_scale * vector_update
    sizes_rms.append(vector_rms)
    norms = jnp.concatenate([jnp.sqrt(square_total / total_tokens), jnp.stack(sizes_rms)])
    return (
        loss_sum,
        norms,
        table_sum,
        rows_new[0][0],
        cols_new[0][0],
        table_new,
        table_copy,
        summed[1],
        rows_new[1],
        cols_new[1],
        new_weights[1],
        new_weights[1].astype(jnp.bfloat16),
        summed[2],
        rows_new[2],
        cols_new[2],
        new_weights[2],
        new_weights[2].astype(jnp.bfloat16),
        summed[3],
        rows_new[3],
        cols_new[3],
        new_weights[3],
        new_weights[3].astype(jnp.bfloat16),
        summed[4],
        rows_new[4],
        cols_new[4],
        new_weights[4],
        new_weights[4].astype(jnp.bfloat16),
        vector_sum,
        vector_state_new,
        vectors_new,
    )


def solution(mesh):
    return jax.shard_map(
        body,
        mesh=mesh,
        in_specs=(
            P(),
            P(),
            P(),
            P(),
            P(("seq", "fsdp"), None),
            P(None, ("seq", "fsdp"), None),
            P(None, ("seq", "fsdp"), None),
            P(None, ("seq", "fsdp"), None),
            P(None, ("seq", "fsdp"), None),
            P(),
            P(("seq", "fsdp")),
            P(),
            P(None, ("seq", "fsdp")),
            P(),
            P(None, ("seq", "fsdp")),
            P(),
            P(None, ("seq", "fsdp")),
            P(),
            P(None, ("seq", "fsdp")),
            P(),
            P(),
        ),
        out_specs=(
            P(),
            P(),
            P(("seq", "fsdp"), None),
            P(("seq", "fsdp")),
            P(),
            P(("seq", "fsdp"), None),
            P(("seq", "fsdp"), None),
            P(None, ("seq", "fsdp"), None),
            P(None, ("seq", "fsdp")),
            P(),
            P(None, ("seq", "fsdp"), None),
            P(None, ("seq", "fsdp"), None),
            P(None, ("seq", "fsdp"), None),
            P(None, ("seq", "fsdp")),
            P(),
            P(None, ("seq", "fsdp"), None),
            P(None, ("seq", "fsdp"), None),
            P(None, ("seq", "fsdp"), None),
            P(None, ("seq", "fsdp")),
            P(),
            P(None, ("seq", "fsdp"), None),
            P(None, ("seq", "fsdp"), None),
            P(None, ("seq", "fsdp"), None),
            P(None, ("seq", "fsdp")),
            P(),
            P(None, ("seq", "fsdp"), None),
            P(None, ("seq", "fsdp"), None),
            P(),
            P(),
            P(),
        ),
        check_vma=False,
    )
```

```python
import functools

import jax
import jax.numpy as jnp
from jax import lax
from jax.experimental import pallas as pl
from jax.experimental.pallas import tpu as pltpu
from jax.sharding import PartitionSpec as P

HEADS = 12
VOCAB = 50304


EPS_NORM = 1e-05
EPS_SQUARE = 1e-30
EPS_SCALE = 0.001
DECAY = 0.5
CLIP = 0.4
RATE = 0.6
SECOND = 0.3
MASKED = -1e30
VMEM_BYTES = 56 * 1024 * 1024
NEAR_FIRST = [(0, 1), (1, 0), (2, 3), (3, 2)]
NEAR_SECOND = [(0, 3), (3, 0), (1, 2), (2, 1)]


def layer_norm(stream, gain, offset):
    center = stream - jnp.mean(stream, -1, keepdims=True)
    spread = jnp.mean(center * center, -1, keepdims=True)
    return center * lax.rsqrt(spread + EPS_NORM) * gain + offset


def gelu_tanh(value):
    return jax.nn.gelu(value, approximate=True)


def positions_of(segments):
    steps_at = jnp.arange(segments.shape[-1], dtype=jnp.int32)
    before = jnp.concatenate(
        [jnp.full(segments.shape[:-1] + (1,), -2, jnp.int32), segments[..., :-1]], -1
    )
    starts = jnp.where(segments != before, steps_at, 0)
    first = lax.cummax(starts, axis=segments.ndim - 1)
    return jnp.where(segments >= 0, steps_at - first, 0)


def product(left, right):
    return jnp.dot(left, right, preferred_element_type=jnp.float32)


def inner(left, right):
    return lax.dot_general(
        left, right, (((1,), (1,)), ((), ())), preferred_element_type=jnp.float32
    )


def outer(left, right):
    return lax.dot_general(
        left, right, (((0,), (0,)), ((), ())), preferred_element_type=jnp.float32
    )


def shift(block, axis, step):
    count = lax.axis_size(axis)
    return lax.ppermute(block, axis, [(i, (i + step) % count) for i in range(count)])


def shift_y(block, step):
    count = lax.axis_size("ctx")
    return lax.ppermute(block, "ctx", [(i, (i + 2 * step) % count) for i in range(count)])


def swap_core(block):
    count = lax.axis_size("ctx")
    return lax.ppermute(block, "ctx", [(i, i ^ 1) for i in range(count)])


def shift_seq(block, step):
    return shift(block, "seq", step)


def shift_fsdp(block, step):
    return shift(block, "fsdp", step)


def pick(parts, at, axis):
    return lax.dynamic_index_in_dim(parts, at, axis, False)


def send_parts(parts, mover, at, axis=0, sent=None):
    count = parts.shape[axis]
    moving = []
    for step in range(1, count):
        piece = pick(parts, lax.rem(at + step, count), axis)
        moving.append(mover(piece if sent is None else piece.astype(sent), step))
    return moving


def add_parts(parts, moved, at, axis=0):
    total = pick(parts, at, axis)
    for piece in moved:
        total = total + piece.astype(total.dtype)
    return total


def scatter_sum(parts, mover, at, axis=0, sent=None):
    return add_parts(parts, send_parts(parts, mover, at, axis, sent), at, axis)


def scatter_fsdp(parts, at):
    count = parts.shape[0]
    if count != 4:
        moved = yield 0, send_parts(parts, shift_fsdp, at, sent=jnp.bfloat16)
        return add_parts(parts, moved, at)
    outside = (at == 0) | (at == 3)
    mine = [jnp.where(outside, 0, 1), jnp.where(outside, 3, 2)]
    other = [jnp.where(outside, 1, 0), jnp.where(outside, 2, 3)]
    away = jnp.stack([pick(parts, slot, 0) for slot in other]).astype(jnp.bfloat16)
    (away,) = yield 0, [lax.ppermute(away, "fsdp", NEAR_FIRST)]
    first, second = (
        pick(parts, slot, 0) + away[k].astype(parts.dtype) for k, slot in enumerate(mine)
    )
    away = jnp.where(at < 2, second, first).astype(jnp.bfloat16)
    (away,) = yield 0, [lax.ppermute(away, "fsdp", NEAR_SECOND)]
    return jnp.where(at < 2, first, second) + away.astype(parts.dtype)


def run(task):
    moving = next(task)[1]
    while True:
        try:
            moving = task.send(moving)[1]
        except StopIteration as stop:
            return stop.value


def sum_hops(block, skip_y=False):
    for axis in ("ctx", "seq", "fsdp"):
        whole = lax.axis_size(axis)
        count = 2 if skip_y and axis == "ctx" else whole
        hop = 1
        while hop < count:
            moved = yield lax.ppermute(block, axis, [(i, i ^ hop) for i in range(whole)])
            block = block + moved
            hop *= 2
    return block


def sum_all(block, skip_y=False):
    hops = sum_hops(block, skip_y)
    moved = next(hops)
    while True:
        try:
            moved = hops.send(moved)
        except StopIteration as stop:
            return stop.value


def order_parts(parts, at):
    count = len(parts)
    if count == 2:
        first, second = parts
        return jnp.stack([jnp.where(at == 0, first, second), jnp.where(at == 0, second, first)])
    order = lax.rem(at - jnp.arange(count, dtype=jnp.int32) + count, count)
    return jnp.take(jnp.stack(parts), order, axis=0, mode="clip")


def gather_near(block):
    n_y = lax.axis_size("ctx") // 2
    column = jnp.concatenate([block] + [shift_y(block, step) for step in range(1, n_y)], 0)
    return jnp.concatenate([column, swap_core(column)], 0)


def scatter_near(parts):
    n_y = lax.axis_size("ctx") // 2
    parts = parts.reshape(2, 2, n_y, -1, parts.shape[2])
    column = parts[:, 0] + swap_core(parts[:, 1])
    total = column[:, 0]
    for step in range(1, n_y):
        away = shift_y(column[:, step].astype(jnp.bfloat16), n_y - step)
        total = total + away.astype(total.dtype)
    return total


def half_of(block, at):
    width = block.shape[-1] // 2
    return jnp.where(at == 0, block[..., :width], block[..., width:])


def qkv_bias(vec):
    return jnp.concatenate([vec[2], jnp.zeros_like(vec[2]), vec[3]])


def head_slabs(ref, lanes, width):
    block = ref[...].astype(jnp.float32)
    lane = lax.broadcasted_iota(jnp.int32, block.shape, 1)
    return [
        jnp.where((lane >= low) & (lane < low + width), block, 0.0).astype(jnp.bfloat16)
        for low in range(0, lanes, width)
    ]


def turned(ref):
    return ref[...].astype(jnp.float32).T.astype(jnp.bfloat16)


def across(left, right):
    return lax.dot_general(
        left, right, (((1,), (1,)), ((), ())), preferred_element_type=jnp.float32
    )


def by_head(parts, width):
    row = lax.broadcasted_iota(jnp.int32, parts[0].shape, 0)
    joined = parts[0]
    for at, part in enumerate(parts[1:], 1):
        joined = jnp.where(row >= at * width, part, joined)
    return joined


def attend_kernel(width, query_ref, key_ref, value_ref, mask_ref, mixed_ref, log_ref):
    lanes = query_ref.shape[1]
    scale = width ** (-0.5)
    value_t = turned(value_ref)
    mixed = []
    for at, query in enumerate(head_slabs(query_ref, lanes, width)):
        scores = across(key_ref[...], query) * scale + mask_ref[...]
        top = jnp.max(scores, 0, keepdims=True)
        probs = jnp.exp(scores - top)
        total = jnp.sum(probs, 0, keepdims=True)
        log_ref[0, at : at + 1, :] = top + jnp.log(total)
        probs_low = (probs * (1.0 / total)).astype(jnp.bfloat16)
        mixed.append(jnp.dot(value_t, probs_low, preferred_element_type=jnp.float32))
    mixed_ref[...] = by_head(mixed, width).T.astype(mixed_ref.dtype)


def attend_back_kernel(
    width, query_ref, key_ref, value_ref, mixed_ref, log_ref, mask_ref, d_query_ref, d_pair_ref
):
    lanes = query_ref.shape[1]
    scale = width ** (-0.5)
    key_t = turned(key_ref)
    queries = head_slabs(query_ref, lanes, width)
    d_heads = head_slabs(mixed_ref, lanes, width)
    d_query = []
    d_key = d_value = None
    for at, (query, d_head) in enumerate(zip(queries, d_heads)):
        scores = across(key_ref[...], query) * scale + mask_ref[...]
        probs = jnp.exp(scores - log_ref[0, at : at + 1, :])
        d_probs = across(value_ref[...], d_head)
        shared = jnp.sum(probs * d_probs, 0, keepdims=True)
        d_scores = (probs * (d_probs - shared)).astype(jnp.bfloat16)
        d_query.append(jnp.dot(key_t, d_scores, preferred_element_type=jnp.float32))
        part = jnp.dot(d_scores, query, preferred_element_type=jnp.float32)
        d_key = part if d_key is None else d_key + part
        part = jnp.dot(
            probs.astype(jnp.bfloat16), d_head, preferred_element_type=jnp.float32
        )
        d_value = part if d_value is None else d_value + part
    d_query_ref[...] = (by_head(d_query, width).T * scale).astype(d_query_ref.dtype)
    d_pair_ref[0] = d_key * scale
    d_pair_ref[1] = d_value


def attend(qkv_low, pairs, mask, head_count, lanes=128):
    row_count = qkv_low.shape[0]
    key_count, feature_width = pairs.shape[0], pairs.shape[1] // 2
    width = feature_width // head_count
    steps = feature_width // lanes
    return pl.pallas_call(
        functools.partial(attend_kernel, width),
        out_shape=(
            jax.ShapeDtypeStruct((row_count, feature_width), jnp.bfloat16),
            jax.ShapeDtypeStruct((steps, lanes // width, row_count), jnp.float32),
        ),
        grid=(steps,),
        in_specs=[
            pl.BlockSpec((row_count, lanes), lambda i: (0, i)),
            pl.BlockSpec((key_count, lanes), lambda i: (0, i)),
            pl.BlockSpec((key_count, lanes), lambda i: (0, steps + i)),
            pl.BlockSpec((key_count, row_count), lambda i: (0, 0)),
        ],
        out_specs=(
            pl.BlockSpec((row_count, lanes), lambda i: (0, i)),
            pl.BlockSpec((1, lanes // width, row_count), lambda i: (i, 0, 0)),
        ),
        compiler_params=pltpu.CompilerParams(vmem_limit_bytes=VMEM_BYTES),
        cost_estimate=pl.CostEstimate(
            flops=4 * row_count * key_count * lanes * head_count,
            bytes_accessed=4 * key_count * row_count + 4 * key_count * feature_width,
            transcendentals=row_count * key_count * head_count,
        ),
    )(qkv_low, pairs, pairs, mask)


def attend_back(qkv_low, pairs, d_mixed, log_total, mask, head_count, lanes=128):
    row_count = qkv_low.shape[0]
    key_count, feature_width = pairs.shape[0], pairs.shape[1] // 2
    width = feature_width // head_count
    steps = feature_width // lanes
    return pl.pallas_call(
        functools.partial(attend_back_kernel, width),
        out_shape=(
            jax.ShapeDtypeStruct((row_count, feature_width), jnp.bfloat16),
            jax.ShapeDtypeStruct((2, key_count, feature_width), jnp.float32),
        ),
        grid=(steps,),
        in_specs=[
            pl.BlockSpec((row_count, lanes), lambda i: (0, i)),
            pl.BlockSpec((key_count, lanes), lambda i: (0, i)),
            pl.BlockSpec((key_count, lanes), lambda i: (0, steps + i)),
            pl.BlockSpec((row_count, lanes), lambda i: (0, i)),
            pl.BlockSpec((1, lanes // width, row_count), lambda i: (i, 0, 0)),
            pl.BlockSpec((key_count, row_count), lambda i: (0, 0)),
        ],
        out_specs=(
            pl.BlockSpec((row_count, lanes), lambda i: (0, i)),
            pl.BlockSpec((2, key_count, lanes), lambda i: (0, 0, i)),
        ),
        compiler_params=pltpu.CompilerParams(vmem_limit_bytes=VMEM_BYTES),
        cost_estimate=pl.CostEstimate(
            flops=10 * row_count * key_count * lanes * head_count,
            bytes_accessed=4 * key_count * row_count + 12 * key_count * feature_width,
            transcendentals=row_count * key_count * head_count,
        ),
    )(qkv_low, pairs, pairs, d_mixed, log_total, mask)


def layer_forward(stream, weights, vec, mask, head_count):
    w_in, w_out, w_fc, w_down = weights
    feature_width = stream.shape[1]
    a_low = layer_norm(stream, vec[0], vec[1]).astype(jnp.bfloat16)
    qkv_low = (product(a_low, w_in) + qkv_bias(vec)).astype(jnp.bfloat16)
    pairs = gather_near(qkv_low[:, feature_width:])
    mixed_low, log_total = attend(qkv_low, pairs, mask, head_count)
    branch = product(mixed_low, w_out) + vec[4]
    middle = stream + branch
    m_low = layer_norm(middle, vec[5], vec[6]).astype(jnp.bfloat16)
    hidden = product(m_low, w_fc) + vec[8:12].reshape(-1)
    output = product(gelu_tanh(hidden).astype(jnp.bfloat16), w_down) + vec[7]
    sums = jnp.stack([jnp.sum(stream * stream), jnp.sum(branch * branch), jnp.sum(output * output)])
    kept = (stream, a_low, qkv_low, pairs, log_total, mixed_low, middle, m_low, hidden)
    return (middle + output, kept, sums)


def swap_pairs(pairs, core_at):
    lefts = [left for left, _ in pairs]
    return swap_core(
        jnp.concatenate(lefts + [half_of(right, 1 - core_at) for _, right in pairs], 1)
    )


def shared_outer(pairs, away, core_at):
    at = 0
    whole_left = []
    for left, _ in pairs:
        whole_left.append(jnp.concatenate([left, away[:, at : at + left.shape[1]]], 0))
        at += left.shape[1]
    grads = []
    for left, (_, right) in zip(whole_left, pairs):
        width = right.shape[1] // 2
        whole_right = jnp.concatenate([half_of(right, core_at), away[:, at : at + width]], 0)
        at += width
        grads.append(outer(left, whole_right))
    return grads


def layer_backward(d_stream, kept, weights, vec, mask, head_count, pending, first_task, later_task):
    stream, a_low, qkv_low, pairs, log_total, mixed_low, middle, m_low, hidden = kept
    w_in, w_out, w_fc, w_down = weights
    feature_width = stream.shape[1]
    norm_back_one = jax.vjp(layer_norm, stream, vec[0], vec[1])[1]
    norm_back_two = jax.vjp(layer_norm, middle, vec[5], vec[6])[1]
    gelu_out, gelu_back = jax.vjp(gelu_tanh, hidden)
    u_low = gelu_out.astype(jnp.bfloat16)
    d_out_low = d_stream.astype(jnp.bfloat16)
    d_hidden_low = gelu_back(inner(d_out_low, w_down))[0].astype(jnp.bfloat16)
    d_hidden_low = pending.point(d_hidden_low)
    pending.add(first_task([(m_low, d_hidden_low), (u_low, d_out_low)]))
    d_m = inner(d_hidden_low, w_fc)
    d_two, d_gain_two, d_bias_two = norm_back_two(d_m)
    d_middle = d_stream + d_two
    d_middle = pending.point(d_middle)
    d_middle_low = d_middle.astype(jnp.bfloat16)
    d_mixed = inner(d_middle_low, w_out).astype(jnp.bfloat16)
    d_query, d_pairs = attend_back(qkv_low, pairs, d_mixed, log_total, mask, head_count)
    d_pairs = pending.point(d_pairs)
    d_pairs = scatter_near(d_pairs).astype(jnp.bfloat16)
    d_qkv_low = jnp.concatenate([d_query, d_pairs[0], d_pairs[1]], 1)
    d_qkv_low = pending.point(d_qkv_low)
    pending.add(later_task([(a_low, d_qkv_low), (mixed_low, d_middle_low)]))
    d_one, d_gain_one, d_bias_one = norm_back_one(inner(d_qkv_low, w_in))
    d_qkv = d_qkv_low.astype(jnp.float32)
    rows_head = jnp.stack(
        [
            d_gain_one,
            d_bias_one,
            jnp.sum(d_qkv[:, :feature_width], 0),
            jnp.sum(d_qkv[:, 2 * feature_width :], 0),
            jnp.sum(d_middle_low.astype(jnp.float32), 0),
            d_gain_two,
            d_bias_two,
            jnp.sum(d_out_low.astype(jnp.float32), 0),
        ]
    )
    vec_grad = jnp.concatenate(
        [rows_head, jnp.sum(d_hidden_low.astype(jnp.float32), 0).reshape(4, feature_width)], 0
    )
    return (pending.point(d_middle + d_one), vec_grad)


def merge_stats(stats):
    for mover, axis in ((shift_seq, "seq"), (shift_fsdp, "fsdp")):
        parts = [stats] + [mover(stats, step) for step in range(1, lax.axis_size(axis))]
        top = parts[0][0]
        for part in parts[1:]:
            top = jnp.maximum(top, part[0])
        total = jnp.exp(parts[0][0] - top)
        picked = parts[0][1]
        for part in parts[1:]:
            total = total + jnp.exp(part[0] - top)
            picked = picked + part[1]
        stats = jnp.stack([top + jnp.log(total), picked])
    return stats


def blocks_of(groups, width, row_block):
    step = max(1, row_block // width)
    return [
        (range(low, low + step), slice(low * width, (low + step) * width))
        for low in range(0, groups, step)
    ]


def side_by_side(ref, at_block):
    return jnp.concatenate([ref[at] for at in at_block], 1)


def masked_logits(logits, live, first):
    column = lax.broadcasted_iota(jnp.int32, logits.shape, 0) + first
    return jnp.where(column < live, logits, MASKED)


def stats_kernel(row_block, live_ref, table_ref, rows_ref, target_ref, out_ref, top_ref, sum_ref, pick_ref):
    at = pl.program_id(0)
    tile = table_ref.shape[0]
    first = at * tile
    live = live_ref[0]

    @pl.when(at == 0)
    def _():
        top_ref[...] = jnp.full_like(top_ref, MASKED)
        sum_ref[...] = jnp.zeros_like(sum_ref)
        pick_ref[...] = jnp.zeros_like(pick_ref)

    def step(masked):
        for at_block, here in blocks_of(rows_ref.shape[0], rows_ref.shape[2], row_block):
            logits = jnp.dot(
                table_ref[...], side_by_side(rows_ref, at_block), preferred_element_type=jnp.float32
            )
            if masked:
                logits = masked_logits(logits, live, first)
            column = lax.broadcasted_iota(jnp.int32, logits.shape, 0)
            hit = column == target_ref[:, here] - first
            cut = logits.reshape(tile // 8, 8, logits.shape[1])
            top = top_ref[:, here]
            joint = jnp.maximum(top, jnp.max(cut, 0))
            total = jnp.sum(jnp.exp(cut - joint[None]), 0)
            sum_ref[:, here] = sum_ref[:, here] * jnp.exp(top - joint) + total
            top_ref[:, here] = joint
            pick_ref[:, here] += jnp.sum(
                jnp.where(hit, logits, 0.0).reshape(cut.shape), 0
            )

    @pl.when(first + tile <= live)
    def _():
        step(False)

    @pl.when((first + tile > live) & (first < live))
    def _():
        step(True)

    @pl.when(at == pl.num_programs(0) - 1)
    def _():
        top = top_ref[...]
        joint = jnp.max(top, 0, keepdims=True)
        total = jnp.sum(sum_ref[...] * jnp.exp(top - joint), 0, keepdims=True)
        out_ref[0:1, :] = joint + jnp.log(total)
        out_ref[1:2, :] = jnp.sum(pick_ref[...], 0, keepdims=True)


def head_stats(live, table_low, rows_t, target, tile=512, row_block=512):
    groups, depth, width = rows_t.shape
    count = groups * width
    height = table_low.shape[0]
    return pl.pallas_call(
        functools.partial(stats_kernel, row_block),
        out_shape=jax.ShapeDtypeStruct((2, count), jnp.float32),
        grid=(height // tile,),
        in_specs=[
            pl.BlockSpec(memory_space=pltpu.SMEM),
            pl.BlockSpec((tile, depth), lambda i: (i, 0)),
            pl.BlockSpec((groups, depth, width), lambda i: (0, 0, 0)),
            pl.BlockSpec((1, count), lambda i: (0, 0)),
        ],
        out_specs=pl.BlockSpec((2, count), lambda i: (0, 0)),
        scratch_shapes=[pltpu.VMEM((8, count), jnp.float32)] * 3,
        compiler_params=pltpu.CompilerParams(vmem_limit_bytes=VMEM_BYTES),
        cost_estimate=pl.CostEstimate(
            flops=2 * height * depth * count,
            bytes_accessed=2 * height * depth + 2 * depth * count,
            transcendentals=height * count,
        ),
    )(live, table_low, rows_t, target)


def back_kernel(row_block, added, live_ref, table_ref, table_t_ref, rows_ref, rows_t_ref, line_ref, *refs):
    if added:
        prior_ref, grad_ref, d_rows_ref = refs
    else:
        grad_ref, d_rows_ref = refs
    at = pl.program_id(0)
    tile = table_ref.shape[0]
    first = at * tile
    live = live_ref[0]
    width = d_rows_ref.shape[2]

    @pl.when(at == 0)
    def _():
        d_rows_ref[...] = jnp.zeros_like(d_rows_ref)

    def step(masked):
        grad = prior_ref[...] if added else None
        for at_block, here in blocks_of(rows_t_ref.shape[0], width, row_block):
            logits = jnp.dot(
                table_ref[...],
                side_by_side(rows_t_ref, at_block),
                preferred_element_type=jnp.float32,
            )
            if masked:
                logits = masked_logits(logits, live, first)
            column = lax.broadcasted_iota(jnp.int32, logits.shape, 0).astype(jnp.float32)
            probs = jnp.exp(logits - line_ref[0:1, here])
            hit = column == line_ref[2:3, here] - first.astype(jnp.float32)
            d_low = (line_ref[1:2, here] * jnp.where(hit, probs - 1.0, probs)).astype(jnp.bfloat16)
            rows = rows_ref[at_block.start : at_block.stop].reshape(-1, rows_ref.shape[2])
            part = jnp.dot(d_low, rows, preferred_element_type=jnp.float32)
            grad = part if grad is None else grad + part
            d_part = jnp.dot(table_t_ref[...], d_low, preferred_element_type=jnp.float32)
            for at_width, at_group in enumerate(at_block):
                d_rows_ref[at_group] += d_part[:, at_width * width : (at_width + 1) * width]
        grad_ref[...] = grad

    @pl.when(first + tile <= live)
    def _():
        step(False)

    @pl.when((first + tile > live) & (first < live))
    def _():
        step(True)

    @pl.when(first >= live)
    def _():
        grad_ref[...] = prior_ref[...] if added else jnp.zeros_like(grad_ref)


def head_back(live, table_low, table_t, rows, rows_t, line, cut=0, prior=None, tile=512):
    groups, _, depth = rows.shape
    height = table_low.shape[0]
    count = line.shape[1]
    width = count // groups
    once = dict(pipeline_mode=pl.Buffered(1))
    grad_spec = pl.BlockSpec((tile, depth), lambda i: (i, 0))
    added = prior is not None
    return pl.pallas_call(
        functools.partial(back_kernel, 1024, added),
        out_shape=(
            jax.ShapeDtypeStruct((height, depth), jnp.float32),
            jax.ShapeDtypeStruct((groups, depth, width), jnp.float32),
        ),
        grid=(height // tile,),
        in_specs=[
            pl.BlockSpec(memory_space=pltpu.SMEM),
            pl.BlockSpec((tile, depth), lambda i: (i, 0)),
            pl.BlockSpec((depth, tile), lambda i: (0, i)),
            pl.BlockSpec((groups, width, depth), lambda i: (0, cut, 0), **once),
            pl.BlockSpec((groups, depth, width), lambda i: (0, 0, cut), **once),
            pl.BlockSpec((3, count), lambda i: (0, 0), **once),
        ]
        + ([grad_spec] if added else []),
        out_specs=(
            grad_spec,
            pl.BlockSpec((groups, depth, width), lambda i: (0, 0, 0), **once),
        ),
        input_output_aliases={6: 0} if added else {},
        compiler_params=pltpu.CompilerParams(vmem_limit_bytes=VMEM_BYTES),
        cost_estimate=pl.CostEstimate(
            flops=6 * height * depth * count,
            bytes_accessed=4 * height * depth + 12 * depth * count + 8 * height * depth,
            transcendentals=height * count,
        ),
    )(live, table_low, table_t, rows, rows_t, line, *((prior,) if added else ()))


def prepare_kernel(row_count, table_ref, low_ref, turned_ref, square_ref):
    at = pl.program_id(0)
    tile = table_ref.shape[0]
    row = lax.broadcasted_iota(jnp.int32, table_ref.shape, 0) + at * tile
    block = jnp.where(row < row_count, table_ref[...], 0.0)
    low_ref[...] = block.astype(jnp.bfloat16)
    turned_ref[...] = block.T.astype(jnp.bfloat16)
    part = jnp.sum((block * block).reshape(tile // 8, 8, block.shape[1]), 0)

    @pl.when(at == 0)
    def _():
        square_ref[...] = part

    @pl.when(at > 0)
    def _():
        square_ref[...] += part


def prepare_table(table, height, tile=512):
    row_count, depth = table.shape
    return pl.pallas_call(
        functools.partial(prepare_kernel, row_count),
        out_shape=(
            jax.ShapeDtypeStruct((height, depth), jnp.bfloat16),
            jax.ShapeDtypeStruct((depth, height), jnp.bfloat16),
            jax.ShapeDtypeStruct((8, depth), jnp.float32),
        ),
        grid=(height // tile,),
        in_specs=[pl.BlockSpec((tile, depth), lambda i: (i, 0))],
        out_specs=(
            pl.BlockSpec((tile, depth), lambda i: (i, 0)),
            pl.BlockSpec((depth, tile), lambda i: (0, i)),
            pl.BlockSpec((8, depth), lambda i: (0, 0)),
        ),
        compiler_params=pltpu.CompilerParams(vmem_limit_bytes=VMEM_BYTES),
        cost_estimate=pl.CostEstimate(
            flops=2 * row_count * depth,
            bytes_accessed=4 * row_count * depth + 4 * height * depth,
            transcendentals=0,
        ),
    )(table)


def update_kernel(used, core_ref, scale_ref, mine_ref, away_ref, mine_rows_ref, away_rows_ref, cols_ref, weight_ref, *outs):
    grad_ref, new_ref, copy_ref = outs
    half = pl.program_id(0) // (pl.num_programs(0) // 2)
    chosen = half == core_ref[0]
    grad = jnp.where(chosen, mine_ref[...], away_ref[...])
    rows = jnp.where(chosen, mine_rows_ref[...], away_rows_ref[...])
    update = grad * lax.rsqrt(rows * cols_ref[...])
    new = weight_ref[...] - scale_ref[0] * update

    @pl.when(pl.program_id(0) < used)
    def _():
        grad_ref[...] = grad
        new_ref[...] = new
        copy_ref[...] = new.astype(copy_ref.dtype)


def update_table(core, scale, mine, away, mine_rows, away_rows, cols, weight):
    row_count, depth = weight.shape
    tile = mine.shape[0] // 4
    steps = mine.shape[0] // tile
    used = -(-row_count // tile)

    def mine_at(i, core_ref):
        return (jnp.clip(i - core_ref[0] * steps, 0, steps - 1), 0)

    def away_at(i, core_ref):
        return (jnp.clip(i - (1 - core_ref[0]) * steps, 0, steps - 1), 0)

    def whole_at(i, core_ref):
        return (jnp.minimum(i, used - 1), 0)

    whole = pl.BlockSpec((tile, depth), whole_at)
    return pl.pallas_call(
        functools.partial(update_kernel, used),
        out_shape=(
            jax.ShapeDtypeStruct(weight.shape, jnp.float32),
            jax.ShapeDtypeStruct(weight.shape, jnp.float32),
            jax.ShapeDtypeStruct(weight.shape, jnp.bfloat16),
        ),
        grid_spec=pltpu.PrefetchScalarGridSpec(
            num_scalar_prefetch=1,
            grid=(2 * steps,),
            in_specs=[
                pl.BlockSpec(memory_space=pltpu.SMEM),
                pl.BlockSpec((tile, depth), mine_at),
                pl.BlockSpec((tile, depth), away_at),
                pl.BlockSpec((tile, 1), mine_at),
                pl.BlockSpec((tile, 1), away_at),
                pl.BlockSpec((1, depth), lambda i, core_ref: (0, 0)),
                whole,
            ],
            out_specs=(whole, whole, whole),
        ),
        compiler_params=pltpu.CompilerParams(vmem_limit_bytes=VMEM_BYTES),
        cost_estimate=pl.CostEstimate(
            flops=6 * row_count * depth,
            bytes_accessed=18 * row_count * depth,
            transcendentals=row_count * depth,
        ),
    )(core, scale, mine, away, mine_rows, away_rows, cols, weight)


class Pending:
    def __init__(self):
        self.active = []

    def add(self, task):
        held, moving = next(task)
        self.active.append([task, held, moving])

    def point(self, main):
        ready = [entry for entry in self.active if entry[1] == 0]
        main, moved = lax.optimization_barrier((main, [entry[2] for entry in ready]))
        for entry in self.active:
            entry[1] -= 1
        for entry, arrived in zip(ready, moved):
            self.advance(entry, arrived)
        return main

    def advance(self, entry, arrived):
        try:
            entry[1:] = entry[0].send(arrived)
        except StopIteration:
            self.active.remove(entry)

    def finish(self):
        while self.active:
            entry = self.active[0]
            self.advance(entry, entry[2])


def local_index(ids, row_low, row_count):
    shifted = ids - row_low
    inside = (shifted >= 0) & (shifted < row_count)
    return (inside, jnp.clip(shifted, 0, row_count - 1))


def body(
    tokens,
    segments,
    next_ids,
    second_ids,
    table,
    attn_in,
    attn_out,
    mlp_in,
    mlp_out,
    vectors,
    table_rows,
    table_cols,
    attn_in_rows,
    attn_in_cols,
    attn_out_rows,
    attn_out_cols,
    mlp_in_rows,
    mlp_in_cols,
    mlp_out_rows,
    mlp_out_cols,
    vector_state,
):
    n_ctx = lax.axis_size("ctx")
    n_seq = lax.axis_size("seq")
    n_fsdp = lax.axis_size("fsdp")
    n_y = n_ctx // 2
    n_group = n_seq * n_fsdp
    ctx_at = lax.axis_index("ctx")
    seq_at = lax.axis_index("seq")
    fsdp_at = lax.axis_index("fsdp")
    y_at = ctx_at // 2
    core_at = lax.rem(ctx_at, 2)
    group_at = seq_at * n_fsdp + fsdp_at
    all_seqs, length = segments.shape
    seqs_dev = all_seqs // n_group
    ctx_span = length // n_ctx
    feature_width = table.shape[1]
    layer_count = attn_in.shape[0]
    head_count = HEADS
    total_tokens = all_seqs * length
    own_rows = seqs_dev * ctx_span
    block_start = ctx_at * ctx_span
    positions = positions_of(segments)

    def block_of(grid):
        return lax.dynamic_slice_in_dim(grid, block_start, ctx_span, 1)

    tok_block = block_of(tokens).reshape(-1)
    valid_block = (block_of(segments) >= 0).astype(jnp.float32).reshape(-1)
    next_block = block_of(next_ids).reshape(-1)
    second_block = block_of(second_ids).reshape(-1)
    my_segments = lax.dynamic_slice_in_dim(segments, group_at * seqs_dev, seqs_dev, 0)
    my_positions = lax.dynamic_slice_in_dim(positions, group_at * seqs_dev, seqs_dev, 0)
    hops = jnp.asarray([(side, step) for side in range(2) for step in range(n_y)], jnp.int32)
    near_ctx = 2 * lax.rem(y_at - hops[:, 1] + n_y, n_y) + lax.rem(core_at + hops[:, 0], 2)

    def near_order(grid):
        cut = grid.reshape(seqs_dev, n_ctx, ctx_span).transpose(1, 0, 2)
        return jnp.take(cut, near_ctx, axis=0, mode="clip").reshape(-1)

    def own_order(grid):
        return block_of(grid).reshape(-1)

    time_grid = jnp.broadcast_to(jnp.arange(length, dtype=jnp.int32)[None], (seqs_dev, length))
    seq_grid = jnp.broadcast_to(jnp.arange(seqs_dev, dtype=jnp.int32)[:, None], (seqs_dev, length))
    q_seg, k_seg = (own_order(my_segments), near_order(my_segments))
    q_time, k_time = (own_order(time_grid), near_order(time_grid))
    q_seq, k_seq = (own_order(seq_grid), near_order(seq_grid))
    allowed = (q_seq[None] == k_seq[:, None]) & (
        (q_time[None] == k_time[:, None])
        | (k_time[:, None] < q_time[None]) & (q_seg[None] == k_seg[:, None]) & (k_seg[:, None] >= 0)
    )
    mask = jnp.where(allowed, 0.0, MASKED)
    rows_dev = table.shape[0]
    row_low = group_at * rows_dev
    rows_group = attn_in.shape[1]
    rows_part = rows_group // n_ctx
    down_cut = mlp_out.shape[1] // rows_group

    in_width, out_width, fc_width = attn_in.shape[2], attn_out.shape[2], mlp_in.shape[2]
    pack_width = in_width + out_width + fc_width + down_cut * feature_width
    part_width = pack_width // n_ctx
    model_rows = n_group * rows_group

    def gather_pack(layer_at):
        down = mlp_out[layer_at].reshape(down_cut, rows_group, feature_width)
        pack = jnp.concatenate(
            [attn_in[layer_at], mlp_in[layer_at], attn_out[layer_at]]
            + [down[cut] for cut in range(down_cut)],
            1,
        ).astype(jnp.bfloat16)
        part = lax.dynamic_slice_in_dim(pack, ctx_at * part_width, part_width, 1)
        if layer_at == layer_count - 1:
            head = lax.dynamic_slice_in_dim(
                attn_out[layer_count].astype(jnp.bfloat16), ctx_at * rows_part, rows_part, 0
            )
            head = jnp.pad(head.reshape(-1), (0, -head.size % part_width)).reshape(-1, part_width)
            part = jnp.concatenate([part, head], 0)
        return lax.all_gather(part, ("ctx", "seq", "fsdp"), axis=0)

    def cut_pack(layer_at, whole):
        whole = whole.reshape(n_ctx, n_group, -1, part_width)
        body_rows = whole[:, :, :rows_group].reshape(n_ctx, model_rows, part_width)

        def columns_of(low, high):
            pieces = []
            for at in range(n_ctx):
                start, stop = max(low, at * part_width), min(high, (at + 1) * part_width)
                if start < stop:
                    pieces.append(body_rows[at, :, start - at * part_width : stop - at * part_width])
            return pieces[0] if len(pieces) == 1 else jnp.concatenate(pieces, 1)

        at = in_width + fc_width
        down = jnp.stack(
            [
                columns_of(low, low + feature_width).reshape(n_group, rows_group, feature_width)
                for low in range(at + out_width, pack_width, feature_width)
            ],
            1,
        )
        weights = (
            columns_of(0, in_width),
            columns_of(at, at + out_width),
            columns_of(in_width, at),
            down.reshape(-1, feature_width),
        )
        head = None
        if layer_at == layer_count - 1:
            head = whole[:, :, rows_group:].reshape(n_ctx, n_group, -1)
            head = head[:, :, : rows_part * out_width].reshape(n_ctx, n_group, rows_part, out_width)
            head = head.transpose(1, 0, 2, 3).reshape(model_rows, out_width)
        return weights, head

    stored = [gather_pack(0)]

    tok_inside, tok_safe = local_index(tok_block, row_low, rows_dev)
    embed_term = jnp.where(
        tok_inside[:, None], jnp.take(table, tok_safe, axis=0, mode="clip"), 0.0
    ).astype(jnp.bfloat16)
    embed_term = embed_term.reshape(n_seq, n_fsdp, own_rows, feature_width)
    place_part = length // n_ctx
    place_low = VOCAB - rows_dev * (n_group - 1)
    places = lax.dynamic_slice_in_dim(table, place_low + ctx_at * place_part, place_part, 0)
    places = jnp.where(group_at == n_group - 1, places, 0.0).astype(jnp.bfloat16)
    def device_order(grid):
        cut = grid.reshape(n_group, seqs_dev, n_ctx, ctx_span)
        return cut.transpose(0, 2, 1, 3).reshape(n_group * n_ctx, own_rows)

    ids_grid = jnp.stack([device_order(tokens), device_order(positions) + VOCAB])
    near = (n_seq, n_fsdp, n_y) == (2, 4, 2)
    if near:
        across = [k << 2 for k in (0, 3, 1, 2)]
        stages = [
            [(0, 0), (0, 1)],
            [(16, 0), (2, 1)],
            [(2, 0), (18, 0), (16, 1), (18, 1)],
        ]
        order = [
            ((seat ^ step ^ side) << 1) | which
            for pieces in stages
            for side in (0, 1)
            for seat, which in pieces
            for step in across
        ]
        order = jnp.asarray(order, jnp.int32) ^ ((group_at * n_ctx + ctx_at) << 1)
        ids_grid = ids_grid.reshape(2, 2 * n_group * n_ctx, own_rows // 2)
        ids_grid = jnp.take(ids_grid, order, axis=1, mode="clip")
    ids_grid = ids_grid.reshape(2, -1)
    part_rows = -(-rows_dev // 512) * 256
    spare = part_rows * 2 - rows_dev
    table_low, table_t, table_square = prepare_table(table, 2 * part_rows)
    if near:
        flat = (-1, feature_width)
        sent = pick(embed_term, 1 - seq_at, 0).reshape(flat)
        away = shift_seq(jnp.concatenate([sent, places], 0), 1)
        away, table_low, table_t, table_square, ids_grid = lax.optimization_barrier(
            (away, table_low, table_t, table_square, ids_grid)
        )
        mine = pick(embed_term, seq_at, 0) + away[:-place_part].reshape(embed_term.shape[1:])
        places = places + away[-place_part:]
        outside = (fsdp_at == 0) | (fsdp_at == 3)
        pair = jnp.where(outside, mine[1:3], jnp.stack([mine[0], mine[3]]))
        sent = jnp.concatenate([pair.reshape(flat), places], 0)
        away = lax.ppermute(sent, "fsdp", NEAR_FIRST)
        kept_pair = jnp.where(outside, jnp.stack([mine[0], mine[3]]), mine[1:3])
        kept_pair = kept_pair + away[:-place_part].reshape(kept_pair.shape)
        places = places + away[-place_part:]
        sent = jnp.concatenate([jnp.where(fsdp_at < 2, kept_pair[1], kept_pair[0]), places], 0)
        away = lax.ppermute(sent, "fsdp", NEAR_SECOND)
        embed_term = jnp.where(fsdp_at < 2, kept_pair[0], kept_pair[1]) + away[:-place_part]
        total = places + away[-place_part:]
    else:
        embed_term = scatter_sum(embed_term, shift_seq, seq_at)
        embed_term = run(scatter_fsdp(embed_term, fsdp_at))
        total = places
        for step in range(1, n_seq):
            total = total + lax.ppermute(places, "seq", [(n_seq - 1, n_seq - 1 - step)])
        places = total
        for step in range(1, n_fsdp):
            total = total + lax.ppermute(places, "fsdp", [(n_fsdp - 1, n_fsdp - 1 - step)])
    places = gather_near(total)
    own_places = own_order(my_positions)
    place_ctx = own_places // place_part
    place_near = lax.rem(core_at + place_ctx, 2) * n_y + lax.rem(y_at - place_ctx // 2 + n_y, n_y)
    place_rows = jnp.take(
        places, place_near * place_part + lax.rem(own_places, place_part), axis=0, mode="clip"
    )
    stream = embed_term.astype(jnp.float32) + place_rows.astype(jnp.float32)
    share = 1.0 / n_ctx
    square_parts = [share * jnp.sum(table_square).reshape(1)] + [
        share * jnp.sum(weight * weight).reshape(1)
        for weight in (attn_in, attn_out, mlp_in, mlp_out)
    ]
    for layer_at in range(1, layer_count):
        stored.append(gather_pack(layer_at))
    kept = []
    squares = []
    for layer_at in range(layer_count):
        if layer_at:
            stream, stored[layer_at] = lax.optimization_barrier((stream, stored[layer_at]))
        stored[layer_at], head_weight = cut_pack(layer_at, stored[layer_at])
        stream, layer_kept, layer_sums = layer_forward(
            stream,
            stored[layer_at],
            vectors[12 * layer_at : 12 * layer_at + 12],
            mask,
            head_count,
        )
        kept.append(layer_kept)
        squares.append(layer_sums)
    final_gain = vectors[12 * layer_count]
    final_bias = vectors[12 * layer_count + 1]
    final_norm, final_back = jax.vjp(layer_norm, stream, final_gain, final_bias)
    final_low = final_norm.astype(jnp.bfloat16)
    second_low = product(final_low, head_weight).astype(jnp.bfloat16)
    live = jnp.clip(VOCAB - row_low, 0, rows_dev).astype(jnp.int32).reshape(1)

    def local_targets(ids):
        inside, safe = local_index(ids, row_low, rows_dev)
        return jnp.where(inside, safe, -1)

    final_all = lax.all_gather(final_low, ("seq", "fsdp"), axis=0)
    second_all = lax.all_gather(second_low, ("seq", "fsdp"), axis=0)
    second_factor = SECOND * valid_block
    final_local, second_local = local_targets(next_block), local_targets(second_block)
    final_t = final_all.swapaxes(1, 2)
    final_stats = head_stats(live, table_low, final_t, final_local[None])
    final_stats, second_all = lax.optimization_barrier((final_stats, second_all))
    second_t = second_all.swapaxes(1, 2)
    second_stats = head_stats(live, table_low, second_t, second_local[None])
    stats = merge_stats(jnp.concatenate([final_stats, second_stats], 1))
    half_rows = final_stats.shape[1]
    final_stats, second_stats = stats[:, :half_rows], stats[:, half_rows:]

    pending = Pending()
    results = {}

    def rows_task(name, d_rows):
        parts = d_rows.reshape((n_seq, n_fsdp) + d_rows.shape[1:])
        moved = yield 0, send_parts(parts, shift_seq, seq_at, sent=jnp.bfloat16)
        mine = add_parts(parts, moved, seq_at)
        results[name] = yield from scatter_fsdp(mine, fsdp_at)

    def line_of(stats, factor, local):
        return jnp.stack([stats[0], factor / total_tokens, local.astype(jnp.float32)])

    final_line = line_of(final_stats, valid_block, final_local)
    table_grad, d_rows = head_back(live, table_low, table_t, final_all, final_t, final_line)
    pending.add(rows_task("final", d_rows))
    second_line = line_of(second_stats, second_factor, second_local)
    cuts = 2 if own_rows % 256 == 0 else 1
    for cut in range(cuts):
        line = second_line.reshape(3, n_group, cuts, -1)[:, :, cut].reshape(3, -1)
        table_grad, d_rows = head_back(
            live, table_low, table_t, second_all, second_t, line, cut, table_grad
        )
        table_grad = pending.point(table_grad)
        pending.add(rows_task(("second", cut), d_rows))
    pending.finish()
    d_final = results["final"].T
    d_second = jnp.concatenate([results["second", cut] for cut in range(cuts)], 1).T
    loss_rows = (final_stats[0] - final_stats[1]) * valid_block + (
        second_stats[0] - second_stats[1]
    ) * second_factor
    loss_part = jnp.sum(
        lax.dynamic_slice_in_dim(loss_rows, group_at * own_rows, own_rows, 0)
    )

    def table_task():
        parts = table_grad.reshape(2, part_rows, feature_width)
        (away,) = yield 0, [swap_core(pick(parts, 1 - core_at, 0))]
        mine = (pick(parts, core_at, 0) + away).astype(jnp.bfloat16)
        totals = []
        quarter = part_rows // 4
        for low, wait in ((0, 2), (2 * quarter, 3)):
            pieces = [mine[low : low + quarter], mine[low + quarter : low + 2 * quarter]]
            if low:
                pieces = yield 0, pieces
            moved = yield wait, [
                [shift_y(piece, step) for step in range(1, n_y)] for piece in pieces
            ]
            for piece, away in zip(pieces, moved):
                ordered = order_parts([piece] + away, y_at).astype(jnp.float32)
                total = ordered[0]
                for step in range(1, n_y):
                    total = total + ordered[step]
                totals.append(total)
        results["table"] = totals

    def bundle_task(pairs, matrices, names, waits):
        (away,) = yield 0, [swap_pairs(pairs, core_at)]
        grads = shared_outer(pairs, away, core_at)
        parts = []
        for grad in grads:
            cut = grad.reshape(n_seq, n_fsdp, -1, rows_group, grad.shape[1])
            parts += [cut[:, :, at] for at in range(cut.shape[2])]
        stacked = jnp.concatenate(parts, -1)
        moved = yield waits[0], send_parts(stacked, shift_seq, seq_at, sent=jnp.bfloat16)
        mine = add_parts(stacked, moved, seq_at)
        mine = mine.reshape(n_fsdp, n_y, rows_group // n_y, -1)
        moved = yield waits[1], send_parts(mine, shift_y, y_at, 1, jnp.bfloat16)
        mine = add_parts(mine, moved, y_at, 1)
        mine = yield from scatter_fsdp(mine, fsdp_at)
        moved = yield 0, [shift_y(mine, step) for step in range(1, n_y)]
        column = order_parts([mine] + moved, y_at).reshape(rows_group, -1)
        (away,) = yield 0, [swap_core(column)]
        both = order_parts([column, away], core_at)
        at = 0
        for matrix, name in zip(matrices, names):
            width = matrix.shape[-1] // 2
            cuts = []
            for _ in range(matrix.shape[-2] // rows_group):
                cuts.append(
                    jnp.concatenate([both[0, :, at : at + width], both[1, :, at : at + width]], 1)
                )
                at += width
            results[name] = jnp.concatenate(cuts, 0)

    pending.add(table_task())
    d_second = pending.point(d_second)
    d_second_low = d_second.astype(jnp.bfloat16)
    d_stream, d_gain_final, d_bias_final = final_back(d_final + inner(d_second_low, head_weight))

    vec_list = [None] * layer_count
    for layer_at in reversed(range(layer_count)):

        def first_task(pairs, at=layer_at):
            matrices, names = [mlp_in[at], mlp_out[at]], [("fc", at), ("down", at)]
            if at == layer_count - 1:
                pairs = [(final_low, d_second_low)] + pairs
                matrices = [attn_out[layer_count]] + matrices
                names = [("out", layer_count)] + names
            return bundle_task(pairs, matrices, names, (1, 3) if at else (1, 0))

        def later_task(pairs, at=layer_at):
            names = [("in", at), ("out", at)]
            return bundle_task(
                pairs, [attn_in[at], attn_out[at]], names, (1, 1) if at else (1, 0)
            )

        d_stream, vec_list[layer_at] = layer_backward(
            d_stream,
            kept[layer_at],
            stored[layer_at],
            vectors[12 * layer_at : 12 * layer_at + 12],
            mask,
            head_count,
            pending,
            first_task,
            later_task,
        )
    part_ids = jnp.arange(part_rows, dtype=jnp.int32)
    part_live = part_ids < rows_dev - core_at * part_rows
    part_ids = jnp.where(part_live, row_low + core_at * part_rows + part_ids, -1)[:, None]

    quarter = part_rows // 4

    def spread(pieces, low, rows, between):
        ids = ids_grid[:, low : low + rows.shape[0]]
        added = []
        for at, piece in enumerate(pieces):
            here = part_ids[at * quarter : (at + 1) * quarter]
            hits = (here == ids[0][None]) | (here == ids[1][None])
            added.append(between(piece + product(hits.astype(jnp.bfloat16), rows)))
        return added

    mine = d_stream.astype(jnp.bfloat16)
    if near:
        half = own_rows // 2
        def flat(block):
            return block.reshape(-1, feature_width)

        mine = jnp.concatenate([mine, lax.ppermute(mine, "fsdp", NEAR_SECOND)], 0)
        mine = jnp.concatenate([mine, lax.ppermute(mine, "fsdp", NEAR_FIRST)], 0)
        mine = mine.reshape(4, 2, half, feature_width)
        front, back = flat(mine[:, 0]), flat(mine[:, 1])
        front_x, back_y = shift_seq(front, 1), shift_y(back, 1)
        here = jnp.concatenate([front, back], 0)
        here = jnp.concatenate([here, swap_core(here)], 0)
        pieces = spread(results["table"], 0, here, pending.point)
        done = here.shape[0]
        pieces[-1], front_x, back_y = lax.optimization_barrier((pieces[-1], front_x, back_y))
        front_y = shift_y(jnp.concatenate([front, front_x], 0), 1)
        back_x = shift_seq(jnp.concatenate([back, back_y], 0), 1)
        here = jnp.concatenate([front_x, back_y], 0)
        here = jnp.concatenate([here, swap_core(here)], 0)
        pieces = spread(pieces, done, here, pending.point)
        done += here.shape[0]
        pending.finish()
        last = jnp.concatenate([front_y, back_x], 0)
        last = jnp.concatenate([last, swap_core(last)], 0)
    else:
        pending.finish()
        last = lax.all_gather(mine, ("seq", "fsdp", "ctx"), axis=0, tiled=True)
        pieces, done = results["table"], 0
    summed = (
        None,
        jnp.stack([results["in", at] for at in range(layer_count)]),
        jnp.stack([results["out", at] for at in range(layer_count + 1)]),
        jnp.stack([results["fc", at] for at in range(layer_count)]),
        jnp.stack([results["down", at] for at in range(layer_count)]),
    )
    vector_grad = jnp.concatenate(vec_list + [jnp.stack([d_gain_final, d_bias_final])], 0)
    row_states = (attn_in_rows, attn_out_rows, mlp_in_rows, mlp_out_rows)
    rows_new = [None]
    col_parts = []
    weighted_parts = []
    row_parts = []
    for grad_sum, row_state in zip(summed[1:], row_states):
        square = grad_sum * grad_sum
        renewed = DECAY * row_state + (1.0 - DECAY) * jnp.mean(square + EPS_SQUARE, -1)
        rows_new.append(renewed)
        col_parts.append(share * jnp.sum(square + EPS_SQUARE, -2))
        weighted_parts.append(share * jnp.sum(square / renewed[..., None], -2))
        row_parts.append(share * jnp.sum(renewed, -1))
    numbers = jnp.concatenate(
        row_parts + square_parts + [loss_part.reshape(1), jnp.stack(squares).reshape(-1)]
    )
    row_count = sum(part.shape[0] for part in row_parts)
    numbers = jnp.pad(numbers, (0, feature_width - numbers.shape[0]))
    col_rows = [part.reshape(-1, feature_width) for part in col_parts]
    weighted_rows = [part.reshape(-1, feature_width) for part in weighted_parts]
    col_count = sum(part.shape[0] for part in col_rows)
    early = jnp.concatenate(col_rows + weighted_rows + [numbers[None], vector_grad], 0)
    early = jnp.pad(early, ((0, -early.shape[0] % 8), (0, 0)))
    hops = sum_hops(early)
    state = [next(hops)]

    def advance(piece):
        piece, state[0] = lax.optimization_barrier((piece, state[0]))
        state[0] = hops.send(state[0])
        return piece

    pieces = spread(pieces, done, last, advance)
    while True:
        try:
            state[0] = hops.send(state[0])
        except StopIteration as stop:
            everything = stop.value
            break
    table_part = jnp.concatenate(pieces, 0)
    table_away = swap_core(table_part)
    state_part = lax.dynamic_slice_in_dim(
        jnp.pad(table_rows, (0, spare)), core_at * part_rows, part_rows, 0
    )
    live_rows = part_live[:, None]
    part_square = table_part * table_part
    part_renewed = DECAY * state_part[:, None] + (1.0 - DECAY) * jnp.mean(
        part_square + EPS_SQUARE, -1, keepdims=True
    )
    part_renewed = jnp.where(live_rows, part_renewed, 1.0)
    away_renewed = swap_core(part_renewed)
    live_count = jnp.sum(part_live.astype(jnp.float32))
    rows_new[0] = jnp.concatenate(
        [
            jnp.where(core_at == 0, part_renewed, away_renewed),
            jnp.where(core_at == 0, away_renewed, part_renewed),
        ],
        0,
    )[:rows_dev, 0][None]
    row_sum = jnp.sum(jnp.where(live_rows, part_renewed, 0.0))
    late = jnp.concatenate(
        [
            (jnp.sum(part_square, 0) + EPS_SQUARE * live_count)[None],
            jnp.sum(part_square / part_renewed, 0)[None],
            jnp.full((6, feature_width), row_sum),
        ],
        0,
    )
    late = sum_all(late, skip_y=True)
    numbers = everything[2 * col_count]
    vector_sum = everything[2 * col_count + 1 : 2 * col_count + 1 + vector_grad.shape[0]]
    loss_sum = numbers[row_count + 5]
    square_total = numbers[row_count + 6 : row_count + 6 + 3 * layer_count]
    matrices = (table[None], attn_in, attn_out, mlp_in, mlp_out)
    col_states = (table_cols[None], attn_in_cols, attn_out_cols, mlp_in_cols, mlp_out_cols)
    row_totals = [rows_dev * n_group] + [weight.shape[1] * n_group for weight in matrices[1:]]
    shares = jnp.concatenate(
        [
            jnp.full((rows.shape[0], 1), (1.0 - DECAY) / row_total, jnp.float32)
            for rows, row_total in zip(col_rows, row_totals[1:])
        ],
        0,
    )
    old_cols = jnp.concatenate([state.reshape(-1, feature_width) for state in col_states[1:]], 0)
    new_cols = DECAY * old_cols + shares * everything[:col_count]
    ratios = jnp.sum(everything[col_count : 2 * col_count] / new_cols, -1)
    cols_new = []
    new_weights = []
    sizes_rms = []
    col_at = 0
    row_at = 0
    for matrix_at in range(5):
        weight, renewed, col_state = matrices[matrix_at], rows_new[matrix_at], col_states[matrix_at]
        if matrix_at == 0:
            renewed_cols = DECAY * col_state + (1.0 - DECAY) / row_totals[0] * late[:1]
            row_mean = late[2, :1] / row_totals[0]
            clip_total = jnp.sum(row_mean * jnp.sum(late[1:2] / renewed_cols, -1))
        else:
            stack_count = weight.shape[0]
            height = col_rows[matrix_at - 1].shape[0]
            renewed_cols = new_cols[col_at : col_at + height].reshape(col_state.shape)
            row_mean = numbers[row_at : row_at + stack_count] / row_totals[matrix_at]
            row_at += stack_count
            ratio = jnp.sum(ratios[col_at : col_at + height].reshape(stack_count, -1), -1)
            col_at += height
            clip_total = jnp.sum(row_mean * ratio)
        entries = weight.size * n_group
        update_rms = jnp.sqrt(clip_total / entries)
        weight_rms = jnp.sqrt(numbers[row_count + matrix_at] / entries)
        step_scale = RATE * jnp.maximum(EPS_SCALE, weight_rms) / jnp.maximum(1.0, update_rms / CLIP)
        cols_new.append(renewed_cols)
        sizes_rms.append(update_rms)
        if matrix_at == 0:
            table_sum, table_new, table_copy = update_table(
                core_at.astype(jnp.int32).reshape(1),
                step_scale.reshape(1),
                table_part,
                table_away,
                part_renewed,
                away_renewed,
                renewed_cols / row_mean[0],
                table,
            )
            new_weights.append(table_new)
            continue
        second_moment = renewed[:, :, None] * renewed_cols[:, None, :] / row_mean[:, None, None]
        update = summed[matrix_at] * lax.rsqrt(second_moment)
        new_weights.append(weight - step_scale * update)
    vector_state_new = DECAY * vector_state + (1.0 - DECAY) * (vector_sum * vector_sum + EPS_SQUARE)
    vector_update = vector_sum * lax.rsqrt(vector_state_new)
    vector_rms = jnp.sqrt(jnp.mean(vector_update * vector_update))
    vector_scale = (
        RATE
        * jnp.maximum(EPS_SCALE, jnp.sqrt(jnp.mean(vectors * vectors)))
        / jnp.maximum(1.0, vector_rms / CLIP)
    )
    vectors_new = vectors - vector_scale * vector_update
    sizes_rms.append(vector_rms)
    norms = jnp.concatenate([jnp.sqrt(square_total / total_tokens), jnp.stack(sizes_rms)])
    return (
        loss_sum,
        norms,
        table_sum,
        rows_new[0][0],
        cols_new[0][0],
        table_new,
        table_copy,
        summed[1],
        rows_new[1],
        cols_new[1],
        new_weights[1],
        new_weights[1].astype(jnp.bfloat16),
        summed[2],
        rows_new[2],
        cols_new[2],
        new_weights[2],
        new_weights[2].astype(jnp.bfloat16),
        summed[3],
        rows_new[3],
        cols_new[3],
        new_weights[3],
        new_weights[3].astype(jnp.bfloat16),
        summed[4],
        rows_new[4],
        cols_new[4],
        new_weights[4],
        new_weights[4].astype(jnp.bfloat16),
        vector_sum,
        vector_state_new,
        vectors_new,
    )


def solution(mesh):
    return jax.shard_map(
        body,
        mesh=mesh,
        in_specs=(
            P(),
            P(),
            P(),
            P(),
            P(("seq", "fsdp"), None),
            P(None, ("seq", "fsdp"), None),
            P(None, ("seq", "fsdp"), None),
            P(None, ("seq", "fsdp"), None),
            P(None, ("seq", "fsdp"), None),
            P(),
            P(("seq", "fsdp")),
            P(),
            P(None, ("seq", "fsdp")),
            P(),
            P(None, ("seq", "fsdp")),
            P(),
            P(None, ("seq", "fsdp")),
            P(),
            P(None, ("seq", "fsdp")),
            P(),
            P(),
        ),
        out_specs=(
            P(),
            P(),
            P(("seq", "fsdp"), None),
            P(("seq", "fsdp")),
            P(),
            P(("seq", "fsdp"), None),
            P(("seq", "fsdp"), None),
            P(None, ("seq", "fsdp"), None),
            P(None, ("seq", "fsdp")),
            P(),
            P(None, ("seq", "fsdp"), None),
            P(None, ("seq", "fsdp"), None),
            P(None, ("seq", "fsdp"), None),
            P(None, ("seq", "fsdp")),
            P(),
            P(None, ("seq", "fsdp"), None),
            P(None, ("seq", "fsdp"), None),
            P(None, ("seq", "fsdp"), None),
            P(None, ("seq", "fsdp")),
            P(),
            P(None, ("seq", "fsdp"), None),
            P(None, ("seq", "fsdp"), None),
            P(None, ("seq", "fsdp"), None),
            P(None, ("seq", "fsdp")),
            P(),
            P(None, ("seq", "fsdp"), None),
            P(None, ("seq", "fsdp"), None),
            P(),
            P(),
            P(),
        ),
        check_vma=False,
    )
```

```python
import functools

import jax
import jax.numpy as jnp
from jax import lax
from jax.experimental import pallas as pl
from jax.experimental.pallas import tpu as pltpu
from jax.sharding import PartitionSpec as P

HEADS = 12
VOCAB = 50304


EPS_NORM = 1e-05
EPS_SQUARE = 1e-30
EPS_SCALE = 0.001
DECAY = 0.5
CLIP = 0.4
RATE = 0.6
SECOND = 0.3
MASKED = -1e30
VMEM_BYTES = 56 * 1024 * 1024
NEAR_FIRST = [(0, 1), (1, 0), (2, 3), (3, 2)]
NEAR_SECOND = [(0, 3), (3, 0), (1, 2), (2, 1)]


def layer_norm(stream, gain, offset):
    center = stream - jnp.mean(stream, -1, keepdims=True)
    spread = jnp.mean(center * center, -1, keepdims=True)
    return center * lax.rsqrt(spread + EPS_NORM) * gain + offset


def gelu_tanh(value):
    return jax.nn.gelu(value, approximate=True)


def positions_of(segments):
    steps_at = jnp.arange(segments.shape[-1], dtype=jnp.int32)
    before = jnp.concatenate(
        [jnp.full(segments.shape[:-1] + (1,), -2, jnp.int32), segments[..., :-1]], -1
    )
    starts = jnp.where(segments != before, steps_at, 0)
    first = lax.cummax(starts, axis=segments.ndim - 1)
    return jnp.where(segments >= 0, steps_at - first, 0)


def product(left, right):
    return jnp.dot(left, right, preferred_element_type=jnp.float32)


def inner(left, right):
    return lax.dot_general(
        left, right, (((1,), (1,)), ((), ())), preferred_element_type=jnp.float32
    )


def outer(left, right):
    return lax.dot_general(
        left, right, (((0,), (0,)), ((), ())), preferred_element_type=jnp.float32
    )


def shift(block, axis, step):
    count = lax.axis_size(axis)
    return lax.ppermute(block, axis, [(i, (i + step) % count) for i in range(count)])


def shift_y(block, step):
    count = lax.axis_size("ctx")
    return lax.ppermute(block, "ctx", [(i, (i + 2 * step) % count) for i in range(count)])


def swap_core(block):
    count = lax.axis_size("ctx")
    return lax.ppermute(block, "ctx", [(i, i ^ 1) for i in range(count)])


def shift_seq(block, step):
    return shift(block, "seq", step)


def shift_fsdp(block, step):
    return shift(block, "fsdp", step)


def pick(parts, at, axis):
    return lax.dynamic_index_in_dim(parts, at, axis, False)


def send_parts(parts, mover, at, axis=0, sent=None):
    count = parts.shape[axis]
    moving = []
    for step in range(1, count):
        piece = pick(parts, lax.rem(at + step, count), axis)
        moving.append(mover(piece if sent is None else piece.astype(sent), step))
    return moving


def add_parts(parts, moved, at, axis=0):
    total = pick(parts, at, axis)
    for piece in moved:
        total = total + piece.astype(total.dtype)
    return total


def scatter_sum(parts, mover, at, axis=0, sent=None):
    return add_parts(parts, send_parts(parts, mover, at, axis, sent), at, axis)


def scatter_fsdp(parts, at):
    count = parts.shape[0]
    if count != 4:
        moved = yield 0, send_parts(parts, shift_fsdp, at, sent=jnp.bfloat16)
        return add_parts(parts, moved, at)
    outside = (at == 0) | (at == 3)
    mine = [jnp.where(outside, 0, 1), jnp.where(outside, 3, 2)]
    other = [jnp.where(outside, 1, 0), jnp.where(outside, 2, 3)]
    away = jnp.stack([pick(parts, slot, 0) for slot in other]).astype(jnp.bfloat16)
    (away,) = yield 0, [lax.ppermute(away, "fsdp", NEAR_FIRST)]
    first, second = (
        pick(parts, slot, 0) + away[k].astype(parts.dtype) for k, slot in enumerate(mine)
    )
    away = jnp.where(at < 2, second, first).astype(jnp.bfloat16)
    (away,) = yield 0, [lax.ppermute(away, "fsdp", NEAR_SECOND)]
    return jnp.where(at < 2, first, second) + away.astype(parts.dtype)


def run(task):
    moving = next(task)[1]
    while True:
        try:
            moving = task.send(moving)[1]
        except StopIteration as stop:
            return stop.value


def sum_hops(block, skip_y=False):
    for axis in ("ctx", "seq", "fsdp"):
        whole = lax.axis_size(axis)
        count = 2 if skip_y and axis == "ctx" else whole
        hop = 1
        while hop < count:
            moved = yield lax.ppermute(block, axis, [(i, i ^ hop) for i in range(whole)])
            block = block + moved
            hop *= 2
    return block


def sum_all(block, skip_y=False):
    hops = sum_hops(block, skip_y)
    moved = next(hops)
    while True:
        try:
            moved = hops.send(moved)
        except StopIteration as stop:
            return stop.value


def order_parts(parts, at):
    count = len(parts)
    if count == 2:
        first, second = parts
        return jnp.stack([jnp.where(at == 0, first, second), jnp.where(at == 0, second, first)])
    order = lax.rem(at - jnp.arange(count, dtype=jnp.int32) + count, count)
    return jnp.take(jnp.stack(parts), order, axis=0, mode="clip")


def gather_near(block):
    n_y = lax.axis_size("ctx") // 2
    column = jnp.concatenate([block] + [shift_y(block, step) for step in range(1, n_y)], 0)
    return jnp.concatenate([column, swap_core(column)], 0)


def scatter_near(parts):
    n_y = lax.axis_size("ctx") // 2
    parts = parts.reshape(2, 2, n_y, -1, parts.shape[2])
    column = parts[:, 0] + swap_core(parts[:, 1])
    total = column[:, 0]
    for step in range(1, n_y):
        away = shift_y(column[:, step].astype(jnp.bfloat16), n_y - step)
        total = total + away.astype(total.dtype)
    return total


def half_of(block, at):
    width = block.shape[-1] // 2
    return jnp.where(at == 0, block[..., :width], block[..., width:])


def qkv_bias(vec):
    return jnp.concatenate([vec[2], jnp.zeros_like(vec[2]), vec[3]])


def head_slabs(ref, lanes, width):
    block = ref[...].astype(jnp.float32)
    lane = lax.broadcasted_iota(jnp.int32, block.shape, 1)
    return [
        jnp.where((lane >= low) & (lane < low + width), block, 0.0).astype(jnp.bfloat16)
        for low in range(0, lanes, width)
    ]


def turned(ref):
    return ref[...].astype(jnp.float32).T.astype(jnp.bfloat16)


def across(left, right):
    return lax.dot_general(
        left, right, (((1,), (1,)), ((), ())), preferred_element_type=jnp.float32
    )


def by_head(parts, width):
    row = lax.broadcasted_iota(jnp.int32, parts[0].shape, 0)
    joined = parts[0]
    for at, part in enumerate(parts[1:], 1):
        joined = jnp.where(row >= at * width, part, joined)
    return joined


def attend_kernel(width, query_ref, key_ref, value_ref, mask_ref, mixed_ref, log_ref):
    lanes = query_ref.shape[1]
    scale = width ** (-0.5)
    value_t = turned(value_ref)
    mixed = []
    for at, query in enumerate(head_slabs(query_ref, lanes, width)):
        scores = across(key_ref[...], query) * scale + mask_ref[...]
        top = jnp.max(scores, 0, keepdims=True)
        probs = jnp.exp(scores - top)
        total = jnp.sum(probs, 0, keepdims=True)
        log_ref[0, at : at + 1, :] = top + jnp.log(total)
        probs_low = (probs * (1.0 / total)).astype(jnp.bfloat16)
        mixed.append(jnp.dot(value_t, probs_low, preferred_element_type=jnp.float32))
    mixed_ref[...] = by_head(mixed, width).T.astype(mixed_ref.dtype)


def attend_back_kernel(
    width, query_ref, key_ref, value_ref, mixed_ref, log_ref, mask_ref, d_query_ref, d_pair_ref
):
    lanes = query_ref.shape[1]
    scale = width ** (-0.5)
    key_t = turned(key_ref)
    queries = head_slabs(query_ref, lanes, width)
    d_heads = head_slabs(mixed_ref, lanes, width)
    d_query = []
    d_key = d_value = None
    for at, (query, d_head) in enumerate(zip(queries, d_heads)):
        scores = across(key_ref[...], query) * scale + mask_ref[...]
        probs = jnp.exp(scores - log_ref[0, at : at + 1, :])
        d_probs = across(value_ref[...], d_head)
        shared = jnp.sum(probs * d_probs, 0, keepdims=True)
        d_scores = (probs * (d_probs - shared)).astype(jnp.bfloat16)
        d_query.append(jnp.dot(key_t, d_scores, preferred_element_type=jnp.float32))
        part = jnp.dot(d_scores, query, preferred_element_type=jnp.float32)
        d_key = part if d_key is None else d_key + part
        part = jnp.dot(
            probs.astype(jnp.bfloat16), d_head, preferred_element_type=jnp.float32
        )
        d_value = part if d_value is None else d_value + part
    d_query_ref[...] = (by_head(d_query, width).T * scale).astype(d_query_ref.dtype)
    d_pair_ref[0] = d_key * scale
    d_pair_ref[1] = d_value


def attend(qkv_low, pairs, mask, head_count, lanes=128):
    row_count = qkv_low.shape[0]
    key_count, feature_width = pairs.shape[0], pairs.shape[1] // 2
    width = feature_width // head_count
    steps = feature_width // lanes
    return pl.pallas_call(
        functools.partial(attend_kernel, width),
        out_shape=(
            jax.ShapeDtypeStruct((row_count, feature_width), jnp.bfloat16),
            jax.ShapeDtypeStruct((steps, lanes // width, row_count), jnp.float32),
        ),
        grid=(steps,),
        in_specs=[
            pl.BlockSpec((row_count, lanes), lambda i: (0, i)),
            pl.BlockSpec((key_count, lanes), lambda i: (0, i)),
            pl.BlockSpec((key_count, lanes), lambda i: (0, steps + i)),
            pl.BlockSpec((key_count, row_count), lambda i: (0, 0)),
        ],
        out_specs=(
            pl.BlockSpec((row_count, lanes), lambda i: (0, i)),
            pl.BlockSpec((1, lanes // width, row_count), lambda i: (i, 0, 0)),
        ),
        compiler_params=pltpu.CompilerParams(vmem_limit_bytes=VMEM_BYTES),
        cost_estimate=pl.CostEstimate(
            flops=4 * row_count * key_count * lanes * head_count,
            bytes_accessed=4 * key_count * row_count + 4 * key_count * feature_width,
            transcendentals=row_count * key_count * head_count,
        ),
    )(qkv_low, pairs, pairs, mask)


def attend_back(qkv_low, pairs, d_mixed, log_total, mask, head_count, lanes=128):
    row_count = qkv_low.shape[0]
    key_count, feature_width = pairs.shape[0], pairs.shape[1] // 2
    width = feature_width // head_count
    steps = feature_width // lanes
    return pl.pallas_call(
        functools.partial(attend_back_kernel, width),
        out_shape=(
            jax.ShapeDtypeStruct((row_count, feature_width), jnp.bfloat16),
            jax.ShapeDtypeStruct((2, key_count, feature_width), jnp.float32),
        ),
        grid=(steps,),
        in_specs=[
            pl.BlockSpec((row_count, lanes), lambda i: (0, i)),
            pl.BlockSpec((key_count, lanes), lambda i: (0, i)),
            pl.BlockSpec((key_count, lanes), lambda i: (0, steps + i)),
            pl.BlockSpec((row_count, lanes), lambda i: (0, i)),
            pl.BlockSpec((1, lanes // width, row_count), lambda i: (i, 0, 0)),
            pl.BlockSpec((key_count, row_count), lambda i: (0, 0)),
        ],
        out_specs=(
            pl.BlockSpec((row_count, lanes), lambda i: (0, i)),
            pl.BlockSpec((2, key_count, lanes), lambda i: (0, 0, i)),
        ),
        compiler_params=pltpu.CompilerParams(vmem_limit_bytes=VMEM_BYTES),
        cost_estimate=pl.CostEstimate(
            flops=10 * row_count * key_count * lanes * head_count,
            bytes_accessed=4 * key_count * row_count + 12 * key_count * feature_width,
            transcendentals=row_count * key_count * head_count,
        ),
    )(qkv_low, pairs, pairs, d_mixed, log_total, mask)


def layer_forward(stream, weights, vec, mask, head_count):
    w_in, w_out, w_fc, w_down = weights
    feature_width = stream.shape[1]
    a_low = layer_norm(stream, vec[0], vec[1]).astype(jnp.bfloat16)
    qkv_low = (product(a_low, w_in) + qkv_bias(vec)).astype(jnp.bfloat16)
    pairs = gather_near(qkv_low[:, feature_width:])
    mixed_low, log_total = attend(qkv_low, pairs, mask, head_count)
    branch = product(mixed_low, w_out) + vec[4]
    middle = stream + branch
    m_low = layer_norm(middle, vec[5], vec[6]).astype(jnp.bfloat16)
    hidden = product(m_low, w_fc) + vec[8:12].reshape(-1)
    output = product(gelu_tanh(hidden).astype(jnp.bfloat16), w_down) + vec[7]
    sums = jnp.stack([jnp.sum(stream * stream), jnp.sum(branch * branch), jnp.sum(output * output)])
    kept = (stream, a_low, qkv_low, pairs, log_total, mixed_low, middle, m_low, hidden)
    return (middle + output, kept, sums)


def swap_pairs(pairs, core_at):
    lefts = [left for left, _ in pairs]
    return swap_core(
        jnp.concatenate(lefts + [half_of(right, 1 - core_at) for _, right in pairs], 1)
    )


def shared_outer(pairs, away, core_at):
    at = 0
    whole_left = []
    for left, _ in pairs:
        whole_left.append(jnp.concatenate([left, away[:, at : at + left.shape[1]]], 0))
        at += left.shape[1]
    grads = []
    for left, (_, right) in zip(whole_left, pairs):
        width = right.shape[1] // 2
        whole_right = jnp.concatenate([half_of(right, core_at), away[:, at : at + width]], 0)
        at += width
        grads.append(outer(left, whole_right))
    return grads


def layer_backward(d_stream, kept, weights, vec, mask, head_count, pending, first_task, later_task):
    stream, a_low, qkv_low, pairs, log_total, mixed_low, middle, m_low, hidden = kept
    w_in, w_out, w_fc, w_down = weights
    feature_width = stream.shape[1]
    norm_back_one = jax.vjp(layer_norm, stream, vec[0], vec[1])[1]
    norm_back_two = jax.vjp(layer_norm, middle, vec[5], vec[6])[1]
    gelu_out, gelu_back = jax.vjp(gelu_tanh, hidden)
    u_low = gelu_out.astype(jnp.bfloat16)
    d_out_low = d_stream.astype(jnp.bfloat16)
    d_hidden_low = gelu_back(inner(d_out_low, w_down))[0].astype(jnp.bfloat16)
    d_hidden_low = pending.point(d_hidden_low)
    pending.add(first_task([(m_low, d_hidden_low), (u_low, d_out_low)]))
    d_m = inner(d_hidden_low, w_fc)
    d_two, d_gain_two, d_bias_two = norm_back_two(d_m)
    d_middle = d_stream + d_two
    d_middle = pending.point(d_middle)
    d_middle_low = d_middle.astype(jnp.bfloat16)
    d_mixed = inner(d_middle_low, w_out).astype(jnp.bfloat16)
    d_query, d_pairs = attend_back(qkv_low, pairs, d_mixed, log_total, mask, head_count)
    d_pairs = pending.point(d_pairs)
    d_pairs = scatter_near(d_pairs).astype(jnp.bfloat16)
    d_qkv_low = jnp.concatenate([d_query, d_pairs[0], d_pairs[1]], 1)
    d_qkv_low = pending.point(d_qkv_low)
    pending.add(later_task([(a_low, d_qkv_low), (mixed_low, d_middle_low)]))
    d_one, d_gain_one, d_bias_one = norm_back_one(inner(d_qkv_low, w_in))
    d_qkv = d_qkv_low.astype(jnp.float32)
    rows_head = jnp.stack(
        [
            d_gain_one,
            d_bias_one,
            jnp.sum(d_qkv[:, :feature_width], 0),
            jnp.sum(d_qkv[:, 2 * feature_width :], 0),
            jnp.sum(d_middle_low.astype(jnp.float32), 0),
            d_gain_two,
            d_bias_two,
            jnp.sum(d_out_low.astype(jnp.float32), 0),
        ]
    )
    vec_grad = jnp.concatenate(
        [rows_head, jnp.sum(d_hidden_low.astype(jnp.float32), 0).reshape(4, feature_width)], 0
    )
    return (pending.point(d_middle + d_one), vec_grad)


def merge_stats(stats):
    for mover, axis in ((shift_seq, "seq"), (shift_fsdp, "fsdp")):
        parts = [stats] + [mover(stats, step) for step in range(1, lax.axis_size(axis))]
        top = parts[0][0]
        for part in parts[1:]:
            top = jnp.maximum(top, part[0])
        total = jnp.exp(parts[0][0] - top)
        picked = parts[0][1]
        for part in parts[1:]:
            total = total + jnp.exp(part[0] - top)
            picked = picked + part[1]
        stats = jnp.stack([top + jnp.log(total), picked])
    return stats


def blocks_of(groups, width, row_block):
    step = max(1, row_block // width)
    return [
        (range(low, low + step), slice(low * width, (low + step) * width))
        for low in range(0, groups, step)
    ]


def side_by_side(ref, at_block):
    return jnp.concatenate([ref[at] for at in at_block], 1)


def masked_logits(logits, live, first):
    column = lax.broadcasted_iota(jnp.int32, logits.shape, 0) + first
    return jnp.where(column < live, logits, MASKED)


def stats_kernel(row_block, live_ref, table_ref, rows_ref, target_ref, out_ref, top_ref, sum_ref, pick_ref):
    at = pl.program_id(0)
    tile = table_ref.shape[0]
    first = at * tile
    live = live_ref[0]

    @pl.when(at == 0)
    def _():
        top_ref[...] = jnp.full_like(top_ref, MASKED)
        sum_ref[...] = jnp.zeros_like(sum_ref)
        pick_ref[...] = jnp.zeros_like(pick_ref)

    def step(masked):
        for at_block, here in blocks_of(rows_ref.shape[0], rows_ref.shape[2], row_block):
            logits = jnp.dot(
                table_ref[...], side_by_side(rows_ref, at_block), preferred_element_type=jnp.float32
            )
            if masked:
                logits = masked_logits(logits, live, first)
            column = lax.broadcasted_iota(jnp.int32, logits.shape, 0)
            hit = column == target_ref[:, here] - first
            cut = logits.reshape(tile // 8, 8, logits.shape[1])
            top = top_ref[:, here]
            joint = jnp.maximum(top, jnp.max(cut, 0))
            total = jnp.sum(jnp.exp(cut - joint[None]), 0)
            sum_ref[:, here] = sum_ref[:, here] * jnp.exp(top - joint) + total
            top_ref[:, here] = joint
            pick_ref[:, here] += jnp.sum(
                jnp.where(hit, logits, 0.0).reshape(cut.shape), 0
            )

    @pl.when(first + tile <= live)
    def _():
        step(False)

    @pl.when((first + tile > live) & (first < live))
    def _():
        step(True)

    @pl.when(at == pl.num_programs(0) - 1)
    def _():
        top = top_ref[...]
        joint = jnp.max(top, 0, keepdims=True)
        total = jnp.sum(sum_ref[...] * jnp.exp(top - joint), 0, keepdims=True)
        out_ref[0:1, :] = joint + jnp.log(total)
        out_ref[1:2, :] = jnp.sum(pick_ref[...], 0, keepdims=True)


def head_stats(live, table_low, rows_t, target, tile=512, row_block=512):
    groups, depth, width = rows_t.shape
    count = groups * width
    height = table_low.shape[0]
    return pl.pallas_call(
        functools.partial(stats_kernel, row_block),
        out_shape=jax.ShapeDtypeStruct((2, count), jnp.float32),
        grid=(height // tile,),
        in_specs=[
            pl.BlockSpec(memory_space=pltpu.SMEM),
            pl.BlockSpec((tile, depth), lambda i: (i, 0)),
            pl.BlockSpec((groups, depth, width), lambda i: (0, 0, 0)),
            pl.BlockSpec((1, count), lambda i: (0, 0)),
        ],
        out_specs=pl.BlockSpec((2, count), lambda i: (0, 0)),
        scratch_shapes=[pltpu.VMEM((8, count), jnp.float32)] * 3,
        compiler_params=pltpu.CompilerParams(vmem_limit_bytes=VMEM_BYTES),
        cost_estimate=pl.CostEstimate(
            flops=2 * height * depth * count,
            bytes_accessed=2 * height * depth + 2 * depth * count,
            transcendentals=height * count,
        ),
    )(live, table_low, rows_t, target)


def back_kernel(row_block, added, live_ref, table_ref, table_t_ref, rows_ref, rows_t_ref, line_ref, *refs):
    if added:
        prior_ref, grad_ref, d_rows_ref = refs
    else:
        grad_ref, d_rows_ref = refs
    at = pl.program_id(0)
    tile = table_ref.shape[0]
    first = at * tile
    live = live_ref[0]
    width = d_rows_ref.shape[2]

    @pl.when(at == 0)
    def _():
        d_rows_ref[...] = jnp.zeros_like(d_rows_ref)

    def step(masked):
        grad = prior_ref[...] if added else None
        for at_block, here in blocks_of(rows_t_ref.shape[0], width, row_block):
            logits = jnp.dot(
                table_ref[...],
                side_by_side(rows_t_ref, at_block),
                preferred_element_type=jnp.float32,
            )
            if masked:
                logits = masked_logits(logits, live, first)
            column = lax.broadcasted_iota(jnp.int32, logits.shape, 0).astype(jnp.float32)
            probs = jnp.exp(logits - line_ref[0:1, here])
            hit = column == line_ref[2:3, here] - first.astype(jnp.float32)
            d_low = (line_ref[1:2, here] * jnp.where(hit, probs - 1.0, probs)).astype(jnp.bfloat16)
            rows = rows_ref[at_block.start : at_block.stop].reshape(-1, rows_ref.shape[2])
            part = jnp.dot(d_low, rows, preferred_element_type=jnp.float32)
            grad = part if grad is None else grad + part
            d_part = jnp.dot(table_t_ref[...], d_low, preferred_element_type=jnp.float32)
            for at_width, at_group in enumerate(at_block):
                d_rows_ref[at_group] += d_part[:, at_width * width : (at_width + 1) * width]
        grad_ref[...] = grad

    @pl.when(first + tile <= live)
    def _():
        step(False)

    @pl.when((first + tile > live) & (first < live))
    def _():
        step(True)

    @pl.when(first >= live)
    def _():
        grad_ref[...] = prior_ref[...] if added else jnp.zeros_like(grad_ref)


def head_back(live, table_low, table_t, rows, rows_t, line, cut=0, prior=None, tile=512):
    groups, _, depth = rows.shape
    height = table_low.shape[0]
    count = line.shape[1]
    width = count // groups
    once = dict(pipeline_mode=pl.Buffered(1))
    grad_spec = pl.BlockSpec((tile, depth), lambda i: (i, 0))
    added = prior is not None
    return pl.pallas_call(
        functools.partial(back_kernel, 1024, added),
        out_shape=(
            jax.ShapeDtypeStruct((height, depth), jnp.float32),
            jax.ShapeDtypeStruct((groups, depth, width), jnp.float32),
        ),
        grid=(height // tile,),
        in_specs=[
            pl.BlockSpec(memory_space=pltpu.SMEM),
            pl.BlockSpec((tile, depth), lambda i: (i, 0)),
            pl.BlockSpec((depth, tile), lambda i: (0, i)),
            pl.BlockSpec((groups, width, depth), lambda i: (0, cut, 0), **once),
            pl.BlockSpec((groups, depth, width), lambda i: (0, 0, cut), **once),
            pl.BlockSpec((3, count), lambda i: (0, 0), **once),
        ]
        + ([grad_spec] if added else []),
        out_specs=(
            grad_spec,
            pl.BlockSpec((groups, depth, width), lambda i: (0, 0, 0), **once),
        ),
        input_output_aliases={6: 0} if added else {},
        compiler_params=pltpu.CompilerParams(vmem_limit_bytes=VMEM_BYTES),
        cost_estimate=pl.CostEstimate(
            flops=6 * height * depth * count,
            bytes_accessed=4 * height * depth + 12 * depth * count + 8 * height * depth,
            transcendentals=height * count,
        ),
    )(live, table_low, table_t, rows, rows_t, line, *((prior,) if added else ()))


def prepare_kernel(row_count, table_ref, low_ref, turned_ref, square_ref):
    at = pl.program_id(0)
    tile = table_ref.shape[0]
    row = lax.broadcasted_iota(jnp.int32, table_ref.shape, 0) + at * tile
    block = jnp.where(row < row_count, table_ref[...], 0.0)
    low_ref[...] = block.astype(jnp.bfloat16)
    turned_ref[...] = block.T.astype(jnp.bfloat16)
    part = jnp.sum((block * block).reshape(tile // 8, 8, block.shape[1]), 0)

    @pl.when(at == 0)
    def _():
        square_ref[...] = part

    @pl.when(at > 0)
    def _():
        square_ref[...] += part


def prepare_table(table, height, tile=512):
    row_count, depth = table.shape
    return pl.pallas_call(
        functools.partial(prepare_kernel, row_count),
        out_shape=(
            jax.ShapeDtypeStruct((height, depth), jnp.bfloat16),
            jax.ShapeDtypeStruct((depth, height), jnp.bfloat16),
            jax.ShapeDtypeStruct((8, depth), jnp.float32),
        ),
        grid=(height // tile,),
        in_specs=[pl.BlockSpec((tile, depth), lambda i: (i, 0))],
        out_specs=(
            pl.BlockSpec((tile, depth), lambda i: (i, 0)),
            pl.BlockSpec((depth, tile), lambda i: (0, i)),
            pl.BlockSpec((8, depth), lambda i: (0, 0)),
        ),
        compiler_params=pltpu.CompilerParams(vmem_limit_bytes=VMEM_BYTES),
        cost_estimate=pl.CostEstimate(
            flops=2 * row_count * depth,
            bytes_accessed=4 * row_count * depth + 4 * height * depth,
            transcendentals=0,
        ),
    )(table)


def update_kernel(used, core_ref, scale_ref, mine_ref, away_ref, mine_rows_ref, away_rows_ref, cols_ref, weight_ref, *outs):
    grad_ref, new_ref, copy_ref = outs
    half = pl.program_id(0) // (pl.num_programs(0) // 2)
    chosen = half == core_ref[0]
    grad = jnp.where(chosen, mine_ref[...], away_ref[...])
    rows = jnp.where(chosen, mine_rows_ref[...], away_rows_ref[...])
    update = grad * lax.rsqrt(rows * cols_ref[...])
    new = weight_ref[...] - scale_ref[0] * update

    @pl.when(pl.program_id(0) < used)
    def _():
        grad_ref[...] = grad
        new_ref[...] = new
        copy_ref[...] = new.astype(copy_ref.dtype)


def update_table(core, scale, mine, away, mine_rows, away_rows, cols, weight):
    row_count, depth = weight.shape
    tile = mine.shape[0] // 4
    steps = mine.shape[0] // tile
    used = -(-row_count // tile)

    def mine_at(i, core_ref):
        return (jnp.clip(i - core_ref[0] * steps, 0, steps - 1), 0)

    def away_at(i, core_ref):
        return (jnp.clip(i - (1 - core_ref[0]) * steps, 0, steps - 1), 0)

    def whole_at(i, core_ref):
        return (jnp.minimum(i, used - 1), 0)

    whole = pl.BlockSpec((tile, depth), whole_at)
    return pl.pallas_call(
        functools.partial(update_kernel, used),
        out_shape=(
            jax.ShapeDtypeStruct(weight.shape, jnp.float32),
            jax.ShapeDtypeStruct(weight.shape, jnp.float32),
            jax.ShapeDtypeStruct(weight.shape, jnp.bfloat16),
        ),
        grid_spec=pltpu.PrefetchScalarGridSpec(
            num_scalar_prefetch=1,
            grid=(2 * steps,),
            in_specs=[
                pl.BlockSpec(memory_space=pltpu.SMEM),
                pl.BlockSpec((tile, depth), mine_at),
                pl.BlockSpec((tile, depth), away_at),
                pl.BlockSpec((tile, 1), mine_at),
                pl.BlockSpec((tile, 1), away_at),
                pl.BlockSpec((1, depth), lambda i, core_ref: (0, 0)),
                whole,
            ],
            out_specs=(whole, whole, whole),
        ),
        compiler_params=pltpu.CompilerParams(vmem_limit_bytes=VMEM_BYTES),
        cost_estimate=pl.CostEstimate(
            flops=6 * row_count * depth,
            bytes_accessed=18 * row_count * depth,
            transcendentals=row_count * depth,
        ),
    )(core, scale, mine, away, mine_rows, away_rows, cols, weight)


class Pending:
    def __init__(self):
        self.active = []

    def add(self, task):
        held, moving = next(task)
        self.active.append([task, held, moving])

    def point(self, main):
        ready = [entry for entry in self.active if entry[1] == 0]
        main, moved = lax.optimization_barrier((main, [entry[2] for entry in ready]))
        for entry in self.active:
            entry[1] -= 1
        for entry, arrived in zip(ready, moved):
            self.advance(entry, arrived)
        return main

    def advance(self, entry, arrived):
        try:
            entry[1:] = entry[0].send(arrived)
        except StopIteration:
            self.active.remove(entry)

    def finish(self):
        while self.active:
            entry = self.active[0]
            self.advance(entry, entry[2])


def local_index(ids, row_low, row_count):
    shifted = ids - row_low
    inside = (shifted >= 0) & (shifted < row_count)
    return (inside, jnp.clip(shifted, 0, row_count - 1))


def body(
    tokens,
    segments,
    next_ids,
    second_ids,
    table,
    attn_in,
    attn_out,
    mlp_in,
    mlp_out,
    vectors,
    table_rows,
    table_cols,
    attn_in_rows,
    attn_in_cols,
    attn_out_rows,
    attn_out_cols,
    mlp_in_rows,
    mlp_in_cols,
    mlp_out_rows,
    mlp_out_cols,
    vector_state,
):
    n_ctx = lax.axis_size("ctx")
    n_seq = lax.axis_size("seq")
    n_fsdp = lax.axis_size("fsdp")
    n_y = n_ctx // 2
    n_group = n_seq * n_fsdp
    ctx_at = lax.axis_index("ctx")
    seq_at = lax.axis_index("seq")
    fsdp_at = lax.axis_index("fsdp")
    y_at = ctx_at // 2
    core_at = lax.rem(ctx_at, 2)
    group_at = seq_at * n_fsdp + fsdp_at
    all_seqs, length = segments.shape
    seqs_dev = all_seqs // n_group
    ctx_span = length // n_ctx
    feature_width = table.shape[1]
    layer_count = attn_in.shape[0]
    head_count = HEADS
    total_tokens = all_seqs * length
    own_rows = seqs_dev * ctx_span
    block_start = ctx_at * ctx_span
    positions = positions_of(segments)

    def block_of(grid):
        return lax.dynamic_slice_in_dim(grid, block_start, ctx_span, 1)

    tok_block = block_of(tokens).reshape(-1)
    valid_block = (block_of(segments) >= 0).astype(jnp.float32).reshape(-1)
    next_block = block_of(next_ids).reshape(-1)
    second_block = block_of(second_ids).reshape(-1)
    my_segments = lax.dynamic_slice_in_dim(segments, group_at * seqs_dev, seqs_dev, 0)
    my_positions = lax.dynamic_slice_in_dim(positions, group_at * seqs_dev, seqs_dev, 0)
    hops = jnp.asarray([(side, step) for side in range(2) for step in range(n_y)], jnp.int32)
    near_ctx = 2 * lax.rem(y_at - hops[:, 1] + n_y, n_y) + lax.rem(core_at + hops[:, 0], 2)

    def near_order(grid):
        cut = grid.reshape(seqs_dev, n_ctx, ctx_span).transpose(1, 0, 2)
        return jnp.take(cut, near_ctx, axis=0, mode="clip").reshape(-1)

    def own_order(grid):
        return block_of(grid).reshape(-1)

    time_grid = jnp.broadcast_to(jnp.arange(length, dtype=jnp.int32)[None], (seqs_dev, length))
    seq_grid = jnp.broadcast_to(jnp.arange(seqs_dev, dtype=jnp.int32)[:, None], (seqs_dev, length))
    q_seg, k_seg = (own_order(my_segments), near_order(my_segments))
    q_time, k_time = (own_order(time_grid), near_order(time_grid))
    q_seq, k_seq = (own_order(seq_grid), near_order(seq_grid))
    allowed = (q_seq[None] == k_seq[:, None]) & (
        (q_time[None] == k_time[:, None])
        | (k_time[:, None] < q_time[None]) & (q_seg[None] == k_seg[:, None]) & (k_seg[:, None] >= 0)
    )
    mask = jnp.where(allowed, 0.0, MASKED)
    rows_dev = table.shape[0]
    row_low = group_at * rows_dev
    rows_group = attn_in.shape[1]
    rows_part = rows_group // n_ctx
    down_cut = mlp_out.shape[1] // rows_group

    in_width, out_width, fc_width = attn_in.shape[2], attn_out.shape[2], mlp_in.shape[2]
    pack_width = in_width + out_width + fc_width + down_cut * feature_width
    part_width = pack_width // n_ctx
    model_rows = n_group * rows_group

    def gather_pack(layer_at):
        down = mlp_out[layer_at].reshape(down_cut, rows_group, feature_width)
        pack = jnp.concatenate(
            [attn_in[layer_at], mlp_in[layer_at], attn_out[layer_at]]
            + [down[cut] for cut in range(down_cut)],
            1,
        ).astype(jnp.bfloat16)
        part = lax.dynamic_slice_in_dim(pack, ctx_at * part_width, part_width, 1)
        if layer_at == layer_count - 1:
            head = lax.dynamic_slice_in_dim(
                attn_out[layer_count].astype(jnp.bfloat16), ctx_at * rows_part, rows_part, 0
            )
            head = jnp.pad(head.reshape(-1), (0, -head.size % part_width)).reshape(-1, part_width)
            part = jnp.concatenate([part, head], 0)
        return lax.all_gather(part, ("ctx", "seq", "fsdp"), axis=0)

    def cut_pack(layer_at, whole):
        whole = whole.reshape(n_ctx, n_group, -1, part_width)
        body_rows = whole[:, :, :rows_group].reshape(n_ctx, model_rows, part_width)

        def columns_of(low, high):
            pieces = []
            for at in range(n_ctx):
                start, stop = max(low, at * part_width), min(high, (at + 1) * part_width)
                if start < stop:
                    pieces.append(body_rows[at, :, start - at * part_width : stop - at * part_width])
            return pieces[0] if len(pieces) == 1 else jnp.concatenate(pieces, 1)

        at = in_width + fc_width
        down = jnp.stack(
            [
                columns_of(low, low + feature_width).reshape(n_group, rows_group, feature_width)
                for low in range(at + out_width, pack_width, feature_width)
            ],
            1,
        )
        weights = (
            columns_of(0, in_width),
            columns_of(at, at + out_width),
            columns_of(in_width, at),
            down.reshape(-1, feature_width),
        )
        head = None
        if layer_at == layer_count - 1:
            head = whole[:, :, rows_group:].reshape(n_ctx, n_group, -1)
            head = head[:, :, : rows_part * out_width].reshape(n_ctx, n_group, rows_part, out_width)
            head = head.transpose(1, 0, 2, 3).reshape(model_rows, out_width)
        return weights, head

    stored = [gather_pack(0)]

    tok_inside, tok_safe = local_index(tok_block, row_low, rows_dev)
    embed_term = jnp.where(
        tok_inside[:, None], jnp.take(table, tok_safe, axis=0, mode="clip"), 0.0
    ).astype(jnp.bfloat16)
    embed_term = embed_term.reshape(n_seq, n_fsdp, own_rows, feature_width)
    place_part = length // n_ctx
    place_low = VOCAB - rows_dev * (n_group - 1)
    places = lax.dynamic_slice_in_dim(table, place_low + ctx_at * place_part, place_part, 0)
    places = jnp.where(group_at == n_group - 1, places, 0.0).astype(jnp.bfloat16)
    def device_order(grid):
        cut = grid.reshape(n_group, seqs_dev, n_ctx, ctx_span)
        return cut.transpose(0, 2, 1, 3).reshape(n_group * n_ctx, own_rows)

    ids_grid = jnp.stack([device_order(tokens), device_order(positions) + VOCAB])
    near = (n_seq, n_fsdp, n_y) == (2, 4, 2)
    if near:
        across = [k << 2 for k in (0, 3, 1, 2)]
        stages = [
            [(0, 0), (0, 1)],
            [(16, 0), (2, 1)],
            [(2, 0), (18, 0), (16, 1), (18, 1)],
        ]
        order = [
            ((seat ^ step ^ side) << 1) | which
            for pieces in stages
            for side in (0, 1)
            for seat, which in pieces
            for step in across
        ]
        order = jnp.asarray(order, jnp.int32) ^ ((group_at * n_ctx + ctx_at) << 1)
        ids_grid = ids_grid.reshape(2, 2 * n_group * n_ctx, own_rows // 2)
        ids_grid = jnp.take(ids_grid, order, axis=1, mode="clip")
    ids_grid = ids_grid.reshape(2, -1)
    part_rows = -(-rows_dev // 512) * 256
    spare = part_rows * 2 - rows_dev
    table_low, table_t, table_square = prepare_table(table, 2 * part_rows)
    if near:
        flat = (-1, feature_width)
        sent = pick(embed_term, 1 - seq_at, 0).reshape(flat)
        away = shift_seq(jnp.concatenate([sent, places], 0), 1)
        away, table_low, table_t, table_square, ids_grid = lax.optimization_barrier(
            (away, table_low, table_t, table_square, ids_grid)
        )
        mine = pick(embed_term, seq_at, 0) + away[:-place_part].reshape(embed_term.shape[1:])
        places = places + away[-place_part:]
        outside = (fsdp_at == 0) | (fsdp_at == 3)
        pair = jnp.where(outside, mine[1:3], jnp.stack([mine[0], mine[3]]))
        sent = jnp.concatenate([pair.reshape(flat), places], 0)
        away = lax.ppermute(sent, "fsdp", NEAR_FIRST)
        kept_pair = jnp.where(outside, jnp.stack([mine[0], mine[3]]), mine[1:3])
        kept_pair = kept_pair + away[:-place_part].reshape(kept_pair.shape)
        places = places + away[-place_part:]
        sent = jnp.concatenate([jnp.where(fsdp_at < 2, kept_pair[1], kept_pair[0]), places], 0)
        away = lax.ppermute(sent, "fsdp", NEAR_SECOND)
        embed_term = jnp.where(fsdp_at < 2, kept_pair[0], kept_pair[1]) + away[:-place_part]
        total = places + away[-place_part:]
    else:
        embed_term = scatter_sum(embed_term, shift_seq, seq_at)
        embed_term = run(scatter_fsdp(embed_term, fsdp_at))
        total = places
        for step in range(1, n_seq):
            total = total + lax.ppermute(places, "seq", [(n_seq - 1, n_seq - 1 - step)])
        places = total
        for step in range(1, n_fsdp):
            total = total + lax.ppermute(places, "fsdp", [(n_fsdp - 1, n_fsdp - 1 - step)])
    places = gather_near(total)
    own_places = own_order(my_positions)
    place_ctx = own_places // place_part
    place_near = lax.rem(core_at + place_ctx, 2) * n_y + lax.rem(y_at - place_ctx // 2 + n_y, n_y)
    place_rows = jnp.take(
        places, place_near * place_part + lax.rem(own_places, place_part), axis=0, mode="clip"
    )
    stream = embed_term.astype(jnp.float32) + place_rows.astype(jnp.float32)
    share = 1.0 / n_ctx
    square_parts = [share * jnp.sum(table_square).reshape(1)] + [
        share * jnp.sum(weight * weight).reshape(1)
        for weight in (attn_in, attn_out, mlp_in, mlp_out)
    ]
    for layer_at in range(1, layer_count):
        stored.append(gather_pack(layer_at))
    kept = []
    squares = []
    for layer_at in range(layer_count):
        if layer_at:
            stream, stored[layer_at] = lax.optimization_barrier((stream, stored[layer_at]))
        stored[layer_at], head_weight = cut_pack(layer_at, stored[layer_at])
        stream, layer_kept, layer_sums = layer_forward(
            stream,
            stored[layer_at],
            vectors[12 * layer_at : 12 * layer_at + 12],
            mask,
            head_count,
        )
        kept.append(layer_kept)
        squares.append(layer_sums)
    final_gain = vectors[12 * layer_count]
    final_bias = vectors[12 * layer_count + 1]
    final_norm, final_back = jax.vjp(layer_norm, stream, final_gain, final_bias)
    final_low = final_norm.astype(jnp.bfloat16)
    second_low = product(final_low, head_weight).astype(jnp.bfloat16)
    live = jnp.clip(VOCAB - row_low, 0, rows_dev).astype(jnp.int32).reshape(1)

    def local_targets(ids):
        inside, safe = local_index(ids, row_low, rows_dev)
        return jnp.where(inside, safe, -1)

    final_all = lax.all_gather(final_low, ("seq", "fsdp"), axis=0)
    second_all = lax.all_gather(second_low, ("seq", "fsdp"), axis=0)
    second_factor = SECOND * valid_block
    final_local, second_local = local_targets(next_block), local_targets(second_block)
    final_t = final_all.swapaxes(1, 2)
    final_stats = head_stats(live, table_low, final_t, final_local[None])
    final_stats, second_all = lax.optimization_barrier((final_stats, second_all))
    second_t = second_all.swapaxes(1, 2)
    second_stats = head_stats(live, table_low, second_t, second_local[None])
    stats = merge_stats(jnp.concatenate([final_stats, second_stats], 1))
    half_rows = final_stats.shape[1]
    final_stats, second_stats = stats[:, :half_rows], stats[:, half_rows:]

    pending = Pending()
    results = {}

    def rows_task(name, d_rows):
        parts = d_rows.reshape((n_seq, n_fsdp) + d_rows.shape[1:])
        moved = yield 0, send_parts(parts, shift_seq, seq_at, sent=jnp.bfloat16)
        mine = add_parts(parts, moved, seq_at)
        results[name] = yield from scatter_fsdp(mine, fsdp_at)

    def line_of(stats, factor, local):
        return jnp.stack([stats[0], factor / total_tokens, local.astype(jnp.float32)])

    final_line = line_of(final_stats, valid_block, final_local)
    table_grad, d_rows = head_back(live, table_low, table_t, final_all, final_t, final_line)
    pending.add(rows_task("final", d_rows))
    second_line = line_of(second_stats, second_factor, second_local)
    cuts = 2 if own_rows % 256 == 0 else 1
    for cut in range(cuts):
        line = second_line.reshape(3, n_group, cuts, -1)[:, :, cut].reshape(3, -1)
        table_grad, d_rows = head_back(
            live, table_low, table_t, second_all, second_t, line, cut, table_grad
        )
        table_grad = pending.point(table_grad)
        pending.add(rows_task(("second", cut), d_rows))
    pending.finish()
    d_final = results["final"].T
    d_second = jnp.concatenate([results["second", cut] for cut in range(cuts)], 1).T
    loss_rows = (final_stats[0] - final_stats[1]) * valid_block + (
        second_stats[0] - second_stats[1]
    ) * second_factor
    loss_part = jnp.sum(
        lax.dynamic_slice_in_dim(loss_rows, group_at * own_rows, own_rows, 0)
    )

    def table_task():
        parts = table_grad.reshape(2, part_rows, feature_width)
        (away,) = yield 0, [swap_core(pick(parts, 1 - core_at, 0))]
        mine = (pick(parts, core_at, 0) + away).astype(jnp.bfloat16)
        totals = []
        quarter = part_rows // 4
        for low, wait in ((0, 3), (2 * quarter, 3)):
            pieces = [mine[low : low + quarter], mine[low + quarter : low + 2 * quarter]]
            if low:
                pieces = yield 0, pieces
            moved = yield wait, [
                [shift_y(piece, step) for step in range(1, n_y)] for piece in pieces
            ]
            for piece, away in zip(pieces, moved):
                ordered = order_parts([piece] + away, y_at).astype(jnp.float32)
                total = ordered[0]
                for step in range(1, n_y):
                    total = total + ordered[step]
                totals.append(total)
        results["table"] = totals

    def bundle_task(pairs, matrices, names, waits):
        (away,) = yield 0, [swap_pairs(pairs, core_at)]
        grads = shared_outer(pairs, away, core_at)
        parts = []
        for grad in grads:
            cut = grad.reshape(n_seq, n_fsdp, -1, rows_group, grad.shape[1])
            parts += [cut[:, :, at] for at in range(cut.shape[2])]
        stacked = jnp.concatenate(parts, -1)
        moved = yield waits[0], send_parts(stacked, shift_seq, seq_at, sent=jnp.bfloat16)
        mine = add_parts(stacked, moved, seq_at)
        mine = mine.reshape(n_fsdp, n_y, rows_group // n_y, -1)
        moved = yield waits[1], send_parts(mine, shift_y, y_at, 1, jnp.bfloat16)
        mine = add_parts(mine, moved, y_at, 1)
        mine = yield from scatter_fsdp(mine, fsdp_at)
        moved = yield 0, [shift_y(mine, step) for step in range(1, n_y)]
        column = order_parts([mine] + moved, y_at).reshape(rows_group, -1)
        (away,) = yield 0, [swap_core(column)]
        both = order_parts([column, away], core_at)
        at = 0
        for matrix, name in zip(matrices, names):
            width = matrix.shape[-1] // 2
            cuts = []
            for _ in range(matrix.shape[-2] // rows_group):
                cuts.append(
                    jnp.concatenate([both[0, :, at : at + width], both[1, :, at : at + width]], 1)
                )
                at += width
            results[name] = jnp.concatenate(cuts, 0)

    pending.add(table_task())
    d_second = pending.point(d_second)
    d_second_low = d_second.astype(jnp.bfloat16)
    d_stream, d_gain_final, d_bias_final = final_back(d_final + inner(d_second_low, head_weight))

    vec_list = [None] * layer_count
    for layer_at in reversed(range(layer_count)):

        def first_task(pairs, at=layer_at):
            matrices, names = [mlp_in[at], mlp_out[at]], [("fc", at), ("down", at)]
            if at == layer_count - 1:
                pairs = [(final_low, d_second_low)] + pairs
                matrices = [attn_out[layer_count]] + matrices
                names = [("out", layer_count)] + names
            return bundle_task(pairs, matrices, names, (2, 3) if at else (2, 0))

        def later_task(pairs, at=layer_at):
            names = [("in", at), ("out", at)]
            return bundle_task(
                pairs, [attn_in[at], attn_out[at]], names, (2, 1) if at else (0, 0)
            )

        d_stream, vec_list[layer_at] = layer_backward(
            d_stream,
            kept[layer_at],
            stored[layer_at],
            vectors[12 * layer_at : 12 * layer_at + 12],
            mask,
            head_count,
            pending,
            first_task,
            later_task,
        )
    part_ids = jnp.arange(part_rows, dtype=jnp.int32)
    part_live = part_ids < rows_dev - core_at * part_rows
    part_ids = jnp.where(part_live, row_low + core_at * part_rows + part_ids, -1)[:, None]

    quarter = part_rows // 4

    def add_hits(piece, at, low, rows):
        ids = ids_grid[:, low : low + rows.shape[0]]
        here = part_ids[at * quarter : (at + 1) * quarter]
        hits = (here == ids[0][None]) | (here == ids[1][None])
        return piece + product(hits.astype(jnp.bfloat16), rows)

    mine = d_stream.astype(jnp.bfloat16)
    if near:
        half = own_rows // 2
        def flat(block):
            return block.reshape(-1, feature_width)

        mine = jnp.concatenate([mine, lax.ppermute(mine, "fsdp", NEAR_SECOND)], 0)
        mine = jnp.concatenate([mine, lax.ppermute(mine, "fsdp", NEAR_FIRST)], 0)
        mine = mine.reshape(4, 2, half, feature_width)
        front, back = flat(mine[:, 0]), flat(mine[:, 1])
        front_x, back_y = shift_seq(front, 1), shift_y(back, 1)
        here = jnp.concatenate([front, back], 0)
        here = jnp.concatenate([here, swap_core(here)], 0)
        pieces = list(results["table"])
        for at in (0, 1):
            pieces[at] = add_hits(pieces[at], at, 0, here)
        pieces[1], front_x, back_y = lax.optimization_barrier((pieces[1], front_x, back_y))
        front_y = shift_y(jnp.concatenate([front, front_x], 0), 1)
        back_x = shift_seq(jnp.concatenate([back, back_y], 0), 1)
        for at in (2, 3):
            pieces[at] = pending.point(add_hits(pieces[at], at, 0, here))
        done = here.shape[0]
        here = jnp.concatenate([front_x, back_y], 0)
        here = jnp.concatenate([here, swap_core(here)], 0)
        for at in range(4):
            pieces[at] = pending.point(add_hits(pieces[at], at, done, here))
        done += here.shape[0]
        pending.finish()
        last = jnp.concatenate([front_y, back_x], 0)
        last = jnp.concatenate([last, swap_core(last)], 0)
    else:
        pending.finish()
        last = lax.all_gather(mine, ("seq", "fsdp", "ctx"), axis=0, tiled=True)
        pieces, done = results["table"], 0
    summed = (
        None,
        jnp.stack([results["in", at] for at in range(layer_count)]),
        jnp.stack([results["out", at] for at in range(layer_count + 1)]),
        jnp.stack([results["fc", at] for at in range(layer_count)]),
        jnp.stack([results["down", at] for at in range(layer_count)]),
    )
    vector_grad = jnp.concatenate(vec_list + [jnp.stack([d_gain_final, d_bias_final])], 0)
    row_states = (attn_in_rows, attn_out_rows, mlp_in_rows, mlp_out_rows)
    rows_new = [None]
    col_parts = []
    weighted_parts = []
    row_parts = []
    for grad_sum, row_state in zip(summed[1:], row_states):
        square = grad_sum * grad_sum
        renewed = DECAY * row_state + (1.0 - DECAY) * jnp.mean(square + EPS_SQUARE, -1)
        rows_new.append(renewed)
        col_parts.append(share * jnp.sum(square + EPS_SQUARE, -2))
        weighted_parts.append(share * jnp.sum(square / renewed[..., None], -2))
        row_parts.append(share * jnp.sum(renewed, -1))
    numbers = jnp.concatenate(
        row_parts + square_parts + [loss_part.reshape(1), jnp.stack(squares).reshape(-1)]
    )
    row_count = sum(part.shape[0] for part in row_parts)
    numbers = jnp.pad(numbers, (0, feature_width - numbers.shape[0]))
    col_rows = [part.reshape(-1, feature_width) for part in col_parts]
    weighted_rows = [part.reshape(-1, feature_width) for part in weighted_parts]
    col_count = sum(part.shape[0] for part in col_rows)
    early = jnp.concatenate(col_rows + weighted_rows + [numbers[None], vector_grad], 0)
    early = jnp.pad(early, ((0, -early.shape[0] % 8), (0, 0)))
    hops = sum_hops(early)
    state = [next(hops)]

    def advance(piece):
        piece, state[0] = lax.optimization_barrier((piece, state[0]))
        state[0] = hops.send(state[0])
        return piece

    pieces = [
        advance(add_hits(piece, at, done, last)) for at, piece in enumerate(pieces)
    ]
    while True:
        try:
            state[0] = hops.send(state[0])
        except StopIteration as stop:
            everything = stop.value
            break
    table_part = jnp.concatenate(pieces, 0)
    table_away = swap_core(table_part)
    state_part = lax.dynamic_slice_in_dim(
        jnp.pad(table_rows, (0, spare)), core_at * part_rows, part_rows, 0
    )
    live_rows = part_live[:, None]
    part_square = table_part * table_part
    part_renewed = DECAY * state_part[:, None] + (1.0 - DECAY) * jnp.mean(
        part_square + EPS_SQUARE, -1, keepdims=True
    )
    part_renewed = jnp.where(live_rows, part_renewed, 1.0)
    away_renewed = swap_core(part_renewed)
    live_count = jnp.sum(part_live.astype(jnp.float32))
    rows_new[0] = jnp.concatenate(
        [
            jnp.where(core_at == 0, part_renewed, away_renewed),
            jnp.where(core_at == 0, away_renewed, part_renewed),
        ],
        0,
    )[:rows_dev, 0][None]
    row_sum = jnp.sum(jnp.where(live_rows, part_renewed, 0.0))
    late = jnp.concatenate(
        [
            (jnp.sum(part_square, 0) + EPS_SQUARE * live_count)[None],
            jnp.sum(part_square / part_renewed, 0)[None],
            jnp.full((6, feature_width), row_sum),
        ],
        0,
    )
    late = sum_all(late, skip_y=True)
    numbers = everything[2 * col_count]
    vector_sum = everything[2 * col_count + 1 : 2 * col_count + 1 + vector_grad.shape[0]]
    loss_sum = numbers[row_count + 5]
    square_total = numbers[row_count + 6 : row_count + 6 + 3 * layer_count]
    matrices = (table[None], attn_in, attn_out, mlp_in, mlp_out)
    col_states = (table_cols[None], attn_in_cols, attn_out_cols, mlp_in_cols, mlp_out_cols)
    row_totals = [rows_dev * n_group] + [weight.shape[1] * n_group for weight in matrices[1:]]
    shares = jnp.concatenate(
        [
            jnp.full((rows.shape[0], 1), (1.0 - DECAY) / row_total, jnp.float32)
            for rows, row_total in zip(col_rows, row_totals[1:])
        ],
        0,
    )
    old_cols = jnp.concatenate([state.reshape(-1, feature_width) for state in col_states[1:]], 0)
    new_cols = DECAY * old_cols + shares * everything[:col_count]
    ratios = jnp.sum(everything[col_count : 2 * col_count] / new_cols, -1)
    cols_new = []
    new_weights = []
    sizes_rms = []
    col_at = 0
    row_at = 0
    for matrix_at in range(5):
        weight, renewed, col_state = matrices[matrix_at], rows_new[matrix_at], col_states[matrix_at]
        if matrix_at == 0:
            renewed_cols = DECAY * col_state + (1.0 - DECAY) / row_totals[0] * late[:1]
            row_mean = late[2, :1] / row_totals[0]
            clip_total = jnp.sum(row_mean * jnp.sum(late[1:2] / renewed_cols, -1))
        else:
            stack_count = weight.shape[0]
            height = col_rows[matrix_at - 1].shape[0]
            renewed_cols = new_cols[col_at : col_at + height].reshape(col_state.shape)
            row_mean = numbers[row_at : row_at + stack_count] / row_totals[matrix_at]
            row_at += stack_count
            ratio = jnp.sum(ratios[col_at : col_at + height].reshape(stack_count, -1), -1)
            col_at += height
            clip_total = jnp.sum(row_mean * ratio)
        entries = weight.size * n_group
        update_rms = jnp.sqrt(clip_total / entries)
        weight_rms = jnp.sqrt(numbers[row_count + matrix_at] / entries)
        step_scale = RATE * jnp.maximum(EPS_SCALE, weight_rms) / jnp.maximum(1.0, update_rms / CLIP)
        cols_new.append(renewed_cols)
        sizes_rms.append(update_rms)
        if matrix_at == 0:
            table_sum, table_new, table_copy = update_table(
                core_at.astype(jnp.int32).reshape(1),
                step_scale.reshape(1),
                table_part,
                table_away,
                part_renewed,
                away_renewed,
                renewed_cols / row_mean[0],
                table,
            )
            new_weights.append(table_new)
            continue
        second_moment = renewed[:, :, None] * renewed_cols[:, None, :] / row_mean[:, None, None]
        update = summed[matrix_at] * lax.rsqrt(second_moment)
        new_weights.append(weight - step_scale * update)
    vector_state_new = DECAY * vector_state + (1.0 - DECAY) * (vector_sum * vector_sum + EPS_SQUARE)
    vector_update = vector_sum * lax.rsqrt(vector_state_new)
    vector_rms = jnp.sqrt(jnp.mean(vector_update * vector_update))
    vector_scale = (
        RATE
        * jnp.maximum(EPS_SCALE, jnp.sqrt(jnp.mean(vectors * vectors)))
        / jnp.maximum(1.0, vector_rms / CLIP)
    )
    vectors_new = vectors - vector_scale * vector_update
    sizes_rms.append(vector_rms)
    norms = jnp.concatenate([jnp.sqrt(square_total / total_tokens), jnp.stack(sizes_rms)])
    return (
        loss_sum,
        norms,
        table_sum,
        rows_new[0][0],
        cols_new[0][0],
        table_new,
        table_copy,
        summed[1],
        rows_new[1],
        cols_new[1],
        new_weights[1],
        new_weights[1].astype(jnp.bfloat16),
        summed[2],
        rows_new[2],
        cols_new[2],
        new_weights[2],
        new_weights[2].astype(jnp.bfloat16),
        summed[3],
        rows_new[3],
        cols_new[3],
        new_weights[3],
        new_weights[3].astype(jnp.bfloat16),
        summed[4],
        rows_new[4],
        cols_new[4],
        new_weights[4],
        new_weights[4].astype(jnp.bfloat16),
        vector_sum,
        vector_state_new,
        vectors_new,
    )


def solution(mesh):
    return jax.shard_map(
        body,
        mesh=mesh,
        in_specs=(
            P(),
            P(),
            P(),
            P(),
            P(("seq", "fsdp"), None),
            P(None, ("seq", "fsdp"), None),
            P(None, ("seq", "fsdp"), None),
            P(None, ("seq", "fsdp"), None),
            P(None, ("seq", "fsdp"), None),
            P(),
            P(("seq", "fsdp")),
            P(),
            P(None, ("seq", "fsdp")),
            P(),
            P(None, ("seq", "fsdp")),
            P(),
            P(None, ("seq", "fsdp")),
            P(),
            P(None, ("seq", "fsdp")),
            P(),
            P(),
        ),
        out_specs=(
            P(),
            P(),
            P(("seq", "fsdp"), None),
            P(("seq", "fsdp")),
            P(),
            P(("seq", "fsdp"), None),
            P(("seq", "fsdp"), None),
            P(None, ("seq", "fsdp"), None),
            P(None, ("seq", "fsdp")),
            P(),
            P(None, ("seq", "fsdp"), None),
            P(None, ("seq", "fsdp"), None),
            P(None, ("seq", "fsdp"), None),
            P(None, ("seq", "fsdp")),
            P(),
            P(None, ("seq", "fsdp"), None),
            P(None, ("seq", "fsdp"), None),
            P(None, ("seq", "fsdp"), None),
            P(None, ("seq", "fsdp")),
            P(),
            P(None, ("seq", "fsdp"), None),
            P(None, ("seq", "fsdp"), None),
            P(None, ("seq", "fsdp"), None),
            P(None, ("seq", "fsdp")),
            P(),
            P(None, ("seq", "fsdp"), None),
            P(None, ("seq", "fsdp"), None),
            P(),
            P(),
            P(),
        ),
        check_vma=False,
    )
```

```python
import functools

import jax
import jax.numpy as jnp
from jax import lax
from jax.experimental import pallas as pl
from jax.experimental.pallas import tpu as pltpu
from jax.sharding import PartitionSpec as P

HEADS = 12
VOCAB = 50304


EPS_NORM = 1e-05
EPS_SQUARE = 1e-30
EPS_SCALE = 0.001
DECAY = 0.5
CLIP = 0.4
RATE = 0.6
SECOND = 0.3
MASKED = -1e30
VMEM_BYTES = 56 * 1024 * 1024
NEAR_FIRST = [(0, 1), (1, 0), (2, 3), (3, 2)]
NEAR_SECOND = [(0, 3), (3, 0), (1, 2), (2, 1)]


def layer_norm(stream, gain, offset):
    center = stream - jnp.mean(stream, -1, keepdims=True)
    spread = jnp.mean(center * center, -1, keepdims=True)
    return center * lax.rsqrt(spread + EPS_NORM) * gain + offset


def gelu_tanh(value):
    return jax.nn.gelu(value, approximate=True)


def positions_of(segments):
    steps_at = jnp.arange(segments.shape[-1], dtype=jnp.int32)
    before = jnp.concatenate(
        [jnp.full(segments.shape[:-1] + (1,), -2, jnp.int32), segments[..., :-1]], -1
    )
    starts = jnp.where(segments != before, steps_at, 0)
    first = lax.cummax(starts, axis=segments.ndim - 1)
    return jnp.where(segments >= 0, steps_at - first, 0)


def product(left, right):
    return jnp.dot(left, right, preferred_element_type=jnp.float32)


def inner(left, right):
    return lax.dot_general(
        left, right, (((1,), (1,)), ((), ())), preferred_element_type=jnp.float32
    )


def outer(left, right):
    return lax.dot_general(
        left, right, (((0,), (0,)), ((), ())), preferred_element_type=jnp.float32
    )


def shift(block, axis, step):
    count = lax.axis_size(axis)
    return lax.ppermute(block, axis, [(i, (i + step) % count) for i in range(count)])


def shift_y(block, step):
    count = lax.axis_size("ctx")
    return lax.ppermute(block, "ctx", [(i, (i + 2 * step) % count) for i in range(count)])


def swap_core(block):
    count = lax.axis_size("ctx")
    return lax.ppermute(block, "ctx", [(i, i ^ 1) for i in range(count)])


def shift_seq(block, step):
    return shift(block, "seq", step)


def shift_fsdp(block, step):
    return shift(block, "fsdp", step)


def pick(parts, at, axis):
    return lax.dynamic_index_in_dim(parts, at, axis, False)


def send_parts(parts, mover, at, axis=0, sent=None):
    count = parts.shape[axis]
    moving = []
    for step in range(1, count):
        piece = pick(parts, lax.rem(at + step, count), axis)
        moving.append(mover(piece if sent is None else piece.astype(sent), step))
    return moving


def add_parts(parts, moved, at, axis=0):
    total = pick(parts, at, axis)
    for piece in moved:
        total = total + piece.astype(total.dtype)
    return total


def scatter_sum(parts, mover, at, axis=0, sent=None):
    return add_parts(parts, send_parts(parts, mover, at, axis, sent), at, axis)


def scatter_fsdp(parts, at):
    count = parts.shape[0]
    if count != 4:
        moved = yield 0, send_parts(parts, shift_fsdp, at, sent=jnp.bfloat16)
        return add_parts(parts, moved, at)
    outside = (at == 0) | (at == 3)
    mine = [jnp.where(outside, 0, 1), jnp.where(outside, 3, 2)]
    other = [jnp.where(outside, 1, 0), jnp.where(outside, 2, 3)]
    away = jnp.stack([pick(parts, slot, 0) for slot in other]).astype(jnp.bfloat16)
    (away,) = yield 0, [lax.ppermute(away, "fsdp", NEAR_FIRST)]
    first, second = (
        pick(parts, slot, 0) + away[k].astype(parts.dtype) for k, slot in enumerate(mine)
    )
    away = jnp.where(at < 2, second, first).astype(jnp.bfloat16)
    (away,) = yield 0, [lax.ppermute(away, "fsdp", NEAR_SECOND)]
    return jnp.where(at < 2, first, second) + away.astype(parts.dtype)


def run(task):
    moving = next(task)[1]
    while True:
        try:
            moving = task.send(moving)[1]
        except StopIteration as stop:
            return stop.value


def sum_hops(block, skip_y=False):
    for axis in ("ctx", "seq", "fsdp"):
        whole = lax.axis_size(axis)
        count = 2 if skip_y and axis == "ctx" else whole
        hop = 1
        while hop < count:
            moved = yield lax.ppermute(block, axis, [(i, i ^ hop) for i in range(whole)])
            block = block + moved
            hop *= 2
    return block


def sum_all(block, skip_y=False):
    hops = sum_hops(block, skip_y)
    moved = next(hops)
    while True:
        try:
            moved = hops.send(moved)
        except StopIteration as stop:
            return stop.value


def order_parts(parts, at):
    count = len(parts)
    if count == 2:
        first, second = parts
        return jnp.stack([jnp.where(at == 0, first, second), jnp.where(at == 0, second, first)])
    order = lax.rem(at - jnp.arange(count, dtype=jnp.int32) + count, count)
    return jnp.take(jnp.stack(parts), order, axis=0, mode="clip")


def gather_near(block):
    n_y = lax.axis_size("ctx") // 2
    column = jnp.concatenate([block] + [shift_y(block, step) for step in range(1, n_y)], 0)
    return jnp.concatenate([column, swap_core(column)], 0)


def scatter_near(parts):
    n_y = lax.axis_size("ctx") // 2
    parts = parts.reshape(2, 2, n_y, -1, parts.shape[2])
    column = parts[:, 0] + swap_core(parts[:, 1])
    total = column[:, 0]
    for step in range(1, n_y):
        away = shift_y(column[:, step].astype(jnp.bfloat16), n_y - step)
        total = total + away.astype(total.dtype)
    return total


def half_of(block, at):
    width = block.shape[-1] // 2
    return jnp.where(at == 0, block[..., :width], block[..., width:])


def qkv_bias(vec):
    return jnp.concatenate([vec[2], jnp.zeros_like(vec[2]), vec[3]])


def head_slabs(ref, lanes, width):
    block = ref[...].astype(jnp.float32)
    lane = lax.broadcasted_iota(jnp.int32, block.shape, 1)
    return [
        jnp.where((lane >= low) & (lane < low + width), block, 0.0).astype(jnp.bfloat16)
        for low in range(0, lanes, width)
    ]


def turned(ref):
    return ref[...].astype(jnp.float32).T.astype(jnp.bfloat16)


def across(left, right):
    return lax.dot_general(
        left, right, (((1,), (1,)), ((), ())), preferred_element_type=jnp.float32
    )


def by_head(parts, width):
    row = lax.broadcasted_iota(jnp.int32, parts[0].shape, 0)
    joined = parts[0]
    for at, part in enumerate(parts[1:], 1):
        joined = jnp.where(row >= at * width, part, joined)
    return joined


def attend_kernel(width, query_ref, key_ref, value_ref, mask_ref, mixed_ref, log_ref):
    lanes = query_ref.shape[1]
    scale = width ** (-0.5)
    value_t = turned(value_ref)
    mixed = []
    for at, query in enumerate(head_slabs(query_ref, lanes, width)):
        scores = jnp.where(
            mask_ref[...] < 0.0, MASKED, across(key_ref[...], query) * scale
        )
        top = jnp.max(scores, 0, keepdims=True)
        probs = jnp.exp(scores - top)
        total = jnp.sum(probs, 0, keepdims=True)
        log_ref[0, at : at + 1, :] = top + jnp.log(total)
        probs_low = (probs * (1.0 / total)).astype(jnp.bfloat16)
        mixed.append(jnp.dot(value_t, probs_low, preferred_element_type=jnp.float32))
    mixed_ref[...] = by_head(mixed, width).T.astype(mixed_ref.dtype)


def attend_back_kernel(
    width, query_ref, key_ref, value_ref, mixed_ref, log_ref, mask_ref, d_query_ref, d_pair_ref
):
    lanes = query_ref.shape[1]
    scale = width ** (-0.5)
    key_t = turned(key_ref)
    queries = head_slabs(query_ref, lanes, width)
    d_heads = head_slabs(mixed_ref, lanes, width)
    d_query = []
    d_key = d_value = None
    for at, (query, d_head) in enumerate(zip(queries, d_heads)):
        scores = jnp.where(
            mask_ref[...] < 0.0, MASKED, across(key_ref[...], query) * scale
        )
        probs = jnp.exp(scores - log_ref[0, at : at + 1, :])
        d_probs = across(value_ref[...], d_head)
        shared = jnp.sum(probs * d_probs, 0, keepdims=True)
        d_scores = (probs * (d_probs - shared)).astype(jnp.bfloat16)
        d_query.append(jnp.dot(key_t, d_scores, preferred_element_type=jnp.float32))
        part = jnp.dot(d_scores, query, preferred_element_type=jnp.float32)
        d_key = part if d_key is None else d_key + part
        part = jnp.dot(
            probs.astype(jnp.bfloat16), d_head, preferred_element_type=jnp.float32
        )
        d_value = part if d_value is None else d_value + part
    d_query_ref[...] = (by_head(d_query, width).T * scale).astype(d_query_ref.dtype)
    d_pair_ref[0] = d_key * scale
    d_pair_ref[1] = d_value


def attend(qkv_low, pairs, mask, head_count, lanes=128):
    row_count = qkv_low.shape[0]
    key_count, feature_width = pairs.shape[0], pairs.shape[1] // 2
    width = feature_width // head_count
    steps = feature_width // lanes
    return pl.pallas_call(
        functools.partial(attend_kernel, width),
        out_shape=(
            jax.ShapeDtypeStruct((row_count, feature_width), jnp.bfloat16),
            jax.ShapeDtypeStruct((steps, lanes // width, row_count), jnp.float32),
        ),
        grid=(steps,),
        in_specs=[
            pl.BlockSpec((row_count, lanes), lambda i: (0, i)),
            pl.BlockSpec((key_count, lanes), lambda i: (0, i)),
            pl.BlockSpec((key_count, lanes), lambda i: (0, steps + i)),
            pl.BlockSpec((key_count, row_count), lambda i: (0, 0)),
        ],
        out_specs=(
            pl.BlockSpec((row_count, lanes), lambda i: (0, i)),
            pl.BlockSpec((1, lanes // width, row_count), lambda i: (i, 0, 0)),
        ),
        compiler_params=pltpu.CompilerParams(vmem_limit_bytes=VMEM_BYTES),
        cost_estimate=pl.CostEstimate(
            flops=4 * row_count * key_count * lanes * head_count,
            bytes_accessed=4 * key_count * row_count + 4 * key_count * feature_width,
            transcendentals=row_count * key_count * head_count,
        ),
    )(qkv_low, pairs, pairs, mask)


def attend_back(qkv_low, pairs, d_mixed, log_total, mask, head_count, lanes=128):
    row_count = qkv_low.shape[0]
    key_count, feature_width = pairs.shape[0], pairs.shape[1] // 2
    width = feature_width // head_count
    steps = feature_width // lanes
    return pl.pallas_call(
        functools.partial(attend_back_kernel, width),
        out_shape=(
            jax.ShapeDtypeStruct((row_count, feature_width), jnp.bfloat16),
            jax.ShapeDtypeStruct((2, key_count, feature_width), jnp.float32),
        ),
        grid=(steps,),
        in_specs=[
            pl.BlockSpec((row_count, lanes), lambda i: (0, i)),
            pl.BlockSpec((key_count, lanes), lambda i: (0, i)),
            pl.BlockSpec((key_count, lanes), lambda i: (0, steps + i)),
            pl.BlockSpec((row_count, lanes), lambda i: (0, i)),
            pl.BlockSpec((1, lanes // width, row_count), lambda i: (i, 0, 0)),
            pl.BlockSpec((key_count, row_count), lambda i: (0, 0)),
        ],
        out_specs=(
            pl.BlockSpec((row_count, lanes), lambda i: (0, i)),
            pl.BlockSpec((2, key_count, lanes), lambda i: (0, 0, i)),
        ),
        compiler_params=pltpu.CompilerParams(vmem_limit_bytes=VMEM_BYTES),
        cost_estimate=pl.CostEstimate(
            flops=10 * row_count * key_count * lanes * head_count,
            bytes_accessed=4 * key_count * row_count + 12 * key_count * feature_width,
            transcendentals=row_count * key_count * head_count,
        ),
    )(qkv_low, pairs, pairs, d_mixed, log_total, mask)


def layer_forward(stream, weights, vec, mask, head_count):
    w_in, w_out, w_fc, w_down = weights
    feature_width = stream.shape[1]
    a_low = layer_norm(stream, vec[0], vec[1]).astype(jnp.bfloat16)
    qkv_low = (product(a_low, w_in) + qkv_bias(vec)).astype(jnp.bfloat16)
    pairs = gather_near(qkv_low[:, feature_width:])
    mixed_low, log_total = attend(qkv_low, pairs, mask, head_count)
    branch = product(mixed_low, w_out) + vec[4]
    middle = stream + branch
    m_low = layer_norm(middle, vec[5], vec[6]).astype(jnp.bfloat16)
    hidden = product(m_low, w_fc) + vec[8:12].reshape(-1)
    output = product(gelu_tanh(hidden).astype(jnp.bfloat16), w_down) + vec[7]
    sums = jnp.stack([jnp.sum(stream * stream), jnp.sum(branch * branch), jnp.sum(output * output)])
    kept = (stream, a_low, qkv_low, pairs, log_total, mixed_low, middle, m_low, hidden)
    return (middle + output, kept, sums)


def swap_pairs(pairs, core_at):
    lefts = [left for left, _ in pairs]
    return swap_core(
        jnp.concatenate(lefts + [half_of(right, 1 - core_at) for _, right in pairs], 1)
    )


def shared_outer(pairs, away, core_at):
    at = 0
    whole_left = []
    for left, _ in pairs:
        whole_left.append(jnp.concatenate([left, away[:, at : at + left.shape[1]]], 0))
        at += left.shape[1]
    grads = []
    for left, (_, right) in zip(whole_left, pairs):
        width = right.shape[1] // 2
        whole_right = jnp.concatenate([half_of(right, core_at), away[:, at : at + width]], 0)
        at += width
        grads.append(outer(left, whole_right))
    return grads


def layer_backward(d_stream, kept, weights, vec, mask, head_count, pending, first_task, later_task):
    stream, a_low, qkv_low, pairs, log_total, mixed_low, middle, m_low, hidden = kept
    w_in, w_out, w_fc, w_down = weights
    feature_width = stream.shape[1]
    norm_back_one = jax.vjp(layer_norm, stream, vec[0], vec[1])[1]
    norm_back_two = jax.vjp(layer_norm, middle, vec[5], vec[6])[1]
    gelu_out, gelu_back = jax.vjp(gelu_tanh, hidden)
    u_low = gelu_out.astype(jnp.bfloat16)
    d_out_low = d_stream.astype(jnp.bfloat16)
    d_hidden_low = gelu_back(inner(d_out_low, w_down))[0].astype(jnp.bfloat16)
    d_hidden_low = pending.point(d_hidden_low)
    pending.add(first_task([(m_low, d_hidden_low), (u_low, d_out_low)]))
    d_m = inner(d_hidden_low, w_fc)
    d_two, d_gain_two, d_bias_two = norm_back_two(d_m)
    d_middle = d_stream + d_two
    d_middle = pending.point(d_middle)
    d_middle_low = d_middle.astype(jnp.bfloat16)
    d_mixed = inner(d_middle_low, w_out).astype(jnp.bfloat16)
    d_query, d_pairs = attend_back(qkv_low, pairs, d_mixed, log_total, mask, head_count)
    d_pairs = pending.point(d_pairs)
    d_pairs = scatter_near(d_pairs).astype(jnp.bfloat16)
    d_qkv_low = jnp.concatenate([d_query, d_pairs[0], d_pairs[1]], 1)
    d_qkv_low = pending.point(d_qkv_low)
    pending.add(later_task([(a_low, d_qkv_low), (mixed_low, d_middle_low)]))
    d_one, d_gain_one, d_bias_one = norm_back_one(inner(d_qkv_low, w_in))
    d_qkv = d_qkv_low.astype(jnp.float32)
    rows_head = jnp.stack(
        [
            d_gain_one,
            d_bias_one,
            jnp.sum(d_qkv[:, :feature_width], 0),
            jnp.sum(d_qkv[:, 2 * feature_width :], 0),
            jnp.sum(d_middle_low.astype(jnp.float32), 0),
            d_gain_two,
            d_bias_two,
            jnp.sum(d_out_low.astype(jnp.float32), 0),
        ]
    )
    vec_grad = jnp.concatenate(
        [rows_head, jnp.sum(d_hidden_low.astype(jnp.float32), 0).reshape(4, feature_width)], 0
    )
    return (pending.point(d_middle + d_one), vec_grad)


def merge_stats(stats):
    for mover, axis in ((shift_seq, "seq"), (shift_fsdp, "fsdp")):
        parts = [stats] + [mover(stats, step) for step in range(1, lax.axis_size(axis))]
        top = parts[0][0]
        for part in parts[1:]:
            top = jnp.maximum(top, part[0])
        total = jnp.exp(parts[0][0] - top)
        picked = parts[0][1]
        for part in parts[1:]:
            total = total + jnp.exp(part[0] - top)
            picked = picked + part[1]
        stats = jnp.stack([top + jnp.log(total), picked])
    return stats


def blocks_of(groups, width, row_block):
    step = max(1, row_block // width)
    return [
        (range(low, low + step), slice(low * width, (low + step) * width))
        for low in range(0, groups, step)
    ]


def side_by_side(ref, at_block):
    return jnp.concatenate([ref[at] for at in at_block], 1)


def masked_logits(logits, live, first):
    column = lax.broadcasted_iota(jnp.int32, logits.shape, 0) + first
    return jnp.where(column < live, logits, MASKED)


def stats_kernel(row_block, live_ref, table_ref, rows_ref, target_ref, out_ref, top_ref, sum_ref, pick_ref):
    at = pl.program_id(0)
    tile = table_ref.shape[0]
    first = at * tile
    live = live_ref[0]

    @pl.when(at == 0)
    def _():
        top_ref[...] = jnp.full_like(top_ref, MASKED)
        sum_ref[...] = jnp.zeros_like(sum_ref)
        pick_ref[...] = jnp.zeros_like(pick_ref)

    def step(masked):
        for at_block, here in blocks_of(rows_ref.shape[0], rows_ref.shape[2], row_block):
            logits = jnp.dot(
                table_ref[...], side_by_side(rows_ref, at_block), preferred_element_type=jnp.float32
            )
            if masked:
                logits = masked_logits(logits, live, first)
            column = lax.broadcasted_iota(jnp.int32, logits.shape, 0)
            hit = column == target_ref[:, here] - first
            cut = logits.reshape(tile // 8, 8, logits.shape[1])
            top = top_ref[:, here]
            joint = jnp.maximum(top, jnp.max(cut, 0))
            total = jnp.sum(jnp.exp(cut - joint[None]), 0)
            sum_ref[:, here] = sum_ref[:, here] * jnp.exp(top - joint) + total
            top_ref[:, here] = joint
            pick_ref[:, here] += jnp.sum(
                jnp.where(hit, logits, 0.0).reshape(cut.shape), 0
            )

    @pl.when(first + tile <= live)
    def _():
        step(False)

    @pl.when((first + tile > live) & (first < live))
    def _():
        step(True)

    @pl.when(at == pl.num_programs(0) - 1)
    def _():
        top = top_ref[...]
        joint = jnp.max(top, 0, keepdims=True)
        total = jnp.sum(sum_ref[...] * jnp.exp(top - joint), 0, keepdims=True)
        out_ref[0:1, :] = joint + jnp.log(total)
        out_ref[1:2, :] = jnp.sum(pick_ref[...], 0, keepdims=True)


def head_stats(live, table_low, rows_t, target, tile=512, row_block=512):
    groups, depth, width = rows_t.shape
    count = groups * width
    height = table_low.shape[0]
    return pl.pallas_call(
        functools.partial(stats_kernel, row_block),
        out_shape=jax.ShapeDtypeStruct((2, count), jnp.float32),
        grid=(height // tile,),
        in_specs=[
            pl.BlockSpec(memory_space=pltpu.SMEM),
            pl.BlockSpec((tile, depth), lambda i: (i, 0)),
            pl.BlockSpec((groups, depth, width), lambda i: (0, 0, 0)),
            pl.BlockSpec((1, count), lambda i: (0, 0)),
        ],
        out_specs=pl.BlockSpec((2, count), lambda i: (0, 0)),
        scratch_shapes=[pltpu.VMEM((8, count), jnp.float32)] * 3,
        compiler_params=pltpu.CompilerParams(vmem_limit_bytes=VMEM_BYTES),
        cost_estimate=pl.CostEstimate(
            flops=2 * height * depth * count,
            bytes_accessed=2 * height * depth + 2 * depth * count,
            transcendentals=height * count,
        ),
    )(live, table_low, rows_t, target)


def back_kernel(row_block, added, live_ref, table_ref, table_t_ref, rows_ref, rows_t_ref, line_ref, *refs):
    if added:
        prior_ref, grad_ref, d_rows_ref = refs
    else:
        grad_ref, d_rows_ref = refs
    at = pl.program_id(0)
    tile = table_ref.shape[0]
    first = at * tile
    live = live_ref[0]
    width = d_rows_ref.shape[2]

    @pl.when(at == 0)
    def _():
        d_rows_ref[...] = jnp.zeros_like(d_rows_ref)

    def step(masked):
        grad = prior_ref[...] if added else None
        for at_block, here in blocks_of(rows_t_ref.shape[0], width, row_block):
            logits = jnp.dot(
                table_ref[...],
                side_by_side(rows_t_ref, at_block),
                preferred_element_type=jnp.float32,
            )
            if masked:
                logits = masked_logits(logits, live, first)
            column = lax.broadcasted_iota(jnp.int32, logits.shape, 0).astype(jnp.float32)
            probs = jnp.exp(logits - line_ref[0:1, here])
            hit = column == line_ref[2:3, here] - first.astype(jnp.float32)
            d_low = (line_ref[1:2, here] * jnp.where(hit, probs - 1.0, probs)).astype(jnp.bfloat16)
            rows = rows_ref[at_block.start : at_block.stop].reshape(-1, rows_ref.shape[2])
            part = jnp.dot(d_low, rows, preferred_element_type=jnp.float32)
            grad = part if grad is None else grad + part
            d_part = jnp.dot(table_t_ref[...], d_low, preferred_element_type=jnp.float32)
            for at_width, at_group in enumerate(at_block):
                d_rows_ref[at_group] += d_part[:, at_width * width : (at_width + 1) * width]
        grad_ref[...] = grad

    @pl.when(first + tile <= live)
    def _():
        step(False)

    @pl.when((first + tile > live) & (first < live))
    def _():
        step(True)

    @pl.when(first >= live)
    def _():
        grad_ref[...] = prior_ref[...] if added else jnp.zeros_like(grad_ref)


def head_back(live, table_low, table_t, rows, rows_t, line, cut=0, prior=None, tile=512):
    groups, _, depth = rows.shape
    height = table_low.shape[0]
    count = line.shape[1]
    width = count // groups
    once = dict(pipeline_mode=pl.Buffered(1))
    grad_spec = pl.BlockSpec((tile, depth), lambda i: (i, 0))
    added = prior is not None
    return pl.pallas_call(
        functools.partial(back_kernel, 1024, added),
        out_shape=(
            jax.ShapeDtypeStruct((height, depth), jnp.float32),
            jax.ShapeDtypeStruct((groups, depth, width), jnp.float32),
        ),
        grid=(height // tile,),
        in_specs=[
            pl.BlockSpec(memory_space=pltpu.SMEM),
            pl.BlockSpec((tile, depth), lambda i: (i, 0)),
            pl.BlockSpec((depth, tile), lambda i: (0, i)),
            pl.BlockSpec((groups, width, depth), lambda i: (0, cut, 0), **once),
            pl.BlockSpec((groups, depth, width), lambda i: (0, 0, cut), **once),
            pl.BlockSpec((3, count), lambda i: (0, 0), **once),
        ]
        + ([grad_spec] if added else []),
        out_specs=(
            grad_spec,
            pl.BlockSpec((groups, depth, width), lambda i: (0, 0, 0), **once),
        ),
        input_output_aliases={6: 0} if added else {},
        compiler_params=pltpu.CompilerParams(vmem_limit_bytes=VMEM_BYTES),
        cost_estimate=pl.CostEstimate(
            flops=6 * height * depth * count,
            bytes_accessed=4 * height * depth + 12 * depth * count + 8 * height * depth,
            transcendentals=height * count,
        ),
    )(live, table_low, table_t, rows, rows_t, line, *((prior,) if added else ()))


def prepare_kernel(row_count, table_ref, low_ref, turned_ref, square_ref):
    at = pl.program_id(0)
    tile = table_ref.shape[0]
    row = lax.broadcasted_iota(jnp.int32, table_ref.shape, 0) + at * tile
    block = jnp.where(row < row_count, table_ref[...], 0.0)
    low_ref[...] = block.astype(jnp.bfloat16)
    turned_ref[...] = block.T.astype(jnp.bfloat16)
    part = jnp.sum((block * block).reshape(tile // 8, 8, block.shape[1]), 0)

    @pl.when(at == 0)
    def _():
        square_ref[...] = part

    @pl.when(at > 0)
    def _():
        square_ref[...] += part


def prepare_table(table, height, tile=512):
    row_count, depth = table.shape
    return pl.pallas_call(
        functools.partial(prepare_kernel, row_count),
        out_shape=(
            jax.ShapeDtypeStruct((height, depth), jnp.bfloat16),
            jax.ShapeDtypeStruct((depth, height), jnp.bfloat16),
            jax.ShapeDtypeStruct((8, depth), jnp.float32),
        ),
        grid=(height // tile,),
        in_specs=[pl.BlockSpec((tile, depth), lambda i: (i, 0))],
        out_specs=(
            pl.BlockSpec((tile, depth), lambda i: (i, 0)),
            pl.BlockSpec((depth, tile), lambda i: (0, i)),
            pl.BlockSpec((8, depth), lambda i: (0, 0)),
        ),
        compiler_params=pltpu.CompilerParams(vmem_limit_bytes=VMEM_BYTES),
        cost_estimate=pl.CostEstimate(
            flops=2 * row_count * depth,
            bytes_accessed=4 * row_count * depth + 4 * height * depth,
            transcendentals=0,
        ),
    )(table)


def update_kernel(used, core_ref, scale_ref, mine_ref, away_ref, mine_rows_ref, away_rows_ref, cols_ref, weight_ref, *outs):
    grad_ref, new_ref, copy_ref = outs
    half = pl.program_id(0) // (pl.num_programs(0) // 2)
    chosen = half == core_ref[0]
    grad = jnp.where(chosen, mine_ref[...], away_ref[...])
    rows = jnp.where(chosen, mine_rows_ref[...], away_rows_ref[...])
    update = grad * lax.rsqrt(rows * cols_ref[...])
    new = weight_ref[...] - scale_ref[0] * update

    @pl.when(pl.program_id(0) < used)
    def _():
        grad_ref[...] = grad
        new_ref[...] = new
        copy_ref[...] = new.astype(copy_ref.dtype)


def update_table(core, scale, mine, away, mine_rows, away_rows, cols, weight):
    row_count, depth = weight.shape
    tile = mine.shape[0] // 4
    steps = mine.shape[0] // tile
    used = -(-row_count // tile)

    def mine_at(i, core_ref):
        return (jnp.clip(i - core_ref[0] * steps, 0, steps - 1), 0)

    def away_at(i, core_ref):
        return (jnp.clip(i - (1 - core_ref[0]) * steps, 0, steps - 1), 0)

    def whole_at(i, core_ref):
        return (jnp.minimum(i, used - 1), 0)

    whole = pl.BlockSpec((tile, depth), whole_at)
    return pl.pallas_call(
        functools.partial(update_kernel, used),
        out_shape=(
            jax.ShapeDtypeStruct(weight.shape, jnp.float32),
            jax.ShapeDtypeStruct(weight.shape, jnp.float32),
            jax.ShapeDtypeStruct(weight.shape, jnp.bfloat16),
        ),
        grid_spec=pltpu.PrefetchScalarGridSpec(
            num_scalar_prefetch=1,
            grid=(2 * steps,),
            in_specs=[
                pl.BlockSpec(memory_space=pltpu.SMEM),
                pl.BlockSpec((tile, depth), mine_at),
                pl.BlockSpec((tile, depth), away_at),
                pl.BlockSpec((tile, 1), mine_at),
                pl.BlockSpec((tile, 1), away_at),
                pl.BlockSpec((1, depth), lambda i, core_ref: (0, 0)),
                whole,
            ],
            out_specs=(whole, whole, whole),
        ),
        compiler_params=pltpu.CompilerParams(vmem_limit_bytes=VMEM_BYTES),
        cost_estimate=pl.CostEstimate(
            flops=6 * row_count * depth,
            bytes_accessed=18 * row_count * depth,
            transcendentals=row_count * depth,
        ),
    )(core, scale, mine, away, mine_rows, away_rows, cols, weight)


class Pending:
    def __init__(self):
        self.active = []

    def add(self, task):
        held, moving = next(task)
        self.active.append([task, held, moving])

    def point(self, main):
        ready = [entry for entry in self.active if entry[1] == 0]
        main, moved = lax.optimization_barrier((main, [entry[2] for entry in ready]))
        for entry in self.active:
            entry[1] -= 1
        for entry, arrived in zip(ready, moved):
            self.advance(entry, arrived)
        return main

    def advance(self, entry, arrived):
        try:
            entry[1:] = entry[0].send(arrived)
        except StopIteration:
            self.active.remove(entry)

    def finish(self):
        while self.active:
            entry = self.active[0]
            self.advance(entry, entry[2])


def local_index(ids, row_low, row_count):
    shifted = ids - row_low
    inside = (shifted >= 0) & (shifted < row_count)
    return (inside, jnp.clip(shifted, 0, row_count - 1))


def body(
    tokens,
    segments,
    next_ids,
    second_ids,
    table,
    attn_in,
    attn_out,
    mlp_in,
    mlp_out,
    vectors,
    table_rows,
    table_cols,
    attn_in_rows,
    attn_in_cols,
    attn_out_rows,
    attn_out_cols,
    mlp_in_rows,
    mlp_in_cols,
    mlp_out_rows,
    mlp_out_cols,
    vector_state,
):
    n_ctx = lax.axis_size("ctx")
    n_seq = lax.axis_size("seq")
    n_fsdp = lax.axis_size("fsdp")
    n_y = n_ctx // 2
    n_group = n_seq * n_fsdp
    ctx_at = lax.axis_index("ctx")
    seq_at = lax.axis_index("seq")
    fsdp_at = lax.axis_index("fsdp")
    y_at = ctx_at // 2
    core_at = lax.rem(ctx_at, 2)
    group_at = seq_at * n_fsdp + fsdp_at
    all_seqs, length = segments.shape
    seqs_dev = all_seqs // n_group
    ctx_span = length // n_ctx
    feature_width = table.shape[1]
    layer_count = attn_in.shape[0]
    head_count = HEADS
    total_tokens = all_seqs * length
    own_rows = seqs_dev * ctx_span
    block_start = ctx_at * ctx_span
    positions = positions_of(segments)

    def block_of(grid):
        return lax.dynamic_slice_in_dim(grid, block_start, ctx_span, 1)

    tok_block = block_of(tokens).reshape(-1)
    valid_block = (block_of(segments) >= 0).astype(jnp.float32).reshape(-1)
    next_block = block_of(next_ids).reshape(-1)
    second_block = block_of(second_ids).reshape(-1)
    my_segments = lax.dynamic_slice_in_dim(segments, group_at * seqs_dev, seqs_dev, 0)
    my_positions = lax.dynamic_slice_in_dim(positions, group_at * seqs_dev, seqs_dev, 0)
    hops = jnp.asarray([(side, step) for side in range(2) for step in range(n_y)], jnp.int32)
    near_ctx = 2 * lax.rem(y_at - hops[:, 1] + n_y, n_y) + lax.rem(core_at + hops[:, 0], 2)

    def near_order(grid):
        cut = grid.reshape(seqs_dev, n_ctx, ctx_span).transpose(1, 0, 2)
        return jnp.take(cut, near_ctx, axis=0, mode="clip").reshape(-1)

    def own_order(grid):
        return block_of(grid).reshape(-1)

    time_grid = jnp.broadcast_to(jnp.arange(length, dtype=jnp.int32)[None], (seqs_dev, length))
    seq_grid = jnp.broadcast_to(jnp.arange(seqs_dev, dtype=jnp.int32)[:, None], (seqs_dev, length))
    q_seg, k_seg = (own_order(my_segments), near_order(my_segments))
    q_time, k_time = (own_order(time_grid), near_order(time_grid))
    q_seq, k_seq = (own_order(seq_grid), near_order(seq_grid))
    allowed = (q_seq[None] == k_seq[:, None]) & (
        (q_time[None] == k_time[:, None])
        | (k_time[:, None] < q_time[None]) & (q_seg[None] == k_seg[:, None]) & (k_seg[:, None] >= 0)
    )
    mask = jnp.where(allowed, 0.0, MASKED)
    rows_dev = table.shape[0]
    row_low = group_at * rows_dev
    rows_group = attn_in.shape[1]
    rows_part = rows_group // n_ctx
    down_cut = mlp_out.shape[1] // rows_group

    in_width, out_width, fc_width = attn_in.shape[2], attn_out.shape[2], mlp_in.shape[2]
    pack_width = in_width + out_width + fc_width + down_cut * feature_width
    part_width = pack_width // n_ctx
    model_rows = n_group * rows_group

    def gather_pack(layer_at):
        down = mlp_out[layer_at].reshape(down_cut, rows_group, feature_width)
        pack = jnp.concatenate(
            [attn_in[layer_at], mlp_in[layer_at], attn_out[layer_at]]
            + [down[cut] for cut in range(down_cut)],
            1,
        ).astype(jnp.bfloat16)
        part = lax.dynamic_slice_in_dim(pack, ctx_at * part_width, part_width, 1)
        if layer_at == layer_count - 1:
            head = lax.dynamic_slice_in_dim(
                attn_out[layer_count].astype(jnp.bfloat16), ctx_at * rows_part, rows_part, 0
            )
            head = jnp.pad(head.reshape(-1), (0, -head.size % part_width)).reshape(-1, part_width)
            part = jnp.concatenate([part, head], 0)
        return lax.all_gather(part, ("ctx", "seq", "fsdp"), axis=0)

    def cut_pack(layer_at, whole):
        whole = whole.reshape(n_ctx, n_group, -1, part_width)
        body_rows = whole[:, :, :rows_group].reshape(n_ctx, model_rows, part_width)

        def columns_of(low, high):
            pieces = []
            for at in range(n_ctx):
                start, stop = max(low, at * part_width), min(high, (at + 1) * part_width)
                if start < stop:
                    pieces.append(body_rows[at, :, start - at * part_width : stop - at * part_width])
            return pieces[0] if len(pieces) == 1 else jnp.concatenate(pieces, 1)

        at = in_width + fc_width
        down = jnp.stack(
            [
                columns_of(low, low + feature_width).reshape(n_group, rows_group, feature_width)
                for low in range(at + out_width, pack_width, feature_width)
            ],
            1,
        )
        weights = (
            columns_of(0, in_width),
            columns_of(at, at + out_width),
            columns_of(in_width, at),
            down.reshape(-1, feature_width),
        )
        head = None
        if layer_at == layer_count - 1:
            head = whole[:, :, rows_group:].reshape(n_ctx, n_group, -1)
            head = head[:, :, : rows_part * out_width].reshape(n_ctx, n_group, rows_part, out_width)
            head = head.transpose(1, 0, 2, 3).reshape(model_rows, out_width)
        return weights, head

    stored = [gather_pack(0)]

    tok_inside, tok_safe = local_index(tok_block, row_low, rows_dev)
    embed_term = jnp.where(
        tok_inside[:, None], jnp.take(table, tok_safe, axis=0, mode="clip"), 0.0
    ).astype(jnp.bfloat16)
    embed_term = embed_term.reshape(n_seq, n_fsdp, own_rows, feature_width)
    place_part = length // n_ctx
    place_low = VOCAB - rows_dev * (n_group - 1)
    places = lax.dynamic_slice_in_dim(table, place_low + ctx_at * place_part, place_part, 0)
    places = jnp.where(group_at == n_group - 1, places, 0.0).astype(jnp.bfloat16)
    def device_order(grid):
        cut = grid.reshape(n_group, seqs_dev, n_ctx, ctx_span)
        return cut.transpose(0, 2, 1, 3).reshape(n_group * n_ctx, own_rows)

    ids_grid = jnp.stack([device_order(tokens), device_order(positions) + VOCAB])
    near = (n_seq, n_fsdp, n_y) == (2, 4, 2)
    if near:
        across = [k << 2 for k in (0, 3, 1, 2)]
        stages = [
            [(0, 0), (0, 1)],
            [(16, 0), (2, 1)],
            [(2, 0), (18, 0), (16, 1), (18, 1)],
        ]
        order = [
            ((seat ^ step ^ side) << 1) | which
            for pieces in stages
            for side in (0, 1)
            for seat, which in pieces
            for step in across
        ]
        order = jnp.asarray(order, jnp.int32) ^ ((group_at * n_ctx + ctx_at) << 1)
        ids_grid = ids_grid.reshape(2, 2 * n_group * n_ctx, own_rows // 2)
        ids_grid = jnp.take(ids_grid, order, axis=1, mode="clip")
    ids_grid = ids_grid.reshape(2, -1)
    part_rows = -(-rows_dev // 512) * 256
    spare = part_rows * 2 - rows_dev
    table_low, table_t, table_square = prepare_table(table, 2 * part_rows)
    if near:
        flat = (-1, feature_width)
        sent = pick(embed_term, 1 - seq_at, 0).reshape(flat)
        away = shift_seq(jnp.concatenate([sent, places], 0), 1)
        away, table_low, table_t, table_square, ids_grid = lax.optimization_barrier(
            (away, table_low, table_t, table_square, ids_grid)
        )
        mine = pick(embed_term, seq_at, 0) + away[:-place_part].reshape(embed_term.shape[1:])
        places = places + away[-place_part:]
        outside = (fsdp_at == 0) | (fsdp_at == 3)
        pair = jnp.where(outside, mine[1:3], jnp.stack([mine[0], mine[3]]))
        sent = jnp.concatenate([pair.reshape(flat), places], 0)
        away = lax.ppermute(sent, "fsdp", NEAR_FIRST)
        kept_pair = jnp.where(outside, jnp.stack([mine[0], mine[3]]), mine[1:3])
        kept_pair = kept_pair + away[:-place_part].reshape(kept_pair.shape)
        places = places + away[-place_part:]
        sent = jnp.concatenate([jnp.where(fsdp_at < 2, kept_pair[1], kept_pair[0]), places], 0)
        away = lax.ppermute(sent, "fsdp", NEAR_SECOND)
        embed_term = jnp.where(fsdp_at < 2, kept_pair[0], kept_pair[1]) + away[:-place_part]
        total = places + away[-place_part:]
    else:
        embed_term = scatter_sum(embed_term, shift_seq, seq_at)
        embed_term = run(scatter_fsdp(embed_term, fsdp_at))
        total = places
        for step in range(1, n_seq):
            total = total + lax.ppermute(places, "seq", [(n_seq - 1, n_seq - 1 - step)])
        places = total
        for step in range(1, n_fsdp):
            total = total + lax.ppermute(places, "fsdp", [(n_fsdp - 1, n_fsdp - 1 - step)])
    places = gather_near(total)
    own_places = own_order(my_positions)
    place_ctx = own_places // place_part
    place_near = lax.rem(core_at + place_ctx, 2) * n_y + lax.rem(y_at - place_ctx // 2 + n_y, n_y)
    place_rows = jnp.take(
        places, place_near * place_part + lax.rem(own_places, place_part), axis=0, mode="clip"
    )
    stream = embed_term.astype(jnp.float32) + place_rows.astype(jnp.float32)
    share = 1.0 / n_ctx
    square_parts = [share * jnp.sum(table_square).reshape(1)] + [
        share * jnp.sum(weight * weight).reshape(1)
        for weight in (attn_in, attn_out, mlp_in, mlp_out)
    ]
    for layer_at in range(1, layer_count):
        stored.append(gather_pack(layer_at))
    kept = []
    squares = []
    for layer_at in range(layer_count):
        if layer_at:
            stream, stored[layer_at] = lax.optimization_barrier((stream, stored[layer_at]))
        stored[layer_at], head_weight = cut_pack(layer_at, stored[layer_at])
        stream, layer_kept, layer_sums = layer_forward(
            stream,
            stored[layer_at],
            vectors[12 * layer_at : 12 * layer_at + 12],
            mask,
            head_count,
        )
        kept.append(layer_kept)
        squares.append(layer_sums)
    final_gain = vectors[12 * layer_count]
    final_bias = vectors[12 * layer_count + 1]
    final_norm, final_back = jax.vjp(layer_norm, stream, final_gain, final_bias)
    final_low = final_norm.astype(jnp.bfloat16)
    second_low = product(final_low, head_weight).astype(jnp.bfloat16)
    live = jnp.clip(VOCAB - row_low, 0, rows_dev).astype(jnp.int32).reshape(1)

    def local_targets(ids):
        inside, safe = local_index(ids, row_low, rows_dev)
        return jnp.where(inside, safe, -1)

    final_all = lax.all_gather(final_low, ("seq", "fsdp"), axis=0)
    second_all = lax.all_gather(second_low, ("seq", "fsdp"), axis=0)
    second_factor = SECOND * valid_block
    final_local, second_local = local_targets(next_block), local_targets(second_block)
    final_t = final_all.swapaxes(1, 2)
    final_stats = head_stats(live, table_low, final_t, final_local[None])
    final_stats, second_all = lax.optimization_barrier((final_stats, second_all))
    second_t = second_all.swapaxes(1, 2)
    second_stats = head_stats(live, table_low, second_t, second_local[None])
    stats = merge_stats(jnp.concatenate([final_stats, second_stats], 1))
    half_rows = final_stats.shape[1]
    final_stats, second_stats = stats[:, :half_rows], stats[:, half_rows:]

    pending = Pending()
    results = {}

    def rows_task(name, d_rows):
        parts = d_rows.reshape((n_seq, n_fsdp) + d_rows.shape[1:])
        moved = yield 0, send_parts(parts, shift_seq, seq_at, sent=jnp.bfloat16)
        mine = add_parts(parts, moved, seq_at)
        results[name] = yield from scatter_fsdp(mine, fsdp_at)

    def line_of(stats, factor, local):
        return jnp.stack([stats[0], factor / total_tokens, local.astype(jnp.float32)])

    final_line = line_of(final_stats, valid_block, final_local)
    table_grad, d_rows = head_back(live, table_low, table_t, final_all, final_t, final_line)
    pending.add(rows_task("final", d_rows))
    second_line = line_of(second_stats, second_factor, second_local)
    cuts = 2 if own_rows % 256 == 0 else 1
    for cut in range(cuts):
        line = second_line.reshape(3, n_group, cuts, -1)[:, :, cut].reshape(3, -1)
        table_grad, d_rows = head_back(
            live, table_low, table_t, second_all, second_t, line, cut, table_grad
        )
        table_grad = pending.point(table_grad)
        pending.add(rows_task(("second", cut), d_rows))
    pending.finish()
    d_final = results["final"].T
    d_second = jnp.concatenate([results["second", cut] for cut in range(cuts)], 1).T
    loss_rows = (final_stats[0] - final_stats[1]) * valid_block + (
        second_stats[0] - second_stats[1]
    ) * second_factor
    loss_part = jnp.sum(
        lax.dynamic_slice_in_dim(loss_rows, group_at * own_rows, own_rows, 0)
    )

    def table_task():
        parts = table_grad.reshape(2, part_rows, feature_width)
        (away,) = yield 0, [swap_core(pick(parts, 1 - core_at, 0))]
        mine = (pick(parts, core_at, 0) + away).astype(jnp.bfloat16)
        totals = []
        quarter = part_rows // 4
        cuts = [mine[low : low + quarter] for low in range(0, part_rows, quarter)]
        for first, last, wait in ((0, 1, 2), (1, 4, 3)):
            pieces = cuts[first:last]
            if first:
                pieces = yield 0, pieces
            moved = yield wait, [
                [shift_y(piece, step) for step in range(1, n_y)] for piece in pieces
            ]
            for piece, away in zip(pieces, moved):
                ordered = order_parts([piece] + away, y_at).astype(jnp.float32)
                total = ordered[0]
                for step in range(1, n_y):
                    total = total + ordered[step]
                totals.append(total)
        results["table"] = totals

    def bundle_task(pairs, matrices, names, waits):
        (away,) = yield 0, [swap_pairs(pairs, core_at)]
        grads = shared_outer(pairs, away, core_at)
        parts = []
        for grad in grads:
            cut = grad.reshape(n_seq, n_fsdp, -1, rows_group, grad.shape[1])
            parts += [cut[:, :, at] for at in range(cut.shape[2])]
        stacked = jnp.concatenate(parts, -1)
        moved = yield waits[0], send_parts(stacked, shift_seq, seq_at, sent=jnp.bfloat16)
        mine = add_parts(stacked, moved, seq_at)
        mine = mine.reshape(n_fsdp, n_y, rows_group // n_y, -1)
        moved = yield waits[1], send_parts(mine, shift_y, y_at, 1, jnp.bfloat16)
        mine = add_parts(mine, moved, y_at, 1)
        mine = yield from scatter_fsdp(mine, fsdp_at)
        moved = yield 0, [shift_y(mine, step) for step in range(1, n_y)]
        column = order_parts([mine] + moved, y_at).reshape(rows_group, -1)
        (away,) = yield 0, [swap_core(column)]
        both = order_parts([column, away], core_at)
        at = 0
        for matrix, name in zip(matrices, names):
            width = matrix.shape[-1] // 2
            cuts = []
            for _ in range(matrix.shape[-2] // rows_group):
                cuts.append(
                    jnp.concatenate([both[0, :, at : at + width], both[1, :, at : at + width]], 1)
                )
                at += width
            results[name] = jnp.concatenate(cuts, 0)

    pending.add(table_task())
    d_second = pending.point(d_second)
    d_second_low = d_second.astype(jnp.bfloat16)
    d_stream, d_gain_final, d_bias_final = final_back(d_final + inner(d_second_low, head_weight))

    vec_list = [None] * layer_count
    for layer_at in reversed(range(layer_count)):

        def first_task(pairs, at=layer_at):
            matrices, names = [mlp_in[at], mlp_out[at]], [("fc", at), ("down", at)]
            if at == layer_count - 1:
                pairs = [(final_low, d_second_low)] + pairs
                matrices = [attn_out[layer_count]] + matrices
                names = [("out", layer_count)] + names
            return bundle_task(pairs, matrices, names, (3, 2) if at else (2, 0))

        def later_task(pairs, at=layer_at):
            names = [("in", at), ("out", at)]
            return bundle_task(
                pairs, [attn_in[at], attn_out[at]], names, (2, 1) if at else (0, 0)
            )

        d_stream, vec_list[layer_at] = layer_backward(
            d_stream,
            kept[layer_at],
            stored[layer_at],
            vectors[12 * layer_at : 12 * layer_at + 12],
            mask,
            head_count,
            pending,
            first_task,
            later_task,
        )
    part_ids = jnp.arange(part_rows, dtype=jnp.int32)
    part_live = part_ids < rows_dev - core_at * part_rows
    part_ids = jnp.where(part_live, row_low + core_at * part_rows + part_ids, -1)[:, None]

    quarter = part_rows // 4

    def add_hits(piece, at, low, rows):
        ids = ids_grid[:, low : low + rows.shape[0]]
        here = part_ids[at * quarter : (at + 1) * quarter]
        hits = (here == ids[0][None]) | (here == ids[1][None])
        return piece + product(hits.astype(jnp.bfloat16), rows)

    mine = d_stream.astype(jnp.bfloat16)
    if near:
        half = own_rows // 2
        def flat(block):
            return block.reshape(-1, feature_width)

        mine = jnp.concatenate([mine, lax.ppermute(mine, "fsdp", NEAR_SECOND)], 0)
        mine = jnp.concatenate([mine, lax.ppermute(mine, "fsdp", NEAR_FIRST)], 0)
        mine = mine.reshape(4, 2, half, feature_width)
        front, back = flat(mine[:, 0]), flat(mine[:, 1])
        front_x, back_y = shift_seq(front, 1), shift_y(back, 1)
        here = jnp.concatenate([front, back], 0)
        here = jnp.concatenate([here, swap_core(here)], 0)
        pieces = list(results["table"])
        for at in (0, 1):
            pieces[at] = add_hits(pieces[at], at, 0, here)
        pieces[1], front_x, back_y = lax.optimization_barrier((pieces[1], front_x, back_y))
        front_y = shift_y(jnp.concatenate([front, front_x], 0), 1)
        back_x = shift_seq(jnp.concatenate([back, back_y], 0), 1)
        for at in (2, 3):
            pieces[at] = pending.point(add_hits(pieces[at], at, 0, here))
        done = here.shape[0]
        here = jnp.concatenate([front_x, back_y], 0)
        here = jnp.concatenate([here, swap_core(here)], 0)
        for at in range(4):
            pieces[at] = pending.point(add_hits(pieces[at], at, done, here))
        done += here.shape[0]
        pending.finish()
        last = jnp.concatenate([front_y, back_x], 0)
        last = jnp.concatenate([last, swap_core(last)], 0)
    else:
        pending.finish()
        last = lax.all_gather(mine, ("seq", "fsdp", "ctx"), axis=0, tiled=True)
        pieces, done = results["table"], 0
    summed = (
        None,
        jnp.stack([results["in", at] for at in range(layer_count)]),
        jnp.stack([results["out", at] for at in range(layer_count + 1)]),
        jnp.stack([results["fc", at] for at in range(layer_count)]),
        jnp.stack([results["down", at] for at in range(layer_count)]),
    )
    vector_grad = jnp.concatenate(vec_list + [jnp.stack([d_gain_final, d_bias_final])], 0)
    row_states = (attn_in_rows, attn_out_rows, mlp_in_rows, mlp_out_rows)
    rows_new = [None]
    col_parts = []
    weighted_parts = []
    row_parts = []
    for grad_sum, row_state in zip(summed[1:], row_states):
        square = grad_sum * grad_sum
        renewed = DECAY * row_state + (1.0 - DECAY) * jnp.mean(square + EPS_SQUARE, -1)
        rows_new.append(renewed)
        col_parts.append(share * jnp.sum(square + EPS_SQUARE, -2))
        weighted_parts.append(share * jnp.sum(square / renewed[..., None], -2))
        row_parts.append(share * jnp.sum(renewed, -1))
    numbers = jnp.concatenate(
        row_parts + square_parts + [loss_part.reshape(1), jnp.stack(squares).reshape(-1)]
    )
    row_count = sum(part.shape[0] for part in row_parts)
    numbers = jnp.pad(numbers, (0, feature_width - numbers.shape[0]))
    col_rows = [part.reshape(-1, feature_width) for part in col_parts]
    weighted_rows = [part.reshape(-1, feature_width) for part in weighted_parts]
    col_count = sum(part.shape[0] for part in col_rows)
    early = jnp.concatenate(col_rows + weighted_rows + [numbers[None], vector_grad], 0)
    early = jnp.pad(early, ((0, -early.shape[0] % 8), (0, 0)))
    hops = sum_hops(early)
    state = [next(hops)]

    def advance(piece):
        piece, state[0] = lax.optimization_barrier((piece, state[0]))
        state[0] = hops.send(state[0])
        return piece

    pieces = [
        advance(add_hits(piece, at, done, last)) for at, piece in enumerate(pieces)
    ]
    while True:
        try:
            state[0] = hops.send(state[0])
        except StopIteration as stop:
            everything = stop.value
            break
    table_part = jnp.concatenate(pieces, 0)
    table_away = swap_core(table_part)
    state_part = lax.dynamic_slice_in_dim(
        jnp.pad(table_rows, (0, spare)), core_at * part_rows, part_rows, 0
    )
    live_rows = part_live[:, None]
    part_square = table_part * table_part
    part_renewed = DECAY * state_part[:, None] + (1.0 - DECAY) * jnp.mean(
        part_square + EPS_SQUARE, -1, keepdims=True
    )
    part_renewed = jnp.where(live_rows, part_renewed, 1.0)
    away_renewed = swap_core(part_renewed)
    live_count = jnp.sum(part_live.astype(jnp.float32))
    rows_new[0] = jnp.concatenate(
        [
            jnp.where(core_at == 0, part_renewed, away_renewed),
            jnp.where(core_at == 0, away_renewed, part_renewed),
        ],
        0,
    )[:rows_dev, 0][None]
    row_sum = jnp.sum(jnp.where(live_rows, part_renewed, 0.0))
    late = jnp.concatenate(
        [
            (jnp.sum(part_square, 0) + EPS_SQUARE * live_count)[None],
            jnp.sum(part_square / part_renewed, 0)[None],
            jnp.full((6, feature_width), row_sum),
        ],
        0,
    )
    late = sum_all(late, skip_y=True)
    numbers = everything[2 * col_count]
    vector_sum = everything[2 * col_count + 1 : 2 * col_count + 1 + vector_grad.shape[0]]
    loss_sum = numbers[row_count + 5]
    square_total = numbers[row_count + 6 : row_count + 6 + 3 * layer_count]
    matrices = (table[None], attn_in, attn_out, mlp_in, mlp_out)
    col_states = (table_cols[None], attn_in_cols, attn_out_cols, mlp_in_cols, mlp_out_cols)
    row_totals = [rows_dev * n_group] + [weight.shape[1] * n_group for weight in matrices[1:]]
    shares = jnp.concatenate(
        [
            jnp.full((rows.shape[0], 1), (1.0 - DECAY) / row_total, jnp.float32)
            for rows, row_total in zip(col_rows, row_totals[1:])
        ],
        0,
    )
    old_cols = jnp.concatenate([state.reshape(-1, feature_width) for state in col_states[1:]], 0)
    new_cols = DECAY * old_cols + shares * everything[:col_count]
    ratios = jnp.sum(everything[col_count : 2 * col_count] / new_cols, -1)
    cols_new = []
    new_weights = []
    sizes_rms = []
    col_at = 0
    row_at = 0
    for matrix_at in range(5):
        weight, renewed, col_state = matrices[matrix_at], rows_new[matrix_at], col_states[matrix_at]
        if matrix_at == 0:
            renewed_cols = DECAY * col_state + (1.0 - DECAY) / row_totals[0] * late[:1]
            row_mean = late[2, :1] / row_totals[0]
            clip_total = jnp.sum(row_mean * jnp.sum(late[1:2] / renewed_cols, -1))
        else:
            stack_count = weight.shape[0]
            height = col_rows[matrix_at - 1].shape[0]
            renewed_cols = new_cols[col_at : col_at + height].reshape(col_state.shape)
            row_mean = numbers[row_at : row_at + stack_count] / row_totals[matrix_at]
            row_at += stack_count
            ratio = jnp.sum(ratios[col_at : col_at + height].reshape(stack_count, -1), -1)
            col_at += height
            clip_total = jnp.sum(row_mean * ratio)
        entries = weight.size * n_group
        update_rms = jnp.sqrt(clip_total / entries)
        weight_rms = jnp.sqrt(numbers[row_count + matrix_at] / entries)
        step_scale = RATE * jnp.maximum(EPS_SCALE, weight_rms) / jnp.maximum(1.0, update_rms / CLIP)
        cols_new.append(renewed_cols)
        sizes_rms.append(update_rms)
        if matrix_at == 0:
            table_sum, table_new, table_copy = update_table(
                core_at.astype(jnp.int32).reshape(1),
                step_scale.reshape(1),
                table_part,
                table_away,
                part_renewed,
                away_renewed,
                renewed_cols / row_mean[0],
                table,
            )
            new_weights.append(table_new)
            continue
        second_moment = renewed[:, :, None] * renewed_cols[:, None, :] / row_mean[:, None, None]
        update = summed[matrix_at] * lax.rsqrt(second_moment)
        new_weights.append(weight - step_scale * update)
    vector_state_new = DECAY * vector_state + (1.0 - DECAY) * (vector_sum * vector_sum + EPS_SQUARE)
    vector_update = vector_sum * lax.rsqrt(vector_state_new)
    vector_rms = jnp.sqrt(jnp.mean(vector_update * vector_update))
    vector_scale = (
        RATE
        * jnp.maximum(EPS_SCALE, jnp.sqrt(jnp.mean(vectors * vectors)))
        / jnp.maximum(1.0, vector_rms / CLIP)
    )
    vectors_new = vectors - vector_scale * vector_update
    sizes_rms.append(vector_rms)
    norms = jnp.concatenate([jnp.sqrt(square_total / total_tokens), jnp.stack(sizes_rms)])
    return (
        loss_sum,
        norms,
        table_sum,
        rows_new[0][0],
        cols_new[0][0],
        table_new,
        table_copy,
        summed[1],
        rows_new[1],
        cols_new[1],
        new_weights[1],
        new_weights[1].astype(jnp.bfloat16),
        summed[2],
        rows_new[2],
        cols_new[2],
        new_weights[2],
        new_weights[2].astype(jnp.bfloat16),
        summed[3],
        rows_new[3],
        cols_new[3],
        new_weights[3],
        new_weights[3].astype(jnp.bfloat16),
        summed[4],
        rows_new[4],
        cols_new[4],
        new_weights[4],
        new_weights[4].astype(jnp.bfloat16),
        vector_sum,
        vector_state_new,
        vectors_new,
    )


def solution(mesh):
    return jax.shard_map(
        body,
        mesh=mesh,
        in_specs=(
            P(),
            P(),
            P(),
            P(),
            P(("seq", "fsdp"), None),
            P(None, ("seq", "fsdp"), None),
            P(None, ("seq", "fsdp"), None),
            P(None, ("seq", "fsdp"), None),
            P(None, ("seq", "fsdp"), None),
            P(),
            P(("seq", "fsdp")),
            P(),
            P(None, ("seq", "fsdp")),
            P(),
            P(None, ("seq", "fsdp")),
            P(),
            P(None, ("seq", "fsdp")),
            P(),
            P(None, ("seq", "fsdp")),
            P(),
            P(),
        ),
        out_specs=(
            P(),
            P(),
            P(("seq", "fsdp"), None),
            P(("seq", "fsdp")),
            P(),
            P(("seq", "fsdp"), None),
            P(("seq", "fsdp"), None),
            P(None, ("seq", "fsdp"), None),
            P(None, ("seq", "fsdp")),
            P(),
            P(None, ("seq", "fsdp"), None),
            P(None, ("seq", "fsdp"), None),
            P(None, ("seq", "fsdp"), None),
            P(None, ("seq", "fsdp")),
            P(),
            P(None, ("seq", "fsdp"), None),
            P(None, ("seq", "fsdp"), None),
            P(None, ("seq", "fsdp"), None),
            P(None, ("seq", "fsdp")),
            P(),
            P(None, ("seq", "fsdp"), None),
            P(None, ("seq", "fsdp"), None),
            P(None, ("seq", "fsdp"), None),
            P(None, ("seq", "fsdp")),
            P(),
            P(None, ("seq", "fsdp"), None),
            P(None, ("seq", "fsdp"), None),
            P(),
            P(),
            P(),
        ),
        check_vma=False,
    )
```
